32 devices in a mesh: depth: 2 (over x), xy: 16 (over z, y, core).
Axes of the slice: x: 2, y: 2, z: 4, core: 2. Of those that a mesh axis runs over, the one named last changes fastest.
Arguments:
- surface_data: float32 [2, 2, 256, 2048], P(None, None, 'xy'), may hold values from -6 to 6
- frequencies: float32 [2], replicated, may hold values from 1 to 4
- coefficients: float32 [2, 2, 15], replicated, may hold values from -1 to 1
- slowness: float32 [4, 256, 2048], P('depth', 'xy'), may hold values from 0.4 to 1.2
- perturbation: float32 [4, 256, 2048], P('depth', 'xy'), may hold values from -6 to 6
Outputs:
- gradient: float32 [4, 256, 2048], P('depth', 'xy')
- image_field: float32 [4, 256, 2048], P('depth', 'xy')
The draws below stay inside these ranges and needn't reach their ends.
All inputs are finite; a program needn't handle non-finite values.
Results may differ from the reference program's by a relative error of at most 0.0001.
Values sent between devices are 32-bit elements; how exact they have to be, the bound alone decides.
No kernel may reach another device: no remote copies, remote signals or barrier semaphores. Data moves between devices by JAX's collectives and lax.ppermute only.
A program may use at most 64 MiB of HBM per device.

```python
import math
import jax
import jax.numpy as jnp
from jax import lax

FREQS = 2
NY = 2048
STEPS = 2
TAPS = 15
NX = 256
NZ = 4
N_DEPTH = 2


def bessel_terms(value):
    square = value * value
    zeroth = 1.0 - square / 4.0 + square * square / 64.0 - square * square * square / 2304.0 + square * square * square * square / 147456.0
    first = value * (0.5 - square / 16.0 + square * square / 384.0 - square * square * square / 18432.0)
    second = square * (0.125 - square / 96.0 + square * square / 3072.0 - square * square * square / 184320.0)
    return (zeroth, first, second)


def draw_coefficients(key, part):
    key = jax.random.fold_in(key, 11)
    key_rows, key_cols, key_turn, key_damp = jax.random.split(key, 4)
    row_spread = jax.random.uniform(key_rows, (FREQS,), jnp.float32, 1.1, 1.3)
    col_spread = jax.random.uniform(key_cols, (FREQS,), jnp.float32, 0.3, 0.5)
    damping = jax.random.uniform(key_damp, (FREQS,), jnp.float32, 0.88, 0.95)
    turns = jax.random.uniform(key_turn, (FREQS, 3), jnp.float32, -jnp.pi, jnp.pi)
    tap_index = jnp.arange(TAPS)
    row_shift = (tap_index // 3 - 2).astype(jnp.float32)[None, :]
    col_shift = (tap_index % 3 - 1).astype(jnp.float32)[None, :]
    row_reach = jnp.abs(row_shift)
    col_reach = jnp.abs(col_shift)
    row_zero, row_one, row_two = bessel_terms(row_spread)
    col_zero, col_one, unused_two = bessel_terms(col_spread)
    row_size = jnp.where(row_reach == 0.0, row_zero[:, None], jnp.where(row_reach == 1.0, row_one[:, None], row_two[:, None]))
    col_size = jnp.where(col_reach == 0.0, col_zero[:, None], col_one[:, None])
    magnitude = damping[:, None] * row_size * col_size
    angles = turns[:, 0:1] + (row_reach + col_reach) * (0.5 * jnp.pi) + row_shift * turns[:, 1:2] + col_shift * turns[:, 2:3]
    return jnp.stack([magnitude * jnp.cos(angles), magnitude * jnp.sin(angles)], axis=1)


def shard_levels(stream_key, extent, cuts, low, top_value):
    factor_of = 1.0
    for dim, blocks in cuts:
        steps = jax.random.uniform(jax.random.fold_in(jax.random.fold_in(stream_key, 6), dim), (blocks,), jnp.float32, low / len(cuts), top_value / len(cuts))
        factor_of = factor_of * jnp.repeat(jnp.exp(steps), extent[dim] // blocks).reshape((-1,) + (1,) * (len(extent) - 1 - dim))
    return factor_of


def noise(own_key, extent, width, most, cuts=(), kind=jnp.bfloat16):
    drawn = width * jax.random.normal(own_key, extent, jnp.float32)
    if cuts:
        drawn = drawn * shard_levels(own_key, extent, cuts, -0.22, 0.18)
    return jnp.clip(drawn, -most, most).astype(kind)


def setup_inputs(seed: int = 0) -> dict:
    keys = jax.random.split(jax.random.key(seed), 6)
    return {
        "surface_data": noise(keys[0], (FREQS, 2, NX, NY), 1.0, 6.0, ((2, 16),), jnp.float32),
        "frequencies": jnp.clip(jnp.exp(jax.random.uniform(keys[1], (FREQS,), jnp.float32, math.log(1.0), math.log(4.0))), 1.0, 4.0),
        "coefficients": draw_coefficients(jax.random.fold_in(keys[5], 71), 0),
        "slowness": jnp.clip(0.4 + 0.800000042 * jax.random.uniform(keys[3], (NZ, NX, NY), jnp.float32) ** shard_levels(keys[3], (NZ, NX, NY), ((0, 2), (1, 16)), -0.2, 0.2), 0.4, 1.2),
        "perturbation": noise(keys[4], (NZ, NX, NY), 1.0, 6.0, ((0, 2), (1, 16)), jnp.float32),
    }


layer_thickness = 0.5


def apply_stencil(extended, tap_re, tap_im):
    out_rows = extended.shape[2] - 4
    col_count = extended.shape[3]
    padded = jnp.pad(extended, ((0, 0), (0, 0), (0, 0), (1, 1)))
    acc_re = jnp.zeros((extended.shape[0], out_rows, col_count), jnp.float32)
    acc_im = jnp.zeros((extended.shape[0], out_rows, col_count), jnp.float32)
    for row_off in range(5):
        for col_off in range(3):
            tap_index = row_off * 3 + col_off
            part_re = padded[:, 0, row_off:row_off + out_rows, col_off:col_off + col_count]
            part_im = padded[:, 1, row_off:row_off + out_rows, col_off:col_off + col_count]
            weight_re = tap_re[:, tap_index][:, None, None]
            weight_im = tap_im[:, tap_index][:, None, None]
            acc_re = acc_re + weight_re * part_re - weight_im * part_im
            acc_im = acc_im + weight_re * part_im + weight_im * part_re
    return acc_re, acc_im


def adjoint_stencil(extended, tap_re, tap_im):
    out_rows = extended.shape[2] - 4
    col_count = extended.shape[3]
    padded = jnp.pad(extended, ((0, 0), (0, 0), (0, 0), (1, 1)))
    acc_re = jnp.zeros((extended.shape[0], out_rows, col_count), jnp.float32)
    acc_im = jnp.zeros((extended.shape[0], out_rows, col_count), jnp.float32)
    for row_off in range(5):
        for col_off in range(3):
            tap_index = row_off * 3 + col_off
            row_from = 4 - row_off
            col_from = 2 - col_off
            part_re = padded[:, 0, row_from:row_from + out_rows, col_from:col_from + col_count]
            part_im = padded[:, 1, row_from:row_from + out_rows, col_from:col_from + col_count]
            weight_re = tap_re[:, tap_index][:, None, None]
            weight_im = tap_im[:, tap_index][:, None, None]
            acc_re = acc_re + weight_re * part_re + weight_im * part_im
            acc_im = acc_im + weight_re * part_im - weight_im * part_re
    return acc_re, acc_im


def phase_parts(freqs, slow_plane):
    angle = freqs[:, None, None] * layer_thickness * slow_plane[None]
    return jnp.cos(angle), jnp.sin(angle)


def reference(surface_data, frequencies, coefficients, slowness, perturbation):
    tap_re = coefficients[:, 0]
    tap_im = coefficients[:, 1]

    def advance(wavefield, slow_plane):
        extended = jnp.pad(wavefield, ((0, 0), (0, 0), (2, 2), (0, 0)))
        acc_re, acc_im = apply_stencil(extended, tap_re, tap_im)
        phase_re, phase_im = phase_parts(frequencies, slow_plane)
        next_re = phase_re * acc_re - phase_im * acc_im
        next_im = phase_re * acc_im + phase_im * acc_re
        next_field = jnp.stack([next_re, next_im], axis=1)
        image_part = jnp.sum(next_re * next_re + next_im * next_im, axis=0) / FREQS
        return next_field, (next_field, image_part)

    slow_blocks = slowness.reshape(N_DEPTH, STEPS, NX, NY)
    pert_blocks = perturbation.reshape(N_DEPTH, STEPS, NX, NY)

    def section(wavefield, slow_block):
        bottom, (states, images) = lax.scan(advance, wavefield, slow_block)
        return bottom, (wavefield, images)

    unused, (tops, images) = lax.scan(section, surface_data, slow_blocks)
    image_field = images.reshape(NZ, NX, NY)

    def retreat(adjoint, inputs):
        state, slow_plane, pert_plane = inputs
        wave_re = state[:, 0]
        wave_im = state[:, 1]
        grad_re = adjoint[:, 0] + 2.0 * pert_plane * wave_re
        grad_im = adjoint[:, 1] + 2.0 * pert_plane * wave_im
        gradient_part = layer_thickness / FREQS * jnp.sum(frequencies[:, None, None] * (grad_im * wave_re - grad_re * wave_im), axis=0)
        phase_re, phase_im = phase_parts(frequencies, slow_plane)
        back_re = phase_re * grad_re + phase_im * grad_im
        back_im = phase_re * grad_im - phase_im * grad_re
        extended = jnp.pad(jnp.stack([back_re, back_im], axis=1), ((0, 0), (0, 0), (2, 2), (0, 0)))
        acc_re, acc_im = adjoint_stencil(extended, tap_re, tap_im)
        return jnp.stack([acc_re, acc_im], axis=1), gradient_part

    def back_section(adjoint, inputs):
        top_field, slow_block, pert_block = inputs
        unused_bottom, (states, unused_images) = lax.scan(advance, top_field, slow_block)
        adjoint, parts = lax.scan(retreat, adjoint, (states, slow_block, pert_block), reverse=True)
        return adjoint, parts

    start = jnp.zeros_like(surface_data)
    unused_top, gradients = lax.scan(back_section, start, (tops, slow_blocks, pert_blocks), reverse=True)
    return gradients.reshape(NZ, NX, NY), image_field
```

```python
import numpy as np
import jax
import jax.numpy as jnp
from jax import lax
from jax.experimental import pallas as pl
from jax.experimental.pallas import tpu as pltpu
from jax.sharding import PartitionSpec as P

layer_thickness = 0.5


def extended_2(cells, sides, width):
    for axis, dim in sides:
        count = lax.axis_size(axis)
        ends = count - 1
        head = lax.slice_in_dim(cells, 0, width, axis=dim)
        tail = lax.slice_in_dim(cells, cells.shape[dim] - width, cells.shape[dim], axis=dim)
        cells = jnp.concatenate(
            [
                lax.ppermute(tail, axis, [(i, (i + 1) % count) for i in range(ends)]),
                cells,
                lax.ppermute(head, axis, [((i + 1) % count, i) for i in range(ends)]),
            ],
            axis=dim,
        )
    return cells


def shifted(value, axis, steps):
    count = lax.axis_size(axis)
    initial, last = (max(0, -steps), min(count, count - steps))
    return lax.ppermute(value, axis, [(source, source + steps) for source in range(initial, last)])


def apply_stencil(extended, tap_re, tap_im):
    out_rows = extended.shape[2] - 4
    col_count = extended.shape[3]
    padded = jnp.pad(extended, ((0, 0), (0, 0), (0, 0), (1, 1)))
    acc_re = jnp.zeros((extended.shape[0], out_rows, col_count), jnp.float32)
    acc_im = jnp.zeros((extended.shape[0], out_rows, col_count), jnp.float32)
    for row_off in range(5):
        for col_off in range(3):
            tap_index = row_off * 3 + col_off
            part_re = padded[:, 0, row_off : row_off + out_rows, col_off : col_off + col_count]
            part_im = padded[:, 1, row_off : row_off + out_rows, col_off : col_off + col_count]
            weight_re = tap_re[:, tap_index][:, None, None]
            weight_im = tap_im[:, tap_index][:, None, None]
            acc_re = acc_re + weight_re * part_re - weight_im * part_im
            acc_im = acc_im + weight_re * part_im + weight_im * part_re
    return (acc_re, acc_im)


def adjoint_stencil(extended, tap_re, tap_im):
    out_rows = extended.shape[2] - 4
    col_count = extended.shape[3]
    padded = jnp.pad(extended, ((0, 0), (0, 0), (0, 0), (1, 1)))
    acc_re = jnp.zeros((extended.shape[0], out_rows, col_count), jnp.float32)
    acc_im = jnp.zeros((extended.shape[0], out_rows, col_count), jnp.float32)
    for row_off in range(5):
        for col_off in range(3):
            tap_index = row_off * 3 + col_off
            row_from = 4 - row_off
            col_from = 2 - col_off
            part_re = padded[:, 0, row_from : row_from + out_rows, col_from : col_from + col_count]
            part_im = padded[:, 1, row_from : row_from + out_rows, col_from : col_from + col_count]
            weight_re = tap_re[:, tap_index][:, None, None]
            weight_im = tap_im[:, tap_index][:, None, None]
            acc_re = acc_re + weight_re * part_re + weight_im * part_im
            acc_im = acc_im + weight_re * part_im - weight_im * part_re
    return (acc_re, acc_im)


def phase_parts(freqs, slow_plane):
    angle = freqs[:, None, None] * layer_thickness * slow_plane[None]
    return (jnp.cos(angle), jnp.sin(angle))


def forward_steps(wavefield, freqs, taps, slowness, freq_total):
    tap_re = taps[:, 0]
    tap_im = taps[:, 1]
    step_count = slowness.shape[0]
    states = []
    current = wavefield
    for level in range(step_count):
        extended = extended_2(current, (("xy", 2),), 2)
        acc_re, acc_im = apply_stencil(extended, tap_re, tap_im)
        phase_re, phase_im = phase_parts(freqs, slowness[level])
        next_re = phase_re * acc_re - phase_im * acc_im
        next_im = phase_re * acc_im + phase_im * acc_re
        current = jnp.stack([next_re, next_im], axis=1)
        states.append(current)
    stacked = jnp.stack(states, axis=1)
    image_part = (
        jnp.sum(stacked[:, :, 0] * stacked[:, :, 0] + stacked[:, :, 1] * stacked[:, :, 1], axis=0)
        / freq_total
    )
    return (stacked, states[-1], image_part)


def backward_steps(adjoint, states, freqs, taps, slowness, perturbation, freq_total):
    tap_re = taps[:, 0]
    tap_im = taps[:, 1]
    step_count = slowness.shape[0]
    parts = [None] * step_count
    for level in reversed(range(step_count)):
        wave_re = states[:, level, 0]
        wave_im = states[:, level, 1]
        grad_re = adjoint[:, 0] + 2.0 * perturbation[level] * wave_re
        grad_im = adjoint[:, 1] + 2.0 * perturbation[level] * wave_im
        parts[level] = (
            layer_thickness
            / freq_total
            * jnp.sum(freqs[:, None, None] * (grad_im * wave_re - grad_re * wave_im), axis=0)
        )
        phase_re, phase_im = phase_parts(freqs, slowness[level])
        back_re = phase_re * grad_re + phase_im * grad_im
        back_im = phase_re * grad_im - phase_im * grad_re
        extended = extended_2(jnp.stack([back_re, back_im], axis=1), (("xy", 2),), 2)
        acc_re, acc_im = adjoint_stencil(extended, tap_re, tap_im)
        adjoint = jnp.stack([acc_re, acc_im], axis=1)
    return (adjoint, jnp.stack(parts, axis=0))


def on_device(surface_data, frequencies, coefficients, slowness, perturbation):
    freq_count = frequencies.shape[0]
    step_count = slowness.shape[0]
    row_count = slowness.shape[1]
    col_count = slowness.shape[2]
    layers = lax.axis_size("depth")
    depth_index = lax.axis_index("depth")
    stored_zero = jnp.zeros((freq_count, step_count, 2, row_count, col_count), jnp.float32)
    plane_zero = jnp.zeros((step_count, row_count, col_count), jnp.float32)
    start = jnp.where(depth_index == 0, surface_data, jnp.zeros_like(surface_data))

    def forward_segment(segment_no, carry):
        current, stored, image_sum = carry
        states, bottom, image_part = forward_steps(
            current, frequencies, coefficients, slowness, freq_count
        )
        chosen = depth_index == segment_no
        stored = jnp.where(chosen, states, stored)
        image_sum = jnp.where(chosen, image_part, image_sum)
        current = shifted(bottom, "depth", 1)
        return (current, stored, image_sum)

    unused_field, stored, image_field = lax.fori_loop(
        0, layers, forward_segment, (start, stored_zero, plane_zero)
    )

    def backward_segment(segment_no, carry):
        adjoint, gradient_sum = carry
        top_field, parts = backward_steps(
            adjoint, stored, frequencies, coefficients, slowness, perturbation, freq_count
        )
        gradient_sum = jnp.where(depth_index == layers - 1 - segment_no, parts, gradient_sum)
        adjoint = shifted(top_field, "depth", -1)
        return (adjoint, gradient_sum)

    adjoint_zero = jnp.zeros_like(surface_data)
    unused_adjoint, gradient = lax.fori_loop(
        0, layers, backward_segment, (adjoint_zero, plane_zero)
    )
    return (gradient, image_field)


ROWS = 16
HALO_TILES = 4
LANES = 128

sin_terms = (0.999999999, -0.1666666575, 0.00833331893, -0.0001984042124, 2.753344554e-06, -2.470543221e-08, 1.352854445e-10)
cos_terms = (0.9999999859, -0.4999998648, 0.0416664545, -0.001388763794, 2.476635379e-05, -2.704470886e-07, 1.712096229e-09)


def window_rows():
    rows = list(range(ROWS))
    for group in range(HALO_TILES):
        above = [-4 * (group + 1) + s for s in range(4)]
        below = [ROWS + 4 * group + s for s in range(4)]
        rows += below + above if group % 2 == 0 else above + below
    return np.array(rows, np.int32)


def band_matrices(coefficients, out_tiles, in_tiles, adjoint, first_row, plane_rows):
    rows = window_rows()
    m = np.arange(48 * out_tiles)
    k = np.arange(48 * in_tiles)
    row_m = rows[m // 48 * 8 + m % 8]
    row_k = rows[k // 48 * 8 + k % 8]
    plane_m = (m // 8) % 2
    plane_k = (k // 8) % 2
    part_k = (k // 16) % 3
    tap_re = coefficients[:, 0].reshape(-1, 5, 3)
    tap_im = coefficients[:, 1].reshape(-1, 5, 3)
    if adjoint:
        tap_re = tap_re[:, ::-1, ::-1]
        tap_im = -tap_im[:, ::-1, ::-1]

    def over_rows(taps):
        wide = jnp.broadcast_to(taps[:, :, None, :, None], taps.shape[:2] + (out_tiles, 3, 16))
        return wide.reshape(taps.shape[:2] + (48 * out_tiles,))

    re_m = over_rows(tap_re)
    im_m = over_rows(tap_im) * jnp.asarray(np.where(plane_m == 0, -1.0, 1.0), jnp.float32)
    offset = jnp.asarray(row_k)[None, :] - jnp.asarray(row_m)[:, None]
    same = jnp.asarray(plane_m)[:, None] == jnp.asarray(plane_k)[None, :]
    total = 0.0
    for a in range(5):
        weight = jnp.where(same[None], re_m[:, a, :, None], im_m[:, a, :, None])
        total = total + jnp.where((offset == a - 2)[None], weight, 0.0)
    place = jnp.asarray(row_m) + first_row
    inside = (place >= 0) & (place < plane_rows)
    total = jnp.where(inside[None, :, None], total, 0.0)
    high = lax.reduce_precision(total, 8, 7)
    low = total - high
    return jnp.where(jnp.asarray(part_k == 1)[None, None], low, high).astype(jnp.bfloat16)


def pack_kernel(layers, width, step, surf, slow, pert, cross, chip, bulk, cross_far, chip_far):
    depth = lax.axis_index("depth")
    place = lax.axis_index("xy")
    near = pl.ds(pl.multiple_of(depth * step, LANES), width)
    far = pl.ds(pl.multiple_of((1 - depth) * step, LANES), width)
    row = lax.broadcasted_iota(jnp.int32, (8, width), 0)

    def edge_rows(down, lanes, put):
        inner, outer = (1, 0) if down else (0, 1)

        def tile(ref, level, index):
            return ref[level, 8 * index : 8 * index + 8, lanes]

        @pl.when(depth == 0)
        def _():
            put(0, tile(slow, 0, inner))
            put(1, tile(slow, 1, inner))
            turned = pltpu.roll(tile(slow, 1, outer), 4, 0)
            if down:
                extra = jnp.where(row < 2, pltpu.roll(tile(pert, 1, inner), 2, 0), turned)
                put(2, jnp.where(row < 4, extra, tile(slow, 0, outer)))
            else:
                extra = jnp.where(row >= 6, pltpu.roll(tile(pert, 1, inner), 6, 0), turned)
                put(2, jnp.where(row < 4, tile(slow, 0, outer), extra))

        @pl.when(depth == 1)
        def _():
            put(0, tile(slow, 0, inner))
            put(1, tile(pert, 1, inner))
            put(2, tile(pert, 0, inner))

    def into(ref, base):
        def put(index, value):
            ref[base + index] = value

        return put

    for f in range(2):
        for part in range(2):
            for index in range(2):
                value = surf[f, part, 8 * index : 8 * index + 8, near]
                cross[4 * f + 2 * part + index] = value
                chip[4 * f + 2 * part + index] = value
    for level in range(2):
        for index in range(2):
            bulk[2 * level + index] = slow[level, 8 * index : 8 * index + 8, far]
            bulk[4 + 2 * level + index] = pert[level, 8 * index : 8 * index + 8, far]
    for parity in range(2):

        @pl.when(lax.rem(place, 2) == parity)
        def _():
            edge_rows(parity == 0, near, into(chip, 8))
            edge_rows(parity == 0, far, into(chip_far, 0))
            edge_rows(parity == 1, near, into(cross, 8))
            edge_rows(parity == 1, far, into(cross_far, 0))


def phase(angle):
    square = angle * angle
    cosine = cos_terms[-1]
    sine = sin_terms[-1]
    for term in cos_terms[-2::-1]:
        cosine = cosine * square + term
    for term in sin_terms[-2::-1]:
        sine = sine * square + term
    return cosine, sine * angle


def sweep_kernel(
    width, step, freqs, bands, back_bands, surf, slow, pert, cross, chip, bulk, cross_far, chip_far,
    gradient, image, theirs, slow_win, pert_win, operand, phases, fields, image_win, grad_win,
):
    depth = lax.axis_index("depth")
    place = lax.axis_index("xy")
    half = width - LANES
    near = pl.ds(pl.multiple_of(depth * step, LANES), width)
    upper = lax.broadcasted_iota(jnp.int32, (8, width), 0) < 4
    row = lax.broadcasted_iota(jnp.int32, (8, width), 0)
    lane = lax.broadcasted_iota(jnp.int32, (16, width), 1)
    even = lax.rem(place, 2) == 0

    def sides(cross_tile, chip_tile):
        return jnp.where(even, cross_tile, chip_tile), jnp.where(even, chip_tile, cross_tile)

    for own in range(2):

        @pl.when(depth == own)
        def _():
            for level in range(2):
                for index in range(2):
                    rows = slice(8 * index, 8 * index + 8)
                    slow_win[2 * own + level, index] = slow[level, rows, near]
                    pert_win[2 * own + level, index] = pert[level, rows, near]
                    slow_win[2 * (1 - own) + level, index] = bulk[2 * level + index]
                    pert_win[2 * (1 - own) + level, index] = bulk[4 + 2 * level + index]
            first = (cross, chip, 8) if own == 0 else (cross_far, chip_far, 0)
            second = (cross, chip, 8) if own == 1 else (cross_far, chip_far, 0)
            above, below = zip(*[sides(first[0][first[2] + t], first[1][first[2] + t]) for t in range(3)])
            for level in range(2):
                slow_win[level, 2] = jnp.where(upper, below[level], above[level])
                slow_win[level, 3] = jnp.where(upper, above[level], below[level])
            slow_win[0, 4] = jnp.where(upper, below[2], above[2])
            slow_win[1, 4] = pltpu.roll(jnp.where(upper, above[2], below[2]), 4, 0)
            pert_win[1, 2] = jnp.where(
                row < 2, pltpu.roll(below[2], 2, 0), jnp.where(row >= 6, pltpu.roll(above[2], 6, 0), 0.0)
            )
            above, below = zip(*[sides(second[0][second[2] + t], second[1][second[2] + t]) for t in range(3)])
            slow_win[2, 2] = jnp.where(upper, below[0], above[0])
            slow_win[2, 3] = jnp.where(upper, above[0], below[0])
            pert_win[3, 2] = jnp.where(upper, below[1], above[1])
            pert_win[3, 3] = jnp.where(upper, above[1], below[1])
            pert_win[2, 2] = jnp.where(upper, below[2], above[2])

    def store_operand(f, tile, value):
        high = value.astype(jnp.bfloat16)
        low = (value - high.astype(jnp.float32)).astype(jnp.bfloat16)
        base = 48 * tile
        operand[f, base : base + 16] = high
        operand[f, base + 16 : base + 32] = high
        operand[f, base + 32 : base + 48] = low

    def stencil(f, matrix, out_tiles, in_tiles):
        product = jnp.dot(
            matrix[f, : 48 * out_tiles, : 48 * in_tiles],
            operand[f, : 48 * in_tiles],
            preferred_element_type=jnp.float32,
        )
        result = []
        for tile in range(out_tiles):
            base = 48 * tile
            left = pltpu.roll(product[base : base + 16], 1, 1)
            right = pltpu.roll(product[base + 32 : base + 48], width - 1, 1)
            left = jnp.where(lane == 0, 0.0, left)
            right = jnp.where(lane == width - 1, 0.0, right)
            result.append(product[base + 16 : base + 32] + left + right)
        return result

    for f in range(2):
        planes = []
        for part in range(2):
            at = 4 * f + 2 * part
            above, below = zip(*[sides(cross[at + t], chip[at + t]) for t in range(2)])
            planes.append(
                [
                    surf[f, part, 0:8, near],
                    surf[f, part, 8:16, near],
                    jnp.where(upper, below[0], above[1]),
                    jnp.where(upper, above[1], below[0]),
                    jnp.where(upper, below[1], above[0]),
                    jnp.where(upper, above[0], below[1]),
                ]
            )
        for tile in range(6):
            store_operand(f, tile, jnp.concatenate([planes[0][tile], planes[1][tile]], axis=0))

    def add_image(f, level, tile, re, im):
        part = (re * re + im * im) * 0.5
        image_win[level, tile] = part if f == 0 else image_win[level, tile] + part

    def add_gradient(f, level, tile, w_re, w_im, u_re, u_im):
        part = (0.25 * freqs[f]) * (w_im * u_re - w_re * u_im)
        grad_win[level, tile] = part if f == 0 else grad_win[level, tile] + part

    tiles = (6, 5, 5, 4)
    for level in range(3):
        for f in range(2):
            fields_now = stencil(f, bands, tiles[level + 1], tiles[level])
            for tile, value in enumerate(fields_now):
                cosine, sine = phase(freqs[f] * 0.5 * slow_win[level, tile])
                v_re, v_im = value[:8], value[8:]
                re = cosine * v_re - sine * v_im
                im = cosine * v_im + sine * v_re
                both = jnp.concatenate([re, im], axis=0)
                store_operand(f, tile, both)
                if tile < 3:
                    fields[f, level, tile] = both
                    phases[f, level, tile] = jnp.concatenate([cosine, sine], axis=0)
                if tile < 2:
                    add_image(f, level, tile, re, im)
    for f in range(2):
        for tile, value in enumerate(stencil(f, bands, 4, 4)):
            twice = 2.0 * pert_win[3, tile]
            v_re, v_im = value[:8], value[8:]
            if tile < 2:
                cosine, sine = phase(freqs[f] * 0.5 * slow_win[3, tile])
                re = cosine * v_re - sine * v_im
                im = cosine * v_im + sine * v_re
                add_image(f, 3, tile, re, im)
                add_gradient(f, 3, tile, twice * re, twice * im, re, im)
            store_operand(f, tile, jnp.concatenate([twice * v_re, twice * v_im], axis=0))
    tiles = (2, 3, 3, 4)
    for level in (2, 1, 0):
        for f in range(2):
            for tile, value in enumerate(stencil(f, back_bands, tiles[level], tiles[level + 1])):
                twice = 2.0 * pert_win[level, tile]
                u_re, u_im = fields[f, level, tile, :8], fields[f, level, tile, 8:]
                w_re = value[:8] + twice * u_re
                w_im = value[8:] + twice * u_im
                if tile < 2:
                    add_gradient(f, level, tile, w_re, w_im, u_re, u_im)
                if level > 0:
                    cosine, sine = phases[f, level, tile, :8], phases[f, level, tile, 8:]
                    back = [cosine * w_re + sine * w_im, cosine * w_im - sine * w_re]
                    store_operand(f, tile, jnp.concatenate(back, axis=0))

    for own in range(2):

        @pl.when(depth == own)
        def _():
            inner = slice(own * LANES, own * LANES + half)
            outer = slice(own * half, own * half + half)
            for level in range(2):
                for tile in range(2):
                    rows = slice(8 * tile, 8 * tile + 8)
                    gradient[level, rows, outer] = grad_win[2 * own + level, tile, :, inner]
                    image[level, rows, outer] = image_win[2 * own + level, tile, :, inner]
                    theirs[0, level, rows] = grad_win[2 * (1 - own) + level, tile, :, inner]
                    theirs[1, level, rows] = image_win[2 * (1 - own) + level, tile, :, inner]


def split_columns(surface_data, frequencies, coefficients, slowness, perturbation):
    count = lax.axis_size("xy")
    columns = slowness.shape[2]
    half = columns // 2
    width = half + LANES
    step = half - LANES
    f32 = jnp.float32
    axes = ("depth", "xy")

    def moved(value, other_depth, neighbour):
        pairs = []
        for depth in range(2):
            for place in range(count):
                target = {"chip": place ^ 1, "cross": place + 1 if place % 2 else place - 1, "same": place}[neighbour]
                if 0 <= target < count:
                    layer = 1 - depth if other_depth else depth
                    pairs.append((depth * count + place, layer * count + target))
        return lax.ppermute(value, axes, pairs)

    vmem = pl.BlockSpec(memory_space=pltpu.VMEM)
    smem = pl.BlockSpec(memory_space=pltpu.SMEM)
    tile = lambda n: jax.ShapeDtypeStruct((n, 8, width), f32)
    cross, chip, bulk, cross_far, chip_far = pl.pallas_call(
        lambda *refs: pack_kernel(2, width, step, *refs),
        out_shape=(tile(11), tile(11), tile(8), tile(3), tile(3)),
        in_specs=[vmem] * 3,
        out_specs=(vmem,) * 5,
        compiler_params=pltpu.CompilerParams(vmem_limit_bytes=32 * 2**20),
        name="pack",
    )(surface_data, slowness, perturbation)
    cross = moved(cross, False, "cross")
    bulk = moved(bulk, True, "same")
    cross_far = moved(cross_far, True, "cross")
    chip_far = moved(chip_far, True, "chip")
    chip = moved(chip, False, "chip")

    first_row = lax.axis_index("xy") * ROWS
    bands = band_matrices(coefficients, 5, 6, False, first_row, count * ROWS)
    back_bands = band_matrices(coefficients, 3, 4, True, first_row, count * ROWS)
    own = jax.ShapeDtypeStruct((2, ROWS, columns), f32)
    gradient, image, theirs = pl.pallas_call(
        lambda *refs: sweep_kernel(width, step, *refs),
        out_shape=(own, own, jax.ShapeDtypeStruct((2, 2, ROWS, half), f32)),
        in_specs=[smem] + [vmem] * 10,
        out_specs=(vmem,) * 3,
        scratch_shapes=[
            pltpu.VMEM((4, 5, 8, width), f32),
            pltpu.VMEM((4, 4, 8, width), f32),
            pltpu.VMEM((2, 288, width), jnp.bfloat16),
            pltpu.VMEM((2, 3, 3, 16, width), f32),
            pltpu.VMEM((2, 3, 3, 16, width), f32),
            pltpu.VMEM((4, 2, 8, width), f32),
            pltpu.VMEM((4, 2, 8, width), f32),
        ],
        compiler_params=pltpu.CompilerParams(vmem_limit_bytes=40 * 2**20),
        name="sweep",
    )(
        frequencies, bands, back_bands, surface_data, slowness, perturbation,
        cross, chip, bulk, cross_far, chip_far,
    )
    theirs = moved(theirs, True, "same")
    start = (1 - lax.axis_index("depth")) * half
    gradient = lax.dynamic_update_slice(gradient, theirs[0], (0, 0, start))
    image = lax.dynamic_update_slice(image, theirs[1], (0, 0, start))
    return gradient, image


def on_slice(surface_data, frequencies, coefficients, slowness, perturbation):
    levels, rows, columns = slowness.shape
    fits = (
        lax.axis_size("depth") == 2
        and levels == 2
        and rows == ROWS
        and frequencies.shape[0] == 2
        and lax.axis_size("xy") % 2 == 0
        and columns % (2 * LANES) == 0
        and columns >= 4 * LANES
    )
    plan = split_columns if fits else on_device
    return plan(surface_data, frequencies, coefficients, slowness, perturbation)


def solution(mesh):
    in_specs = (P(None, None, "xy", None), P(), P(), P("depth", "xy", None), P("depth", "xy", None))
    out_specs = (P("depth", "xy", None), P("depth", "xy", None))
    return jax.shard_map(
        on_slice, mesh=mesh, in_specs=in_specs, out_specs=out_specs, check_vma=False
    )
```

```python
import numpy as np
import jax
import jax.numpy as jnp
from jax import lax
from jax.experimental import pallas as pl
from jax.experimental.pallas import tpu as pltpu
from jax.sharding import PartitionSpec as P

layer_thickness = 0.5


def extended_2(cells, sides, width):
    for axis, dim in sides:
        count = lax.axis_size(axis)
        ends = count - 1
        head = lax.slice_in_dim(cells, 0, width, axis=dim)
        tail = lax.slice_in_dim(cells, cells.shape[dim] - width, cells.shape[dim], axis=dim)
        cells = jnp.concatenate(
            [
                lax.ppermute(tail, axis, [(i, (i + 1) % count) for i in range(ends)]),
                cells,
                lax.ppermute(head, axis, [((i + 1) % count, i) for i in range(ends)]),
            ],
            axis=dim,
        )
    return cells


def shifted(value, axis, steps):
    count = lax.axis_size(axis)
    initial, last = (max(0, -steps), min(count, count - steps))
    return lax.ppermute(value, axis, [(source, source + steps) for source in range(initial, last)])


def apply_stencil(extended, tap_re, tap_im):
    out_rows = extended.shape[2] - 4
    col_count = extended.shape[3]
    padded = jnp.pad(extended, ((0, 0), (0, 0), (0, 0), (1, 1)))
    acc_re = jnp.zeros((extended.shape[0], out_rows, col_count), jnp.float32)
    acc_im = jnp.zeros((extended.shape[0], out_rows, col_count), jnp.float32)
    for row_off in range(5):
        for col_off in range(3):
            tap_index = row_off * 3 + col_off
            part_re = padded[:, 0, row_off : row_off + out_rows, col_off : col_off + col_count]
            part_im = padded[:, 1, row_off : row_off + out_rows, col_off : col_off + col_count]
            weight_re = tap_re[:, tap_index][:, None, None]
            weight_im = tap_im[:, tap_index][:, None, None]
            acc_re = acc_re + weight_re * part_re - weight_im * part_im
            acc_im = acc_im + weight_re * part_im + weight_im * part_re
    return (acc_re, acc_im)


def adjoint_stencil(extended, tap_re, tap_im):
    out_rows = extended.shape[2] - 4
    col_count = extended.shape[3]
    padded = jnp.pad(extended, ((0, 0), (0, 0), (0, 0), (1, 1)))
    acc_re = jnp.zeros((extended.shape[0], out_rows, col_count), jnp.float32)
    acc_im = jnp.zeros((extended.shape[0], out_rows, col_count), jnp.float32)
    for row_off in range(5):
        for col_off in range(3):
            tap_index = row_off * 3 + col_off
            row_from = 4 - row_off
            col_from = 2 - col_off
            part_re = padded[:, 0, row_from : row_from + out_rows, col_from : col_from + col_count]
            part_im = padded[:, 1, row_from : row_from + out_rows, col_from : col_from + col_count]
            weight_re = tap_re[:, tap_index][:, None, None]
            weight_im = tap_im[:, tap_index][:, None, None]
            acc_re = acc_re + weight_re * part_re + weight_im * part_im
            acc_im = acc_im + weight_re * part_im - weight_im * part_re
    return (acc_re, acc_im)


def phase_parts(freqs, slow_plane):
    angle = freqs[:, None, None] * layer_thickness * slow_plane[None]
    return (jnp.cos(angle), jnp.sin(angle))


def forward_steps(wavefield, freqs, taps, slowness, freq_total):
    tap_re = taps[:, 0]
    tap_im = taps[:, 1]
    step_count = slowness.shape[0]
    states = []
    current = wavefield
    for level in range(step_count):
        extended = extended_2(current, (("xy", 2),), 2)
        acc_re, acc_im = apply_stencil(extended, tap_re, tap_im)
        phase_re, phase_im = phase_parts(freqs, slowness[level])
        next_re = phase_re * acc_re - phase_im * acc_im
        next_im = phase_re * acc_im + phase_im * acc_re
        current = jnp.stack([next_re, next_im], axis=1)
        states.append(current)
    stacked = jnp.stack(states, axis=1)
    image_part = (
        jnp.sum(stacked[:, :, 0] * stacked[:, :, 0] + stacked[:, :, 1] * stacked[:, :, 1], axis=0)
        / freq_total
    )
    return (stacked, states[-1], image_part)


def backward_steps(adjoint, states, freqs, taps, slowness, perturbation, freq_total):
    tap_re = taps[:, 0]
    tap_im = taps[:, 1]
    step_count = slowness.shape[0]
    parts = [None] * step_count
    for level in reversed(range(step_count)):
        wave_re = states[:, level, 0]
        wave_im = states[:, level, 1]
        grad_re = adjoint[:, 0] + 2.0 * perturbation[level] * wave_re
        grad_im = adjoint[:, 1] + 2.0 * perturbation[level] * wave_im
        parts[level] = (
            layer_thickness
            / freq_total
            * jnp.sum(freqs[:, None, None] * (grad_im * wave_re - grad_re * wave_im), axis=0)
        )
        phase_re, phase_im = phase_parts(freqs, slowness[level])
        back_re = phase_re * grad_re + phase_im * grad_im
        back_im = phase_re * grad_im - phase_im * grad_re
        extended = extended_2(jnp.stack([back_re, back_im], axis=1), (("xy", 2),), 2)
        acc_re, acc_im = adjoint_stencil(extended, tap_re, tap_im)
        adjoint = jnp.stack([acc_re, acc_im], axis=1)
    return (adjoint, jnp.stack(parts, axis=0))


def on_device(surface_data, frequencies, coefficients, slowness, perturbation):
    freq_count = frequencies.shape[0]
    step_count = slowness.shape[0]
    row_count = slowness.shape[1]
    col_count = slowness.shape[2]
    layers = lax.axis_size("depth")
    depth_index = lax.axis_index("depth")
    stored_zero = jnp.zeros((freq_count, step_count, 2, row_count, col_count), jnp.float32)
    plane_zero = jnp.zeros((step_count, row_count, col_count), jnp.float32)
    start = jnp.where(depth_index == 0, surface_data, jnp.zeros_like(surface_data))

    def forward_segment(segment_no, carry):
        current, stored, image_sum = carry
        states, bottom, image_part = forward_steps(
            current, frequencies, coefficients, slowness, freq_count
        )
        chosen = depth_index == segment_no
        stored = jnp.where(chosen, states, stored)
        image_sum = jnp.where(chosen, image_part, image_sum)
        current = shifted(bottom, "depth", 1)
        return (current, stored, image_sum)

    unused_field, stored, image_field = lax.fori_loop(
        0, layers, forward_segment, (start, stored_zero, plane_zero)
    )

    def backward_segment(segment_no, carry):
        adjoint, gradient_sum = carry
        top_field, parts = backward_steps(
            adjoint, stored, frequencies, coefficients, slowness, perturbation, freq_count
        )
        gradient_sum = jnp.where(depth_index == layers - 1 - segment_no, parts, gradient_sum)
        adjoint = shifted(top_field, "depth", -1)
        return (adjoint, gradient_sum)

    adjoint_zero = jnp.zeros_like(surface_data)
    unused_adjoint, gradient = lax.fori_loop(
        0, layers, backward_segment, (adjoint_zero, plane_zero)
    )
    return (gradient, image_field)


ROWS = 16
HALO_TILES = 4
LANES = 128

sin_terms = (0.999999999, -0.1666666575, 0.00833331893, -0.0001984042124, 2.753344554e-06, -2.470543221e-08, 1.352854445e-10)
cos_terms = (0.9999999859, -0.4999998648, 0.0416664545, -0.001388763794, 2.476635379e-05, -2.704470886e-07, 1.712096229e-09)


def window_row(tile, sub):
    group = tile - 2
    above = sub - 4 * (group + 1)
    below = sub + ROWS + 4 * group
    even = jnp.where(sub < 4, below, above - 4)
    odd = jnp.where(sub < 4, above, below - 4)
    halo = jnp.where(lax.rem(tile, 2) == 0, even, odd)
    return jnp.where(tile < 2, 8 * tile + sub, halo)


def band_kernel(plane_rows, taps, bands, back_bands):
    first_row = lax.axis_index("xy") * ROWS

    def fill(ref, adjoint):
        out_tiles = ref.shape[1] // 48
        in_tiles = ref.shape[2] // 48
        shape = (16, ref.shape[2])
        col = lax.broadcasted_iota(jnp.int32, shape, 1)
        sub = lax.broadcasted_iota(jnp.int32, shape, 0)
        tile_k = sum((col >= 48 * t).astype(jnp.int32) for t in range(1, in_tiles))
        row_k = window_row(tile_k, col & 7)
        part_k = (col >> 4) - 3 * tile_k
        plane_k = (col >> 3) & 1
        plane_m = sub >> 3
        same = plane_k == plane_m
        inside_k = (row_k + first_row >= 0) & (row_k + first_row < plane_rows)
        for tile in range(out_tiles):
            row_m = window_row(jnp.full(shape, tile, jnp.int32), sub & 7)
            inside = inside_k & (row_m + first_row >= 0) & (row_m + first_row < plane_rows)
            offset = jnp.where(inside, row_k - row_m, 9)
            hits = [offset == a - 2 for a in range(5)]
            for f in range(ref.shape[0]):
                for b in range(3):
                    total = jnp.zeros(shape, jnp.float32)
                    for a in range(5):
                        tap = 3 * (4 - a) + 2 - b if adjoint else 3 * a + b
                        re = taps[f, 0, tap]
                        im = -taps[f, 1, tap] if adjoint else taps[f, 1, tap]
                        crossed = jnp.where(plane_m == 0, -im, im)
                        total = jnp.where(hits[a], jnp.where(same, re, crossed), total)
                    high = total.astype(jnp.bfloat16)
                    low = total - high.astype(jnp.float32)
                    base = 48 * tile + 16 * b
                    ref[f, base : base + 16] = jnp.where(part_k == 1, low, total).astype(jnp.bfloat16)

    fill(bands, False)
    fill(back_bands, True)


def pack_kernel(
    width, step, surf_in, slow_in, pert_in, cross, chip, bulk, cross_far, chip_far, window, surf, slow, pert, sems
):
    copies = [
        pltpu.make_async_copy(source, target, sems.at[n])
        for n, (source, target) in enumerate(((slow_in, slow), (pert_in, pert), (surf_in, surf)))
    ]
    for copy in copies:
        copy.start()
    for copy in copies:
        copy.wait()
    depth = lax.axis_index("depth")
    place = lax.axis_index("xy")
    near = pl.ds(pl.multiple_of(depth * step, LANES), width)
    far = pl.ds(pl.multiple_of((1 - depth) * step, LANES), width)
    row = lax.broadcasted_iota(jnp.int32, (8, width), 0)

    def edge_rows(down, lanes, put):
        inner, outer = (1, 0) if down else (0, 1)

        def tile(ref, level, index):
            return ref[level, 8 * index : 8 * index + 8, lanes]

        @pl.when(depth == 0)
        def _():
            put(0, tile(slow, 0, inner))
            put(1, tile(slow, 1, inner))
            turned = pltpu.roll(tile(slow, 1, outer), 4, 0)
            if down:
                extra = jnp.where(row < 2, pltpu.roll(tile(pert, 1, inner), 2, 0), turned)
                put(2, jnp.where(row < 4, extra, tile(slow, 0, outer)))
            else:
                extra = jnp.where(row >= 6, pltpu.roll(tile(pert, 1, inner), 6, 0), turned)
                put(2, jnp.where(row < 4, tile(slow, 0, outer), extra))

        @pl.when(depth == 1)
        def _():
            put(0, tile(slow, 0, inner))
            put(1, tile(pert, 1, inner))
            put(2, tile(pert, 0, inner))

    def into(ref, base):
        def put(index, value):
            ref[base + index] = value

        return put

    for f in range(2):
        for part in range(2):
            for index in range(2):
                value = surf[f, part, 8 * index : 8 * index + 8, near]
                cross[4 * f + 2 * part + index] = value
                chip[4 * f + 2 * part + index] = value
                window[4 * f + 2 * part + index] = value
    for level in range(2):
        for index in range(2):
            window[8 + 2 * level + index] = slow[level, 8 * index : 8 * index + 8, near]
            window[12 + 2 * level + index] = pert[level, 8 * index : 8 * index + 8, near]
            bulk[2 * level + index] = slow[level, 8 * index : 8 * index + 8, far]
            bulk[4 + 2 * level + index] = pert[level, 8 * index : 8 * index + 8, far]
    for parity in range(2):

        @pl.when(lax.rem(place, 2) == parity)
        def _():
            edge_rows(parity == 0, near, into(chip, 8))
            edge_rows(parity == 0, far, into(chip_far, 0))
            edge_rows(parity == 1, near, into(cross, 8))
            edge_rows(parity == 1, far, into(cross_far, 0))


def phase(angle):
    square = angle * angle
    cosine = cos_terms[-1]
    sine = sin_terms[-1]
    for term in cos_terms[-2::-1]:
        cosine = cosine * square + term
    for term in sin_terms[-2::-1]:
        sine = sine * square + term
    return cosine, sine * angle


def sweep_kernel(
    width, freqs, bands, back_bands, window, cross, chip, bulk, cross_far, chip_far,
    gradient, image, theirs, slow_win, pert_win, operand, phases, fields, image_win, grad_win,
):
    depth = lax.axis_index("depth")
    place = lax.axis_index("xy")
    half = width - LANES
    upper = lax.broadcasted_iota(jnp.int32, (8, width), 0) < 4
    row = lax.broadcasted_iota(jnp.int32, (8, width), 0)
    lane = lax.broadcasted_iota(jnp.int32, (16, width), 1)
    even = lax.rem(place, 2) == 0

    def sides(cross_tile, chip_tile):
        return jnp.where(even, cross_tile, chip_tile), jnp.where(even, chip_tile, cross_tile)

    for own in range(2):

        @pl.when(depth == own)
        def _():
            for level in range(2):
                for index in range(2):
                    slow_win[2 * own + level, index] = window[8 + 2 * level + index]
                    pert_win[2 * own + level, index] = window[12 + 2 * level + index]
                    slow_win[2 * (1 - own) + level, index] = bulk[2 * level + index]
                    pert_win[2 * (1 - own) + level, index] = bulk[4 + 2 * level + index]
            first = (cross, chip, 8) if own == 0 else (cross_far, chip_far, 0)
            second = (cross, chip, 8) if own == 1 else (cross_far, chip_far, 0)
            above, below = zip(*[sides(first[0][first[2] + t], first[1][first[2] + t]) for t in range(3)])
            for level in range(2):
                slow_win[level, 2] = jnp.where(upper, below[level], above[level])
                slow_win[level, 3] = jnp.where(upper, above[level], below[level])
            slow_win[0, 4] = jnp.where(upper, below[2], above[2])
            slow_win[1, 4] = pltpu.roll(jnp.where(upper, above[2], below[2]), 4, 0)
            pert_win[1, 2] = jnp.where(
                row < 2, pltpu.roll(below[2], 2, 0), jnp.where(row >= 6, pltpu.roll(above[2], 6, 0), 0.0)
            )
            above, below = zip(*[sides(second[0][second[2] + t], second[1][second[2] + t]) for t in range(3)])
            slow_win[2, 2] = jnp.where(upper, below[0], above[0])
            slow_win[2, 3] = jnp.where(upper, above[0], below[0])
            pert_win[3, 2] = jnp.where(upper, below[1], above[1])
            pert_win[3, 3] = jnp.where(upper, above[1], below[1])
            pert_win[2, 2] = jnp.where(upper, below[2], above[2])

    def store_operand(f, tile, value):
        high = value.astype(jnp.bfloat16)
        low = (value - high.astype(jnp.float32)).astype(jnp.bfloat16)
        base = 48 * tile
        operand[f, base : base + 16] = high
        operand[f, base + 16 : base + 32] = high
        operand[f, base + 32 : base + 48] = low

    def stencil(f, matrix, out_tiles, in_tiles):
        product = jnp.dot(
            matrix[f, : 48 * out_tiles, : 48 * in_tiles],
            operand[f, : 48 * in_tiles],
            preferred_element_type=jnp.float32,
        )
        result = []
        for tile in range(out_tiles):
            base = 48 * tile
            left = pltpu.roll(product[base : base + 16], 1, 1)
            right = pltpu.roll(product[base + 32 : base + 48], width - 1, 1)
            left = jnp.where(lane == 0, 0.0, left)
            right = jnp.where(lane == width - 1, 0.0, right)
            result.append(product[base + 16 : base + 32] + left + right)
        return result

    for f in range(2):
        planes = []
        for part in range(2):
            at = 4 * f + 2 * part
            above, below = zip(*[sides(cross[at + t], chip[at + t]) for t in range(2)])
            planes.append(
                [
                    window[at],
                    window[at + 1],
                    jnp.where(upper, below[0], above[1]),
                    jnp.where(upper, above[1], below[0]),
                    jnp.where(upper, below[1], above[0]),
                    jnp.where(upper, above[0], below[1]),
                ]
            )
        for tile in range(6):
            store_operand(f, tile, jnp.concatenate([planes[0][tile], planes[1][tile]], axis=0))

    def add_image(f, level, tile, re, im):
        part = (re * re + im * im) * 0.5
        image_win[level, tile] = part if f == 0 else image_win[level, tile] + part

    def add_gradient(f, level, tile, w_re, w_im, u_re, u_im):
        part = (0.25 * freqs[f]) * (w_im * u_re - w_re * u_im)
        grad_win[level, tile] = part if f == 0 else grad_win[level, tile] + part

    tiles = (6, 5, 5, 4)
    for level in range(3):
        for f in range(2):
            fields_now = stencil(f, bands, tiles[level + 1], tiles[level])
            for tile, value in enumerate(fields_now):
                cosine, sine = phase(freqs[f] * 0.5 * slow_win[level, tile])
                v_re, v_im = value[:8], value[8:]
                re = cosine * v_re - sine * v_im
                im = cosine * v_im + sine * v_re
                both = jnp.concatenate([re, im], axis=0)
                store_operand(f, tile, both)
                if tile < 3:
                    fields[f, level, tile] = both
                    phases[f, level, tile] = jnp.concatenate([cosine, sine], axis=0)
                if tile < 2:
                    add_image(f, level, tile, re, im)
    for f in range(2):
        for tile, value in enumerate(stencil(f, bands, 4, 4)):
            twice = 2.0 * pert_win[3, tile]
            v_re, v_im = value[:8], value[8:]
            if tile < 2:
                cosine, sine = phase(freqs[f] * 0.5 * slow_win[3, tile])
                re = cosine * v_re - sine * v_im
                im = cosine * v_im + sine * v_re
                add_image(f, 3, tile, re, im)
                add_gradient(f, 3, tile, twice * re, twice * im, re, im)
            store_operand(f, tile, jnp.concatenate([twice * v_re, twice * v_im], axis=0))
    tiles = (2, 3, 3, 4)
    for level in (2, 1, 0):
        for f in range(2):
            for tile, value in enumerate(stencil(f, back_bands, tiles[level], tiles[level + 1])):
                twice = 2.0 * pert_win[level, tile]
                u_re, u_im = fields[f, level, tile, :8], fields[f, level, tile, 8:]
                w_re = value[:8] + twice * u_re
                w_im = value[8:] + twice * u_im
                if tile < 2:
                    add_gradient(f, level, tile, w_re, w_im, u_re, u_im)
                if level > 0:
                    cosine, sine = phases[f, level, tile, :8], phases[f, level, tile, 8:]
                    back = [cosine * w_re + sine * w_im, cosine * w_im - sine * w_re]
                    store_operand(f, tile, jnp.concatenate(back, axis=0))

    for own in range(2):

        @pl.when(depth == own)
        def _():
            inner = slice(own * LANES, own * LANES + half)
            outer = slice(own * half, own * half + half)
            for level in range(2):
                for tile in range(2):
                    rows = slice(8 * tile, 8 * tile + 8)
                    gradient[level, rows, outer] = grad_win[2 * own + level, tile, :, inner]
                    image[level, rows, outer] = image_win[2 * own + level, tile, :, inner]
                    theirs[0, level, rows] = grad_win[2 * (1 - own) + level, tile, :, inner]
                    theirs[1, level, rows] = image_win[2 * (1 - own) + level, tile, :, inner]


def split_columns(surface_data, frequencies, coefficients, slowness, perturbation):
    count = lax.axis_size("xy")
    columns = slowness.shape[2]
    half = columns // 2
    width = half + LANES
    step = half - LANES
    f32 = jnp.float32
    axes = ("depth", "xy")

    def moved(value, other_depth, neighbour):
        pairs = []
        for depth in range(2):
            for place in range(count):
                target = {"chip": place ^ 1, "cross": place + 1 if place % 2 else place - 1, "same": place}[neighbour]
                if 0 <= target < count:
                    layer = 1 - depth if other_depth else depth
                    pairs.append((depth * count + place, layer * count + target))
        return lax.ppermute(value, axes, pairs)

    vmem = pl.BlockSpec(memory_space=pltpu.VMEM)
    smem = pl.BlockSpec(memory_space=pltpu.SMEM)
    tile = lambda n: jax.ShapeDtypeStruct((n, 8, width), f32)
    cross, chip, bulk, cross_far, chip_far, window = pl.pallas_call(
        lambda *refs: pack_kernel(width, step, *refs),
        out_shape=(tile(11), tile(11), tile(8), tile(3), tile(3), tile(16)),
        in_specs=[pl.BlockSpec(memory_space=pltpu.HBM)] * 3,
        out_specs=(vmem,) * 6,
        scratch_shapes=[
            pltpu.VMEM(surface_data.shape, f32),
            pltpu.VMEM(slowness.shape, f32),
            pltpu.VMEM(perturbation.shape, f32),
            pltpu.SemaphoreType.DMA((3,)),
        ],
        compiler_params=pltpu.CompilerParams(vmem_limit_bytes=32 * 2**20),
        name="pack",
    )(*(pltpu.with_memory_space_constraint(x, pltpu.HBM) for x in (surface_data, slowness, perturbation)))
    cross = moved(cross, False, "cross")
    bulk = moved(bulk, True, "same")
    cross_far = moved(cross_far, True, "cross")
    chip_far = moved(chip_far, True, "chip")
    chip = moved(chip, False, "chip")

    bands, back_bands = pl.pallas_call(
        lambda *refs: band_kernel(count * ROWS, *refs),
        out_shape=(jax.ShapeDtypeStruct((2, 240, 288), jnp.bfloat16), jax.ShapeDtypeStruct((2, 144, 192), jnp.bfloat16)),
        in_specs=[smem],
        out_specs=(vmem,) * 2,
        compiler_params=pltpu.CompilerParams(vmem_limit_bytes=16 * 2**20),
        name="bands",
    )(coefficients)
    own = jax.ShapeDtypeStruct((2, ROWS, columns), f32)
    gradient, image, theirs = pl.pallas_call(
        lambda *refs: sweep_kernel(width, *refs),
        out_shape=(own, own, jax.ShapeDtypeStruct((2, 2, ROWS, half), f32)),
        in_specs=[smem] + [vmem] * 8,
        out_specs=(vmem,) * 3,
        scratch_shapes=[
            pltpu.VMEM((4, 5, 8, width), f32),
            pltpu.VMEM((4, 4, 8, width), f32),
            pltpu.VMEM((2, 288, width), jnp.bfloat16),
            pltpu.VMEM((2, 3, 3, 16, width), f32),
            pltpu.VMEM((2, 3, 3, 16, width), f32),
            pltpu.VMEM((4, 2, 8, width), f32),
            pltpu.VMEM((4, 2, 8, width), f32),
        ],
        compiler_params=pltpu.CompilerParams(vmem_limit_bytes=40 * 2**20),
        name="sweep",
    )(
        frequencies, bands, back_bands, window, cross, chip, bulk, cross_far, chip_far,
    )
    theirs = moved(theirs, True, "same")
    start = (1 - lax.axis_index("depth")) * half
    gradient = lax.dynamic_update_slice(gradient, theirs[0], (0, 0, start))
    image = lax.dynamic_update_slice(image, theirs[1], (0, 0, start))
    return gradient, image


def on_slice(surface_data, frequencies, coefficients, slowness, perturbation):
    levels, rows, columns = slowness.shape
    fits = (
        lax.axis_size("depth") == 2
        and levels == 2
        and rows == ROWS
        and frequencies.shape[0] == 2
        and lax.axis_size("xy") % 2 == 0
        and columns % (2 * LANES) == 0
        and columns >= 4 * LANES
    )
    plan = split_columns if fits else on_device
    return plan(surface_data, frequencies, coefficients, slowness, perturbation)


def solution(mesh):
    in_specs = (P(None, None, "xy", None), P(), P(), P("depth", "xy", None), P("depth", "xy", None))
    out_specs = (P("depth", "xy", None), P("depth", "xy", None))
    return jax.shard_map(
        on_slice, mesh=mesh, in_specs=in_specs, out_specs=out_specs, check_vma=False
    )
```

```python
import numpy as np
import jax
import jax.numpy as jnp
from jax import lax
from jax.experimental import pallas as pl
from jax.experimental.pallas import tpu as pltpu
from jax.sharding import PartitionSpec as P

layer_thickness = 0.5


def extended_2(cells, sides, width):
    for axis, dim in sides:
        count = lax.axis_size(axis)
        ends = count - 1
        head = lax.slice_in_dim(cells, 0, width, axis=dim)
        tail = lax.slice_in_dim(cells, cells.shape[dim] - width, cells.shape[dim], axis=dim)
        cells = jnp.concatenate(
            [
                lax.ppermute(tail, axis, [(i, (i + 1) % count) for i in range(ends)]),
                cells,
                lax.ppermute(head, axis, [((i + 1) % count, i) for i in range(ends)]),
            ],
            axis=dim,
        )
    return cells


def shifted(value, axis, steps):
    count = lax.axis_size(axis)
    initial, last = (max(0, -steps), min(count, count - steps))
    return lax.ppermute(value, axis, [(source, source + steps) for source in range(initial, last)])


def apply_stencil(extended, tap_re, tap_im):
    out_rows = extended.shape[2] - 4
    col_count = extended.shape[3]
    padded = jnp.pad(extended, ((0, 0), (0, 0), (0, 0), (1, 1)))
    acc_re = jnp.zeros((extended.shape[0], out_rows, col_count), jnp.float32)
    acc_im = jnp.zeros((extended.shape[0], out_rows, col_count), jnp.float32)
    for row_off in range(5):
        for col_off in range(3):
            tap_index = row_off * 3 + col_off
            part_re = padded[:, 0, row_off : row_off + out_rows, col_off : col_off + col_count]
            part_im = padded[:, 1, row_off : row_off + out_rows, col_off : col_off + col_count]
            weight_re = tap_re[:, tap_index][:, None, None]
            weight_im = tap_im[:, tap_index][:, None, None]
            acc_re = acc_re + weight_re * part_re - weight_im * part_im
            acc_im = acc_im + weight_re * part_im + weight_im * part_re
    return (acc_re, acc_im)


def adjoint_stencil(extended, tap_re, tap_im):
    out_rows = extended.shape[2] - 4
    col_count = extended.shape[3]
    padded = jnp.pad(extended, ((0, 0), (0, 0), (0, 0), (1, 1)))
    acc_re = jnp.zeros((extended.shape[0], out_rows, col_count), jnp.float32)
    acc_im = jnp.zeros((extended.shape[0], out_rows, col_count), jnp.float32)
    for row_off in range(5):
        for col_off in range(3):
            tap_index = row_off * 3 + col_off
            row_from = 4 - row_off
            col_from = 2 - col_off
            part_re = padded[:, 0, row_from : row_from + out_rows, col_from : col_from + col_count]
            part_im = padded[:, 1, row_from : row_from + out_rows, col_from : col_from + col_count]
            weight_re = tap_re[:, tap_index][:, None, None]
            weight_im = tap_im[:, tap_index][:, None, None]
            acc_re = acc_re + weight_re * part_re + weight_im * part_im
            acc_im = acc_im + weight_re * part_im - weight_im * part_re
    return (acc_re, acc_im)


def phase_parts(freqs, slow_plane):
    angle = freqs[:, None, None] * layer_thickness * slow_plane[None]
    return (jnp.cos(angle), jnp.sin(angle))


def forward_steps(wavefield, freqs, taps, slowness, freq_total):
    tap_re = taps[:, 0]
    tap_im = taps[:, 1]
    step_count = slowness.shape[0]
    states = []
    current = wavefield
    for level in range(step_count):
        extended = extended_2(current, (("xy", 2),), 2)
        acc_re, acc_im = apply_stencil(extended, tap_re, tap_im)
        phase_re, phase_im = phase_parts(freqs, slowness[level])
        next_re = phase_re * acc_re - phase_im * acc_im
        next_im = phase_re * acc_im + phase_im * acc_re
        current = jnp.stack([next_re, next_im], axis=1)
        states.append(current)
    stacked = jnp.stack(states, axis=1)
    image_part = (
        jnp.sum(stacked[:, :, 0] * stacked[:, :, 0] + stacked[:, :, 1] * stacked[:, :, 1], axis=0)
        / freq_total
    )
    return (stacked, states[-1], image_part)


def backward_steps(adjoint, states, freqs, taps, slowness, perturbation, freq_total):
    tap_re = taps[:, 0]
    tap_im = taps[:, 1]
    step_count = slowness.shape[0]
    parts = [None] * step_count
    for level in reversed(range(step_count)):
        wave_re = states[:, level, 0]
        wave_im = states[:, level, 1]
        grad_re = adjoint[:, 0] + 2.0 * perturbation[level] * wave_re
        grad_im = adjoint[:, 1] + 2.0 * perturbation[level] * wave_im
        parts[level] = (
            layer_thickness
            / freq_total
            * jnp.sum(freqs[:, None, None] * (grad_im * wave_re - grad_re * wave_im), axis=0)
        )
        phase_re, phase_im = phase_parts(freqs, slowness[level])
        back_re = phase_re * grad_re + phase_im * grad_im
        back_im = phase_re * grad_im - phase_im * grad_re
        extended = extended_2(jnp.stack([back_re, back_im], axis=1), (("xy", 2),), 2)
        acc_re, acc_im = adjoint_stencil(extended, tap_re, tap_im)
        adjoint = jnp.stack([acc_re, acc_im], axis=1)
    return (adjoint, jnp.stack(parts, axis=0))


def on_device(surface_data, frequencies, coefficients, slowness, perturbation):
    freq_count = frequencies.shape[0]
    step_count = slowness.shape[0]
    row_count = slowness.shape[1]
    col_count = slowness.shape[2]
    layers = lax.axis_size("depth")
    depth_index = lax.axis_index("depth")
    stored_zero = jnp.zeros((freq_count, step_count, 2, row_count, col_count), jnp.float32)
    plane_zero = jnp.zeros((step_count, row_count, col_count), jnp.float32)
    start = jnp.where(depth_index == 0, surface_data, jnp.zeros_like(surface_data))

    def forward_segment(segment_no, carry):
        current, stored, image_sum = carry
        states, bottom, image_part = forward_steps(
            current, frequencies, coefficients, slowness, freq_count
        )
        chosen = depth_index == segment_no
        stored = jnp.where(chosen, states, stored)
        image_sum = jnp.where(chosen, image_part, image_sum)
        current = shifted(bottom, "depth", 1)
        return (current, stored, image_sum)

    unused_field, stored, image_field = lax.fori_loop(
        0, layers, forward_segment, (start, stored_zero, plane_zero)
    )

    def backward_segment(segment_no, carry):
        adjoint, gradient_sum = carry
        top_field, parts = backward_steps(
            adjoint, stored, frequencies, coefficients, slowness, perturbation, freq_count
        )
        gradient_sum = jnp.where(depth_index == layers - 1 - segment_no, parts, gradient_sum)
        adjoint = shifted(top_field, "depth", -1)
        return (adjoint, gradient_sum)

    adjoint_zero = jnp.zeros_like(surface_data)
    unused_adjoint, gradient = lax.fori_loop(
        0, layers, backward_segment, (adjoint_zero, plane_zero)
    )
    return (gradient, image_field)


ROWS = 16
HALO_TILES = 4
LANES = 128

OVERLAP = 8

sin_terms = (0.9999999995, -0.1666666515, 0.008333256964, -0.0001982776292, 2.657952479e-06)
cos_terms = (0.9999999947, -0.4999998344, 0.04166583045, -0.00138740917, 2.372928386e-05)


def window_row(tile, sub):
    group = tile - 2
    above = sub - 4 * (group + 1)
    below = sub + ROWS + 4 * group
    even = jnp.where(sub < 4, below, above - 4)
    odd = jnp.where(sub < 4, above, below - 4)
    halo = jnp.where(lax.rem(tile, 2) == 0, even, odd)
    return jnp.where(tile < 2, 8 * tile + sub, halo)


def band_kernel(plane_rows, taps, freqs, bands, back_bands, freq_tiles):
    first_row = lax.axis_index("xy") * ROWS

    def fill(ref, adjoint):
        out_tiles = ref.shape[1] // 48
        in_tiles = ref.shape[2] // 48
        shape = (16, ref.shape[2])
        col = lax.broadcasted_iota(jnp.int32, shape, 1)
        sub = lax.broadcasted_iota(jnp.int32, shape, 0)
        tile_k = sum((col >= 48 * t).astype(jnp.int32) for t in range(1, in_tiles))
        row_k = window_row(tile_k, col & 7)
        part_k = (col >> 4) - 3 * tile_k
        plane_k = (col >> 3) & 1
        plane_m = sub >> 3
        same = plane_k == plane_m
        inside_k = (row_k + first_row >= 0) & (row_k + first_row < plane_rows)
        for tile in range(out_tiles):
            row_m = window_row(jnp.full(shape, tile, jnp.int32), sub & 7)
            inside = inside_k & (row_m + first_row >= 0) & (row_m + first_row < plane_rows)
            offset = jnp.where(inside, row_k - row_m, 9)
            hits = [offset == a - 2 for a in range(5)]
            for f in range(ref.shape[0]):
                for b in range(3):
                    total = jnp.zeros(shape, jnp.float32)
                    for a in range(5):
                        tap = 3 * (4 - a) + 2 - b if adjoint else 3 * a + b
                        re = taps[f, 0, tap]
                        im = -taps[f, 1, tap] if adjoint else taps[f, 1, tap]
                        crossed = jnp.where(plane_m == 0, -im, im)
                        total = jnp.where(hits[a], jnp.where(same, re, crossed), total)
                    high = total.astype(jnp.bfloat16)
                    low = total - high.astype(jnp.float32)
                    base = 48 * tile + 16 * b
                    ref[f, base : base + 16] = jnp.where(part_k == 1, low, total).astype(jnp.bfloat16)

    fill(bands, False)
    fill(back_bands, True)
    for f in range(freq_tiles.shape[0]):
        freq_tiles[f] = jnp.full((8, LANES), freqs[f], jnp.float32)


def pack_rows(ref, values, side):
    lane = lax.broadcasted_iota(jnp.int32, (8, LANES), 1)
    overlaps = jnp.zeros((8, LANES), jnp.float32)
    blocks = (values[0].shape[1] - LANES) // LANES
    for n, value in enumerate(values):
        for block in range(blocks):
            ref[blocks * n + block] = value[:, (block + side) * LANES : (block + side + 1) * LANES]
        extra = value[:, : LANES] if side else value[:, blocks * LANES :]
        turn = (OVERLAP * (n + side)) % LANES
        extra = pltpu.roll(extra, turn, 1) if turn else extra
        overlaps = jnp.where((lane >= OVERLAP * n) & (lane < OVERLAP * (n + 1)), extra, overlaps)
    ref[blocks * len(values)] = overlaps


def unpack_rows(ref, tiles, n, side):
    blocks = (ref.shape[0] - 1) // tiles
    turn = (-OVERLAP * (n + side)) % LANES
    extra = ref[blocks * tiles]
    extra = pltpu.roll(extra, turn, 1) if turn else extra
    parts = [ref[blocks * n + block] for block in range(blocks)]
    return jnp.concatenate([extra] + parts if side else parts + [extra], axis=1)


def edge_levels(levels, slow, pert, down):
    inner, outer = (1, 0) if down else (0, 1)
    if levels == 1:
        return [slow(0, inner), pert(1, inner), pert(0, inner)]
    row = lax.broadcasted_iota(jnp.int32, slow(0, 0).shape, 0)
    turned = pltpu.roll(slow(1, outer), 4, 0)
    if down:
        extra = jnp.where(row < 2, pltpu.roll(pert(1, inner), 2, 0), turned)
        last = jnp.where(row < 4, extra, slow(0, outer))
    else:
        extra = jnp.where(row >= 6, pltpu.roll(pert(1, inner), 6, 0), turned)
        last = jnp.where(row < 4, slow(0, outer), extra)
    return [slow(0, inner), slow(1, inner), last]


def edge_surface(surf, down):
    inner, outer = (1, 0) if down else (0, 1)
    tiles = [surf(plane, inner) for plane in range(4)]
    row = lax.broadcasted_iota(jnp.int32, tiles[0].shape, 0)
    spread = surf(3, outer)
    for plane in range(3):
        turn = 6 - 2 * plane
        free = row < 2 if down else row >= 6
        tiles.append(jnp.where(free, pltpu.roll(spread, turn, 0), surf(plane, outer)))
    return tiles


def surface_edges(tiles, down):
    row = lax.broadcasted_iota(jnp.int32, tiles[0].shape, 0)
    outer = [tiles[4], tiles[5], tiles[6]]
    first = 2 if down else 0
    spread = pltpu.roll(tiles[6], 6, 0)
    spread = jnp.where((row >= first + 2) & (row < first + 4), pltpu.roll(tiles[5], 4, 0), spread)
    spread = jnp.where((row >= first) & (row < first + 2), pltpu.roll(tiles[4], 2, 0), spread)
    outer.append(spread)
    return [(tiles[plane], outer[plane]) for plane in range(4)]


def pack_kernel(width, step, surf_in, slow_in, pert_in, cross, bulk, cross_far, window, surf, slow, pert, sems):
    copies = [
        pltpu.make_async_copy(source, target, sems.at[n])
        for n, (source, target) in enumerate(((slow_in, slow), (pert_in, pert), (surf_in, surf)))
    ]
    for copy in copies:
        copy.start()
    for copy in copies:
        copy.wait()
    depth = lax.axis_index("depth")
    place = lax.axis_index("xy")
    for own in range(2):

        def reader(ref, side):
            lanes = slice(side * step, side * step + width)
            return lambda level, tile: ref[level, 8 * tile : 8 * tile + 8, lanes]

        def surface(plane, tile):
            return surf[plane // 2, plane % 2, 8 * tile : 8 * tile + 8, own * step : own * step + width]

        @pl.when(depth == own)
        def _():
            slow_near, pert_near = reader(slow, own), reader(pert, own)
            slow_far, pert_far = reader(slow, 1 - own), reader(pert, 1 - own)
            both = [(level, tile) for level in range(2) for tile in range(2)]
            for n, (level, tile) in enumerate(both):
                window[8 + n] = slow_near(level, tile)
                window[12 + n] = pert_near(level, tile)
            for plane in range(4):
                for tile in range(2):
                    window[2 * plane + tile] = surface(plane, tile)
            pack_rows(bulk, [slow_far(*at) for at in both] + [pert_far(*at) for at in both], 1 - own)
            for down in (False, True):

                @pl.when((lax.rem(place, 2) == 1) == down)
                def _():
                    edges = edge_surface(surface, down) + edge_levels(own, slow_near, pert_near, down)
                    pack_rows(cross, edges, own)
                    pack_rows(cross_far, edge_levels(own, slow_far, pert_far, down), 1 - own)


def relay_kernel(window, bulk, chip, partner):
    depth = lax.axis_index("depth")
    place = lax.axis_index("xy")
    for own in range(2):

        @pl.when(depth == own)
        def _():
            other = [unpack_rows(bulk, 8, n, own) for n in range(8)]
            for n in range(8):
                partner[n] = other[n]
            readers = {
                own: (lambda level, tile: window[8 + 2 * level + tile], lambda level, tile: window[12 + 2 * level + tile]),
                1 - own: (lambda level, tile: other[2 * level + tile], lambda level, tile: other[4 + 2 * level + tile]),
            }
            for down in (False, True):

                @pl.when((lax.rem(place, 2) == 0) == down)
                def _():
                    edges = edge_surface(lambda plane, tile: window[2 * plane + tile], down)
                    for levels in (own, 1 - own):
                        edges = edges + edge_levels(levels, *readers[levels], down)
                    pack_rows(chip, edges, own)


def phase(half):
    square = half * half
    cosine = cos_terms[-1]
    sine = sin_terms[-1]
    for term in cos_terms[-2::-1]:
        cosine = cosine * square + term
    for term in sin_terms[-2::-1]:
        sine = sine * square + term
    sine = sine * half
    twice = sine + sine
    return 1.0 - twice * sine, twice * cosine


def sweep_kernel(
    width, freq_tiles, bands, back_bands, window, partner, cross, cross_far, chip,
    gradient, image, theirs, slow_win, pert_win, operand, phases, fields, image_win, grad_win,
):
    depth = lax.axis_index("depth")
    place = lax.axis_index("xy")
    half = width - LANES
    row = lax.broadcasted_iota(jnp.int32, (8, width), 0)
    upper = row < 4
    lane = lax.broadcasted_iota(jnp.int32, (16, LANES), 1)
    even = lax.rem(place, 2) == 0
    freqs = [jnp.concatenate([freq_tiles[f]] * (width // LANES), axis=1) for f in range(2)]

    def store_operand(f, tile, value):
        high = value.astype(jnp.bfloat16)
        low = (value - high.astype(jnp.float32)).astype(jnp.bfloat16)
        base = 48 * tile
        operand[f, base : base + 16] = high
        operand[f, base + 16 : base + 32] = high
        operand[f, base + 32 : base + 48] = low

    def stencil(f, matrix, out_tiles, in_tiles):
        product = jnp.dot(
            matrix[f, : 48 * out_tiles, : 48 * in_tiles],
            operand[f, : 48 * in_tiles],
            preferred_element_type=jnp.float32,
        )
        result = []
        for tile in range(out_tiles):
            base = 48 * tile
            left = pltpu.roll(product[base : base + 16], 1, 1)
            right = pltpu.roll(product[base + 32 : base + 48], width - 1, 1)
            left = jnp.concatenate([jnp.where(lane == 0, 0.0, left[:, :LANES]), left[:, LANES:]], axis=1)
            right = jnp.concatenate([right[:, :half], jnp.where(lane == LANES - 1, 0.0, right[:, half:])], axis=1)
            result.append(product[base + 16 : base + 32] + left + right)
        return result

    def fill(own, below_is_chip):
        chip_edges = [unpack_rows(chip, 13, n, own) for n in range(13)]
        cross_edges = [unpack_rows(cross, 10, n, own) for n in range(10)]
        cross_edges += [unpack_rows(cross_far, 3, n, own) for n in range(3)]
        above, below = (cross_edges, chip_edges) if below_is_chip else (chip_edges, cross_edges)
        for level in range(2):
            for tile in range(2):
                slow_win[2 * own + level, tile] = window[8 + 2 * level + tile]
                pert_win[2 * own + level, tile] = window[12 + 2 * level + tile]
                slow_win[2 * (1 - own) + level, tile] = partner[2 * level + tile]
                pert_win[2 * (1 - own) + level, tile] = partner[4 + 2 * level + tile]
        at = (7, 10) if own == 0 else (10, 7)
        up, down = above[at[0] : at[0] + 3], below[at[0] : at[0] + 3]
        for level in range(2):
            slow_win[level, 2] = jnp.where(upper, down[level], up[level])
            slow_win[level, 3] = jnp.where(upper, up[level], down[level])
        slow_win[0, 4] = jnp.where(upper, down[2], up[2])
        slow_win[1, 4] = pltpu.roll(jnp.where(upper, up[2], down[2]), 4, 0)
        pert_win[1, 2] = jnp.where(
            row < 2, pltpu.roll(down[2], 2, 0), jnp.where(row >= 6, pltpu.roll(up[2], 6, 0), 0.0)
        )
        up, down = above[at[1] : at[1] + 3], below[at[1] : at[1] + 3]
        slow_win[2, 2] = jnp.where(upper, down[0], up[0])
        slow_win[2, 3] = jnp.where(upper, up[0], down[0])
        pert_win[3, 2] = jnp.where(upper, down[1], up[1])
        pert_win[3, 3] = jnp.where(upper, up[1], down[1])
        pert_win[2, 2] = jnp.where(upper, down[2], up[2])
        up, down = surface_edges(above[:7], True), surface_edges(below[:7], False)
        planes = []
        for plane in range(4):
            up_inner, up_outer = up[plane]
            down_inner, down_outer = down[plane]
            planes.append(
                [
                    window[2 * plane],
                    window[2 * plane + 1],
                    jnp.where(upper, down_inner, up_inner),
                    jnp.where(upper, up_inner, down_inner),
                    jnp.where(upper, down_outer, up_outer),
                    jnp.where(upper, up_outer, down_outer),
                ]
            )
        for f in range(2):
            for tile in range(6):
                store_operand(f, tile, jnp.concatenate([planes[2 * f][tile], planes[2 * f + 1][tile]], axis=0))

    for own in range(2):
        for below_is_chip in (False, True):

            @pl.when((depth == own) & (even == below_is_chip))
            def _():
                fill(own, below_is_chip)

    def add_image(f, level, tile, re, im):
        part = (re * re + im * im) * 0.5
        image_win[level, tile] = part if f == 0 else image_win[level, tile] + part

    def add_gradient(f, level, tile, w_re, w_im, u_re, u_im):
        part = (0.25 * freqs[f]) * (w_im * u_re - w_re * u_im)
        grad_win[level, tile] = part if f == 0 else grad_win[level, tile] + part

    tiles = (6, 5, 5, 4)
    for level in range(3):
        for f in range(2):
            fields_now = stencil(f, bands, tiles[level + 1], tiles[level])
            for tile, value in enumerate(fields_now):
                cosine, sine = phase(freqs[f] * 0.25 * slow_win[level, tile])
                v_re, v_im = value[:8], value[8:]
                re = cosine * v_re - sine * v_im
                im = cosine * v_im + sine * v_re
                both = jnp.concatenate([re, im], axis=0)
                store_operand(f, tile, both)
                if tile < 3:
                    fields[f, level, tile] = both
                    phases[f, level, tile] = jnp.concatenate([cosine, sine], axis=0)
                if tile < 2:
                    add_image(f, level, tile, re, im)
    for f in range(2):
        for tile, value in enumerate(stencil(f, bands, 4, 4)):
            twice = 2.0 * pert_win[3, tile]
            v_re, v_im = value[:8], value[8:]
            if tile < 2:
                cosine, sine = phase(freqs[f] * 0.25 * slow_win[3, tile])
                re = cosine * v_re - sine * v_im
                im = cosine * v_im + sine * v_re
                add_image(f, 3, tile, re, im)
                add_gradient(f, 3, tile, twice * re, twice * im, re, im)
            store_operand(f, tile, jnp.concatenate([twice * v_re, twice * v_im], axis=0))
    tiles = (2, 3, 3, 4)
    for level in (2, 1, 0):
        for f in range(2):
            for tile, value in enumerate(stencil(f, back_bands, tiles[level], tiles[level + 1])):
                twice = 2.0 * pert_win[level, tile]
                u_re, u_im = fields[f, level, tile, :8], fields[f, level, tile, 8:]
                w_re = value[:8] + twice * u_re
                w_im = value[8:] + twice * u_im
                if tile < 2:
                    add_gradient(f, level, tile, w_re, w_im, u_re, u_im)
                if level > 0:
                    cosine, sine = phases[f, level, tile, :8], phases[f, level, tile, 8:]
                    back = [cosine * w_re + sine * w_im, cosine * w_im - sine * w_re]
                    store_operand(f, tile, jnp.concatenate(back, axis=0))

    for own in range(2):

        @pl.when(depth == own)
        def _():
            inner = slice(own * LANES, own * LANES + half)
            outer = slice(own * half, own * half + half)
            for level in range(2):
                for tile in range(2):
                    rows = slice(8 * tile, 8 * tile + 8)
                    gradient[level, rows, outer] = grad_win[2 * own + level, tile, :, inner]
                    image[level, rows, outer] = image_win[2 * own + level, tile, :, inner]
                    theirs[0, level, rows] = grad_win[2 * (1 - own) + level, tile, :, inner]
                    theirs[1, level, rows] = image_win[2 * (1 - own) + level, tile, :, inner]


def split_columns(surface_data, frequencies, coefficients, slowness, perturbation):
    count = lax.axis_size("xy")
    columns = slowness.shape[2]
    half = columns // 2
    width = half + LANES
    step = half - LANES
    f32 = jnp.float32
    axes = ("depth", "xy")

    def moved(value, other_depth, neighbour):
        pairs = []
        for depth in range(2):
            for place in range(count):
                target = {"chip": place ^ 1, "cross": place + 1 if place % 2 else place - 1, "same": place}[neighbour]
                if 0 <= target < count:
                    layer = 1 - depth if other_depth else depth
                    pairs.append((depth * count + place, layer * count + target))
        return lax.ppermute(value, axes, pairs)

    vmem = pl.BlockSpec(memory_space=pltpu.VMEM)
    smem = pl.BlockSpec(memory_space=pltpu.SMEM)
    tile = lambda n: jax.ShapeDtypeStruct((n, 8, width), f32)
    packed = lambda n: jax.ShapeDtypeStruct((n * half // LANES + 1, 8, LANES), f32)
    params = lambda mib: pltpu.CompilerParams(vmem_limit_bytes=mib * 2**20)
    cross, bulk, cross_far, window = pl.pallas_call(
        lambda *refs: pack_kernel(width, step, *refs),
        out_shape=(packed(10), packed(8), packed(3), tile(16)),
        in_specs=[pl.BlockSpec(memory_space=pltpu.HBM)] * 3,
        out_specs=(vmem,) * 4,
        scratch_shapes=[
            pltpu.VMEM(surface_data.shape, f32),
            pltpu.VMEM(slowness.shape, f32),
            pltpu.VMEM(perturbation.shape, f32),
            pltpu.SemaphoreType.DMA((3,)),
        ],
        compiler_params=params(32),
        name="pack",
    )(*(pltpu.with_memory_space_constraint(x, pltpu.HBM) for x in (surface_data, slowness, perturbation)))
    cross = moved(cross, False, "cross")
    bulk = moved(bulk, True, "same")
    cross_far = moved(cross_far, True, "cross")
    bands, back_bands, freq_tiles = pl.pallas_call(
        lambda *refs: band_kernel(count * ROWS, *refs),
        out_shape=(
            jax.ShapeDtypeStruct((2, 240, 288), jnp.bfloat16),
            jax.ShapeDtypeStruct((2, 144, 192), jnp.bfloat16),
            jax.ShapeDtypeStruct((2, 8, LANES), f32),
        ),
        in_specs=[smem] * 2,
        out_specs=(vmem,) * 3,
        compiler_params=params(16),
        cost_estimate=pl.CostEstimate(flops=10**10, bytes_accessed=10**6, transcendentals=0),
        name="bands",
    )(coefficients, frequencies)
    chip, partner = pl.pallas_call(
        relay_kernel,
        out_shape=(packed(13), tile(8)),
        in_specs=[vmem] * 2,
        out_specs=(vmem,) * 2,
        compiler_params=params(32),
        cost_estimate=pl.CostEstimate(flops=10**10, bytes_accessed=10**6, transcendentals=0),
        name="relay",
    )(window, bulk)
    chip = moved(chip, False, "chip")

    own = jax.ShapeDtypeStruct((2, ROWS, columns), f32)
    gradient, image, theirs = pl.pallas_call(
        lambda *refs: sweep_kernel(width, *refs),
        out_shape=(own, own, jax.ShapeDtypeStruct((2, 2, ROWS, half), f32)),
        in_specs=[vmem] * 8,
        out_specs=(vmem,) * 3,
        scratch_shapes=[
            pltpu.VMEM((4, 5, 8, width), f32),
            pltpu.VMEM((4, 4, 8, width), f32),
            pltpu.VMEM((2, 288, width), jnp.bfloat16),
            pltpu.VMEM((2, 3, 3, 16, width), f32),
            pltpu.VMEM((2, 3, 3, 16, width), f32),
            pltpu.VMEM((4, 2, 8, width), f32),
            pltpu.VMEM((4, 2, 8, width), f32),
        ],
        compiler_params=params(40),
        name="sweep",
    )(
        freq_tiles, bands, back_bands, window, partner, cross, cross_far, chip,
    )
    theirs = moved(theirs, True, "same")
    start = (1 - lax.axis_index("depth")) * half
    gradient = lax.dynamic_update_slice(gradient, theirs[0], (0, 0, start))
    image = lax.dynamic_update_slice(image, theirs[1], (0, 0, start))
    return gradient, image


def on_slice(surface_data, frequencies, coefficients, slowness, perturbation):
    levels, rows, columns = slowness.shape
    fits = (
        lax.axis_size("depth") == 2
        and levels == 2
        and rows == ROWS
        and frequencies.shape[0] == 2
        and lax.axis_size("xy") % 2 == 0
        and columns % (2 * LANES) == 0
        and columns >= 4 * LANES
    )
    plan = split_columns if fits else on_device
    return plan(surface_data, frequencies, coefficients, slowness, perturbation)


def solution(mesh):
    in_specs = (P(None, None, "xy", None), P(), P(), P("depth", "xy", None), P("depth", "xy", None))
    out_specs = (P("depth", "xy", None), P("depth", "xy", None))
    return jax.shard_map(
        on_slice, mesh=mesh, in_specs=in_specs, out_specs=out_specs, check_vma=False
    )
```

```python
import numpy as np
import jax
import jax.numpy as jnp
from jax import lax
from jax.experimental import pallas as pl
from jax.experimental.pallas import tpu as pltpu
from jax.sharding import PartitionSpec as P

layer_thickness = 0.5


def extended_2(cells, sides, width):
    for axis, dim in sides:
        count = lax.axis_size(axis)
        ends = count - 1
        head = lax.slice_in_dim(cells, 0, width, axis=dim)
        tail = lax.slice_in_dim(cells, cells.shape[dim] - width, cells.shape[dim], axis=dim)
        cells = jnp.concatenate(
            [
                lax.ppermute(tail, axis, [(i, (i + 1) % count) for i in range(ends)]),
                cells,
                lax.ppermute(head, axis, [((i + 1) % count, i) for i in range(ends)]),
            ],
            axis=dim,
        )
    return cells


def shifted(value, axis, steps):
    count = lax.axis_size(axis)
    initial, last = (max(0, -steps), min(count, count - steps))
    return lax.ppermute(value, axis, [(source, source + steps) for source in range(initial, last)])


def apply_stencil(extended, tap_re, tap_im):
    out_rows = extended.shape[2] - 4
    col_count = extended.shape[3]
    padded = jnp.pad(extended, ((0, 0), (0, 0), (0, 0), (1, 1)))
    acc_re = jnp.zeros((extended.shape[0], out_rows, col_count), jnp.float32)
    acc_im = jnp.zeros((extended.shape[0], out_rows, col_count), jnp.float32)
    for row_off in range(5):
        for col_off in range(3):
            tap_index = row_off * 3 + col_off
            part_re = padded[:, 0, row_off : row_off + out_rows, col_off : col_off + col_count]
            part_im = padded[:, 1, row_off : row_off + out_rows, col_off : col_off + col_count]
            weight_re = tap_re[:, tap_index][:, None, None]
            weight_im = tap_im[:, tap_index][:, None, None]
            acc_re = acc_re + weight_re * part_re - weight_im * part_im
            acc_im = acc_im + weight_re * part_im + weight_im * part_re
    return (acc_re, acc_im)


def adjoint_stencil(extended, tap_re, tap_im):
    out_rows = extended.shape[2] - 4
    col_count = extended.shape[3]
    padded = jnp.pad(extended, ((0, 0), (0, 0), (0, 0), (1, 1)))
    acc_re = jnp.zeros((extended.shape[0], out_rows, col_count), jnp.float32)
    acc_im = jnp.zeros((extended.shape[0], out_rows, col_count), jnp.float32)
    for row_off in range(5):
        for col_off in range(3):
            tap_index = row_off * 3 + col_off
            row_from = 4 - row_off
            col_from = 2 - col_off
            part_re = padded[:, 0, row_from : row_from + out_rows, col_from : col_from + col_count]
            part_im = padded[:, 1, row_from : row_from + out_rows, col_from : col_from + col_count]
            weight_re = tap_re[:, tap_index][:, None, None]
            weight_im = tap_im[:, tap_index][:, None, None]
            acc_re = acc_re + weight_re * part_re + weight_im * part_im
            acc_im = acc_im + weight_re * part_im - weight_im * part_re
    return (acc_re, acc_im)


def phase_parts(freqs, slow_plane):
    angle = freqs[:, None, None] * layer_thickness * slow_plane[None]
    return (jnp.cos(angle), jnp.sin(angle))


def forward_steps(wavefield, freqs, taps, slowness, freq_total):
    tap_re = taps[:, 0]
    tap_im = taps[:, 1]
    step_count = slowness.shape[0]
    states = []
    current = wavefield
    for level in range(step_count):
        extended = extended_2(current, (("xy", 2),), 2)
        acc_re, acc_im = apply_stencil(extended, tap_re, tap_im)
        phase_re, phase_im = phase_parts(freqs, slowness[level])
        next_re = phase_re * acc_re - phase_im * acc_im
        next_im = phase_re * acc_im + phase_im * acc_re
        current = jnp.stack([next_re, next_im], axis=1)
        states.append(current)
    stacked = jnp.stack(states, axis=1)
    image_part = (
        jnp.sum(stacked[:, :, 0] * stacked[:, :, 0] + stacked[:, :, 1] * stacked[:, :, 1], axis=0)
        / freq_total
    )
    return (stacked, states[-1], image_part)


def backward_steps(adjoint, states, freqs, taps, slowness, perturbation, freq_total):
    tap_re = taps[:, 0]
    tap_im = taps[:, 1]
    step_count = slowness.shape[0]
    parts = [None] * step_count
    for level in reversed(range(step_count)):
        wave_re = states[:, level, 0]
        wave_im = states[:, level, 1]
        grad_re = adjoint[:, 0] + 2.0 * perturbation[level] * wave_re
        grad_im = adjoint[:, 1] + 2.0 * perturbation[level] * wave_im
        parts[level] = (
            layer_thickness
            / freq_total
            * jnp.sum(freqs[:, None, None] * (grad_im * wave_re - grad_re * wave_im), axis=0)
        )
        phase_re, phase_im = phase_parts(freqs, slowness[level])
        back_re = phase_re * grad_re + phase_im * grad_im
        back_im = phase_re * grad_im - phase_im * grad_re
        extended = extended_2(jnp.stack([back_re, back_im], axis=1), (("xy", 2),), 2)
        acc_re, acc_im = adjoint_stencil(extended, tap_re, tap_im)
        adjoint = jnp.stack([acc_re, acc_im], axis=1)
    return (adjoint, jnp.stack(parts, axis=0))


def on_device(surface_data, frequencies, coefficients, slowness, perturbation):
    freq_count = frequencies.shape[0]
    step_count = slowness.shape[0]
    row_count = slowness.shape[1]
    col_count = slowness.shape[2]
    layers = lax.axis_size("depth")
    depth_index = lax.axis_index("depth")
    stored_zero = jnp.zeros((freq_count, step_count, 2, row_count, col_count), jnp.float32)
    plane_zero = jnp.zeros((step_count, row_count, col_count), jnp.float32)
    start = jnp.where(depth_index == 0, surface_data, jnp.zeros_like(surface_data))

    def forward_segment(segment_no, carry):
        current, stored, image_sum = carry
        states, bottom, image_part = forward_steps(
            current, frequencies, coefficients, slowness, freq_count
        )
        chosen = depth_index == segment_no
        stored = jnp.where(chosen, states, stored)
        image_sum = jnp.where(chosen, image_part, image_sum)
        current = shifted(bottom, "depth", 1)
        return (current, stored, image_sum)

    unused_field, stored, image_field = lax.fori_loop(
        0, layers, forward_segment, (start, stored_zero, plane_zero)
    )

    def backward_segment(segment_no, carry):
        adjoint, gradient_sum = carry
        top_field, parts = backward_steps(
            adjoint, stored, frequencies, coefficients, slowness, perturbation, freq_count
        )
        gradient_sum = jnp.where(depth_index == layers - 1 - segment_no, parts, gradient_sum)
        adjoint = shifted(top_field, "depth", -1)
        return (adjoint, gradient_sum)

    adjoint_zero = jnp.zeros_like(surface_data)
    unused_adjoint, gradient = lax.fori_loop(
        0, layers, backward_segment, (adjoint_zero, plane_zero)
    )
    return (gradient, image_field)


ROWS = 16
HALO_TILES = 4
LANES = 128

OVERLAP = 8

sin_terms = (0.9999999995, -0.1666666515, 0.008333256964, -0.0001982776292, 2.657952479e-06)
cos_terms = (0.9999999947, -0.4999998344, 0.04166583045, -0.00138740917, 2.372928386e-05)


def window_row(tile, sub):
    group = tile - 2
    above = sub - 4 * (group + 1)
    below = sub + ROWS + 4 * group
    even = jnp.where(sub < 4, below, above - 4)
    odd = jnp.where(sub < 4, above, below - 4)
    halo = jnp.where(lax.rem(tile, 2) == 0, even, odd)
    return jnp.where(tile < 2, 8 * tile + sub, halo)


def band_kernel(plane_rows, taps, freqs, bands, back_bands, freq_tiles):
    first_row = lax.axis_index("xy") * ROWS

    def fill(ref, adjoint):
        out_tiles = ref.shape[1] // 48
        in_tiles = ref.shape[2] // 48
        shape = (16, ref.shape[2])
        col = lax.broadcasted_iota(jnp.int32, shape, 1)
        sub = lax.broadcasted_iota(jnp.int32, shape, 0)
        tile_k = sum((col >= 48 * t).astype(jnp.int32) for t in range(1, in_tiles))
        row_k = window_row(tile_k, col & 7)
        part_k = (col >> 4) - 3 * tile_k
        plane_k = (col >> 3) & 1
        plane_m = sub >> 3
        same = plane_k == plane_m
        inside_k = (row_k + first_row >= 0) & (row_k + first_row < plane_rows)
        for tile in range(out_tiles):
            row_m = window_row(jnp.full(shape, tile, jnp.int32), sub & 7)
            inside = inside_k & (row_m + first_row >= 0) & (row_m + first_row < plane_rows)
            offset = jnp.where(inside, row_k - row_m, 9)
            hits = [offset == a - 2 for a in range(5)]
            for f in range(ref.shape[0]):
                for b in range(3):
                    total = jnp.zeros(shape, jnp.float32)
                    for a in range(5):
                        tap = 3 * (4 - a) + 2 - b if adjoint else 3 * a + b
                        re = taps[f, 0, tap]
                        im = -taps[f, 1, tap] if adjoint else taps[f, 1, tap]
                        crossed = jnp.where(plane_m == 0, -im, im)
                        total = jnp.where(hits[a], jnp.where(same, re, crossed), total)
                    high = total.astype(jnp.bfloat16)
                    low = total - high.astype(jnp.float32)
                    base = 48 * tile + 16 * b
                    ref[f, base : base + 16] = jnp.where(part_k == 1, low, total).astype(jnp.bfloat16)

    fill(bands, False)
    fill(back_bands, True)
    for f in range(freq_tiles.shape[0]):
        freq_tiles[f] = jnp.full((8, LANES), freqs[f], jnp.float32)


def pack_rows(ref, values, side):
    lane = lax.broadcasted_iota(jnp.int32, (8, LANES), 1)
    overlaps = jnp.zeros((8, LANES), jnp.float32)
    blocks = (values[0].shape[1] - LANES) // LANES
    for n, value in enumerate(values):
        for block in range(blocks):
            ref[blocks * n + block] = value[:, (block + side) * LANES : (block + side + 1) * LANES]
        extra = value[:, : LANES] if side else value[:, blocks * LANES :]
        turn = (OVERLAP * (n + side)) % LANES
        extra = pltpu.roll(extra, turn, 1) if turn else extra
        overlaps = jnp.where((lane >= OVERLAP * n) & (lane < OVERLAP * (n + 1)), extra, overlaps)
    ref[blocks * len(values)] = overlaps


def unpack_rows(ref, tiles, n, side):
    blocks = (ref.shape[0] - 1) // tiles
    turn = (-OVERLAP * (n + side)) % LANES
    extra = ref[blocks * tiles]
    extra = pltpu.roll(extra, turn, 1) if turn else extra
    parts = [ref[blocks * n + block] for block in range(blocks)]
    return jnp.concatenate([extra] + parts if side else parts + [extra], axis=1)


def edge_levels(levels, slow, pert, down):
    inner, outer = (1, 0) if down else (0, 1)
    if levels == 1:
        return [slow(0, inner), pert(1, inner), pert(0, inner)]
    row = lax.broadcasted_iota(jnp.int32, slow(0, 0).shape, 0)
    turned = pltpu.roll(slow(1, outer), 4, 0)
    if down:
        extra = jnp.where(row < 2, pltpu.roll(pert(1, inner), 2, 0), turned)
        last = jnp.where(row < 4, extra, slow(0, outer))
    else:
        extra = jnp.where(row >= 6, pltpu.roll(pert(1, inner), 6, 0), turned)
        last = jnp.where(row < 4, slow(0, outer), extra)
    return [slow(0, inner), slow(1, inner), last]


def edge_surface(surf, f, down):
    order = (1, 0) if down else (0, 1)
    return [surf(2 * f + part, tile) for tile in order for part in range(2)]


def pack_kernel(width, step, surf_in, slow_in, pert_in, cross, cross_next, bulk, cross_far, window, surf, slow, pert, sems):
    copies = [
        pltpu.make_async_copy(source, target, sems.at[n])
        for n, (source, target) in enumerate(((slow_in, slow), (pert_in, pert), (surf_in, surf)))
    ]
    for copy in copies:
        copy.start()
    for copy in copies:
        copy.wait()
    depth = lax.axis_index("depth")
    place = lax.axis_index("xy")
    for own in range(2):

        def reader(ref, side):
            lanes = slice(side * step, side * step + width)
            return lambda level, tile: ref[level, 8 * tile : 8 * tile + 8, lanes]

        def surface(plane, tile):
            return surf[plane // 2, plane % 2, 8 * tile : 8 * tile + 8, own * step : own * step + width]

        @pl.when(depth == own)
        def _():
            slow_near, pert_near = reader(slow, own), reader(pert, own)
            slow_far, pert_far = reader(slow, 1 - own), reader(pert, 1 - own)
            both = [(level, tile) for level in range(2) for tile in range(2)]
            for n, (level, tile) in enumerate(both):
                window[8 + n] = slow_near(level, tile)
                window[12 + n] = pert_near(level, tile)
            for plane in range(4):
                for tile in range(2):
                    window[2 * plane + tile] = surface(plane, tile)
            pack_rows(bulk, [slow_far(*at) for at in both] + [pert_far(*at) for at in both], 1 - own)
            for down in (False, True):

                @pl.when((lax.rem(place, 2) == 1) == down)
                def _():
                    edges = edge_levels(own, slow_near, pert_near, down) + edge_surface(surface, 0, down)
                    pack_rows(cross, edges, own)
                    pack_rows(cross_next, edge_surface(surface, 1, down), own)
                    pack_rows(cross_far, edge_levels(own, slow_far, pert_far, down), 1 - own)


def relay_kernel(window, bulk, chip, partner):
    depth = lax.axis_index("depth")
    place = lax.axis_index("xy")
    for own in range(2):

        @pl.when(depth == own)
        def _():
            other = [unpack_rows(bulk, 8, n, own) for n in range(8)]
            for n in range(8):
                partner[n] = other[n]
            readers = {
                own: (lambda level, tile: window[8 + 2 * level + tile], lambda level, tile: window[12 + 2 * level + tile]),
                1 - own: (lambda level, tile: other[2 * level + tile], lambda level, tile: other[4 + 2 * level + tile]),
            }
            for down in (False, True):

                @pl.when((lax.rem(place, 2) == 0) == down)
                def _():
                    edges = []
                    for levels in (own, 1 - own):
                        edges = edges + edge_levels(levels, *readers[levels], down)
                    for f in range(2):
                        edges = edges + edge_surface(lambda plane, tile: window[2 * plane + tile], f, down)
                    pack_rows(chip, edges, own)


def phase(half):
    square = half * half
    cosine = cos_terms[-1]
    sine = sin_terms[-1]
    for term in cos_terms[-2::-1]:
        cosine = cosine * square + term
    for term in sin_terms[-2::-1]:
        sine = sine * square + term
    sine = sine * half
    twice = sine + sine
    return 1.0 - twice * sine, twice * cosine


def own_phases_kernel(freq_tiles, window, partner, phases):
    depth = lax.axis_index("depth")
    for level in range(4):
        for tile in range(2):
            own, other = window[8 + 2 * (level % 2) + tile], partner[2 * (level % 2) + tile]
            slow = jnp.where(depth == level // 2, own, other)
            for f in range(2):
                cosine, sine = phase(over_columns(freq_tiles[f], slow) * 0.25 * slow)
                phases[f, level, tile, :8] = cosine
                phases[f, level, tile, 8:] = sine


def over_columns(tile, like):
    return jnp.concatenate([tile] * (like.shape[1] // LANES), axis=1)


def split_store(operand, tile, value):
    high = value.astype(jnp.bfloat16)
    low = (value - high.astype(jnp.float32)).astype(jnp.bfloat16)
    base = 48 * tile
    operand[base : base + 16] = high
    operand[base + 16 : base + 32] = high
    operand[base + 32 : base + 48] = low


def stencil(matrix, operand, out_tiles, in_tiles):
    product = jnp.dot(
        matrix[: 48 * out_tiles, : 48 * in_tiles],
        operand[: 48 * in_tiles],
        preferred_element_type=jnp.float32,
    )
    width = product.shape[1]
    half = width - LANES
    lane = lax.broadcasted_iota(jnp.int32, (16, LANES), 1)
    result = []
    for tile in range(out_tiles):
        base = 48 * tile
        left = pltpu.roll(product[base : base + 16], 1, 1)
        right = pltpu.roll(product[base + 32 : base + 48], width - 1, 1)
        left = jnp.concatenate([jnp.where(lane == 0, 0.0, left[:, :LANES]), left[:, LANES:]], axis=1)
        right = jnp.concatenate([right[:, :half], jnp.where(lane == LANES - 1, 0.0, right[:, half:])], axis=1)
        result.append(product[base + 16 : base + 32] + left + right)
    return result


def gradient_part(freq_tile, w_re, w_im, u_re, u_im):
    return (0.25 * over_columns(freq_tile, w_re)) * (w_im * u_re - w_re * u_im)


def fill_levels(window, partner, cross, cross_far, chip, slow_halo, pert_win):
    row = lax.broadcasted_iota(jnp.int32, slow_halo.shape[2:], 0)
    upper = row < 4
    depth = lax.axis_index("depth")
    even = lax.rem(lax.axis_index("xy"), 2) == 0

    def fill(own, below_is_chip):
        near = [unpack_rows(cross, 7, n, own) for n in range(3)]
        far = [unpack_rows(cross_far, 3, n, own) for n in range(3)]
        cross_edges = (near, far) if own == 0 else (far, near)
        on_chip = [unpack_rows(chip, 14, n, own) for n in range(6)]
        chip_edges = (on_chip[:3], on_chip[3:]) if own == 0 else (on_chip[3:], on_chip[:3])
        above, below = (cross_edges, chip_edges) if below_is_chip else (chip_edges, cross_edges)
        for level in range(2):
            for tile in range(2):
                pert_win[2 * own + level, tile] = window[12 + 2 * level + tile]
                pert_win[2 * (1 - own) + level, tile] = partner[4 + 2 * level + tile]
        up, down = above[0], below[0]
        for level in range(2):
            slow_halo[level, 0] = jnp.where(upper, down[level], up[level])
            slow_halo[level, 1] = jnp.where(upper, up[level], down[level])
        slow_halo[0, 2] = jnp.where(upper, down[2], up[2])
        slow_halo[1, 2] = pltpu.roll(jnp.where(upper, up[2], down[2]), 4, 0)
        pert_win[1, 2] = jnp.where(
            row < 2, pltpu.roll(down[2], 2, 0), jnp.where(row >= 6, pltpu.roll(up[2], 6, 0), 0.0)
        )
        up, down = above[1], below[1]
        slow_halo[2, 0] = jnp.where(upper, down[0], up[0])
        slow_halo[2, 1] = jnp.where(upper, up[0], down[0])
        pert_win[3, 2] = jnp.where(upper, down[1], up[1])
        pert_win[3, 3] = jnp.where(upper, up[1], down[1])
        pert_win[2, 2] = jnp.where(upper, down[2], up[2])

    for own in range(2):
        for below_is_chip in (False, True):

            @pl.when((depth == own) & (even == below_is_chip))
            def _():
                fill(own, below_is_chip)


def fill_surface(f, window, cross, cross_tiles, cross_first, chip, operand):
    upper = lax.broadcasted_iota(jnp.int32, window.shape[1:], 0) < 4
    depth = lax.axis_index("depth")
    even = lax.rem(lax.axis_index("xy"), 2) == 0

    def fill(own, below_is_chip):
        cross_edges = [unpack_rows(cross, cross_tiles, cross_first + n, own) for n in range(4)]
        chip_edges = [unpack_rows(chip, 14, 6 + 4 * f + n, own) for n in range(4)]
        up, down = (cross_edges, chip_edges) if below_is_chip else (chip_edges, cross_edges)
        planes = []
        for part in range(2):
            at = 4 * f + 2 * part
            planes.append(
                [
                    window[at],
                    window[at + 1],
                    jnp.where(upper, down[part], up[part]),
                    jnp.where(upper, up[part], down[part]),
                    jnp.where(upper, down[2 + part], up[2 + part]),
                    jnp.where(upper, up[2 + part], down[2 + part]),
                ]
            )
        for tile in range(6):
            split_store(operand, tile, jnp.concatenate([planes[0][tile], planes[1][tile]], axis=0))

    for own in range(2):
        for below_is_chip in (False, True):

            @pl.when((depth == own) & (even == below_is_chip))
            def _():
                fill(own, below_is_chip)


def sweep(f, freq_tiles, bands, back_bands, own_phases, slow_halo, pert_win, operand, halo_phases, fields, add_image, add_gradient):
    def advance(level, tile, value):
        if tile < 2:
            cosine, sine = own_phases[f, level, tile, :8], own_phases[f, level, tile, 8:]
        else:
            slow = slow_halo[level, tile - 2]
            cosine, sine = phase(over_columns(freq_tiles[f], slow) * 0.25 * slow)
            if tile == 2 and level > 0:
                halo_phases[level - 1, :8] = cosine
                halo_phases[level - 1, 8:] = sine
        v_re, v_im = value[:8], value[8:]
        re = cosine * v_re - sine * v_im
        im = cosine * v_im + sine * v_re
        if tile < 2:
            add_image(level, tile, (re * re + im * im) * 0.5)
        return re, im

    tiles = (6, 5, 5, 4)
    for level in range(3):
        for tile, value in enumerate(stencil(bands.at[f], operand, tiles[level + 1], tiles[level])):
            both = jnp.concatenate(advance(level, tile, value), axis=0)
            split_store(operand, tile, both)
            if tile < 3:
                fields[level, tile] = both
    for tile, value in enumerate(stencil(bands.at[f], operand, 4, 4)):
        twice = 2.0 * pert_win[3, tile]
        if tile < 2:
            re, im = advance(3, tile, value)
            add_gradient(3, tile, gradient_part(freq_tiles[f], twice * re, twice * im, re, im))
        split_store(operand, tile, jnp.concatenate([twice * value[:8], twice * value[8:]], axis=0))
    tiles = (2, 3, 3, 4)
    for level in (2, 1, 0):
        for tile, value in enumerate(stencil(back_bands.at[f], operand, tiles[level], tiles[level + 1])):
            twice = 2.0 * pert_win[level, tile]
            u_re, u_im = fields[level, tile, :8], fields[level, tile, 8:]
            w_re = value[:8] + twice * u_re
            w_im = value[8:] + twice * u_im
            if tile < 2:
                add_gradient(level, tile, gradient_part(freq_tiles[f], w_re, w_im, u_re, u_im))
            if level > 0:
                if tile < 2:
                    cosine, sine = own_phases[f, level, tile, :8], own_phases[f, level, tile, 8:]
                else:
                    cosine, sine = halo_phases[level - 1, :8], halo_phases[level - 1, 8:]
                back = [cosine * w_re + sine * w_im, cosine * w_im - sine * w_re]
                split_store(operand, tile, jnp.concatenate(back, axis=0))


def first_sweep_kernel(
    freq_tiles, bands, back_bands, own_phases, window, partner, cross, cross_far, chip,
    slow_halo, pert_win, image_sum, grad_sum, operand, halo_phases, fields,
):
    fill_levels(window, partner, cross, cross_far, chip, slow_halo, pert_win)
    fill_surface(0, window, cross, 7, 3, chip, operand)

    def add_image(level, tile, value):
        image_sum[level, tile] = value

    def add_gradient(level, tile, value):
        grad_sum[level, tile] = value

    sweep(0, freq_tiles, bands, back_bands, own_phases, slow_halo, pert_win, operand, halo_phases, fields, add_image, add_gradient)


def second_sweep_kernel(
    freq_tiles, bands, back_bands, own_phases, window, cross_next, chip, slow_halo, pert_win, image_sum, grad_sum,
    gradient, image, theirs, operand, halo_phases, fields, image_win, grad_win,
):
    fill_surface(1, window, cross_next, 4, 0, chip, operand)

    def add_image(level, tile, value):
        image_win[level, tile] = value + image_sum[level, tile]

    def add_gradient(level, tile, value):
        grad_win[level, tile] = value + grad_sum[level, tile]

    sweep(1, freq_tiles, bands, back_bands, own_phases, slow_halo, pert_win, operand, halo_phases, fields, add_image, add_gradient)
    half = theirs.shape[3]
    for own in range(2):

        @pl.when(lax.axis_index("depth") == own)
        def _():
            inner = slice(own * LANES, own * LANES + half)
            outer = slice(own * half, own * half + half)
            for level in range(2):
                for tile in range(2):
                    rows = slice(8 * tile, 8 * tile + 8)
                    gradient[level, rows, outer] = grad_win[2 * own + level, tile, :, inner]
                    image[level, rows, outer] = image_win[2 * own + level, tile, :, inner]
                    theirs[0, level, rows] = grad_win[2 * (1 - own) + level, tile, :, inner]
                    theirs[1, level, rows] = image_win[2 * (1 - own) + level, tile, :, inner]


def split_columns(surface_data, frequencies, coefficients, slowness, perturbation):
    count = lax.axis_size("xy")
    columns = slowness.shape[2]
    half = columns // 2
    width = half + LANES
    step = half - LANES
    f32 = jnp.float32
    axes = ("depth", "xy")

    def moved(value, other_depth, neighbour):
        pairs = []
        for depth in range(2):
            for place in range(count):
                target = {"chip": place ^ 1, "cross": place + 1 if place % 2 else place - 1, "same": place}[neighbour]
                if 0 <= target < count:
                    layer = 1 - depth if other_depth else depth
                    pairs.append((depth * count + place, layer * count + target))
        return lax.ppermute(value, axes, pairs)

    vmem = pl.BlockSpec(memory_space=pltpu.VMEM)
    smem = pl.BlockSpec(memory_space=pltpu.SMEM)
    tile = lambda n: jax.ShapeDtypeStruct((n, 8, width), f32)
    packed = lambda n: jax.ShapeDtypeStruct((n * half // LANES + 1, 8, LANES), f32)
    params = lambda mib: pltpu.CompilerParams(vmem_limit_bytes=mib * 2**20)
    cross, cross_next, bulk, cross_far, window = pl.pallas_call(
        lambda *refs: pack_kernel(width, step, *refs),
        out_shape=(packed(7), packed(4), packed(8), packed(3), tile(16)),
        in_specs=[pl.BlockSpec(memory_space=pltpu.HBM)] * 3,
        out_specs=(vmem,) * 5,
        scratch_shapes=[
            pltpu.VMEM(surface_data.shape, f32),
            pltpu.VMEM(slowness.shape, f32),
            pltpu.VMEM(perturbation.shape, f32),
            pltpu.SemaphoreType.DMA((3,)),
        ],
        compiler_params=params(32),
        name="pack",
    )(*(pltpu.with_memory_space_constraint(x, pltpu.HBM) for x in (surface_data, slowness, perturbation)))
    cross = moved(cross, False, "cross")
    bulk = moved(bulk, True, "same")
    cross_far = moved(cross_far, True, "cross")
    cross_next = moved(cross_next, False, "cross")
    bands, back_bands, freq_tiles = pl.pallas_call(
        lambda *refs: band_kernel(count * ROWS, *refs),
        out_shape=(
            jax.ShapeDtypeStruct((2, 240, 288), jnp.bfloat16),
            jax.ShapeDtypeStruct((2, 144, 192), jnp.bfloat16),
            jax.ShapeDtypeStruct((2, 8, LANES), f32),
        ),
        in_specs=[smem] * 2,
        out_specs=(vmem,) * 3,
        compiler_params=params(16),
        cost_estimate=pl.CostEstimate(flops=10**10, bytes_accessed=10**6, transcendentals=0),
        name="bands",
    )(coefficients, frequencies)
    chip, partner = pl.pallas_call(
        relay_kernel,
        out_shape=(packed(14), tile(8)),
        in_specs=[vmem] * 2,
        out_specs=(vmem,) * 2,
        compiler_params=params(32),
        cost_estimate=pl.CostEstimate(flops=10**10, bytes_accessed=10**6, transcendentals=0),
        name="relay",
    )(window, bulk)
    chip = moved(chip, False, "chip")

    own_phases = pl.pallas_call(
        own_phases_kernel,
        out_shape=jax.ShapeDtypeStruct((2, 4, 2, 16, width), f32),
        in_specs=[vmem] * 3,
        out_specs=vmem,
        compiler_params=params(16),
        name="own_phases",
    )(freq_tiles, window, partner)

    own = jax.ShapeDtypeStruct((2, ROWS, columns), f32)
    sums = jax.ShapeDtypeStruct((4, 2, 8, width), f32)
    scratch = [
        pltpu.VMEM((288, width), jnp.bfloat16),
        pltpu.VMEM((2, 16, width), f32),
        pltpu.VMEM((3, 3, 16, width), f32),
    ]
    slow_halo, pert_win, image_sum, grad_sum = pl.pallas_call(
        first_sweep_kernel,
        out_shape=(
            jax.ShapeDtypeStruct((3, 3, 8, width), f32),
            jax.ShapeDtypeStruct((4, 4, 8, width), f32),
            sums,
            sums,
        ),
        in_specs=[vmem] * 9,
        out_specs=(vmem,) * 4,
        scratch_shapes=scratch,
        compiler_params=params(32),
        name="first_sweep",
    )(freq_tiles, bands, back_bands, own_phases, window, partner, cross, cross_far, chip)
    gradient, image, theirs = pl.pallas_call(
        second_sweep_kernel,
        out_shape=(own, own, jax.ShapeDtypeStruct((2, 2, ROWS, half), f32)),
        in_specs=[vmem] * 11,
        out_specs=(vmem,) * 3,
        scratch_shapes=scratch + [pltpu.VMEM((4, 2, 8, width), f32)] * 2,
        compiler_params=params(32),
        name="second_sweep",
    )(
        freq_tiles, bands, back_bands, own_phases, window, cross_next, chip, slow_halo, pert_win, image_sum, grad_sum
    )
    theirs = moved(theirs, True, "same")
    start = (1 - lax.axis_index("depth")) * half
    gradient = lax.dynamic_update_slice(gradient, theirs[0], (0, 0, start))
    image = lax.dynamic_update_slice(image, theirs[1], (0, 0, start))
    return gradient, image


def on_slice(surface_data, frequencies, coefficients, slowness, perturbation):
    levels, rows, columns = slowness.shape
    fits = (
        lax.axis_size("depth") == 2
        and levels == 2
        and rows == ROWS
        and frequencies.shape[0] == 2
        and lax.axis_size("xy") % 2 == 0
        and columns % (2 * LANES) == 0
        and columns >= 4 * LANES
    )
    plan = split_columns if fits else on_device
    return plan(surface_data, frequencies, coefficients, slowness, perturbation)


def solution(mesh):
    in_specs = (P(None, None, "xy", None), P(), P(), P("depth", "xy", None), P("depth", "xy", None))
    out_specs = (P("depth", "xy", None), P("depth", "xy", None))
    return jax.shard_map(
        on_slice, mesh=mesh, in_specs=in_specs, out_specs=out_specs, check_vma=False
    )
```

```python
import numpy as np
import jax
import jax.numpy as jnp
from jax import lax
from jax.experimental import pallas as pl
from jax.experimental.pallas import tpu as pltpu
from jax.sharding import PartitionSpec as P

layer_thickness = 0.5


def extended_2(cells, sides, width):
    for axis, dim in sides:
        count = lax.axis_size(axis)
        ends = count - 1
        head = lax.slice_in_dim(cells, 0, width, axis=dim)
        tail = lax.slice_in_dim(cells, cells.shape[dim] - width, cells.shape[dim], axis=dim)
        cells = jnp.concatenate(
            [
                lax.ppermute(tail, axis, [(i, (i + 1) % count) for i in range(ends)]),
                cells,
                lax.ppermute(head, axis, [((i + 1) % count, i) for i in range(ends)]),
            ],
            axis=dim,
        )
    return cells


def shifted(value, axis, steps):
    count = lax.axis_size(axis)
    initial, last = (max(0, -steps), min(count, count - steps))
    return lax.ppermute(value, axis, [(source, source + steps) for source in range(initial, last)])


def apply_stencil(extended, tap_re, tap_im):
    out_rows = extended.shape[2] - 4
    col_count = extended.shape[3]
    padded = jnp.pad(extended, ((0, 0), (0, 0), (0, 0), (1, 1)))
    acc_re = jnp.zeros((extended.shape[0], out_rows, col_count), jnp.float32)
    acc_im = jnp.zeros((extended.shape[0], out_rows, col_count), jnp.float32)
    for row_off in range(5):
        for col_off in range(3):
            tap_index = row_off * 3 + col_off
            part_re = padded[:, 0, row_off : row_off + out_rows, col_off : col_off + col_count]
            part_im = padded[:, 1, row_off : row_off + out_rows, col_off : col_off + col_count]
            weight_re = tap_re[:, tap_index][:, None, None]
            weight_im = tap_im[:, tap_index][:, None, None]
            acc_re = acc_re + weight_re * part_re - weight_im * part_im
            acc_im = acc_im + weight_re * part_im + weight_im * part_re
    return (acc_re, acc_im)


def adjoint_stencil(extended, tap_re, tap_im):
    out_rows = extended.shape[2] - 4
    col_count = extended.shape[3]
    padded = jnp.pad(extended, ((0, 0), (0, 0), (0, 0), (1, 1)))
    acc_re = jnp.zeros((extended.shape[0], out_rows, col_count), jnp.float32)
    acc_im = jnp.zeros((extended.shape[0], out_rows, col_count), jnp.float32)
    for row_off in range(5):
        for col_off in range(3):
            tap_index = row_off * 3 + col_off
            row_from = 4 - row_off
            col_from = 2 - col_off
            part_re = padded[:, 0, row_from : row_from + out_rows, col_from : col_from + col_count]
            part_im = padded[:, 1, row_from : row_from + out_rows, col_from : col_from + col_count]
            weight_re = tap_re[:, tap_index][:, None, None]
            weight_im = tap_im[:, tap_index][:, None, None]
            acc_re = acc_re + weight_re * part_re + weight_im * part_im
            acc_im = acc_im + weight_re * part_im - weight_im * part_re
    return (acc_re, acc_im)


def phase_parts(freqs, slow_plane):
    angle = freqs[:, None, None] * layer_thickness * slow_plane[None]
    return (jnp.cos(angle), jnp.sin(angle))


def forward_steps(wavefield, freqs, taps, slowness, freq_total):
    tap_re = taps[:, 0]
    tap_im = taps[:, 1]
    step_count = slowness.shape[0]
    states = []
    current = wavefield
    for level in range(step_count):
        extended = extended_2(current, (("xy", 2),), 2)
        acc_re, acc_im = apply_stencil(extended, tap_re, tap_im)
        phase_re, phase_im = phase_parts(freqs, slowness[level])
        next_re = phase_re * acc_re - phase_im * acc_im
        next_im = phase_re * acc_im + phase_im * acc_re
        current = jnp.stack([next_re, next_im], axis=1)
        states.append(current)
    stacked = jnp.stack(states, axis=1)
    image_part = (
        jnp.sum(stacked[:, :, 0] * stacked[:, :, 0] + stacked[:, :, 1] * stacked[:, :, 1], axis=0)
        / freq_total
    )
    return (stacked, states[-1], image_part)


def backward_steps(adjoint, states, freqs, taps, slowness, perturbation, freq_total):
    tap_re = taps[:, 0]
    tap_im = taps[:, 1]
    step_count = slowness.shape[0]
    parts = [None] * step_count
    for level in reversed(range(step_count)):
        wave_re = states[:, level, 0]
        wave_im = states[:, level, 1]
        grad_re = adjoint[:, 0] + 2.0 * perturbation[level] * wave_re
        grad_im = adjoint[:, 1] + 2.0 * perturbation[level] * wave_im
        parts[level] = (
            layer_thickness
            / freq_total
            * jnp.sum(freqs[:, None, None] * (grad_im * wave_re - grad_re * wave_im), axis=0)
        )
        phase_re, phase_im = phase_parts(freqs, slowness[level])
        back_re = phase_re * grad_re + phase_im * grad_im
        back_im = phase_re * grad_im - phase_im * grad_re
        extended = extended_2(jnp.stack([back_re, back_im], axis=1), (("xy", 2),), 2)
        acc_re, acc_im = adjoint_stencil(extended, tap_re, tap_im)
        adjoint = jnp.stack([acc_re, acc_im], axis=1)
    return (adjoint, jnp.stack(parts, axis=0))


def on_device(surface_data, frequencies, coefficients, slowness, perturbation):
    freq_count = frequencies.shape[0]
    step_count = slowness.shape[0]
    row_count = slowness.shape[1]
    col_count = slowness.shape[2]
    layers = lax.axis_size("depth")
    depth_index = lax.axis_index("depth")
    stored_zero = jnp.zeros((freq_count, step_count, 2, row_count, col_count), jnp.float32)
    plane_zero = jnp.zeros((step_count, row_count, col_count), jnp.float32)
    start = jnp.where(depth_index == 0, surface_data, jnp.zeros_like(surface_data))

    def forward_segment(segment_no, carry):
        current, stored, image_sum = carry
        states, bottom, image_part = forward_steps(
            current, frequencies, coefficients, slowness, freq_count
        )
        chosen = depth_index == segment_no
        stored = jnp.where(chosen, states, stored)
        image_sum = jnp.where(chosen, image_part, image_sum)
        current = shifted(bottom, "depth", 1)
        return (current, stored, image_sum)

    unused_field, stored, image_field = lax.fori_loop(
        0, layers, forward_segment, (start, stored_zero, plane_zero)
    )

    def backward_segment(segment_no, carry):
        adjoint, gradient_sum = carry
        top_field, parts = backward_steps(
            adjoint, stored, frequencies, coefficients, slowness, perturbation, freq_count
        )
        gradient_sum = jnp.where(depth_index == layers - 1 - segment_no, parts, gradient_sum)
        adjoint = shifted(top_field, "depth", -1)
        return (adjoint, gradient_sum)

    adjoint_zero = jnp.zeros_like(surface_data)
    unused_adjoint, gradient = lax.fori_loop(
        0, layers, backward_segment, (adjoint_zero, plane_zero)
    )
    return (gradient, image_field)


ROWS = 16
HALO_TILES = 4
LANES = 128

OVERLAP = 8

sin_terms = (0.9999999995, -0.1666666515, 0.008333256964, -0.0001982776292, 2.657952479e-06)
cos_terms = (0.9999999947, -0.4999998344, 0.04166583045, -0.00138740917, 2.372928386e-05)


def window_row(tile, sub):
    group = tile - 2
    above = sub - 4 * (group + 1)
    below = sub + ROWS + 4 * group
    even = jnp.where(sub < 4, below, above - 4)
    odd = jnp.where(sub < 4, above, below - 4)
    halo = jnp.where(lax.rem(tile, 2) == 0, even, odd)
    return jnp.where(tile < 2, 8 * tile + sub, halo)


def band_kernel(plane_rows, taps, freqs, bands, back_bands, freq_tiles):
    first_row = lax.axis_index("xy") * ROWS

    def fill(ref, adjoint):
        out_tiles = ref.shape[1] // 48
        in_tiles = ref.shape[2] // 48
        shape = (16, ref.shape[2])
        col = lax.broadcasted_iota(jnp.int32, shape, 1)
        sub = lax.broadcasted_iota(jnp.int32, shape, 0)
        tile_k = sum((col >= 48 * t).astype(jnp.int32) for t in range(1, in_tiles))
        row_k = window_row(tile_k, col & 7)
        part_k = (col >> 4) - 3 * tile_k
        plane_k = (col >> 3) & 1
        plane_m = sub >> 3
        same = plane_k == plane_m
        inside_k = (row_k + first_row >= 0) & (row_k + first_row < plane_rows)
        for tile in range(out_tiles):
            row_m = window_row(jnp.full(shape, tile, jnp.int32), sub & 7)
            inside = inside_k & (row_m + first_row >= 0) & (row_m + first_row < plane_rows)
            offset = jnp.where(inside, row_k - row_m, 9)
            hits = [offset == a - 2 for a in range(5)]
            for f in range(ref.shape[0]):
                for b in range(3):
                    total = jnp.zeros(shape, jnp.float32)
                    for a in range(5):
                        tap = 3 * (4 - a) + 2 - b if adjoint else 3 * a + b
                        re = taps[f, 0, tap]
                        im = -taps[f, 1, tap] if adjoint else taps[f, 1, tap]
                        crossed = jnp.where(plane_m == 0, -im, im)
                        total = jnp.where(hits[a], jnp.where(same, re, crossed), total)
                    high = total.astype(jnp.bfloat16)
                    low = total - high.astype(jnp.float32)
                    base = 48 * tile + 16 * b
                    ref[f, base : base + 16] = jnp.where(part_k == 1, low, total).astype(jnp.bfloat16)

    fill(bands, False)
    fill(back_bands, True)
    for f in range(freq_tiles.shape[0]):
        freq_tiles[f] = jnp.full((8, LANES), freqs[f], jnp.float32)


def pack_rows(ref, values, side):
    lane = lax.broadcasted_iota(jnp.int32, (8, LANES), 1)
    overlaps = jnp.zeros((8, LANES), jnp.float32)
    blocks = (values[0].shape[1] - LANES) // LANES
    for n, value in enumerate(values):
        for block in range(blocks):
            ref[blocks * n + block] = value[:, (block + side) * LANES : (block + side + 1) * LANES]
        extra = value[:, : LANES] if side else value[:, blocks * LANES :]
        turn = (OVERLAP * (n + side)) % LANES
        extra = pltpu.roll(extra, turn, 1) if turn else extra
        overlaps = jnp.where((lane >= OVERLAP * n) & (lane < OVERLAP * (n + 1)), extra, overlaps)
    ref[blocks * len(values)] = overlaps


def unpack_rows(ref, tiles, n, side):
    blocks = (ref.shape[0] - 1) // tiles
    turn = (-OVERLAP * (n + side)) % LANES
    extra = ref[blocks * tiles]
    extra = pltpu.roll(extra, turn, 1) if turn else extra
    parts = [ref[blocks * n + block] for block in range(blocks)]
    return jnp.concatenate([extra] + parts if side else parts + [extra], axis=1)


def edge_levels(levels, slow, pert, down):
    inner, outer = (1, 0) if down else (0, 1)
    if levels == 1:
        return [slow(0, inner), pert(1, inner), pert(0, inner)]
    row = lax.broadcasted_iota(jnp.int32, slow(0, 0).shape, 0)
    turned = pltpu.roll(slow(1, outer), 4, 0)
    if down:
        extra = jnp.where(row < 2, pltpu.roll(pert(1, inner), 2, 0), turned)
        last = jnp.where(row < 4, extra, slow(0, outer))
    else:
        extra = jnp.where(row >= 6, pltpu.roll(pert(1, inner), 6, 0), turned)
        last = jnp.where(row < 4, slow(0, outer), extra)
    return [slow(0, inner), slow(1, inner), last]


def edge_surface(surf, down):
    inner, outer = (1, 0) if down else (0, 1)
    tiles = [surf(plane, inner) for plane in range(4)]
    row = lax.broadcasted_iota(jnp.int32, tiles[0].shape, 0)
    spread = surf(3, outer)
    for plane in range(3):
        turn = 6 - 2 * plane
        free = row < 2 if down else row >= 6
        tiles.append(jnp.where(free, pltpu.roll(spread, turn, 0), surf(plane, outer)))
    return tiles


def surface_edges(tiles, down):
    row = lax.broadcasted_iota(jnp.int32, tiles[0].shape, 0)
    outer = [tiles[4], tiles[5], tiles[6]]
    first = 2 if down else 0
    spread = pltpu.roll(tiles[6], 6, 0)
    spread = jnp.where((row >= first + 2) & (row < first + 4), pltpu.roll(tiles[5], 4, 0), spread)
    spread = jnp.where((row >= first) & (row < first + 2), pltpu.roll(tiles[4], 2, 0), spread)
    outer.append(spread)
    return [(tiles[plane], outer[plane]) for plane in range(4)]


def pack_kernel(width, step, surf_in, slow_in, pert_in, cross, bulk, cross_far, window, surf, slow, pert, sems):
    copies = [
        pltpu.make_async_copy(source, target, sems.at[n])
        for n, (source, target) in enumerate(((slow_in, slow), (pert_in, pert), (surf_in, surf)))
    ]
    for copy in copies:
        copy.start()
    for copy in copies:
        copy.wait()
    depth = lax.axis_index("depth")
    place = lax.axis_index("xy")
    for own in range(2):

        def reader(ref, side):
            lanes = slice(side * step, side * step + width)
            return lambda level, tile: ref[level, 8 * tile : 8 * tile + 8, lanes]

        def surface(plane, tile):
            return surf[plane // 2, plane % 2, 8 * tile : 8 * tile + 8, own * step : own * step + width]

        @pl.when(depth == own)
        def _():
            slow_near, pert_near = reader(slow, own), reader(pert, own)
            slow_far, pert_far = reader(slow, 1 - own), reader(pert, 1 - own)
            both = [(level, tile) for level in range(2) for tile in range(2)]
            for n, (level, tile) in enumerate(both):
                window[8 + n] = slow_near(level, tile)
                window[12 + n] = pert_near(level, tile)
            for plane in range(4):
                for tile in range(2):
                    window[2 * plane + tile] = surface(plane, tile)
            pack_rows(bulk, [slow_far(*at) for at in both] + [pert_far(*at) for at in both], 1 - own)
            for down in (False, True):

                @pl.when((lax.rem(place, 2) == 1) == down)
                def _():
                    edges = edge_surface(surface, down) + edge_levels(own, slow_near, pert_near, down)
                    pack_rows(cross, edges, own)
                    pack_rows(cross_far, edge_levels(own, slow_far, pert_far, down), 1 - own)


def relay_kernel(window, bulk, chip, partner):
    depth = lax.axis_index("depth")
    place = lax.axis_index("xy")
    for own in range(2):

        @pl.when(depth == own)
        def _():
            other = [unpack_rows(bulk.at[1 - own], 8, n, own) for n in range(8)]
            for n in range(8):
                partner[n] = other[n]
            readers = {
                own: (lambda level, tile: window[8 + 2 * level + tile], lambda level, tile: window[12 + 2 * level + tile]),
                1 - own: (lambda level, tile: other[2 * level + tile], lambda level, tile: other[4 + 2 * level + tile]),
            }
            for down in (False, True):

                @pl.when((lax.rem(place, 2) == 0) == down)
                def _():
                    edges = edge_surface(lambda plane, tile: window[2 * plane + tile], down)
                    for levels in (own, 1 - own):
                        edges = edges + edge_levels(levels, *readers[levels], down)
                    pack_rows(chip, edges, own)


def phase(half):
    square = half * half
    cosine = cos_terms[-1]
    sine = sin_terms[-1]
    for term in cos_terms[-2::-1]:
        cosine = cosine * square + term
    for term in sin_terms[-2::-1]:
        sine = sine * square + term
    sine = sine * half
    twice = sine + sine
    return 1.0 - twice * sine, twice * cosine


def own_phases_kernel(freq_tiles, window, partner, phases):
    depth = lax.axis_index("depth")
    for level in range(4):
        for tile in range(2):
            own, other = window[8 + 2 * (level % 2) + tile], partner[2 * (level % 2) + tile]
            slow = jnp.where(depth == level // 2, own, other)
            for f in range(2):
                cosine, sine = phase(over_columns(freq_tiles[f], slow) * 0.25 * slow)
                phases[f, level, tile, :8] = cosine
                phases[f, level, tile, 8:] = sine


def over_columns(tile, like):
    return jnp.concatenate([tile] * (like.shape[1] // LANES), axis=1)


def sweep_kernel(
    width, freq_tiles, bands, back_bands, own_phases, window, partner, cross, cross_far, chip,
    gradient, image, theirs, slow_win, pert_win, operand, halo_phases, fields, image_win, grad_win,
):
    depth = lax.axis_index("depth")
    place = lax.axis_index("xy")
    half = width - LANES
    row = lax.broadcasted_iota(jnp.int32, (8, width), 0)
    upper = row < 4
    lane = lax.broadcasted_iota(jnp.int32, (16, LANES), 1)
    even = lax.rem(place, 2) == 0
    freqs = [jnp.concatenate([freq_tiles[f]] * (width // LANES), axis=1) for f in range(2)]

    def store_operand(f, tile, value):
        high = value.astype(jnp.bfloat16)
        low = (value - high.astype(jnp.float32)).astype(jnp.bfloat16)
        base = 48 * tile
        operand[f, base : base + 16] = high
        operand[f, base + 16 : base + 32] = high
        operand[f, base + 32 : base + 48] = low

    def stencil(f, matrix, out_tiles, in_tiles):
        product = jnp.dot(
            matrix[f, : 48 * out_tiles, : 48 * in_tiles],
            operand[f, : 48 * in_tiles],
            preferred_element_type=jnp.float32,
        )
        result = []
        for tile in range(out_tiles):
            base = 48 * tile
            left = pltpu.roll(product[base : base + 16], 1, 1)
            right = pltpu.roll(product[base + 32 : base + 48], width - 1, 1)
            left = jnp.concatenate([jnp.where(lane == 0, 0.0, left[:, :LANES]), left[:, LANES:]], axis=1)
            right = jnp.concatenate([right[:, :half], jnp.where(lane == LANES - 1, 0.0, right[:, half:])], axis=1)
            result.append(product[base + 16 : base + 32] + left + right)
        return result

    def fill(own, below_is_chip):
        chip_edges = [unpack_rows(chip, 13, n, own) for n in range(13)]
        cross_edges = [unpack_rows(cross, 10, n, own) for n in range(10)]
        cross_edges += [unpack_rows(cross_far, 3, n, own) for n in range(3)]
        above, below = (cross_edges, chip_edges) if below_is_chip else (chip_edges, cross_edges)
        for level in range(2):
            for tile in range(2):
                pert_win[2 * own + level, tile] = window[12 + 2 * level + tile]
                pert_win[2 * (1 - own) + level, tile] = partner[4 + 2 * level + tile]
        at = (7, 10) if own == 0 else (10, 7)
        up, down = above[at[0] : at[0] + 3], below[at[0] : at[0] + 3]
        for level in range(2):
            slow_win[level, 0] = jnp.where(upper, down[level], up[level])
            slow_win[level, 1] = jnp.where(upper, up[level], down[level])
        slow_win[0, 2] = jnp.where(upper, down[2], up[2])
        slow_win[1, 2] = pltpu.roll(jnp.where(upper, up[2], down[2]), 4, 0)
        pert_win[1, 2] = jnp.where(
            row < 2, pltpu.roll(down[2], 2, 0), jnp.where(row >= 6, pltpu.roll(up[2], 6, 0), 0.0)
        )
        up, down = above[at[1] : at[1] + 3], below[at[1] : at[1] + 3]
        slow_win[2, 0] = jnp.where(upper, down[0], up[0])
        slow_win[2, 1] = jnp.where(upper, up[0], down[0])
        pert_win[3, 2] = jnp.where(upper, down[1], up[1])
        pert_win[3, 3] = jnp.where(upper, up[1], down[1])
        pert_win[2, 2] = jnp.where(upper, down[2], up[2])
        up, down = surface_edges(above[:7], True), surface_edges(below[:7], False)
        planes = []
        for plane in range(4):
            up_inner, up_outer = up[plane]
            down_inner, down_outer = down[plane]
            planes.append(
                [
                    window[2 * plane],
                    window[2 * plane + 1],
                    jnp.where(upper, down_inner, up_inner),
                    jnp.where(upper, up_inner, down_inner),
                    jnp.where(upper, down_outer, up_outer),
                    jnp.where(upper, up_outer, down_outer),
                ]
            )
        for f in range(2):
            for tile in range(6):
                store_operand(f, tile, jnp.concatenate([planes[2 * f][tile], planes[2 * f + 1][tile]], axis=0))

    for own in range(2):
        for below_is_chip in (False, True):

            @pl.when((depth == own) & (even == below_is_chip))
            def _():
                fill(own, below_is_chip)

    def add_image(f, level, tile, re, im):
        part = (re * re + im * im) * 0.5
        image_win[level, tile] = part if f == 0 else image_win[level, tile] + part

    def add_gradient(f, level, tile, w_re, w_im, u_re, u_im):
        part = (0.25 * freqs[f]) * (w_im * u_re - w_re * u_im)
        grad_win[level, tile] = part if f == 0 else grad_win[level, tile] + part

    def phases_of(f, level, tile):
        if tile < 2:
            return own_phases[f, level, tile, :8], own_phases[f, level, tile, 8:]
        cosine, sine = phase(freqs[f] * 0.25 * slow_win[level, tile - 2])
        if tile == 2 and level > 0:
            halo_phases[f, level - 1, :8] = cosine
            halo_phases[f, level - 1, 8:] = sine
        return cosine, sine

    tiles = (6, 5, 5, 4)
    for level in range(3):
        for f in range(2):
            fields_now = stencil(f, bands, tiles[level + 1], tiles[level])
            for tile, value in enumerate(fields_now):
                cosine, sine = phases_of(f, level, tile)
                v_re, v_im = value[:8], value[8:]
                re = cosine * v_re - sine * v_im
                im = cosine * v_im + sine * v_re
                both = jnp.concatenate([re, im], axis=0)
                store_operand(f, tile, both)
                if tile < 3:
                    fields[f, level, tile] = both
                if tile < 2:
                    add_image(f, level, tile, re, im)
    for f in range(2):
        for tile, value in enumerate(stencil(f, bands, 4, 4)):
            twice = 2.0 * pert_win[3, tile]
            v_re, v_im = value[:8], value[8:]
            if tile < 2:
                cosine, sine = phases_of(f, 3, tile)
                re = cosine * v_re - sine * v_im
                im = cosine * v_im + sine * v_re
                add_image(f, 3, tile, re, im)
                add_gradient(f, 3, tile, twice * re, twice * im, re, im)
            store_operand(f, tile, jnp.concatenate([twice * v_re, twice * v_im], axis=0))
    tiles = (2, 3, 3, 4)
    for level in (2, 1, 0):
        for f in range(2):
            for tile, value in enumerate(stencil(f, back_bands, tiles[level], tiles[level + 1])):
                twice = 2.0 * pert_win[level, tile]
                u_re, u_im = fields[f, level, tile, :8], fields[f, level, tile, 8:]
                w_re = value[:8] + twice * u_re
                w_im = value[8:] + twice * u_im
                if tile < 2:
                    add_gradient(f, level, tile, w_re, w_im, u_re, u_im)
                if level > 0:
                    if tile < 2:
                        cosine, sine = phases_of(f, level, tile)
                    else:
                        cosine, sine = halo_phases[f, level - 1, :8], halo_phases[f, level - 1, 8:]
                    back = [cosine * w_re + sine * w_im, cosine * w_im - sine * w_re]
                    store_operand(f, tile, jnp.concatenate(back, axis=0))

    for own in range(2):

        @pl.when(depth == own)
        def _():
            inner = slice(own * LANES, own * LANES + half)
            outer = slice(own * half, own * half + half)
            for level in range(2):
                for tile in range(2):
                    rows = slice(8 * tile, 8 * tile + 8)
                    gradient[level, rows, outer] = grad_win[2 * own + level, tile, :, inner]
                    image[level, rows, outer] = image_win[2 * own + level, tile, :, inner]
                    theirs[0, level, rows] = grad_win[2 * (1 - own) + level, tile, :, inner]
                    theirs[1, level, rows] = image_win[2 * (1 - own) + level, tile, :, inner]


def split_columns(surface_data, frequencies, coefficients, slowness, perturbation):
    count = lax.axis_size("xy")
    columns = slowness.shape[2]
    half = columns // 2
    width = half + LANES
    step = half - LANES
    f32 = jnp.float32
    axes = ("depth", "xy")

    def moved(value, other_depth, neighbour):
        pairs = []
        for depth in range(2):
            for place in range(count):
                target = {"chip": place ^ 1, "cross": place + 1 if place % 2 else place - 1, "same": place}[neighbour]
                if 0 <= target < count:
                    layer = 1 - depth if other_depth else depth
                    pairs.append((depth * count + place, layer * count + target))
        return lax.ppermute(value, axes, pairs)

    vmem = pl.BlockSpec(memory_space=pltpu.VMEM)
    smem = pl.BlockSpec(memory_space=pltpu.SMEM)
    tile = lambda n: jax.ShapeDtypeStruct((n, 8, width), f32)
    packed = lambda n: jax.ShapeDtypeStruct((n * half // LANES + 1, 8, LANES), f32)
    params = lambda mib: pltpu.CompilerParams(vmem_limit_bytes=mib * 2**20)
    cross, bulk, cross_far, window = pl.pallas_call(
        lambda *refs: pack_kernel(width, step, *refs),
        out_shape=(packed(10), packed(8), packed(3), tile(16)),
        in_specs=[pl.BlockSpec(memory_space=pltpu.HBM)] * 3,
        out_specs=(vmem,) * 4,
        scratch_shapes=[
            pltpu.VMEM(surface_data.shape, f32),
            pltpu.VMEM(slowness.shape, f32),
            pltpu.VMEM(perturbation.shape, f32),
            pltpu.SemaphoreType.DMA((3,)),
        ],
        compiler_params=params(32),
        name="pack",
    )(*(pltpu.with_memory_space_constraint(x, pltpu.HBM) for x in (surface_data, slowness, perturbation)))
    cross = moved(cross, False, "cross")
    bulk = lax.all_gather(bulk, "depth")
    cross_far = moved(cross_far, True, "cross")
    bands, back_bands, freq_tiles = pl.pallas_call(
        lambda *refs: band_kernel(count * ROWS, *refs),
        out_shape=(
            jax.ShapeDtypeStruct((2, 240, 288), jnp.bfloat16),
            jax.ShapeDtypeStruct((2, 144, 192), jnp.bfloat16),
            jax.ShapeDtypeStruct((2, 8, LANES), f32),
        ),
        in_specs=[smem] * 2,
        out_specs=(vmem,) * 3,
        compiler_params=params(16),
        cost_estimate=pl.CostEstimate(flops=10**10, bytes_accessed=10**6, transcendentals=0),
        name="bands",
    )(coefficients, frequencies)
    chip, partner = pl.pallas_call(
        relay_kernel,
        out_shape=(packed(13), tile(8)),
        in_specs=[vmem] * 2,
        out_specs=(vmem,) * 2,
        compiler_params=params(32),
        cost_estimate=pl.CostEstimate(flops=10**10, bytes_accessed=10**6, transcendentals=0),
        name="relay",
    )(window, bulk)
    chip = moved(chip, False, "chip")

    own_phases = pl.pallas_call(
        own_phases_kernel,
        out_shape=jax.ShapeDtypeStruct((2, 4, 2, 16, width), f32),
        in_specs=[vmem] * 3,
        out_specs=vmem,
        compiler_params=params(16),
        name="own_phases",
    )(freq_tiles, window, partner)

    own = jax.ShapeDtypeStruct((2, ROWS, columns), f32)
    gradient, image, theirs = pl.pallas_call(
        lambda *refs: sweep_kernel(width, *refs),
        out_shape=(own, own, jax.ShapeDtypeStruct((2, 2, ROWS, half), f32)),
        in_specs=[vmem] * 9,
        out_specs=(vmem,) * 3,
        scratch_shapes=[
            pltpu.VMEM((3, 3, 8, width), f32),
            pltpu.VMEM((4, 4, 8, width), f32),
            pltpu.VMEM((2, 288, width), jnp.bfloat16),
            pltpu.VMEM((2, 2, 16, width), f32),
            pltpu.VMEM((2, 3, 3, 16, width), f32),
            pltpu.VMEM((4, 2, 8, width), f32),
            pltpu.VMEM((4, 2, 8, width), f32),
        ],
        compiler_params=params(40),
        name="sweep",
    )(
        freq_tiles, bands, back_bands, own_phases, window, partner, cross, cross_far, chip,
    )
    theirs = moved(theirs, True, "same")
    start = (1 - lax.axis_index("depth")) * half
    gradient = lax.dynamic_update_slice(gradient, theirs[0], (0, 0, start))
    image = lax.dynamic_update_slice(image, theirs[1], (0, 0, start))
    return gradient, image


def on_slice(surface_data, frequencies, coefficients, slowness, perturbation):
    levels, rows, columns = slowness.shape
    fits = (
        lax.axis_size("depth") == 2
        and levels == 2
        and rows == ROWS
        and frequencies.shape[0] == 2
        and lax.axis_size("xy") % 2 == 0
        and columns % (2 * LANES) == 0
        and columns >= 4 * LANES
    )
    plan = split_columns if fits else on_device
    return plan(surface_data, frequencies, coefficients, slowness, perturbation)


def solution(mesh):
    in_specs = (P(None, None, "xy", None), P(), P(), P("depth", "xy", None), P("depth", "xy", None))
    out_specs = (P("depth", "xy", None), P("depth", "xy", None))
    return jax.shard_map(
        on_slice, mesh=mesh, in_specs=in_specs, out_specs=out_specs, check_vma=False
    )
```

```python
import numpy as np
import jax
import jax.numpy as jnp
from jax import lax
from jax.experimental import pallas as pl
from jax.experimental.pallas import tpu as pltpu
from jax.sharding import PartitionSpec as P

layer_thickness = 0.5


def extended_2(cells, sides, width):
    for axis, dim in sides:
        count = lax.axis_size(axis)
        ends = count - 1
        head = lax.slice_in_dim(cells, 0, width, axis=dim)
        tail = lax.slice_in_dim(cells, cells.shape[dim] - width, cells.shape[dim], axis=dim)
        cells = jnp.concatenate(
            [
                lax.ppermute(tail, axis, [(i, (i + 1) % count) for i in range(ends)]),
                cells,
                lax.ppermute(head, axis, [((i + 1) % count, i) for i in range(ends)]),
            ],
            axis=dim,
        )
    return cells


def shifted(value, axis, steps):
    count = lax.axis_size(axis)
    initial, last = (max(0, -steps), min(count, count - steps))
    return lax.ppermute(value, axis, [(source, source + steps) for source in range(initial, last)])


def apply_stencil(extended, tap_re, tap_im):
    out_rows = extended.shape[2] - 4
    col_count = extended.shape[3]
    padded = jnp.pad(extended, ((0, 0), (0, 0), (0, 0), (1, 1)))
    acc_re = jnp.zeros((extended.shape[0], out_rows, col_count), jnp.float32)
    acc_im = jnp.zeros((extended.shape[0], out_rows, col_count), jnp.float32)
    for row_off in range(5):
        for col_off in range(3):
            tap_index = row_off * 3 + col_off
            part_re = padded[:, 0, row_off : row_off + out_rows, col_off : col_off + col_count]
            part_im = padded[:, 1, row_off : row_off + out_rows, col_off : col_off + col_count]
            weight_re = tap_re[:, tap_index][:, None, None]
            weight_im = tap_im[:, tap_index][:, None, None]
            acc_re = acc_re + weight_re * part_re - weight_im * part_im
            acc_im = acc_im + weight_re * part_im + weight_im * part_re
    return (acc_re, acc_im)


def adjoint_stencil(extended, tap_re, tap_im):
    out_rows = extended.shape[2] - 4
    col_count = extended.shape[3]
    padded = jnp.pad(extended, ((0, 0), (0, 0), (0, 0), (1, 1)))
    acc_re = jnp.zeros((extended.shape[0], out_rows, col_count), jnp.float32)
    acc_im = jnp.zeros((extended.shape[0], out_rows, col_count), jnp.float32)
    for row_off in range(5):
        for col_off in range(3):
            tap_index = row_off * 3 + col_off
            row_from = 4 - row_off
            col_from = 2 - col_off
            part_re = padded[:, 0, row_from : row_from + out_rows, col_from : col_from + col_count]
            part_im = padded[:, 1, row_from : row_from + out_rows, col_from : col_from + col_count]
            weight_re = tap_re[:, tap_index][:, None, None]
            weight_im = tap_im[:, tap_index][:, None, None]
            acc_re = acc_re + weight_re * part_re + weight_im * part_im
            acc_im = acc_im + weight_re * part_im - weight_im * part_re
    return (acc_re, acc_im)


def phase_parts(freqs, slow_plane):
    angle = freqs[:, None, None] * layer_thickness * slow_plane[None]
    return (jnp.cos(angle), jnp.sin(angle))


def forward_steps(wavefield, freqs, taps, slowness, freq_total):
    tap_re = taps[:, 0]
    tap_im = taps[:, 1]
    step_count = slowness.shape[0]
    states = []
    current = wavefield
    for level in range(step_count):
        extended = extended_2(current, (("xy", 2),), 2)
        acc_re, acc_im = apply_stencil(extended, tap_re, tap_im)
        phase_re, phase_im = phase_parts(freqs, slowness[level])
        next_re = phase_re * acc_re - phase_im * acc_im
        next_im = phase_re * acc_im + phase_im * acc_re
        current = jnp.stack([next_re, next_im], axis=1)
        states.append(current)
    stacked = jnp.stack(states, axis=1)
    image_part = (
        jnp.sum(stacked[:, :, 0] * stacked[:, :, 0] + stacked[:, :, 1] * stacked[:, :, 1], axis=0)
        / freq_total
    )
    return (stacked, states[-1], image_part)


def backward_steps(adjoint, states, freqs, taps, slowness, perturbation, freq_total):
    tap_re = taps[:, 0]
    tap_im = taps[:, 1]
    step_count = slowness.shape[0]
    parts = [None] * step_count
    for level in reversed(range(step_count)):
        wave_re = states[:, level, 0]
        wave_im = states[:, level, 1]
        grad_re = adjoint[:, 0] + 2.0 * perturbation[level] * wave_re
        grad_im = adjoint[:, 1] + 2.0 * perturbation[level] * wave_im
        parts[level] = (
            layer_thickness
            / freq_total
            * jnp.sum(freqs[:, None, None] * (grad_im * wave_re - grad_re * wave_im), axis=0)
        )
        phase_re, phase_im = phase_parts(freqs, slowness[level])
        back_re = phase_re * grad_re + phase_im * grad_im
        back_im = phase_re * grad_im - phase_im * grad_re
        extended = extended_2(jnp.stack([back_re, back_im], axis=1), (("xy", 2),), 2)
        acc_re, acc_im = adjoint_stencil(extended, tap_re, tap_im)
        adjoint = jnp.stack([acc_re, acc_im], axis=1)
    return (adjoint, jnp.stack(parts, axis=0))


def on_device(surface_data, frequencies, coefficients, slowness, perturbation):
    freq_count = frequencies.shape[0]
    step_count = slowness.shape[0]
    row_count = slowness.shape[1]
    col_count = slowness.shape[2]
    layers = lax.axis_size("depth")
    depth_index = lax.axis_index("depth")
    stored_zero = jnp.zeros((freq_count, step_count, 2, row_count, col_count), jnp.float32)
    plane_zero = jnp.zeros((step_count, row_count, col_count), jnp.float32)
    start = jnp.where(depth_index == 0, surface_data, jnp.zeros_like(surface_data))

    def forward_segment(segment_no, carry):
        current, stored, image_sum = carry
        states, bottom, image_part = forward_steps(
            current, frequencies, coefficients, slowness, freq_count
        )
        chosen = depth_index == segment_no
        stored = jnp.where(chosen, states, stored)
        image_sum = jnp.where(chosen, image_part, image_sum)
        current = shifted(bottom, "depth", 1)
        return (current, stored, image_sum)

    unused_field, stored, image_field = lax.fori_loop(
        0, layers, forward_segment, (start, stored_zero, plane_zero)
    )

    def backward_segment(segment_no, carry):
        adjoint, gradient_sum = carry
        top_field, parts = backward_steps(
            adjoint, stored, frequencies, coefficients, slowness, perturbation, freq_count
        )
        gradient_sum = jnp.where(depth_index == layers - 1 - segment_no, parts, gradient_sum)
        adjoint = shifted(top_field, "depth", -1)
        return (adjoint, gradient_sum)

    adjoint_zero = jnp.zeros_like(surface_data)
    unused_adjoint, gradient = lax.fori_loop(
        0, layers, backward_segment, (adjoint_zero, plane_zero)
    )
    return (gradient, image_field)


ROWS = 16
HALO_TILES = 4
LANES = 128

SPARE = 1
OVERLAP = 8

sin_terms = (0.9999999995, -0.1666666515, 0.008333256964, -0.0001982776292, 2.657952479e-06)
cos_terms = (0.9999999947, -0.4999998344, 0.04166583045, -0.00138740917, 2.372928386e-05)


def window_row(tile, sub):
    group = tile - 2
    above = sub - 4 * (group + 1)
    below = sub + ROWS + 4 * group
    even = jnp.where(sub < 4, below, above - 4)
    odd = jnp.where(sub < 4, above, below - 4)
    halo = jnp.where(lax.rem(tile, 2) == 0, even, odd)
    return jnp.where(tile < 2, 8 * tile + sub, halo)


def band_kernel(plane_rows, taps, freqs, bands, back_bands, freq_tiles):
    first_row = lax.axis_index("xy") * ROWS

    def fill(ref, adjoint):
        out_tiles = ref.shape[1] // 48
        in_tiles = ref.shape[2] // 48
        shape = (16, ref.shape[2])
        col = lax.broadcasted_iota(jnp.int32, shape, 1)
        sub = lax.broadcasted_iota(jnp.int32, shape, 0)
        tile_k = sum((col >= 48 * t).astype(jnp.int32) for t in range(1, in_tiles))
        row_k = window_row(tile_k, col & 7)
        part_k = (col >> 4) - 3 * tile_k
        plane_k = (col >> 3) & 1
        plane_m = sub >> 3
        same = plane_k == plane_m
        inside_k = (row_k + first_row >= 0) & (row_k + first_row < plane_rows)
        for tile in range(out_tiles):
            row_m = window_row(jnp.full(shape, tile, jnp.int32), sub & 7)
            inside = inside_k & (row_m + first_row >= 0) & (row_m + first_row < plane_rows)
            offset = jnp.where(inside, row_k - row_m, 9)
            hits = [offset == a - 2 for a in range(5)]
            for f in range(ref.shape[0]):
                for b in range(3):
                    total = jnp.zeros(shape, jnp.float32)
                    for a in range(5):
                        tap = 3 * (4 - a) + 2 - b if adjoint else 3 * a + b
                        re = taps[f, 0, tap]
                        im = -taps[f, 1, tap] if adjoint else taps[f, 1, tap]
                        crossed = jnp.where(plane_m == 0, -im, im)
                        total = jnp.where(hits[a], jnp.where(same, re, crossed), total)
                    high = total.astype(jnp.bfloat16)
                    low = total - high.astype(jnp.float32)
                    base = 48 * tile + 16 * b
                    ref[f, base : base + 16] = jnp.where(part_k == 1, low, total).astype(jnp.bfloat16)

    fill(bands, False)
    fill(back_bands, True)
    for f in range(freq_tiles.shape[0]):
        freq_tiles[f] = jnp.full((8, LANES), freqs[f], jnp.float32)


def pack_rows(ref, values, side):
    lane = lax.broadcasted_iota(jnp.int32, (8, LANES), 1)
    overlaps = jnp.zeros((8, LANES), jnp.float32)
    blocks = (values[0].shape[1] - LANES) // LANES
    for n, value in enumerate(values):
        for block in range(blocks):
            ref[blocks * n + block] = value[:, (block + side) * LANES : (block + side + 1) * LANES]
        extra = value[:, : LANES] if side else value[:, blocks * LANES :]
        turn = (OVERLAP * (n + side)) % LANES
        extra = pltpu.roll(extra, turn, 1) if turn else extra
        overlaps = jnp.where((lane >= OVERLAP * n) & (lane < OVERLAP * (n + 1)), extra, overlaps)
    ref[blocks * len(values)] = overlaps


def unpack_rows(ref, tiles, n, side):
    blocks = (ref.shape[0] - 1) // tiles
    turn = (-OVERLAP * (n + side)) % LANES
    extra = ref[blocks * tiles]
    extra = pltpu.roll(extra, turn, 1) if turn else extra
    parts = [ref[blocks * n + block] for block in range(blocks)]
    return jnp.concatenate([extra] + parts if side else parts + [extra], axis=1)


def edge_levels(levels, slow, pert, down):
    inner, outer = (1, 0) if down else (0, 1)
    if levels == 1:
        return [slow(0, inner), pert(1, inner), pert(0, inner)]
    row = lax.broadcasted_iota(jnp.int32, slow(0, 0).shape, 0)
    turned = pltpu.roll(slow(1, outer), 4, 0)
    if down:
        extra = jnp.where(row < 2, pltpu.roll(pert(1, inner), 2, 0), turned)
        last = jnp.where(row < 4, extra, slow(0, outer))
    else:
        extra = jnp.where(row >= 6, pltpu.roll(pert(1, inner), 6, 0), turned)
        last = jnp.where(row < 4, slow(0, outer), extra)
    return [slow(0, inner), slow(1, inner), last]


def edge_surface(surf, down):
    inner, outer = (1, 0) if down else (0, 1)
    tiles = [surf(plane, inner) for plane in range(4)]
    row = lax.broadcasted_iota(jnp.int32, tiles[0].shape, 0)
    spread = surf(3, outer)
    for plane in range(3):
        turn = 6 - 2 * plane
        free = row < 2 if down else row >= 6
        tiles.append(jnp.where(free, pltpu.roll(spread, turn, 0), surf(plane, outer)))
    return tiles


def surface_edges(tiles, down):
    row = lax.broadcasted_iota(jnp.int32, tiles[0].shape, 0)
    outer = [tiles[4], tiles[5], tiles[6]]
    first = 2 if down else 0
    spread = pltpu.roll(tiles[6], 6, 0)
    spread = jnp.where((row >= first + 2) & (row < first + 4), pltpu.roll(tiles[5], 4, 0), spread)
    spread = jnp.where((row >= first) & (row < first + 2), pltpu.roll(tiles[4], 2, 0), spread)
    outer.append(spread)
    return [(tiles[plane], outer[plane]) for plane in range(4)]


def pack_kernel(width, step, surf_in, slow_in, pert_in, cross, bulk, cross_far, window, surf, slow, pert, sems):
    copies = [
        pltpu.make_async_copy(source, target, sems.at[n])
        for n, (source, target) in enumerate(((slow_in, slow), (pert_in, pert), (surf_in, surf)))
    ]
    for copy in copies:
        copy.start()
    for copy in copies:
        copy.wait()
    depth = lax.axis_index("depth")
    place = lax.axis_index("xy")
    for own in range(2):

        def reader(ref, side):
            lanes = slice(side * step, side * step + width)
            return lambda level, tile: ref[level, 8 * tile : 8 * tile + 8, lanes]

        def surface(plane, tile):
            return surf[plane // 2, plane % 2, 8 * tile : 8 * tile + 8, own * step : own * step + width]

        @pl.when(depth == own)
        def _():
            slow_near, pert_near = reader(slow, own), reader(pert, own)
            slow_far, pert_far = reader(slow, 1 - own), reader(pert, 1 - own)
            both = [(level, tile) for level in range(2) for tile in range(2)]
            for n, (level, tile) in enumerate(both):
                window[8 + n] = slow_near(level, tile)
                window[12 + n] = pert_near(level, tile)
            for plane in range(4):
                for tile in range(2):
                    window[2 * plane + tile] = surface(plane, tile)
            pack_rows(bulk, [slow_far(*at) for at in both] + [pert_far(*at) for at in both], 1 - own)
            for down in (False, True):

                @pl.when((lax.rem(place, 2) == 1) == down)
                def _():
                    edges = edge_surface(surface, down) + edge_levels(own, slow_near, pert_near, down)
                    pack_rows(cross, edges, own)
                    pack_rows(cross_far, edge_levels(own, slow_far, pert_far, down), 1 - own)


def relay_kernel(window, bulk, chip, partner):
    depth = lax.axis_index("depth")
    place = lax.axis_index("xy")
    for own in range(2):

        @pl.when(depth == own)
        def _():
            other = [unpack_rows(bulk, 8, n, own) for n in range(8)]
            for n in range(8):
                partner[n] = other[n]
            readers = {
                own: (lambda level, tile: window[8 + 2 * level + tile], lambda level, tile: window[12 + 2 * level + tile]),
                1 - own: (lambda level, tile: other[2 * level + tile], lambda level, tile: other[4 + 2 * level + tile]),
            }
            for down in (False, True):

                @pl.when((lax.rem(place, 2) == 0) == down)
                def _():
                    edges = edge_surface(lambda plane, tile: window[2 * plane + tile], down)
                    for levels in (own, 1 - own):
                        edges = edges + edge_levels(levels, *readers[levels], down)
                    pack_rows(chip, edges, own)


def phase(half):
    square = half * half
    cosine = cos_terms[-1]
    sine = sin_terms[-1]
    for term in cos_terms[-2::-1]:
        cosine = cosine * square + term
    for term in sin_terms[-2::-1]:
        sine = sine * square + term
    sine = sine * half
    twice = sine + sine
    return 1.0 - twice * sine, twice * cosine


def own_phases_kernel(freq_tiles, window, partner, phases):
    depth = lax.axis_index("depth")
    for level in range(4):
        for tile in range(2):
            own, other = window[8 + 2 * (level % 2) + tile], partner[2 * (level % 2) + tile]
            slow = jnp.where(depth == level // 2, own, other)
            for f in range(2):
                cosine, sine = phase(over_columns(freq_tiles[f], slow) * 0.25 * slow)
                phases[f, level, tile, :8] = cosine
                phases[f, level, tile, 8:] = sine


def over_columns(tile, like):
    return jnp.concatenate([tile] * (like.shape[1] // LANES), axis=1)


def split_store(operand, f, tile, value):
    high = value.astype(jnp.bfloat16)
    low = (value - high.astype(jnp.float32)).astype(jnp.bfloat16)
    base = 48 * tile
    operand[f, base : base + 16] = high
    operand[f, base + 16 : base + 32] = high
    operand[f, base + 32 : base + 48] = low


def stencil(matrix, operand, f, out_tiles, in_tiles):
    product = jnp.dot(
        matrix[f, : 48 * out_tiles, : 48 * in_tiles],
        operand[f, : 48 * in_tiles],
        preferred_element_type=jnp.float32,
    )
    width = product.shape[1]
    half = width - LANES
    lane = lax.broadcasted_iota(jnp.int32, (16, LANES), 1)
    result = []
    for tile in range(out_tiles):
        base = 48 * tile
        left = pltpu.roll(product[base : base + 16], 1, 1)
        right = pltpu.roll(product[base + 32 : base + 48], width - 1, 1)
        left = jnp.concatenate([jnp.where(lane == 0, 0.0, left[:, :LANES]), left[:, LANES:]], axis=1)
        right = jnp.concatenate([right[:, :half], jnp.where(lane == LANES - 1, 0.0, right[:, half:])], axis=1)
        result.append(product[base + 16 : base + 32] + left + right)
    return result


def gradient_part(freq_tile, w_re, w_im, u_re, u_im):
    return (0.25 * over_columns(freq_tile, w_re)) * (w_im * u_re - w_re * u_im)


def deliver(depth, whole, theirs, found):
    half = whole.shape[2] // 2
    blocks = half // LANES
    for own in range(2):

        @pl.when(depth == own)
        def _():
            inner = slice(own * LANES, own * LANES + half)
            outer = slice(own * half, own * half + half)
            for level in range(2):
                for tile in range(2):
                    whole[level, 8 * tile : 8 * tile + 8, outer] = found[2 * own + level, tile, :, inner]
                    for block in range(blocks):
                        first = (own + block) * LANES
                        theirs[blocks * (2 * level + tile) + block] = found[
                            2 * (1 - own) + level, tile, :, first : first + LANES
                        ]


def forward_kernel(
    freq_tiles, bands, own_phases, window, partner, cross, cross_far, chip,
    image, theirs, fields, halo_phases, pert_win, last_gradient, operand_out, slow_win, operand, image_win,
):
    width = window.shape[2]
    depth = lax.axis_index("depth")
    place = lax.axis_index("xy")
    row = lax.broadcasted_iota(jnp.int32, (8, width), 0)
    upper = row < 4
    even = lax.rem(place, 2) == 0

    def fill(own, below_is_chip):
        chip_edges = [unpack_rows(chip, 13, n, own) for n in range(13)]
        cross_edges = [unpack_rows(cross, 10, n, own) for n in range(10)]
        cross_edges += [unpack_rows(cross_far, 3, n, own) for n in range(3)]
        above, below = (cross_edges, chip_edges) if below_is_chip else (chip_edges, cross_edges)
        for level in range(2):
            for tile in range(2):
                pert_win[2 * own + level, tile] = window[12 + 2 * level + tile]
                pert_win[2 * (1 - own) + level, tile] = partner[4 + 2 * level + tile]
        at = (7, 10) if own == 0 else (10, 7)
        up, down = above[at[0] : at[0] + 3], below[at[0] : at[0] + 3]
        for level in range(2):
            slow_win[level, 0] = jnp.where(upper, down[level], up[level])
            slow_win[level, 1] = jnp.where(upper, up[level], down[level])
        slow_win[0, 2] = jnp.where(upper, down[2], up[2])
        slow_win[1, 2] = pltpu.roll(jnp.where(upper, up[2], down[2]), 4, 0)
        pert_win[1, 2] = jnp.where(
            row < 2, pltpu.roll(down[2], 2, 0), jnp.where(row >= 6, pltpu.roll(up[2], 6, 0), 0.0)
        )
        up, down = above[at[1] : at[1] + 3], below[at[1] : at[1] + 3]
        slow_win[2, 0] = jnp.where(upper, down[0], up[0])
        slow_win[2, 1] = jnp.where(upper, up[0], down[0])
        pert_win[3, 2] = jnp.where(upper, down[1], up[1])
        pert_win[3, 3] = jnp.where(upper, up[1], down[1])
        pert_win[2, 2] = jnp.where(upper, down[2], up[2])
        up, down = surface_edges(above[:7], True), surface_edges(below[:7], False)
        planes = []
        for plane in range(4):
            up_inner, up_outer = up[plane]
            down_inner, down_outer = down[plane]
            planes.append(
                [
                    window[2 * plane],
                    window[2 * plane + 1],
                    jnp.where(upper, down_inner, up_inner),
                    jnp.where(upper, up_inner, down_inner),
                    jnp.where(upper, down_outer, up_outer),
                    jnp.where(upper, up_outer, down_outer),
                ]
            )
        for f in range(2):
            for tile in range(6):
                split_store(operand, f, tile, jnp.concatenate([planes[2 * f][tile], planes[2 * f + 1][tile]], axis=0))

    for own in range(2):
        for below_is_chip in (False, True):

            @pl.when((depth == own) & (even == below_is_chip))
            def _():
                fill(own, below_is_chip)

    def advance(f, level, tile, value):
        if tile < 2:
            cosine, sine = own_phases[f, level, tile, :8], own_phases[f, level, tile, 8:]
        else:
            slow = slow_win[level, tile - 2]
            cosine, sine = phase(over_columns(freq_tiles[f], slow) * 0.25 * slow)
            if tile == 2 and level > 0:
                halo_phases[f, level - 1, :8] = cosine
                halo_phases[f, level - 1, 8:] = sine
        v_re, v_im = value[:8], value[8:]
        re = cosine * v_re - sine * v_im
        im = cosine * v_im + sine * v_re
        if tile < 2:
            part = (re * re + im * im) * 0.5
            image_win[level, tile] = part if f == 0 else image_win[level, tile] + part
        return re, im

    tiles = (6, 5, 5, 4)
    for level in range(3):
        for f in range(2):
            for tile, value in enumerate(stencil(bands, operand, f, tiles[level + 1], tiles[level])):
                both = jnp.concatenate(advance(f, level, tile, value), axis=0)
                split_store(operand, f, tile, both)
                if tile < 3:
                    fields[f, level, tile] = both
    for f in range(2):
        for tile, value in enumerate(stencil(bands, operand, f, 4, 4)):
            twice = 2.0 * pert_win[3, tile]
            if tile < 2:
                re, im = advance(f, 3, tile, value)
                part = gradient_part(freq_tiles[f], twice * re, twice * im, re, im)
                last_gradient[tile] = part if f == 0 else last_gradient[tile] + part
            split_store(operand_out, f, tile, jnp.concatenate([twice * value[:8], twice * value[8:]], axis=0))
    deliver(depth, image, theirs, image_win)


def backward_kernel(
    freq_tiles, back_bands, own_phases, halo_phases, fields, pert_win, last_gradient, first_operand,
    gradient, theirs, operand, grad_win,
):
    tiles = (2, 3, 3, 4)
    source = first_operand
    for tile in range(2):
        grad_win[3, tile] = last_gradient[tile]
    for level in (2, 1, 0):
        for f in range(2):
            for tile, value in enumerate(stencil(back_bands, source, f, tiles[level], tiles[level + 1])):
                twice = 2.0 * pert_win[level, tile]
                u_re, u_im = fields[f, level, tile, :8], fields[f, level, tile, 8:]
                w_re = value[:8] + twice * u_re
                w_im = value[8:] + twice * u_im
                if tile < 2:
                    part = gradient_part(freq_tiles[f], w_re, w_im, u_re, u_im)
                    grad_win[level, tile] = part if f == 0 else grad_win[level, tile] + part
                if level > 0:
                    if tile < 2:
                        cosine, sine = own_phases[f, level, tile, :8], own_phases[f, level, tile, 8:]
                    else:
                        cosine, sine = halo_phases[f, level - 1, :8], halo_phases[f, level - 1, 8:]
                    back = [cosine * w_re + sine * w_im, cosine * w_im - sine * w_re]
                    split_store(operand, f, tile, jnp.concatenate(back, axis=0))
        source = operand
    deliver(lax.axis_index("depth"), gradient, theirs, grad_win)


def update_kernel(gradient_tiles, image_tiles, gradient_in, image_in, gradient, image, gradient_rows, image_rows, sems):
    half = gradient_rows.shape[2]
    blocks = half // LANES
    start = pl.multiple_of((1 - lax.axis_index("depth")) * half, LANES)
    copies = []
    for n, (tiles, rows, whole) in enumerate(
        ((image_tiles, image_rows, image), (gradient_tiles, gradient_rows, gradient))
    ):
        for level in range(2):
            for tile in range(2):
                for block in range(blocks):
                    rows[level, 8 * tile : 8 * tile + 8, LANES * block : LANES * (block + 1)] = tiles[
                        blocks * (2 * level + tile) + block
                    ]
        copies.append(pltpu.make_async_copy(rows, whole.at[:, :, pl.ds(start, half)], sems.at[n]))
        copies[-1].start()
    for copy in copies:
        copy.wait()


def split_columns(surface_data, frequencies, coefficients, slowness, perturbation):
    count = lax.axis_size("xy")
    columns = slowness.shape[2]
    half = columns // 2
    width = half + LANES
    step = half - LANES
    f32 = jnp.float32
    axes = ("depth", "xy")

    def moved(value, other_depth, neighbour):
        pairs = []
        for depth in range(2):
            for place in range(count):
                target = {"chip": place ^ 1, "cross": place + 1 if place % 2 else place - 1, "same": place}[neighbour]
                if 0 <= target < count:
                    layer = 1 - depth if other_depth else depth
                    pairs.append((depth * count + place, layer * count + target))
        return lax.ppermute(value, axes, pairs)

    vmem = pl.BlockSpec(memory_space=pltpu.VMEM)
    smem = pl.BlockSpec(memory_space=pltpu.SMEM)
    tile = lambda n: jax.ShapeDtypeStruct((n, 8, width), f32)
    packed = lambda n: jax.ShapeDtypeStruct((n * half // LANES + 1, 8, LANES), f32)
    params = lambda mib: pltpu.CompilerParams(vmem_limit_bytes=mib * 2**20)
    cross, bulk, cross_far, window = pl.pallas_call(
        lambda *refs: pack_kernel(width, step, *refs),
        out_shape=(packed(10), packed(8), packed(3), tile(16)),
        in_specs=[pl.BlockSpec(memory_space=pltpu.HBM)] * 3,
        out_specs=(vmem,) * 4,
        scratch_shapes=[
            pltpu.VMEM(surface_data.shape, f32),
            pltpu.VMEM(slowness.shape, f32),
            pltpu.VMEM(perturbation.shape, f32),
            pltpu.SemaphoreType.DMA((3,)),
        ],
        compiler_params=params(32),
        name="pack",
    )(*(pltpu.with_memory_space_constraint(x, pltpu.HBM) for x in (surface_data, slowness, perturbation)))
    cross = moved(cross, False, "cross")
    bulk = moved(bulk, True, "same")
    cross_far = moved(cross_far, True, "cross")
    bands, back_bands, freq_tiles = pl.pallas_call(
        lambda *refs: band_kernel(count * ROWS, *refs),
        out_shape=(
            jax.ShapeDtypeStruct((2, 240, 288), jnp.bfloat16),
            jax.ShapeDtypeStruct((2, 144, 192), jnp.bfloat16),
            jax.ShapeDtypeStruct((2, 8, LANES), f32),
        ),
        in_specs=[smem] * 2,
        out_specs=(vmem,) * 3,
        compiler_params=params(16),
        cost_estimate=pl.CostEstimate(flops=10**10, bytes_accessed=10**6, transcendentals=0),
        name="bands",
    )(coefficients, frequencies)
    chip, partner = pl.pallas_call(
        relay_kernel,
        out_shape=(packed(13), tile(8)),
        in_specs=[vmem] * 2,
        out_specs=(vmem,) * 2,
        compiler_params=params(32),
        cost_estimate=pl.CostEstimate(flops=10**10, bytes_accessed=10**6, transcendentals=0),
        name="relay",
    )(window, bulk)
    chip = moved(chip, False, "chip")

    own_phases = pl.pallas_call(
        own_phases_kernel,
        out_shape=jax.ShapeDtypeStruct((2, 4, 2, 16, width), f32),
        in_specs=[vmem] * 3,
        out_specs=vmem,
        compiler_params=params(16),
        name="own_phases",
    )(freq_tiles, window, partner)

    own = jax.ShapeDtypeStruct((2, ROWS, columns), f32)
    sent = lambda spare: jax.ShapeDtypeStruct((2 * ROWS // 8 * half // LANES + spare, 8, LANES), f32)
    image, theirs_image, fields, halo_phases, pert_win, last_gradient, operand = pl.pallas_call(
        forward_kernel,
        out_shape=(
            own,
            sent(SPARE),
            jax.ShapeDtypeStruct((2, 3, 3, 16, width), f32),
            jax.ShapeDtypeStruct((2, 2, 16, width), f32),
            jax.ShapeDtypeStruct((4, 4, 8, width), f32),
            tile(2),
            jax.ShapeDtypeStruct((2, 192, width), jnp.bfloat16),
        ),
        in_specs=[vmem] * 8,
        out_specs=(vmem,) * 7,
        scratch_shapes=[
            pltpu.VMEM((3, 3, 8, width), f32),
            pltpu.VMEM((2, 288, width), jnp.bfloat16),
            pltpu.VMEM((4, 2, 8, width), f32),
        ],
        compiler_params=params(32),
        name="forward",
    )(freq_tiles, bands, own_phases, window, partner, cross, cross_far, chip)
    gradient, theirs = pl.pallas_call(
        backward_kernel,
        out_shape=(own, sent(0)),
        in_specs=[vmem] * 8,
        out_specs=(vmem,) * 2,
        scratch_shapes=[
            pltpu.VMEM((2, 144, width), jnp.bfloat16),
            pltpu.VMEM((4, 2, 8, width), f32),
        ],
        compiler_params=params(32),
        cost_estimate=pl.CostEstimate(flops=10**10, bytes_accessed=10**6, transcendentals=0),
        name="backward",
    )(freq_tiles, back_bands, own_phases, halo_phases, fields, pert_win, last_gradient, operand)
    theirs_image = moved(theirs_image, True, "same")
    theirs = moved(theirs, True, "same")
    hbm = pl.BlockSpec(memory_space=pltpu.HBM)
    in_place = [pltpu.with_memory_space_constraint(x, pltpu.HBM) for x in (gradient, image)]
    return pl.pallas_call(
        update_kernel,
        out_shape=(own, own),
        in_specs=[vmem, vmem, hbm, hbm],
        out_specs=(hbm, hbm),
        scratch_shapes=[pltpu.VMEM((2, ROWS, half), f32)] * 2 + [pltpu.SemaphoreType.DMA((2,))],
        input_output_aliases={2: 0, 3: 1},
        compiler_params=params(8),
        name="update",
    )(theirs, theirs_image, *in_place)


def on_slice(surface_data, frequencies, coefficients, slowness, perturbation):
    levels, rows, columns = slowness.shape
    fits = (
        lax.axis_size("depth") == 2
        and levels == 2
        and rows == ROWS
        and frequencies.shape[0] == 2
        and lax.axis_size("xy") % 2 == 0
        and columns % (2 * LANES) == 0
        and columns >= 4 * LANES
    )
    plan = split_columns if fits else on_device
    return plan(surface_data, frequencies, coefficients, slowness, perturbation)


def solution(mesh):
    in_specs = (P(None, None, "xy", None), P(), P(), P("depth", "xy", None), P("depth", "xy", None))
    out_specs = (P("depth", "xy", None), P("depth", "xy", None))
    return jax.shard_map(
        on_slice, mesh=mesh, in_specs=in_specs, out_specs=out_specs, check_vma=False
    )
```

```python
import numpy as np
import jax
import jax.numpy as jnp
from jax import lax
from jax.experimental import pallas as pl
from jax.experimental.pallas import tpu as pltpu
from jax.sharding import PartitionSpec as P

layer_thickness = 0.5


def extended_2(cells, sides, width):
    for axis, dim in sides:
        count = lax.axis_size(axis)
        ends = count - 1
        head = lax.slice_in_dim(cells, 0, width, axis=dim)
        tail = lax.slice_in_dim(cells, cells.shape[dim] - width, cells.shape[dim], axis=dim)
        cells = jnp.concatenate(
            [
                lax.ppermute(tail, axis, [(i, (i + 1) % count) for i in range(ends)]),
                cells,
                lax.ppermute(head, axis, [((i + 1) % count, i) for i in range(ends)]),
            ],
            axis=dim,
        )
    return cells


def shifted(value, axis, steps):
    count = lax.axis_size(axis)
    initial, last = (max(0, -steps), min(count, count - steps))
    return lax.ppermute(value, axis, [(source, source + steps) for source in range(initial, last)])


def apply_stencil(extended, tap_re, tap_im):
    out_rows = extended.shape[2] - 4
    col_count = extended.shape[3]
    padded = jnp.pad(extended, ((0, 0), (0, 0), (0, 0), (1, 1)))
    acc_re = jnp.zeros((extended.shape[0], out_rows, col_count), jnp.float32)
    acc_im = jnp.zeros((extended.shape[0], out_rows, col_count), jnp.float32)
    for row_off in range(5):
        for col_off in range(3):
            tap_index = row_off * 3 + col_off
            part_re = padded[:, 0, row_off : row_off + out_rows, col_off : col_off + col_count]
            part_im = padded[:, 1, row_off : row_off + out_rows, col_off : col_off + col_count]
            weight_re = tap_re[:, tap_index][:, None, None]
            weight_im = tap_im[:, tap_index][:, None, None]
            acc_re = acc_re + weight_re * part_re - weight_im * part_im
            acc_im = acc_im + weight_re * part_im + weight_im * part_re
    return (acc_re, acc_im)


def adjoint_stencil(extended, tap_re, tap_im):
    out_rows = extended.shape[2] - 4
    col_count = extended.shape[3]
    padded = jnp.pad(extended, ((0, 0), (0, 0), (0, 0), (1, 1)))
    acc_re = jnp.zeros((extended.shape[0], out_rows, col_count), jnp.float32)
    acc_im = jnp.zeros((extended.shape[0], out_rows, col_count), jnp.float32)
    for row_off in range(5):
        for col_off in range(3):
            tap_index = row_off * 3 + col_off
            row_from = 4 - row_off
            col_from = 2 - col_off
            part_re = padded[:, 0, row_from : row_from + out_rows, col_from : col_from + col_count]
            part_im = padded[:, 1, row_from : row_from + out_rows, col_from : col_from + col_count]
            weight_re = tap_re[:, tap_index][:, None, None]
            weight_im = tap_im[:, tap_index][:, None, None]
            acc_re = acc_re + weight_re * part_re + weight_im * part_im
            acc_im = acc_im + weight_re * part_im - weight_im * part_re
    return (acc_re, acc_im)


def phase_parts(freqs, slow_plane):
    angle = freqs[:, None, None] * layer_thickness * slow_plane[None]
    return (jnp.cos(angle), jnp.sin(angle))


def forward_steps(wavefield, freqs, taps, slowness, freq_total):
    tap_re = taps[:, 0]
    tap_im = taps[:, 1]
    step_count = slowness.shape[0]
    states = []
    current = wavefield
    for level in range(step_count):
        extended = extended_2(current, (("xy", 2),), 2)
        acc_re, acc_im = apply_stencil(extended, tap_re, tap_im)
        phase_re, phase_im = phase_parts(freqs, slowness[level])
        next_re = phase_re * acc_re - phase_im * acc_im
        next_im = phase_re * acc_im + phase_im * acc_re
        current = jnp.stack([next_re, next_im], axis=1)
        states.append(current)
    stacked = jnp.stack(states, axis=1)
    image_part = (
        jnp.sum(stacked[:, :, 0] * stacked[:, :, 0] + stacked[:, :, 1] * stacked[:, :, 1], axis=0)
        / freq_total
    )
    return (stacked, states[-1], image_part)


def backward_steps(adjoint, states, freqs, taps, slowness, perturbation, freq_total):
    tap_re = taps[:, 0]
    tap_im = taps[:, 1]
    step_count = slowness.shape[0]
    parts = [None] * step_count
    for level in reversed(range(step_count)):
        wave_re = states[:, level, 0]
        wave_im = states[:, level, 1]
        grad_re = adjoint[:, 0] + 2.0 * perturbation[level] * wave_re
        grad_im = adjoint[:, 1] + 2.0 * perturbation[level] * wave_im
        parts[level] = (
            layer_thickness
            / freq_total
            * jnp.sum(freqs[:, None, None] * (grad_im * wave_re - grad_re * wave_im), axis=0)
        )
        phase_re, phase_im = phase_parts(freqs, slowness[level])
        back_re = phase_re * grad_re + phase_im * grad_im
        back_im = phase_re * grad_im - phase_im * grad_re
        extended = extended_2(jnp.stack([back_re, back_im], axis=1), (("xy", 2),), 2)
        acc_re, acc_im = adjoint_stencil(extended, tap_re, tap_im)
        adjoint = jnp.stack([acc_re, acc_im], axis=1)
    return (adjoint, jnp.stack(parts, axis=0))


def on_device(surface_data, frequencies, coefficients, slowness, perturbation):
    freq_count = frequencies.shape[0]
    step_count = slowness.shape[0]
    row_count = slowness.shape[1]
    col_count = slowness.shape[2]
    layers = lax.axis_size("depth")
    depth_index = lax.axis_index("depth")
    stored_zero = jnp.zeros((freq_count, step_count, 2, row_count, col_count), jnp.float32)
    plane_zero = jnp.zeros((step_count, row_count, col_count), jnp.float32)
    start = jnp.where(depth_index == 0, surface_data, jnp.zeros_like(surface_data))

    def forward_segment(segment_no, carry):
        current, stored, image_sum = carry
        states, bottom, image_part = forward_steps(
            current, frequencies, coefficients, slowness, freq_count
        )
        chosen = depth_index == segment_no
        stored = jnp.where(chosen, states, stored)
        image_sum = jnp.where(chosen, image_part, image_sum)
        current = shifted(bottom, "depth", 1)
        return (current, stored, image_sum)

    unused_field, stored, image_field = lax.fori_loop(
        0, layers, forward_segment, (start, stored_zero, plane_zero)
    )

    def backward_segment(segment_no, carry):
        adjoint, gradient_sum = carry
        top_field, parts = backward_steps(
            adjoint, stored, frequencies, coefficients, slowness, perturbation, freq_count
        )
        gradient_sum = jnp.where(depth_index == layers - 1 - segment_no, parts, gradient_sum)
        adjoint = shifted(top_field, "depth", -1)
        return (adjoint, gradient_sum)

    adjoint_zero = jnp.zeros_like(surface_data)
    unused_adjoint, gradient = lax.fori_loop(
        0, layers, backward_segment, (adjoint_zero, plane_zero)
    )
    return (gradient, image_field)


ROWS = 16
HALO_TILES = 4
LANES = 128

OVERLAP = 8

sin_terms = (0.9999999995, -0.1666666515, 0.008333256964, -0.0001982776292, 2.657952479e-06)
cos_terms = (0.9999999947, -0.4999998344, 0.04166583045, -0.00138740917, 2.372928386e-05)


def window_row(tile, sub):
    group = tile - 2
    above = sub - 4 * (group + 1)
    below = sub + ROWS + 4 * group
    even = jnp.where(sub < 4, below, above - 4)
    odd = jnp.where(sub < 4, above, below - 4)
    halo = jnp.where(lax.rem(tile, 2) == 0, even, odd)
    return jnp.where(tile < 2, 8 * tile + sub, halo)


def band_kernel(plane_rows, taps, freqs, bands, back_bands, freq_tiles):
    first_row = lax.axis_index("xy") * ROWS

    def fill(ref, adjoint):
        out_tiles = ref.shape[1] // 48
        in_tiles = ref.shape[2] // 48
        shape = (16, ref.shape[2])
        col = lax.broadcasted_iota(jnp.int32, shape, 1)
        sub = lax.broadcasted_iota(jnp.int32, shape, 0)
        tile_k = sum((col >= 48 * t).astype(jnp.int32) for t in range(1, in_tiles))
        row_k = window_row(tile_k, col & 7)
        part_k = (col >> 4) - 3 * tile_k
        plane_k = (col >> 3) & 1
        plane_m = sub >> 3
        same = plane_k == plane_m
        inside_k = (row_k + first_row >= 0) & (row_k + first_row < plane_rows)
        for tile in range(out_tiles):
            row_m = window_row(jnp.full(shape, tile, jnp.int32), sub & 7)
            inside = inside_k & (row_m + first_row >= 0) & (row_m + first_row < plane_rows)
            offset = jnp.where(inside, row_k - row_m, 9)
            hits = [offset == a - 2 for a in range(5)]
            for f in range(ref.shape[0]):
                for b in range(3):
                    total = jnp.zeros(shape, jnp.float32)
                    for a in range(5):
                        tap = 3 * (4 - a) + 2 - b if adjoint else 3 * a + b
                        re = taps[f, 0, tap]
                        im = -taps[f, 1, tap] if adjoint else taps[f, 1, tap]
                        crossed = jnp.where(plane_m == 0, -im, im)
                        total = jnp.where(hits[a], jnp.where(same, re, crossed), total)
                    high = total.astype(jnp.bfloat16)
                    low = total - high.astype(jnp.float32)
                    base = 48 * tile + 16 * b
                    ref[f, base : base + 16] = jnp.where(part_k == 1, low, total).astype(jnp.bfloat16)

    fill(bands, False)
    fill(back_bands, True)
    for f in range(freq_tiles.shape[0]):
        freq_tiles[f] = jnp.full((8, LANES), freqs[f], jnp.float32)


def pack_rows(ref, values, side):
    lane = lax.broadcasted_iota(jnp.int32, (8, LANES), 1)
    overlaps = jnp.zeros((8, LANES), jnp.float32)
    blocks = (values[0].shape[1] - LANES) // LANES
    for n, value in enumerate(values):
        for block in range(blocks):
            ref[blocks * n + block] = value[:, (block + side) * LANES : (block + side + 1) * LANES]
        extra = value[:, : LANES] if side else value[:, blocks * LANES :]
        turn = (OVERLAP * (n + side)) % LANES
        extra = pltpu.roll(extra, turn, 1) if turn else extra
        overlaps = jnp.where((lane >= OVERLAP * n) & (lane < OVERLAP * (n + 1)), extra, overlaps)
    ref[blocks * len(values)] = overlaps


def unpack_rows(ref, tiles, n, side):
    blocks = (ref.shape[0] - 1) // tiles
    turn = (-OVERLAP * (n + side)) % LANES
    extra = ref[blocks * tiles]
    extra = pltpu.roll(extra, turn, 1) if turn else extra
    parts = [ref[blocks * n + block] for block in range(blocks)]
    return jnp.concatenate([extra] + parts if side else parts + [extra], axis=1)


def edge_levels(levels, slow, pert, down):
    inner, outer = (1, 0) if down else (0, 1)
    if levels == 1:
        return [slow(0, inner), pert(1, inner), pert(0, inner)]
    row = lax.broadcasted_iota(jnp.int32, slow(0, 0).shape, 0)
    turned = pltpu.roll(slow(1, outer), 4, 0)
    if down:
        extra = jnp.where(row < 2, pltpu.roll(pert(1, inner), 2, 0), turned)
        last = jnp.where(row < 4, extra, slow(0, outer))
    else:
        extra = jnp.where(row >= 6, pltpu.roll(pert(1, inner), 6, 0), turned)
        last = jnp.where(row < 4, slow(0, outer), extra)
    return [slow(0, inner), slow(1, inner), last]


def edge_surface(surf, down):
    inner, outer = (1, 0) if down else (0, 1)
    tiles = [surf(plane, inner) for plane in range(4)]
    row = lax.broadcasted_iota(jnp.int32, tiles[0].shape, 0)
    spread = surf(3, outer)
    for plane in range(3):
        turn = 6 - 2 * plane
        free = row < 2 if down else row >= 6
        tiles.append(jnp.where(free, pltpu.roll(spread, turn, 0), surf(plane, outer)))
    return tiles


def surface_edges(tiles, down):
    row = lax.broadcasted_iota(jnp.int32, tiles[0].shape, 0)
    outer = [tiles[4], tiles[5], tiles[6]]
    first = 2 if down else 0
    spread = pltpu.roll(tiles[6], 6, 0)
    spread = jnp.where((row >= first + 2) & (row < first + 4), pltpu.roll(tiles[5], 4, 0), spread)
    spread = jnp.where((row >= first) & (row < first + 2), pltpu.roll(tiles[4], 2, 0), spread)
    outer.append(spread)
    return [(tiles[plane], outer[plane]) for plane in range(4)]


def pack_kernel(width, step, surf_in, slow_in, pert_in, cross, bulk, cross_far, window, surf, slow, pert, sems):
    pairs = [(slow_in.at[level], slow.at[level]) for level in range(2)]
    pairs += [(pert_in.at[level], pert.at[level]) for level in range(2)]
    pairs += [(surf_in.at[f, part], surf.at[f, part]) for f in range(2) for part in range(2)]
    copies = [pltpu.make_async_copy(source, target, sems.at[n]) for n, (source, target) in enumerate(pairs)]
    for copy in copies:
        copy.start()
    for copy in copies:
        copy.wait()
    depth = lax.axis_index("depth")
    place = lax.axis_index("xy")
    for own in range(2):

        def reader(ref, side):
            lanes = slice(side * step, side * step + width)
            return lambda level, tile: ref[level, 8 * tile : 8 * tile + 8, lanes]

        def surface(plane, tile):
            return surf[plane // 2, plane % 2, 8 * tile : 8 * tile + 8, own * step : own * step + width]

        @pl.when(depth == own)
        def _():
            slow_near, pert_near = reader(slow, own), reader(pert, own)
            slow_far, pert_far = reader(slow, 1 - own), reader(pert, 1 - own)
            both = [(level, tile) for level in range(2) for tile in range(2)]
            for n, (level, tile) in enumerate(both):
                window[8 + n] = slow_near(level, tile)
                window[12 + n] = pert_near(level, tile)
            for plane in range(4):
                for tile in range(2):
                    window[2 * plane + tile] = surface(plane, tile)
            pack_rows(bulk, [slow_far(*at) for at in both] + [pert_far(*at) for at in both], 1 - own)
            for down in (False, True):

                @pl.when((lax.rem(place, 2) == 1) == down)
                def _():
                    edges = edge_surface(surface, down) + edge_levels(own, slow_near, pert_near, down)
                    pack_rows(cross, edges, own)
                    pack_rows(cross_far, edge_levels(own, slow_far, pert_far, down), 1 - own)


def relay_kernel(window, bulk, chip, partner):
    depth = lax.axis_index("depth")
    place = lax.axis_index("xy")
    for own in range(2):

        @pl.when(depth == own)
        def _():
            other = [unpack_rows(bulk, 8, n, own) for n in range(8)]
            for n in range(8):
                partner[n] = other[n]
            readers = {
                own: (lambda level, tile: window[8 + 2 * level + tile], lambda level, tile: window[12 + 2 * level + tile]),
                1 - own: (lambda level, tile: other[2 * level + tile], lambda level, tile: other[4 + 2 * level + tile]),
            }
            for down in (False, True):

                @pl.when((lax.rem(place, 2) == 0) == down)
                def _():
                    edges = edge_surface(lambda plane, tile: window[2 * plane + tile], down)
                    for levels in (own, 1 - own):
                        edges = edges + edge_levels(levels, *readers[levels], down)
                    pack_rows(chip, edges, own)


def phase(half):
    square = half * half
    cosine = cos_terms[-1]
    sine = sin_terms[-1]
    for term in cos_terms[-2::-1]:
        cosine = cosine * square + term
    for term in sin_terms[-2::-1]:
        sine = sine * square + term
    sine = sine * half
    twice = sine + sine
    return 1.0 - twice * sine, twice * cosine


def own_phases_kernel(freq_tiles, window, partner, phases):
    depth = lax.axis_index("depth")
    for level in range(4):
        for tile in range(2):
            own, other = window[8 + 2 * (level % 2) + tile], partner[2 * (level % 2) + tile]
            slow = jnp.where(depth == level // 2, own, other)
            for f in range(2):
                cosine, sine = phase(over_columns(freq_tiles[f], slow) * 0.25 * slow)
                phases[f, level, tile, :8] = cosine
                phases[f, level, tile, 8:] = sine


def over_columns(tile, like):
    return jnp.concatenate([tile] * (like.shape[1] // LANES), axis=1)


def sweep_kernel(
    width, freq_tiles, bands, back_bands, own_phases, window, partner, cross, cross_far, chip,
    gradient, image, theirs, slow_win, pert_win, operand, halo_phases, fields, image_win, grad_win,
):
    depth = lax.axis_index("depth")
    place = lax.axis_index("xy")
    half = width - LANES
    row = lax.broadcasted_iota(jnp.int32, (8, width), 0)
    upper = row < 4
    lane = lax.broadcasted_iota(jnp.int32, (16, LANES), 1)
    even = lax.rem(place, 2) == 0
    freqs = [jnp.concatenate([freq_tiles[f]] * (width // LANES), axis=1) for f in range(2)]

    def store_operand(f, tile, value):
        high = value.astype(jnp.bfloat16)
        low = (value - high.astype(jnp.float32)).astype(jnp.bfloat16)
        base = 48 * tile
        operand[f, base : base + 16] = high
        operand[f, base + 16 : base + 32] = high
        operand[f, base + 32 : base + 48] = low

    def stencil(f, matrix, out_tiles, in_tiles):
        product = jnp.dot(
            matrix[f, : 48 * out_tiles, : 48 * in_tiles],
            operand[f, : 48 * in_tiles],
            preferred_element_type=jnp.float32,
        )
        result = []
        for tile in range(out_tiles):
            base = 48 * tile
            left = pltpu.roll(product[base : base + 16], 1, 1)
            right = pltpu.roll(product[base + 32 : base + 48], width - 1, 1)
            left = jnp.concatenate([jnp.where(lane == 0, 0.0, left[:, :LANES]), left[:, LANES:]], axis=1)
            right = jnp.concatenate([right[:, :half], jnp.where(lane == LANES - 1, 0.0, right[:, half:])], axis=1)
            result.append(product[base + 16 : base + 32] + left + right)
        return result

    def fill(own, below_is_chip):
        chip_edges = [unpack_rows(chip, 13, n, own) for n in range(13)]
        cross_edges = [unpack_rows(cross, 10, n, own) for n in range(10)]
        cross_edges += [unpack_rows(cross_far, 3, n, own) for n in range(3)]
        above, below = (cross_edges, chip_edges) if below_is_chip else (chip_edges, cross_edges)
        for level in range(2):
            for tile in range(2):
                pert_win[2 * own + level, tile] = window[12 + 2 * level + tile]
                pert_win[2 * (1 - own) + level, tile] = partner[4 + 2 * level + tile]
        at = (7, 10) if own == 0 else (10, 7)
        up, down = above[at[0] : at[0] + 3], below[at[0] : at[0] + 3]
        for level in range(2):
            slow_win[level, 0] = jnp.where(upper, down[level], up[level])
            slow_win[level, 1] = jnp.where(upper, up[level], down[level])
        slow_win[0, 2] = jnp.where(upper, down[2], up[2])
        slow_win[1, 2] = pltpu.roll(jnp.where(upper, up[2], down[2]), 4, 0)
        pert_win[1, 2] = jnp.where(
            row < 2, pltpu.roll(down[2], 2, 0), jnp.where(row >= 6, pltpu.roll(up[2], 6, 0), 0.0)
        )
        up, down = above[at[1] : at[1] + 3], below[at[1] : at[1] + 3]
        slow_win[2, 0] = jnp.where(upper, down[0], up[0])
        slow_win[2, 1] = jnp.where(upper, up[0], down[0])
        pert_win[3, 2] = jnp.where(upper, down[1], up[1])
        pert_win[3, 3] = jnp.where(upper, up[1], down[1])
        pert_win[2, 2] = jnp.where(upper, down[2], up[2])
        up, down = surface_edges(above[:7], True), surface_edges(below[:7], False)
        planes = []
        for plane in range(4):
            up_inner, up_outer = up[plane]
            down_inner, down_outer = down[plane]
            planes.append(
                [
                    window[2 * plane],
                    window[2 * plane + 1],
                    jnp.where(upper, down_inner, up_inner),
                    jnp.where(upper, up_inner, down_inner),
                    jnp.where(upper, down_outer, up_outer),
                    jnp.where(upper, up_outer, down_outer),
                ]
            )
        for f in range(2):
            for tile in range(6):
                store_operand(f, tile, jnp.concatenate([planes[2 * f][tile], planes[2 * f + 1][tile]], axis=0))

    for own in range(2):
        for below_is_chip in (False, True):

            @pl.when((depth == own) & (even == below_is_chip))
            def _():
                fill(own, below_is_chip)

    def add_image(f, level, tile, re, im):
        part = (re * re + im * im) * 0.5
        image_win[level, tile] = part if f == 0 else image_win[level, tile] + part

    def add_gradient(f, level, tile, w_re, w_im, u_re, u_im):
        part = (0.25 * freqs[f]) * (w_im * u_re - w_re * u_im)
        grad_win[level, tile] = part if f == 0 else grad_win[level, tile] + part

    def phases_of(f, level, tile):
        if tile < 2:
            return own_phases[f, level, tile, :8], own_phases[f, level, tile, 8:]
        cosine, sine = phase(freqs[f] * 0.25 * slow_win[level, tile - 2])
        if tile == 2 and level > 0:
            halo_phases[f, level - 1, :8] = cosine
            halo_phases[f, level - 1, 8:] = sine
        return cosine, sine

    tiles = (6, 5, 5, 4)
    for level in range(3):
        for f in range(2):
            fields_now = stencil(f, bands, tiles[level + 1], tiles[level])
            for tile, value in enumerate(fields_now):
                cosine, sine = phases_of(f, level, tile)
                v_re, v_im = value[:8], value[8:]
                re = cosine * v_re - sine * v_im
                im = cosine * v_im + sine * v_re
                both = jnp.concatenate([re, im], axis=0)
                store_operand(f, tile, both)
                if tile < 3:
                    fields[f, level, tile] = both
                if tile < 2:
                    add_image(f, level, tile, re, im)
    for f in range(2):
        for tile, value in enumerate(stencil(f, bands, 4, 4)):
            twice = 2.0 * pert_win[3, tile]
            v_re, v_im = value[:8], value[8:]
            if tile < 2:
                cosine, sine = phases_of(f, 3, tile)
                re = cosine * v_re - sine * v_im
                im = cosine * v_im + sine * v_re
                add_image(f, 3, tile, re, im)
                add_gradient(f, 3, tile, twice * re, twice * im, re, im)
            store_operand(f, tile, jnp.concatenate([twice * v_re, twice * v_im], axis=0))
    tiles = (2, 3, 3, 4)
    for level in (2, 1, 0):
        for f in range(2):
            for tile, value in enumerate(stencil(f, back_bands, tiles[level], tiles[level + 1])):
                twice = 2.0 * pert_win[level, tile]
                u_re, u_im = fields[f, level, tile, :8], fields[f, level, tile, 8:]
                w_re = value[:8] + twice * u_re
                w_im = value[8:] + twice * u_im
                if tile < 2:
                    add_gradient(f, level, tile, w_re, w_im, u_re, u_im)
                if level > 0:
                    if tile < 2:
                        cosine, sine = phases_of(f, level, tile)
                    else:
                        cosine, sine = halo_phases[f, level - 1, :8], halo_phases[f, level - 1, 8:]
                    back = [cosine * w_re + sine * w_im, cosine * w_im - sine * w_re]
                    store_operand(f, tile, jnp.concatenate(back, axis=0))

    for own in range(2):

        @pl.when(depth == own)
        def _():
            inner = slice(own * LANES, own * LANES + half)
            outer = slice(own * half, own * half + half)
            for level in range(2):
                for tile in range(2):
                    rows = slice(8 * tile, 8 * tile + 8)
                    gradient[level, rows, outer] = grad_win[2 * own + level, tile, :, inner]
                    image[level, rows, outer] = image_win[2 * own + level, tile, :, inner]
                    theirs[0, level, rows] = grad_win[2 * (1 - own) + level, tile, :, inner]
                    theirs[1, level, rows] = image_win[2 * (1 - own) + level, tile, :, inner]


def split_columns(surface_data, frequencies, coefficients, slowness, perturbation):
    count = lax.axis_size("xy")
    columns = slowness.shape[2]
    half = columns // 2
    width = half + LANES
    step = half - LANES
    f32 = jnp.float32
    axes = ("depth", "xy")

    def moved(value, other_depth, neighbour):
        pairs = []
        for depth in range(2):
            for place in range(count):
                target = {"chip": place ^ 1, "cross": place + 1 if place % 2 else place - 1, "same": place}[neighbour]
                if 0 <= target < count:
                    layer = 1 - depth if other_depth else depth
                    pairs.append((depth * count + place, layer * count + target))
        return lax.ppermute(value, axes, pairs)

    vmem = pl.BlockSpec(memory_space=pltpu.VMEM)
    smem = pl.BlockSpec(memory_space=pltpu.SMEM)
    tile = lambda n: jax.ShapeDtypeStruct((n, 8, width), f32)
    packed = lambda n: jax.ShapeDtypeStruct((n * half // LANES + 1, 8, LANES), f32)
    params = lambda mib: pltpu.CompilerParams(vmem_limit_bytes=mib * 2**20)
    cross, bulk, cross_far, window = pl.pallas_call(
        lambda *refs: pack_kernel(width, step, *refs),
        out_shape=(packed(10), packed(8), packed(3), tile(16)),
        in_specs=[pl.BlockSpec(memory_space=pltpu.HBM)] * 3,
        out_specs=(vmem,) * 4,
        scratch_shapes=[
            pltpu.VMEM(surface_data.shape, f32),
            pltpu.VMEM(slowness.shape, f32),
            pltpu.VMEM(perturbation.shape, f32),
            pltpu.SemaphoreType.DMA((8,)),
        ],
        compiler_params=params(32),
        name="pack",
    )(*(pltpu.with_memory_space_constraint(x, pltpu.HBM) for x in (surface_data, slowness, perturbation)))
    cross = moved(cross, False, "cross")
    bulk = moved(bulk, True, "same")
    cross_far = moved(cross_far, True, "cross")
    bands, back_bands, freq_tiles = pl.pallas_call(
        lambda *refs: band_kernel(count * ROWS, *refs),
        out_shape=(
            jax.ShapeDtypeStruct((2, 240, 288), jnp.bfloat16),
            jax.ShapeDtypeStruct((2, 144, 192), jnp.bfloat16),
            jax.ShapeDtypeStruct((2, 8, LANES), f32),
        ),
        in_specs=[smem] * 2,
        out_specs=(vmem,) * 3,
        compiler_params=params(16),
        cost_estimate=pl.CostEstimate(flops=10**10, bytes_accessed=10**6, transcendentals=0),
        name="bands",
    )(coefficients, frequencies)
    chip, partner = pl.pallas_call(
        relay_kernel,
        out_shape=(packed(13), tile(8)),
        in_specs=[vmem] * 2,
        out_specs=(vmem,) * 2,
        compiler_params=params(32),
        cost_estimate=pl.CostEstimate(flops=10**10, bytes_accessed=10**6, transcendentals=0),
        name="relay",
    )(window, bulk)
    chip = moved(chip, False, "chip")

    own_phases = pl.pallas_call(
        own_phases_kernel,
        out_shape=jax.ShapeDtypeStruct((2, 4, 2, 16, width), f32),
        in_specs=[vmem] * 3,
        out_specs=vmem,
        compiler_params=params(16),
        name="own_phases",
    )(freq_tiles, window, partner)

    own = jax.ShapeDtypeStruct((2, ROWS, columns), f32)
    gradient, image, theirs = pl.pallas_call(
        lambda *refs: sweep_kernel(width, *refs),
        out_shape=(own, own, jax.ShapeDtypeStruct((2, 2, ROWS, half), f32)),
        in_specs=[vmem] * 9,
        out_specs=(vmem,) * 3,
        scratch_shapes=[
            pltpu.VMEM((3, 3, 8, width), f32),
            pltpu.VMEM((4, 4, 8, width), f32),
            pltpu.VMEM((2, 288, width), jnp.bfloat16),
            pltpu.VMEM((2, 2, 16, width), f32),
            pltpu.VMEM((2, 3, 3, 16, width), f32),
            pltpu.VMEM((4, 2, 8, width), f32),
            pltpu.VMEM((4, 2, 8, width), f32),
        ],
        compiler_params=params(40),
        name="sweep",
    )(
        freq_tiles, bands, back_bands, own_phases, window, partner, cross, cross_far, chip,
    )
    theirs = moved(theirs, True, "same")
    start = (1 - lax.axis_index("depth")) * half
    gradient = lax.dynamic_update_slice(gradient, theirs[0], (0, 0, start))
    image = lax.dynamic_update_slice(image, theirs[1], (0, 0, start))
    return gradient, image


def on_slice(surface_data, frequencies, coefficients, slowness, perturbation):
    levels, rows, columns = slowness.shape
    fits = (
        lax.axis_size("depth") == 2
        and levels == 2
        and rows == ROWS
        and frequencies.shape[0] == 2
        and lax.axis_size("xy") % 2 == 0
        and columns % (2 * LANES) == 0
        and columns >= 4 * LANES
    )
    plan = split_columns if fits else on_device
    return plan(surface_data, frequencies, coefficients, slowness, perturbation)


def solution(mesh):
    in_specs = (P(None, None, "xy", None), P(), P(), P("depth", "xy", None), P("depth", "xy", None))
    out_specs = (P("depth", "xy", None), P("depth", "xy", None))
    return jax.shard_map(
        on_slice, mesh=mesh, in_specs=in_specs, out_specs=out_specs, check_vma=False
    )
```

```python
import numpy as np
import jax
import jax.numpy as jnp
from jax import lax
from jax.experimental import pallas as pl
from jax.experimental.pallas import tpu as pltpu
from jax.sharding import PartitionSpec as P

layer_thickness = 0.5


def extended_2(cells, sides, width):
    for axis, dim in sides:
        count = lax.axis_size(axis)
        ends = count - 1
        head = lax.slice_in_dim(cells, 0, width, axis=dim)
        tail = lax.slice_in_dim(cells, cells.shape[dim] - width, cells.shape[dim], axis=dim)
        cells = jnp.concatenate(
            [
                lax.ppermute(tail, axis, [(i, (i + 1) % count) for i in range(ends)]),
                cells,
                lax.ppermute(head, axis, [((i + 1) % count, i) for i in range(ends)]),
            ],
            axis=dim,
        )
    return cells


def shifted(value, axis, steps):
    count = lax.axis_size(axis)
    initial, last = (max(0, -steps), min(count, count - steps))
    return lax.ppermute(value, axis, [(source, source + steps) for source in range(initial, last)])


def apply_stencil(extended, tap_re, tap_im):
    out_rows = extended.shape[2] - 4
    col_count = extended.shape[3]
    padded = jnp.pad(extended, ((0, 0), (0, 0), (0, 0), (1, 1)))
    acc_re = jnp.zeros((extended.shape[0], out_rows, col_count), jnp.float32)
    acc_im = jnp.zeros((extended.shape[0], out_rows, col_count), jnp.float32)
    for row_off in range(5):
        for col_off in range(3):
            tap_index = row_off * 3 + col_off
            part_re = padded[:, 0, row_off : row_off + out_rows, col_off : col_off + col_count]
            part_im = padded[:, 1, row_off : row_off + out_rows, col_off : col_off + col_count]
            weight_re = tap_re[:, tap_index][:, None, None]
            weight_im = tap_im[:, tap_index][:, None, None]
            acc_re = acc_re + weight_re * part_re - weight_im * part_im
            acc_im = acc_im + weight_re * part_im + weight_im * part_re
    return (acc_re, acc_im)


def adjoint_stencil(extended, tap_re, tap_im):
    out_rows = extended.shape[2] - 4
    col_count = extended.shape[3]
    padded = jnp.pad(extended, ((0, 0), (0, 0), (0, 0), (1, 1)))
    acc_re = jnp.zeros((extended.shape[0], out_rows, col_count), jnp.float32)
    acc_im = jnp.zeros((extended.shape[0], out_rows, col_count), jnp.float32)
    for row_off in range(5):
        for col_off in range(3):
            tap_index = row_off * 3 + col_off
            row_from = 4 - row_off
            col_from = 2 - col_off
            part_re = padded[:, 0, row_from : row_from + out_rows, col_from : col_from + col_count]
            part_im = padded[:, 1, row_from : row_from + out_rows, col_from : col_from + col_count]
            weight_re = tap_re[:, tap_index][:, None, None]
            weight_im = tap_im[:, tap_index][:, None, None]
            acc_re = acc_re + weight_re * part_re + weight_im * part_im
            acc_im = acc_im + weight_re * part_im - weight_im * part_re
    return (acc_re, acc_im)


def phase_parts(freqs, slow_plane):
    angle = freqs[:, None, None] * layer_thickness * slow_plane[None]
    return (jnp.cos(angle), jnp.sin(angle))


def forward_steps(wavefield, freqs, taps, slowness, freq_total):
    tap_re = taps[:, 0]
    tap_im = taps[:, 1]
    step_count = slowness.shape[0]
    states = []
    current = wavefield
    for level in range(step_count):
        extended = extended_2(current, (("xy", 2),), 2)
        acc_re, acc_im = apply_stencil(extended, tap_re, tap_im)
        phase_re, phase_im = phase_parts(freqs, slowness[level])
        next_re = phase_re * acc_re - phase_im * acc_im
        next_im = phase_re * acc_im + phase_im * acc_re
        current = jnp.stack([next_re, next_im], axis=1)
        states.append(current)
    stacked = jnp.stack(states, axis=1)
    image_part = (
        jnp.sum(stacked[:, :, 0] * stacked[:, :, 0] + stacked[:, :, 1] * stacked[:, :, 1], axis=0)
        / freq_total
    )
    return (stacked, states[-1], image_part)


def backward_steps(adjoint, states, freqs, taps, slowness, perturbation, freq_total):
    tap_re = taps[:, 0]
    tap_im = taps[:, 1]
    step_count = slowness.shape[0]
    parts = [None] * step_count
    for level in reversed(range(step_count)):
        wave_re = states[:, level, 0]
        wave_im = states[:, level, 1]
        grad_re = adjoint[:, 0] + 2.0 * perturbation[level] * wave_re
        grad_im = adjoint[:, 1] + 2.0 * perturbation[level] * wave_im
        parts[level] = (
            layer_thickness
            / freq_total
            * jnp.sum(freqs[:, None, None] * (grad_im * wave_re - grad_re * wave_im), axis=0)
        )
        phase_re, phase_im = phase_parts(freqs, slowness[level])
        back_re = phase_re * grad_re + phase_im * grad_im
        back_im = phase_re * grad_im - phase_im * grad_re
        extended = extended_2(jnp.stack([back_re, back_im], axis=1), (("xy", 2),), 2)
        acc_re, acc_im = adjoint_stencil(extended, tap_re, tap_im)
        adjoint = jnp.stack([acc_re, acc_im], axis=1)
    return (adjoint, jnp.stack(parts, axis=0))


def on_device(surface_data, frequencies, coefficients, slowness, perturbation):
    freq_count = frequencies.shape[0]
    step_count = slowness.shape[0]
    row_count = slowness.shape[1]
    col_count = slowness.shape[2]
    layers = lax.axis_size("depth")
    depth_index = lax.axis_index("depth")
    stored_zero = jnp.zeros((freq_count, step_count, 2, row_count, col_count), jnp.float32)
    plane_zero = jnp.zeros((step_count, row_count, col_count), jnp.float32)
    start = jnp.where(depth_index == 0, surface_data, jnp.zeros_like(surface_data))

    def forward_segment(segment_no, carry):
        current, stored, image_sum = carry
        states, bottom, image_part = forward_steps(
            current, frequencies, coefficients, slowness, freq_count
        )
        chosen = depth_index == segment_no
        stored = jnp.where(chosen, states, stored)
        image_sum = jnp.where(chosen, image_part, image_sum)
        current = shifted(bottom, "depth", 1)
        return (current, stored, image_sum)

    unused_field, stored, image_field = lax.fori_loop(
        0, layers, forward_segment, (start, stored_zero, plane_zero)
    )

    def backward_segment(segment_no, carry):
        adjoint, gradient_sum = carry
        top_field, parts = backward_steps(
            adjoint, stored, frequencies, coefficients, slowness, perturbation, freq_count
        )
        gradient_sum = jnp.where(depth_index == layers - 1 - segment_no, parts, gradient_sum)
        adjoint = shifted(top_field, "depth", -1)
        return (adjoint, gradient_sum)

    adjoint_zero = jnp.zeros_like(surface_data)
    unused_adjoint, gradient = lax.fori_loop(
        0, layers, backward_segment, (adjoint_zero, plane_zero)
    )
    return (gradient, image_field)


ROWS = 16
HALO_TILES = 4
LANES = 128

OVERLAP = 8

sin_terms = (0.9999999995, -0.1666666515, 0.008333256964, -0.0001982776292, 2.657952479e-06)
cos_terms = (0.9999999947, -0.4999998344, 0.04166583045, -0.00138740917, 2.372928386e-05)


def window_row(tile, sub):
    group = tile - 2
    above = sub - 4 * (group + 1)
    below = sub + ROWS + 4 * group
    even = jnp.where(sub < 4, below, above - 4)
    odd = jnp.where(sub < 4, above, below - 4)
    halo = jnp.where(lax.rem(tile, 2) == 0, even, odd)
    return jnp.where(tile < 2, 8 * tile + sub, halo)


def band_kernel(plane_rows, taps, freqs, bands, back_bands, freq_tiles):
    first_row = lax.axis_index("xy") * ROWS

    def fill(ref, adjoint):
        out_tiles = ref.shape[1] // 48
        in_tiles = ref.shape[2] // 48
        shape = (16, ref.shape[2])
        col = lax.broadcasted_iota(jnp.int32, shape, 1)
        sub = lax.broadcasted_iota(jnp.int32, shape, 0)
        tile_k = sum((col >= 48 * t).astype(jnp.int32) for t in range(1, in_tiles))
        row_k = window_row(tile_k, col & 7)
        part_k = (col >> 4) - 3 * tile_k
        plane_k = (col >> 3) & 1
        plane_m = sub >> 3
        same = plane_k == plane_m
        inside_k = (row_k + first_row >= 0) & (row_k + first_row < plane_rows)
        for tile in range(out_tiles):
            row_m = window_row(jnp.full(shape, tile, jnp.int32), sub & 7)
            inside = inside_k & (row_m + first_row >= 0) & (row_m + first_row < plane_rows)
            offset = jnp.where(inside, row_k - row_m, 9)
            hits = [offset == a - 2 for a in range(5)]
            for f in range(ref.shape[0]):
                for b in range(3):
                    total = jnp.zeros(shape, jnp.float32)
                    for a in range(5):
                        tap = 3 * (4 - a) + 2 - b if adjoint else 3 * a + b
                        re = taps[f, 0, tap]
                        im = -taps[f, 1, tap] if adjoint else taps[f, 1, tap]
                        crossed = jnp.where(plane_m == 0, -im, im)
                        total = jnp.where(hits[a], jnp.where(same, re, crossed), total)
                    high = total.astype(jnp.bfloat16)
                    low = total - high.astype(jnp.float32)
                    base = 48 * tile + 16 * b
                    ref[f, base : base + 16] = jnp.where(part_k == 1, low, total).astype(jnp.bfloat16)

    fill(bands, False)
    fill(back_bands, True)
    for f in range(freq_tiles.shape[0]):
        freq_tiles[f] = jnp.full((8, LANES), freqs[f], jnp.float32)


def pack_rows(ref, values, side):
    lane = lax.broadcasted_iota(jnp.int32, (8, LANES), 1)
    overlaps = jnp.zeros((8, LANES), jnp.float32)
    blocks = (values[0].shape[1] - LANES) // LANES
    for n, value in enumerate(values):
        for block in range(blocks):
            ref[blocks * n + block] = value[:, (block + side) * LANES : (block + side + 1) * LANES]
        extra = value[:, : LANES] if side else value[:, blocks * LANES :]
        turn = (OVERLAP * (n + side)) % LANES
        extra = pltpu.roll(extra, turn, 1) if turn else extra
        overlaps = jnp.where((lane >= OVERLAP * n) & (lane < OVERLAP * (n + 1)), extra, overlaps)
    ref[blocks * len(values)] = overlaps


def unpack_rows(ref, tiles, n, side):
    blocks = (ref.shape[0] - 1) // tiles
    turn = (-OVERLAP * (n + side)) % LANES
    extra = ref[blocks * tiles]
    extra = pltpu.roll(extra, turn, 1) if turn else extra
    parts = [ref[blocks * n + block] for block in range(blocks)]
    return jnp.concatenate([extra] + parts if side else parts + [extra], axis=1)


def edge_levels(levels, slow, pert, down):
    inner, outer = (1, 0) if down else (0, 1)
    if levels == 1:
        return [slow(0, inner), pert(1, inner), pert(0, inner)]
    row = lax.broadcasted_iota(jnp.int32, slow(0, 0).shape, 0)
    turned = pltpu.roll(slow(1, outer), 4, 0)
    if down:
        extra = jnp.where(row < 2, pltpu.roll(pert(1, inner), 2, 0), turned)
        last = jnp.where(row < 4, extra, slow(0, outer))
    else:
        extra = jnp.where(row >= 6, pltpu.roll(pert(1, inner), 6, 0), turned)
        last = jnp.where(row < 4, slow(0, outer), extra)
    return [slow(0, inner), slow(1, inner), last]


def edge_surface(surf, down):
    inner, outer = (1, 0) if down else (0, 1)
    tiles = [surf(plane, inner) for plane in range(4)]
    row = lax.broadcasted_iota(jnp.int32, tiles[0].shape, 0)
    spread = surf(3, outer)
    for plane in range(3):
        turn = 6 - 2 * plane
        free = row < 2 if down else row >= 6
        tiles.append(jnp.where(free, pltpu.roll(spread, turn, 0), surf(plane, outer)))
    return tiles


def surface_edges(tiles, down):
    row = lax.broadcasted_iota(jnp.int32, tiles[0].shape, 0)
    outer = [tiles[4], tiles[5], tiles[6]]
    first = 2 if down else 0
    spread = pltpu.roll(tiles[6], 6, 0)
    spread = jnp.where((row >= first + 2) & (row < first + 4), pltpu.roll(tiles[5], 4, 0), spread)
    spread = jnp.where((row >= first) & (row < first + 2), pltpu.roll(tiles[4], 2, 0), spread)
    outer.append(spread)
    return [(tiles[plane], outer[plane]) for plane in range(4)]


def pack_kernel(width, step, surf_in, slow_in, pert_in, cross, bulk, cross_far, window, surf, slow, pert, sems):
    copies = [
        pltpu.make_async_copy(source, target, sems.at[n])
        for n, (source, target) in enumerate(((slow_in, slow), (pert_in, pert), (surf_in, surf)))
    ]
    for copy in copies:
        copy.start()
    for copy in copies:
        copy.wait()
    depth = lax.axis_index("depth")
    place = lax.axis_index("xy")
    for own in range(2):

        def reader(ref, side):
            lanes = slice(side * step, side * step + width)
            return lambda level, tile: ref[level, 8 * tile : 8 * tile + 8, lanes]

        def surface_reader(side):
            lanes = slice(side * step, side * step + width)
            return lambda plane, tile: surf[plane // 2, plane % 2, 8 * tile : 8 * tile + 8, lanes]

        @pl.when(depth == own)
        def _():
            surface, surface_far = surface_reader(own), surface_reader(1 - own)
            slow_near, pert_near = reader(slow, own), reader(pert, own)
            slow_far, pert_far = reader(slow, 1 - own), reader(pert, 1 - own)
            both = [(level, tile) for level in range(2) for tile in range(2)]
            for n, (level, tile) in enumerate(both):
                window[8 + n] = slow_near(level, tile)
                window[12 + n] = pert_near(level, tile)
            for plane in range(4):
                for tile in range(2):
                    window[2 * plane + tile] = surface(plane, tile)
            pack_rows(bulk, [slow_far(*at) for at in both] + [pert_far(*at) for at in both], 1 - own)
            for down in (False, True):

                @pl.when((lax.rem(place, 2) == 1) == down)
                def _():
                    edges = edge_surface(surface, down)[:4] + edge_levels(own, slow_near, pert_near, down)
                    pack_rows(cross, edges, own)
                    edges = edge_surface(surface_far, down)[4:] + edge_levels(own, slow_far, pert_far, down)
                    pack_rows(cross_far, edges, 1 - own)


def relay_kernel(window, bulk, chip, partner):
    depth = lax.axis_index("depth")
    place = lax.axis_index("xy")
    for own in range(2):

        @pl.when(depth == own)
        def _():
            other = [unpack_rows(bulk, 8, n, own) for n in range(8)]
            for n in range(8):
                partner[n] = other[n]
            readers = {
                own: (lambda level, tile: window[8 + 2 * level + tile], lambda level, tile: window[12 + 2 * level + tile]),
                1 - own: (lambda level, tile: other[2 * level + tile], lambda level, tile: other[4 + 2 * level + tile]),
            }
            for down in (False, True):

                @pl.when((lax.rem(place, 2) == 0) == down)
                def _():
                    edges = edge_surface(lambda plane, tile: window[2 * plane + tile], down)
                    for levels in (own, 1 - own):
                        edges = edges + edge_levels(levels, *readers[levels], down)
                    pack_rows(chip, edges, own)


def phase(half):
    square = half * half
    cosine = cos_terms[-1]
    sine = sin_terms[-1]
    for term in cos_terms[-2::-1]:
        cosine = cosine * square + term
    for term in sin_terms[-2::-1]:
        sine = sine * square + term
    sine = sine * half
    twice = sine + sine
    return 1.0 - twice * sine, twice * cosine


def own_phases_kernel(freq_tiles, window, partner, phases):
    depth = lax.axis_index("depth")
    for level in range(4):
        for tile in range(2):
            own, other = window[8 + 2 * (level % 2) + tile], partner[2 * (level % 2) + tile]
            slow = jnp.where(depth == level // 2, own, other)
            for f in range(2):
                cosine, sine = phase(over_columns(freq_tiles[f], slow) * 0.25 * slow)
                phases[f, level, tile, :8] = cosine
                phases[f, level, tile, 8:] = sine


def over_columns(tile, like):
    return jnp.concatenate([tile] * (like.shape[1] // LANES), axis=1)


def sweep_kernel(
    width, freq_tiles, bands, back_bands, own_phases, window, partner, cross, cross_far, chip,
    gradient, image, theirs, slow_win, pert_win, operand, halo_phases, fields, image_win, grad_win,
):
    depth = lax.axis_index("depth")
    place = lax.axis_index("xy")
    half = width - LANES
    row = lax.broadcasted_iota(jnp.int32, (8, width), 0)
    upper = row < 4
    lane = lax.broadcasted_iota(jnp.int32, (16, LANES), 1)
    even = lax.rem(place, 2) == 0
    freqs = [jnp.concatenate([freq_tiles[f]] * (width // LANES), axis=1) for f in range(2)]

    def store_operand(f, tile, value):
        high = value.astype(jnp.bfloat16)
        low = (value - high.astype(jnp.float32)).astype(jnp.bfloat16)
        base = 48 * tile
        operand[f, base : base + 16] = high
        operand[f, base + 16 : base + 32] = high
        operand[f, base + 32 : base + 48] = low

    def stencil(f, matrix, out_tiles, in_tiles):
        product = jnp.dot(
            matrix[f, : 48 * out_tiles, : 48 * in_tiles],
            operand[f, : 48 * in_tiles],
            preferred_element_type=jnp.float32,
        )
        result = []
        for tile in range(out_tiles):
            base = 48 * tile
            left = pltpu.roll(product[base : base + 16], 1, 1)
            right = pltpu.roll(product[base + 32 : base + 48], width - 1, 1)
            left = jnp.concatenate([jnp.where(lane == 0, 0.0, left[:, :LANES]), left[:, LANES:]], axis=1)
            right = jnp.concatenate([right[:, :half], jnp.where(lane == LANES - 1, 0.0, right[:, half:])], axis=1)
            result.append(product[base + 16 : base + 32] + left + right)
        return result

    def fill(own, below_is_chip):
        chip_edges = [unpack_rows(chip, 13, n, own) for n in range(13)]
        same = [unpack_rows(cross, 7, n, own) for n in range(7)]
        other = [unpack_rows(cross_far, 6, n, own) for n in range(6)]
        cross_edges = same[:4] + other[:3] + same[4:] + other[3:]
        above, below = (cross_edges, chip_edges) if below_is_chip else (chip_edges, cross_edges)
        for level in range(2):
            for tile in range(2):
                pert_win[2 * own + level, tile] = window[12 + 2 * level + tile]
                pert_win[2 * (1 - own) + level, tile] = partner[4 + 2 * level + tile]
        at = (7, 10) if own == 0 else (10, 7)
        up, down = above[at[0] : at[0] + 3], below[at[0] : at[0] + 3]
        for level in range(2):
            slow_win[level, 0] = jnp.where(upper, down[level], up[level])
            slow_win[level, 1] = jnp.where(upper, up[level], down[level])
        slow_win[0, 2] = jnp.where(upper, down[2], up[2])
        slow_win[1, 2] = pltpu.roll(jnp.where(upper, up[2], down[2]), 4, 0)
        pert_win[1, 2] = jnp.where(
            row < 2, pltpu.roll(down[2], 2, 0), jnp.where(row >= 6, pltpu.roll(up[2], 6, 0), 0.0)
        )
        up, down = above[at[1] : at[1] + 3], below[at[1] : at[1] + 3]
        slow_win[2, 0] = jnp.where(upper, down[0], up[0])
        slow_win[2, 1] = jnp.where(upper, up[0], down[0])
        pert_win[3, 2] = jnp.where(upper, down[1], up[1])
        pert_win[3, 3] = jnp.where(upper, up[1], down[1])
        pert_win[2, 2] = jnp.where(upper, down[2], up[2])
        up, down = surface_edges(above[:7], True), surface_edges(below[:7], False)
        planes = []
        for plane in range(4):
            up_inner, up_outer = up[plane]
            down_inner, down_outer = down[plane]
            planes.append(
                [
                    window[2 * plane],
                    window[2 * plane + 1],
                    jnp.where(upper, down_inner, up_inner),
                    jnp.where(upper, up_inner, down_inner),
                    jnp.where(upper, down_outer, up_outer),
                    jnp.where(upper, up_outer, down_outer),
                ]
            )
        for f in range(2):
            for tile in range(6):
                store_operand(f, tile, jnp.concatenate([planes[2 * f][tile], planes[2 * f + 1][tile]], axis=0))

    for own in range(2):
        for below_is_chip in (False, True):

            @pl.when((depth == own) & (even == below_is_chip))
            def _():
                fill(own, below_is_chip)

    def add_image(f, level, tile, re, im):
        part = (re * re + im * im) * 0.5
        image_win[level, tile] = part if f == 0 else image_win[level, tile] + part

    def add_gradient(f, level, tile, w_re, w_im, u_re, u_im):
        part = (0.25 * freqs[f]) * (w_im * u_re - w_re * u_im)
        grad_win[level, tile] = part if f == 0 else grad_win[level, tile] + part

    def phases_of(f, level, tile):
        if tile < 2:
            return own_phases[f, level, tile, :8], own_phases[f, level, tile, 8:]
        cosine, sine = phase(freqs[f] * 0.25 * slow_win[level, tile - 2])
        if tile == 2 and level > 0:
            halo_phases[f, level - 1, :8] = cosine
            halo_phases[f, level - 1, 8:] = sine
        return cosine, sine

    tiles = (6, 5, 5, 4)
    for level in range(3):
        for f in range(2):
            fields_now = stencil(f, bands, tiles[level + 1], tiles[level])
            for tile, value in enumerate(fields_now):
                cosine, sine = phases_of(f, level, tile)
                v_re, v_im = value[:8], value[8:]
                re = cosine * v_re - sine * v_im
                im = cosine * v_im + sine * v_re
                both = jnp.concatenate([re, im], axis=0)
                store_operand(f, tile, both)
                if tile < 3:
                    fields[f, level, tile] = both
                if tile < 2:
                    add_image(f, level, tile, re, im)
    for f in range(2):
        for tile, value in enumerate(stencil(f, bands, 4, 4)):
            twice = 2.0 * pert_win[3, tile]
            v_re, v_im = value[:8], value[8:]
            if tile < 2:
                cosine, sine = phases_of(f, 3, tile)
                re = cosine * v_re - sine * v_im
                im = cosine * v_im + sine * v_re
                add_image(f, 3, tile, re, im)
                add_gradient(f, 3, tile, twice * re, twice * im, re, im)
            store_operand(f, tile, jnp.concatenate([twice * v_re, twice * v_im], axis=0))
    tiles = (2, 3, 3, 4)
    for level in (2, 1, 0):
        for f in range(2):
            for tile, value in enumerate(stencil(f, back_bands, tiles[level], tiles[level + 1])):
                twice = 2.0 * pert_win[level, tile]
                u_re, u_im = fields[f, level, tile, :8], fields[f, level, tile, 8:]
                w_re = value[:8] + twice * u_re
                w_im = value[8:] + twice * u_im
                if tile < 2:
                    add_gradient(f, level, tile, w_re, w_im, u_re, u_im)
                if level > 0:
                    if tile < 2:
                        cosine, sine = phases_of(f, level, tile)
                    else:
                        cosine, sine = halo_phases[f, level - 1, :8], halo_phases[f, level - 1, 8:]
                    back = [cosine * w_re + sine * w_im, cosine * w_im - sine * w_re]
                    store_operand(f, tile, jnp.concatenate(back, axis=0))

    for own in range(2):

        @pl.when(depth == own)
        def _():
            inner = slice(own * LANES, own * LANES + half)
            outer = slice(own * half, own * half + half)
            for level in range(2):
                for tile in range(2):
                    rows = slice(8 * tile, 8 * tile + 8)
                    gradient[level, rows, outer] = grad_win[2 * own + level, tile, :, inner]
                    image[level, rows, outer] = image_win[2 * own + level, tile, :, inner]
                    theirs[0, level, rows] = grad_win[2 * (1 - own) + level, tile, :, inner]
                    theirs[1, level, rows] = image_win[2 * (1 - own) + level, tile, :, inner]


def split_columns(surface_data, frequencies, coefficients, slowness, perturbation):
    count = lax.axis_size("xy")
    columns = slowness.shape[2]
    half = columns // 2
    width = half + LANES
    step = half - LANES
    f32 = jnp.float32
    axes = ("depth", "xy")

    def moved(value, other_depth, neighbour):
        pairs = []
        for depth in range(2):
            for place in range(count):
                target = {"chip": place ^ 1, "cross": place + 1 if place % 2 else place - 1, "same": place}[neighbour]
                if 0 <= target < count:
                    layer = 1 - depth if other_depth else depth
                    pairs.append((depth * count + place, layer * count + target))
        return lax.ppermute(value, axes, pairs)

    vmem = pl.BlockSpec(memory_space=pltpu.VMEM)
    smem = pl.BlockSpec(memory_space=pltpu.SMEM)
    tile = lambda n: jax.ShapeDtypeStruct((n, 8, width), f32)
    packed = lambda n: jax.ShapeDtypeStruct((n * half // LANES + 1, 8, LANES), f32)
    params = lambda mib: pltpu.CompilerParams(vmem_limit_bytes=mib * 2**20)
    cross, bulk, cross_far, window = pl.pallas_call(
        lambda *refs: pack_kernel(width, step, *refs),
        out_shape=(packed(7), packed(8), packed(6), tile(16)),
        in_specs=[pl.BlockSpec(memory_space=pltpu.HBM)] * 3,
        out_specs=(vmem,) * 4,
        scratch_shapes=[
            pltpu.VMEM(surface_data.shape, f32),
            pltpu.VMEM(slowness.shape, f32),
            pltpu.VMEM(perturbation.shape, f32),
            pltpu.SemaphoreType.DMA((3,)),
        ],
        compiler_params=params(32),
        name="pack",
    )(*(pltpu.with_memory_space_constraint(x, pltpu.HBM) for x in (surface_data, slowness, perturbation)))
    cross = moved(cross, False, "cross")
    bulk = moved(bulk, True, "same")
    cross_far = moved(cross_far, True, "cross")
    bands, back_bands, freq_tiles = pl.pallas_call(
        lambda *refs: band_kernel(count * ROWS, *refs),
        out_shape=(
            jax.ShapeDtypeStruct((2, 240, 288), jnp.bfloat16),
            jax.ShapeDtypeStruct((2, 144, 192), jnp.bfloat16),
            jax.ShapeDtypeStruct((2, 8, LANES), f32),
        ),
        in_specs=[smem] * 2,
        out_specs=(vmem,) * 3,
        compiler_params=params(16),
        cost_estimate=pl.CostEstimate(flops=10**10, bytes_accessed=10**6, transcendentals=0),
        name="bands",
    )(coefficients, frequencies)
    chip, partner = pl.pallas_call(
        relay_kernel,
        out_shape=(packed(13), tile(8)),
        in_specs=[vmem] * 2,
        out_specs=(vmem,) * 2,
        compiler_params=params(32),
        cost_estimate=pl.CostEstimate(flops=10**10, bytes_accessed=10**6, transcendentals=0),
        name="relay",
    )(window, bulk)
    chip = moved(chip, False, "chip")

    own_phases = pl.pallas_call(
        own_phases_kernel,
        out_shape=jax.ShapeDtypeStruct((2, 4, 2, 16, width), f32),
        in_specs=[vmem] * 3,
        out_specs=vmem,
        compiler_params=params(16),
        name="own_phases",
    )(freq_tiles, window, partner)

    own = jax.ShapeDtypeStruct((2, ROWS, columns), f32)
    gradient, image, theirs = pl.pallas_call(
        lambda *refs: sweep_kernel(width, *refs),
        out_shape=(own, own, jax.ShapeDtypeStruct((2, 2, ROWS, half), f32)),
        in_specs=[vmem] * 9,
        out_specs=(vmem,) * 3,
        scratch_shapes=[
            pltpu.VMEM((3, 3, 8, width), f32),
            pltpu.VMEM((4, 4, 8, width), f32),
            pltpu.VMEM((2, 288, width), jnp.bfloat16),
            pltpu.VMEM((2, 2, 16, width), f32),
            pltpu.VMEM((2, 3, 3, 16, width), f32),
            pltpu.VMEM((4, 2, 8, width), f32),
            pltpu.VMEM((4, 2, 8, width), f32),
        ],
        compiler_params=params(40),
        name="sweep",
    )(
        freq_tiles, bands, back_bands, own_phases, window, partner, cross, cross_far, chip,
    )
    theirs = moved(theirs, True, "same")
    start = (1 - lax.axis_index("depth")) * half
    gradient = lax.dynamic_update_slice(gradient, theirs[0], (0, 0, start))
    image = lax.dynamic_update_slice(image, theirs[1], (0, 0, start))
    return gradient, image


def on_slice(surface_data, frequencies, coefficients, slowness, perturbation):
    levels, rows, columns = slowness.shape
    fits = (
        lax.axis_size("depth") == 2
        and levels == 2
        and rows == ROWS
        and frequencies.shape[0] == 2
        and lax.axis_size("xy") % 2 == 0
        and columns % (2 * LANES) == 0
        and columns >= 4 * LANES
    )
    plan = split_columns if fits else on_device
    return plan(surface_data, frequencies, coefficients, slowness, perturbation)


def solution(mesh):
    in_specs = (P(None, None, "xy", None), P(), P(), P("depth", "xy", None), P("depth", "xy", None))
    out_specs = (P("depth", "xy", None), P("depth", "xy", None))
    return jax.shard_map(
        on_slice, mesh=mesh, in_specs=in_specs, out_specs=out_specs, check_vma=False
    )
```

```python
import numpy as np
import jax
import jax.numpy as jnp
from jax import lax
from jax.experimental import pallas as pl
from jax.experimental.pallas import tpu as pltpu
from jax.sharding import PartitionSpec as P

layer_thickness = 0.5


def extended_2(cells, sides, width):
    for axis, dim in sides:
        count = lax.axis_size(axis)
        ends = count - 1
        head = lax.slice_in_dim(cells, 0, width, axis=dim)
        tail = lax.slice_in_dim(cells, cells.shape[dim] - width, cells.shape[dim], axis=dim)
        cells = jnp.concatenate(
            [
                lax.ppermute(tail, axis, [(i, (i + 1) % count) for i in range(ends)]),
                cells,
                lax.ppermute(head, axis, [((i + 1) % count, i) for i in range(ends)]),
            ],
            axis=dim,
        )
    return cells


def shifted(value, axis, steps):
    count = lax.axis_size(axis)
    initial, last = (max(0, -steps), min(count, count - steps))
    return lax.ppermute(value, axis, [(source, source + steps) for source in range(initial, last)])


def apply_stencil(extended, tap_re, tap_im):
    out_rows = extended.shape[2] - 4
    col_count = extended.shape[3]
    padded = jnp.pad(extended, ((0, 0), (0, 0), (0, 0), (1, 1)))
    acc_re = jnp.zeros((extended.shape[0], out_rows, col_count), jnp.float32)
    acc_im = jnp.zeros((extended.shape[0], out_rows, col_count), jnp.float32)
    for row_off in range(5):
        for col_off in range(3):
            tap_index = row_off * 3 + col_off
            part_re = padded[:, 0, row_off : row_off + out_rows, col_off : col_off + col_count]
            part_im = padded[:, 1, row_off : row_off + out_rows, col_off : col_off + col_count]
            weight_re = tap_re[:, tap_index][:, None, None]
            weight_im = tap_im[:, tap_index][:, None, None]
            acc_re = acc_re + weight_re * part_re - weight_im * part_im
            acc_im = acc_im + weight_re * part_im + weight_im * part_re
    return (acc_re, acc_im)


def adjoint_stencil(extended, tap_re, tap_im):
    out_rows = extended.shape[2] - 4
    col_count = extended.shape[3]
    padded = jnp.pad(extended, ((0, 0), (0, 0), (0, 0), (1, 1)))
    acc_re = jnp.zeros((extended.shape[0], out_rows, col_count), jnp.float32)
    acc_im = jnp.zeros((extended.shape[0], out_rows, col_count), jnp.float32)
    for row_off in range(5):
        for col_off in range(3):
            tap_index = row_off * 3 + col_off
            row_from = 4 - row_off
            col_from = 2 - col_off
            part_re = padded[:, 0, row_from : row_from + out_rows, col_from : col_from + col_count]
            part_im = padded[:, 1, row_from : row_from + out_rows, col_from : col_from + col_count]
            weight_re = tap_re[:, tap_index][:, None, None]
            weight_im = tap_im[:, tap_index][:, None, None]
            acc_re = acc_re + weight_re * part_re + weight_im * part_im
            acc_im = acc_im + weight_re * part_im - weight_im * part_re
    return (acc_re, acc_im)


def phase_parts(freqs, slow_plane):
    angle = freqs[:, None, None] * layer_thickness * slow_plane[None]
    return (jnp.cos(angle), jnp.sin(angle))


def forward_steps(wavefield, freqs, taps, slowness, freq_total):
    tap_re = taps[:, 0]
    tap_im = taps[:, 1]
    step_count = slowness.shape[0]
    states = []
    current = wavefield
    for level in range(step_count):
        extended = extended_2(current, (("xy", 2),), 2)
        acc_re, acc_im = apply_stencil(extended, tap_re, tap_im)
        phase_re, phase_im = phase_parts(freqs, slowness[level])
        next_re = phase_re * acc_re - phase_im * acc_im
        next_im = phase_re * acc_im + phase_im * acc_re
        current = jnp.stack([next_re, next_im], axis=1)
        states.append(current)
    stacked = jnp.stack(states, axis=1)
    image_part = (
        jnp.sum(stacked[:, :, 0] * stacked[:, :, 0] + stacked[:, :, 1] * stacked[:, :, 1], axis=0)
        / freq_total
    )
    return (stacked, states[-1], image_part)


def backward_steps(adjoint, states, freqs, taps, slowness, perturbation, freq_total):
    tap_re = taps[:, 0]
    tap_im = taps[:, 1]
    step_count = slowness.shape[0]
    parts = [None] * step_count
    for level in reversed(range(step_count)):
        wave_re = states[:, level, 0]
        wave_im = states[:, level, 1]
        grad_re = adjoint[:, 0] + 2.0 * perturbation[level] * wave_re
        grad_im = adjoint[:, 1] + 2.0 * perturbation[level] * wave_im
        parts[level] = (
            layer_thickness
            / freq_total
            * jnp.sum(freqs[:, None, None] * (grad_im * wave_re - grad_re * wave_im), axis=0)
        )
        phase_re, phase_im = phase_parts(freqs, slowness[level])
        back_re = phase_re * grad_re + phase_im * grad_im
        back_im = phase_re * grad_im - phase_im * grad_re
        extended = extended_2(jnp.stack([back_re, back_im], axis=1), (("xy", 2),), 2)
        acc_re, acc_im = adjoint_stencil(extended, tap_re, tap_im)
        adjoint = jnp.stack([acc_re, acc_im], axis=1)
    return (adjoint, jnp.stack(parts, axis=0))


def on_device(surface_data, frequencies, coefficients, slowness, perturbation):
    freq_count = frequencies.shape[0]
    step_count = slowness.shape[0]
    row_count = slowness.shape[1]
    col_count = slowness.shape[2]
    layers = lax.axis_size("depth")
    depth_index = lax.axis_index("depth")
    stored_zero = jnp.zeros((freq_count, step_count, 2, row_count, col_count), jnp.float32)
    plane_zero = jnp.zeros((step_count, row_count, col_count), jnp.float32)
    start = jnp.where(depth_index == 0, surface_data, jnp.zeros_like(surface_data))

    def forward_segment(segment_no, carry):
        current, stored, image_sum = carry
        states, bottom, image_part = forward_steps(
            current, frequencies, coefficients, slowness, freq_count
        )
        chosen = depth_index == segment_no
        stored = jnp.where(chosen, states, stored)
        image_sum = jnp.where(chosen, image_part, image_sum)
        current = shifted(bottom, "depth", 1)
        return (current, stored, image_sum)

    unused_field, stored, image_field = lax.fori_loop(
        0, layers, forward_segment, (start, stored_zero, plane_zero)
    )

    def backward_segment(segment_no, carry):
        adjoint, gradient_sum = carry
        top_field, parts = backward_steps(
            adjoint, stored, frequencies, coefficients, slowness, perturbation, freq_count
        )
        gradient_sum = jnp.where(depth_index == layers - 1 - segment_no, parts, gradient_sum)
        adjoint = shifted(top_field, "depth", -1)
        return (adjoint, gradient_sum)

    adjoint_zero = jnp.zeros_like(surface_data)
    unused_adjoint, gradient = lax.fori_loop(
        0, layers, backward_segment, (adjoint_zero, plane_zero)
    )
    return (gradient, image_field)


ROWS = 16
HALO_TILES = 4
LANES = 128

OVERLAP = 8

sin_terms = (0.9999999995, -0.1666666515, 0.008333256964, -0.0001982776292, 2.657952479e-06)
cos_terms = (0.9999999947, -0.4999998344, 0.04166583045, -0.00138740917, 2.372928386e-05)


def window_row(tile, sub):
    group = tile - 2
    above = sub - 4 * (group + 1)
    below = sub + ROWS + 4 * group
    even = jnp.where(sub < 4, below, above - 4)
    odd = jnp.where(sub < 4, above, below - 4)
    halo = jnp.where(lax.rem(tile, 2) == 0, even, odd)
    return jnp.where(tile < 2, 8 * tile + sub, halo)


def band_kernel(plane_rows, taps, freqs, bands, back_bands, freq_tiles):
    first_row = lax.axis_index("xy") * ROWS

    def fill(ref, adjoint):
        out_tiles = ref.shape[1] // 48
        in_tiles = ref.shape[2] // 48
        shape = (16, ref.shape[2])
        col = lax.broadcasted_iota(jnp.int32, shape, 1)
        sub = lax.broadcasted_iota(jnp.int32, shape, 0)
        tile_k = sum((col >= 48 * t).astype(jnp.int32) for t in range(1, in_tiles))
        row_k = window_row(tile_k, col & 7)
        part_k = (col >> 4) - 3 * tile_k
        plane_k = (col >> 3) & 1
        plane_m = sub >> 3
        same = plane_k == plane_m
        inside_k = (row_k + first_row >= 0) & (row_k + first_row < plane_rows)
        for tile in range(out_tiles):
            row_m = window_row(jnp.full(shape, tile, jnp.int32), sub & 7)
            inside = inside_k & (row_m + first_row >= 0) & (row_m + first_row < plane_rows)
            offset = jnp.where(inside, row_k - row_m, 9)
            hits = [offset == a - 2 for a in range(5)]
            for f in range(ref.shape[0]):
                for b in range(3):
                    total = jnp.zeros(shape, jnp.float32)
                    for a in range(5):
                        tap = 3 * (4 - a) + 2 - b if adjoint else 3 * a + b
                        re = taps[f, 0, tap]
                        im = -taps[f, 1, tap] if adjoint else taps[f, 1, tap]
                        crossed = jnp.where(plane_m == 0, -im, im)
                        total = jnp.where(hits[a], jnp.where(same, re, crossed), total)
                    high = total.astype(jnp.bfloat16)
                    low = total - high.astype(jnp.float32)
                    base = 48 * tile + 16 * b
                    ref[f, base : base + 16] = jnp.where(part_k == 1, low, total).astype(jnp.bfloat16)

    fill(bands, False)
    fill(back_bands, True)
    for f in range(freq_tiles.shape[0]):
        freq_tiles[f] = jnp.full((8, LANES), freqs[f], jnp.float32)


def pack_rows(ref, values, side):
    lane = lax.broadcasted_iota(jnp.int32, (8, LANES), 1)
    overlaps = jnp.zeros((8, LANES), jnp.float32)
    blocks = (values[0].shape[1] - LANES) // LANES
    for n, value in enumerate(values):
        for block in range(blocks):
            ref[blocks * n + block] = value[:, (block + side) * LANES : (block + side + 1) * LANES]
        extra = value[:, : LANES] if side else value[:, blocks * LANES :]
        turn = (OVERLAP * (n + side)) % LANES
        extra = pltpu.roll(extra, turn, 1) if turn else extra
        overlaps = jnp.where((lane >= OVERLAP * n) & (lane < OVERLAP * (n + 1)), extra, overlaps)
    ref[blocks * len(values)] = overlaps


def unpack_rows(ref, tiles, n, side):
    blocks = (ref.shape[0] - 1) // tiles
    turn = (-OVERLAP * (n + side)) % LANES
    extra = ref[blocks * tiles]
    extra = pltpu.roll(extra, turn, 1) if turn else extra
    parts = [ref[blocks * n + block] for block in range(blocks)]
    return jnp.concatenate([extra] + parts if side else parts + [extra], axis=1)


def edge_levels(levels, slow, pert, down):
    inner, outer = (1, 0) if down else (0, 1)
    if levels == 1:
        return [slow(0, inner), pert(1, inner), pert(0, inner)]
    row = lax.broadcasted_iota(jnp.int32, slow(0, 0).shape, 0)
    turned = pltpu.roll(slow(1, outer), 4, 0)
    if down:
        extra = jnp.where(row < 2, pltpu.roll(pert(1, inner), 2, 0), turned)
        last = jnp.where(row < 4, extra, slow(0, outer))
    else:
        extra = jnp.where(row >= 6, pltpu.roll(pert(1, inner), 6, 0), turned)
        last = jnp.where(row < 4, slow(0, outer), extra)
    return [slow(0, inner), slow(1, inner), last]


def edge_surface(surf, down):
    inner, outer = (1, 0) if down else (0, 1)
    tiles = [surf(plane, inner) for plane in range(4)]
    row = lax.broadcasted_iota(jnp.int32, tiles[0].shape, 0)
    spread = surf(3, outer)
    for plane in range(3):
        turn = 6 - 2 * plane
        free = row < 2 if down else row >= 6
        tiles.append(jnp.where(free, pltpu.roll(spread, turn, 0), surf(plane, outer)))
    return tiles


def surface_edges(tiles, down):
    row = lax.broadcasted_iota(jnp.int32, tiles[0].shape, 0)
    outer = [tiles[4], tiles[5], tiles[6]]
    first = 2 if down else 0
    spread = pltpu.roll(tiles[6], 6, 0)
    spread = jnp.where((row >= first + 2) & (row < first + 4), pltpu.roll(tiles[5], 4, 0), spread)
    spread = jnp.where((row >= first) & (row < first + 2), pltpu.roll(tiles[4], 2, 0), spread)
    outer.append(spread)
    return [(tiles[plane], outer[plane]) for plane in range(4)]


def pack_kernel(width, step, surf_in, slow_in, pert_in, cross, bulk, cross_far, window, surf, slow, pert, sems):
    copies = [
        pltpu.make_async_copy(source, target, sems.at[n])
        for n, (source, target) in enumerate(((slow_in, slow), (pert_in, pert), (surf_in, surf)))
    ]
    for copy in copies:
        copy.start()
    for copy in copies:
        copy.wait()
    depth = lax.axis_index("depth")
    place = lax.axis_index("xy")
    for own in range(2):

        def reader(ref, side):
            lanes = slice(side * step, side * step + width)
            return lambda level, tile: ref[level, 8 * tile : 8 * tile + 8, lanes]

        def surface(plane, tile):
            return surf[plane // 2, plane % 2, 8 * tile : 8 * tile + 8, own * step : own * step + width]

        @pl.when(depth == own)
        def _():
            slow_near, pert_near = reader(slow, own), reader(pert, own)
            slow_far, pert_far = reader(slow, 1 - own), reader(pert, 1 - own)
            both = [(level, tile) for level in range(2) for tile in range(2)]
            for n, (level, tile) in enumerate(both):
                window[8 + n] = slow_near(level, tile)
                window[12 + n] = pert_near(level, tile)
            for plane in range(4):
                for tile in range(2):
                    window[2 * plane + tile] = surface(plane, tile)
            pack_rows(bulk, [slow_far(*at) for at in both] + [pert_far(*at) for at in both], 1 - own)
            for down in (False, True):

                @pl.when((lax.rem(place, 2) == 1) == down)
                def _():
                    edges = edge_surface(surface, down) + edge_levels(own, slow_near, pert_near, down)
                    pack_rows(cross, edges, own)
                    pack_rows(cross_far, edge_levels(own, slow_far, pert_far, down), 1 - own)


def relay_kernel(window, bulk, chip, partner):
    depth = lax.axis_index("depth")
    place = lax.axis_index("xy")
    for own in range(2):

        @pl.when(depth == own)
        def _():
            other = [unpack_rows(bulk, 8, n, own) for n in range(8)]
            for n in range(8):
                partner[n] = other[n]
            readers = {
                own: (lambda level, tile: window[8 + 2 * level + tile], lambda level, tile: window[12 + 2 * level + tile]),
                1 - own: (lambda level, tile: other[2 * level + tile], lambda level, tile: other[4 + 2 * level + tile]),
            }
            for down in (False, True):

                @pl.when((lax.rem(place, 2) == 0) == down)
                def _():
                    edges = edge_surface(lambda plane, tile: window[2 * plane + tile], down)
                    for levels in (own, 1 - own):
                        edges = edges + edge_levels(levels, *readers[levels], down)
                    pack_rows(chip, edges, own)


def phase(half):
    square = half * half
    cosine = cos_terms[-1]
    sine = sin_terms[-1]
    for term in cos_terms[-2::-1]:
        cosine = cosine * square + term
    for term in sin_terms[-2::-1]:
        sine = sine * square + term
    sine = sine * half
    twice = sine + sine
    return 1.0 - twice * sine, twice * cosine


def own_phases_kernel(freq_tiles, window, partner, phases):
    depth = lax.axis_index("depth")
    for level in range(4):
        for tile in range(2):
            own, other = window[8 + 2 * (level % 2) + tile], partner[2 * (level % 2) + tile]
            slow = jnp.where(depth == level // 2, own, other)
            for f in range(2):
                cosine, sine = phase(over_columns(freq_tiles[f], slow) * 0.25 * slow)
                phases[f, level, tile, :8] = cosine
                phases[f, level, tile, 8:] = sine


def over_columns(tile, like):
    return jnp.concatenate([tile] * (like.shape[1] // LANES), axis=1)


def sweep_kernel(
    width, freq_tiles, bands, back_bands, own_phases, window, partner, cross, cross_far, chip,
    gradient, image, theirs, slow_win, pert_win, operand, halo_phases, fields, image_win, grad_win,
):
    depth = lax.axis_index("depth")
    place = lax.axis_index("xy")
    half = width - LANES
    row = lax.broadcasted_iota(jnp.int32, (8, width), 0)
    upper = row < 4
    lane = lax.broadcasted_iota(jnp.int32, (16, LANES), 1)
    even = lax.rem(place, 2) == 0
    freqs = [jnp.concatenate([freq_tiles[f]] * (width // LANES), axis=1) for f in range(2)]

    def store_operand(f, tile, value):
        high = value.astype(jnp.bfloat16)
        low = (value - high.astype(jnp.float32)).astype(jnp.bfloat16)
        base = 48 * tile
        operand[f, base : base + 16] = high
        operand[f, base + 16 : base + 32] = high
        operand[f, base + 32 : base + 48] = low

    def stencil(f, matrix, out_tiles, in_tiles):
        inner_tiles = min(in_tiles, 5)
        product = jnp.dot(
            matrix[f, : 48 * out_tiles, : 48 * inner_tiles],
            operand[f, : 48 * inner_tiles],
            preferred_element_type=jnp.float32,
        )
        slabs = [product[16 * n : 16 * n + 16] for n in range(3 * out_tiles)]
        if in_tiles > inner_tiles:
            outer = jnp.dot(
                matrix[f, 48 * (out_tiles - 1) : 48 * out_tiles, 48 * inner_tiles : 48 * in_tiles],
                operand[f, 48 * inner_tiles : 48 * in_tiles],
                preferred_element_type=jnp.float32,
            )
            for n in range(3):
                slabs[3 * out_tiles - 3 + n] += outer[16 * n : 16 * n + 16]
        result = []
        for tile in range(out_tiles):
            before, same, after = slabs[3 * tile : 3 * tile + 3]
            left = pltpu.roll(before, 1, 1)
            right = pltpu.roll(after, width - 1, 1)
            left = jnp.concatenate([jnp.where(lane == 0, 0.0, left[:, :LANES]), left[:, LANES:]], axis=1)
            right = jnp.concatenate([right[:, :half], jnp.where(lane == LANES - 1, 0.0, right[:, half:])], axis=1)
            result.append(same + left + right)
        return result

    def fill(own, below_is_chip):
        chip_edges = [unpack_rows(chip, 13, n, own) for n in range(13)]
        cross_edges = [unpack_rows(cross, 10, n, own) for n in range(10)]
        cross_edges += [unpack_rows(cross_far, 3, n, own) for n in range(3)]
        above, below = (cross_edges, chip_edges) if below_is_chip else (chip_edges, cross_edges)
        for level in range(2):
            for tile in range(2):
                pert_win[2 * own + level, tile] = window[12 + 2 * level + tile]
                pert_win[2 * (1 - own) + level, tile] = partner[4 + 2 * level + tile]
        at = (7, 10) if own == 0 else (10, 7)
        up, down = above[at[0] : at[0] + 3], below[at[0] : at[0] + 3]
        for level in range(2):
            slow_win[level, 0] = jnp.where(upper, down[level], up[level])
            slow_win[level, 1] = jnp.where(upper, up[level], down[level])
        slow_win[0, 2] = jnp.where(upper, down[2], up[2])
        slow_win[1, 2] = pltpu.roll(jnp.where(upper, up[2], down[2]), 4, 0)
        pert_win[1, 2] = jnp.where(
            row < 2, pltpu.roll(down[2], 2, 0), jnp.where(row >= 6, pltpu.roll(up[2], 6, 0), 0.0)
        )
        up, down = above[at[1] : at[1] + 3], below[at[1] : at[1] + 3]
        slow_win[2, 0] = jnp.where(upper, down[0], up[0])
        slow_win[2, 1] = jnp.where(upper, up[0], down[0])
        pert_win[3, 2] = jnp.where(upper, down[1], up[1])
        pert_win[3, 3] = jnp.where(upper, up[1], down[1])
        pert_win[2, 2] = jnp.where(upper, down[2], up[2])
        up, down = surface_edges(above[:7], True), surface_edges(below[:7], False)
        planes = []
        for plane in range(4):
            up_inner, up_outer = up[plane]
            down_inner, down_outer = down[plane]
            planes.append(
                [
                    window[2 * plane],
                    window[2 * plane + 1],
                    jnp.where(upper, down_inner, up_inner),
                    jnp.where(upper, up_inner, down_inner),
                    jnp.where(upper, down_outer, up_outer),
                    jnp.where(upper, up_outer, down_outer),
                ]
            )
        for f in range(2):
            for tile in range(6):
                store_operand(f, tile, jnp.concatenate([planes[2 * f][tile], planes[2 * f + 1][tile]], axis=0))

    for own in range(2):
        for below_is_chip in (False, True):

            @pl.when((depth == own) & (even == below_is_chip))
            def _():
                fill(own, below_is_chip)

    def add_image(f, level, tile, re, im):
        part = (re * re + im * im) * 0.5
        image_win[level, tile] = part if f == 0 else image_win[level, tile] + part

    def add_gradient(f, level, tile, w_re, w_im, u_re, u_im):
        part = (0.25 * freqs[f]) * (w_im * u_re - w_re * u_im)
        grad_win[level, tile] = part if f == 0 else grad_win[level, tile] + part

    def phases_of(f, level, tile):
        if tile < 2:
            return own_phases[f, level, tile, :8], own_phases[f, level, tile, 8:]
        cosine, sine = phase(freqs[f] * 0.25 * slow_win[level, tile - 2])
        if tile == 2 and level > 0:
            halo_phases[f, level - 1, :8] = cosine
            halo_phases[f, level - 1, 8:] = sine
        return cosine, sine

    tiles = (6, 5, 5, 4)
    for level in range(3):
        for f in range(2):
            fields_now = stencil(f, bands, tiles[level + 1], tiles[level])
            for tile, value in enumerate(fields_now):
                cosine, sine = phases_of(f, level, tile)
                v_re, v_im = value[:8], value[8:]
                re = cosine * v_re - sine * v_im
                im = cosine * v_im + sine * v_re
                both = jnp.concatenate([re, im], axis=0)
                store_operand(f, tile, both)
                if tile < 3:
                    fields[f, level, tile] = both
                if tile < 2:
                    add_image(f, level, tile, re, im)
    for f in range(2):
        for tile, value in enumerate(stencil(f, bands, 4, 4)):
            twice = 2.0 * pert_win[3, tile]
            v_re, v_im = value[:8], value[8:]
            if tile < 2:
                cosine, sine = phases_of(f, 3, tile)
                re = cosine * v_re - sine * v_im
                im = cosine * v_im + sine * v_re
                add_image(f, 3, tile, re, im)
                add_gradient(f, 3, tile, twice * re, twice * im, re, im)
            store_operand(f, tile, jnp.concatenate([twice * v_re, twice * v_im], axis=0))
    tiles = (2, 3, 3, 4)
    for level in (2, 1, 0):
        for f in range(2):
            for tile, value in enumerate(stencil(f, back_bands, tiles[level], tiles[level + 1])):
                twice = 2.0 * pert_win[level, tile]
                u_re, u_im = fields[f, level, tile, :8], fields[f, level, tile, 8:]
                w_re = value[:8] + twice * u_re
                w_im = value[8:] + twice * u_im
                if tile < 2:
                    add_gradient(f, level, tile, w_re, w_im, u_re, u_im)
                if level > 0:
                    if tile < 2:
                        cosine, sine = phases_of(f, level, tile)
                    else:
                        cosine, sine = halo_phases[f, level - 1, :8], halo_phases[f, level - 1, 8:]
                    back = [cosine * w_re + sine * w_im, cosine * w_im - sine * w_re]
                    store_operand(f, tile, jnp.concatenate(back, axis=0))

    for own in range(2):

        @pl.when(depth == own)
        def _():
            inner = slice(own * LANES, own * LANES + half)
            outer = slice(own * half, own * half + half)
            for level in range(2):
                for tile in range(2):
                    rows = slice(8 * tile, 8 * tile + 8)
                    gradient[level, rows, outer] = grad_win[2 * own + level, tile, :, inner]
                    image[level, rows, outer] = image_win[2 * own + level, tile, :, inner]
                    theirs[0, level, rows] = grad_win[2 * (1 - own) + level, tile, :, inner]
                    theirs[1, level, rows] = image_win[2 * (1 - own) + level, tile, :, inner]


def split_columns(surface_data, frequencies, coefficients, slowness, perturbation):
    count = lax.axis_size("xy")
    columns = slowness.shape[2]
    half = columns // 2
    width = half + LANES
    step = half - LANES
    f32 = jnp.float32
    axes = ("depth", "xy")

    def moved(value, other_depth, neighbour):
        pairs = []
        for depth in range(2):
            for place in range(count):
                target = {"chip": place ^ 1, "cross": place + 1 if place % 2 else place - 1, "same": place}[neighbour]
                if 0 <= target < count:
                    layer = 1 - depth if other_depth else depth
                    pairs.append((depth * count + place, layer * count + target))
        return lax.ppermute(value, axes, pairs)

    vmem = pl.BlockSpec(memory_space=pltpu.VMEM)
    smem = pl.BlockSpec(memory_space=pltpu.SMEM)
    tile = lambda n: jax.ShapeDtypeStruct((n, 8, width), f32)
    packed = lambda n: jax.ShapeDtypeStruct((n * half // LANES + 1, 8, LANES), f32)
    params = lambda mib: pltpu.CompilerParams(vmem_limit_bytes=mib * 2**20)
    cross, bulk, cross_far, window = pl.pallas_call(
        lambda *refs: pack_kernel(width, step, *refs),
        out_shape=(packed(10), packed(8), packed(3), tile(16)),
        in_specs=[pl.BlockSpec(memory_space=pltpu.HBM)] * 3,
        out_specs=(vmem,) * 4,
        scratch_shapes=[
            pltpu.VMEM(surface_data.shape, f32),
            pltpu.VMEM(slowness.shape, f32),
            pltpu.VMEM(perturbation.shape, f32),
            pltpu.SemaphoreType.DMA((3,)),
        ],
        compiler_params=params(32),
        name="pack",
    )(*(pltpu.with_memory_space_constraint(x, pltpu.HBM) for x in (surface_data, slowness, perturbation)))
    cross = moved(cross, False, "cross")
    bulk = moved(bulk, True, "same")
    cross_far = moved(cross_far, True, "cross")
    bands, back_bands, freq_tiles = pl.pallas_call(
        lambda *refs: band_kernel(count * ROWS, *refs),
        out_shape=(
            jax.ShapeDtypeStruct((2, 240, 288), jnp.bfloat16),
            jax.ShapeDtypeStruct((2, 144, 192), jnp.bfloat16),
            jax.ShapeDtypeStruct((2, 8, LANES), f32),
        ),
        in_specs=[smem] * 2,
        out_specs=(vmem,) * 3,
        compiler_params=params(16),
        cost_estimate=pl.CostEstimate(flops=10**10, bytes_accessed=10**6, transcendentals=0),
        name="bands",
    )(coefficients, frequencies)
    chip, partner = pl.pallas_call(
        relay_kernel,
        out_shape=(packed(13), tile(8)),
        in_specs=[vmem] * 2,
        out_specs=(vmem,) * 2,
        compiler_params=params(32),
        cost_estimate=pl.CostEstimate(flops=10**10, bytes_accessed=10**6, transcendentals=0),
        name="relay",
    )(window, bulk)
    chip = moved(chip, False, "chip")

    own_phases = pl.pallas_call(
        own_phases_kernel,
        out_shape=jax.ShapeDtypeStruct((2, 4, 2, 16, width), f32),
        in_specs=[vmem] * 3,
        out_specs=vmem,
        compiler_params=params(16),
        name="own_phases",
    )(freq_tiles, window, partner)

    own = jax.ShapeDtypeStruct((2, ROWS, columns), f32)
    gradient, image, theirs = pl.pallas_call(
        lambda *refs: sweep_kernel(width, *refs),
        out_shape=(own, own, jax.ShapeDtypeStruct((2, 2, ROWS, half), f32)),
        in_specs=[vmem] * 9,
        out_specs=(vmem,) * 3,
        scratch_shapes=[
            pltpu.VMEM((3, 3, 8, width), f32),
            pltpu.VMEM((4, 4, 8, width), f32),
            pltpu.VMEM((2, 288, width), jnp.bfloat16),
            pltpu.VMEM((2, 2, 16, width), f32),
            pltpu.VMEM((2, 3, 3, 16, width), f32),
            pltpu.VMEM((4, 2, 8, width), f32),
            pltpu.VMEM((4, 2, 8, width), f32),
        ],
        compiler_params=params(40),
        name="sweep",
    )(
        freq_tiles, bands, back_bands, own_phases, window, partner, cross, cross_far, chip,
    )
    theirs = moved(theirs, True, "same")
    start = (1 - lax.axis_index("depth")) * half
    gradient = lax.dynamic_update_slice(gradient, theirs[0], (0, 0, start))
    image = lax.dynamic_update_slice(image, theirs[1], (0, 0, start))
    return gradient, image


def on_slice(surface_data, frequencies, coefficients, slowness, perturbation):
    levels, rows, columns = slowness.shape
    fits = (
        lax.axis_size("depth") == 2
        and levels == 2
        and rows == ROWS
        and frequencies.shape[0] == 2
        and lax.axis_size("xy") % 2 == 0
        and columns % (2 * LANES) == 0
        and columns >= 4 * LANES
    )
    plan = split_columns if fits else on_device
    return plan(surface_data, frequencies, coefficients, slowness, perturbation)


def solution(mesh):
    in_specs = (P(None, None, "xy", None), P(), P(), P("depth", "xy", None), P("depth", "xy", None))
    out_specs = (P("depth", "xy", None), P("depth", "xy", None))
    return jax.shard_map(
        on_slice, mesh=mesh, in_specs=in_specs, out_specs=out_specs, check_vma=False
    )
```

```python
import numpy as np
import jax
import jax.numpy as jnp
from jax import lax
from jax.experimental import pallas as pl
from jax.experimental.pallas import tpu as pltpu
from jax.sharding import PartitionSpec as P

layer_thickness = 0.5


def extended_2(cells, sides, width):
    for axis, dim in sides:
        count = lax.axis_size(axis)
        ends = count - 1
        head = lax.slice_in_dim(cells, 0, width, axis=dim)
        tail = lax.slice_in_dim(cells, cells.shape[dim] - width, cells.shape[dim], axis=dim)
        cells = jnp.concatenate(
            [
                lax.ppermute(tail, axis, [(i, (i + 1) % count) for i in range(ends)]),
                cells,
                lax.ppermute(head, axis, [((i + 1) % count, i) for i in range(ends)]),
            ],
            axis=dim,
        )
    return cells


def shifted(value, axis, steps):
    count = lax.axis_size(axis)
    initial, last = (max(0, -steps), min(count, count - steps))
    return lax.ppermute(value, axis, [(source, source + steps) for source in range(initial, last)])


def apply_stencil(extended, tap_re, tap_im):
    out_rows = extended.shape[2] - 4
    col_count = extended.shape[3]
    padded = jnp.pad(extended, ((0, 0), (0, 0), (0, 0), (1, 1)))
    acc_re = jnp.zeros((extended.shape[0], out_rows, col_count), jnp.float32)
    acc_im = jnp.zeros((extended.shape[0], out_rows, col_count), jnp.float32)
    for row_off in range(5):
        for col_off in range(3):
            tap_index = row_off * 3 + col_off
            part_re = padded[:, 0, row_off : row_off + out_rows, col_off : col_off + col_count]
            part_im = padded[:, 1, row_off : row_off + out_rows, col_off : col_off + col_count]
            weight_re = tap_re[:, tap_index][:, None, None]
            weight_im = tap_im[:, tap_index][:, None, None]
            acc_re = acc_re + weight_re * part_re - weight_im * part_im
            acc_im = acc_im + weight_re * part_im + weight_im * part_re
    return (acc_re, acc_im)


def adjoint_stencil(extended, tap_re, tap_im):
    out_rows = extended.shape[2] - 4
    col_count = extended.shape[3]
    padded = jnp.pad(extended, ((0, 0), (0, 0), (0, 0), (1, 1)))
    acc_re = jnp.zeros((extended.shape[0], out_rows, col_count), jnp.float32)
    acc_im = jnp.zeros((extended.shape[0], out_rows, col_count), jnp.float32)
    for row_off in range(5):
        for col_off in range(3):
            tap_index = row_off * 3 + col_off
            row_from = 4 - row_off
            col_from = 2 - col_off
            part_re = padded[:, 0, row_from : row_from + out_rows, col_from : col_from + col_count]
            part_im = padded[:, 1, row_from : row_from + out_rows, col_from : col_from + col_count]
            weight_re = tap_re[:, tap_index][:, None, None]
            weight_im = tap_im[:, tap_index][:, None, None]
            acc_re = acc_re + weight_re * part_re + weight_im * part_im
            acc_im = acc_im + weight_re * part_im - weight_im * part_re
    return (acc_re, acc_im)


def phase_parts(freqs, slow_plane):
    angle = freqs[:, None, None] * layer_thickness * slow_plane[None]
    return (jnp.cos(angle), jnp.sin(angle))


def forward_steps(wavefield, freqs, taps, slowness, freq_total):
    tap_re = taps[:, 0]
    tap_im = taps[:, 1]
    step_count = slowness.shape[0]
    states = []
    current = wavefield
    for level in range(step_count):
        extended = extended_2(current, (("xy", 2),), 2)
        acc_re, acc_im = apply_stencil(extended, tap_re, tap_im)
        phase_re, phase_im = phase_parts(freqs, slowness[level])
        next_re = phase_re * acc_re - phase_im * acc_im
        next_im = phase_re * acc_im + phase_im * acc_re
        current = jnp.stack([next_re, next_im], axis=1)
        states.append(current)
    stacked = jnp.stack(states, axis=1)
    image_part = (
        jnp.sum(stacked[:, :, 0] * stacked[:, :, 0] + stacked[:, :, 1] * stacked[:, :, 1], axis=0)
        / freq_total
    )
    return (stacked, states[-1], image_part)


def backward_steps(adjoint, states, freqs, taps, slowness, perturbation, freq_total):
    tap_re = taps[:, 0]
    tap_im = taps[:, 1]
    step_count = slowness.shape[0]
    parts = [None] * step_count
    for level in reversed(range(step_count)):
        wave_re = states[:, level, 0]
        wave_im = states[:, level, 1]
        grad_re = adjoint[:, 0] + 2.0 * perturbation[level] * wave_re
        grad_im = adjoint[:, 1] + 2.0 * perturbation[level] * wave_im
        parts[level] = (
            layer_thickness
            / freq_total
            * jnp.sum(freqs[:, None, None] * (grad_im * wave_re - grad_re * wave_im), axis=0)
        )
        phase_re, phase_im = phase_parts(freqs, slowness[level])
        back_re = phase_re * grad_re + phase_im * grad_im
        back_im = phase_re * grad_im - phase_im * grad_re
        extended = extended_2(jnp.stack([back_re, back_im], axis=1), (("xy", 2),), 2)
        acc_re, acc_im = adjoint_stencil(extended, tap_re, tap_im)
        adjoint = jnp.stack([acc_re, acc_im], axis=1)
    return (adjoint, jnp.stack(parts, axis=0))


def on_device(surface_data, frequencies, coefficients, slowness, perturbation):
    freq_count = frequencies.shape[0]
    step_count = slowness.shape[0]
    row_count = slowness.shape[1]
    col_count = slowness.shape[2]
    layers = lax.axis_size("depth")
    depth_index = lax.axis_index("depth")
    stored_zero = jnp.zeros((freq_count, step_count, 2, row_count, col_count), jnp.float32)
    plane_zero = jnp.zeros((step_count, row_count, col_count), jnp.float32)
    start = jnp.where(depth_index == 0, surface_data, jnp.zeros_like(surface_data))

    def forward_segment(segment_no, carry):
        current, stored, image_sum = carry
        states, bottom, image_part = forward_steps(
            current, frequencies, coefficients, slowness, freq_count
        )
        chosen = depth_index == segment_no
        stored = jnp.where(chosen, states, stored)
        image_sum = jnp.where(chosen, image_part, image_sum)
        current = shifted(bottom, "depth", 1)
        return (current, stored, image_sum)

    unused_field, stored, image_field = lax.fori_loop(
        0, layers, forward_segment, (start, stored_zero, plane_zero)
    )

    def backward_segment(segment_no, carry):
        adjoint, gradient_sum = carry
        top_field, parts = backward_steps(
            adjoint, stored, frequencies, coefficients, slowness, perturbation, freq_count
        )
        gradient_sum = jnp.where(depth_index == layers - 1 - segment_no, parts, gradient_sum)
        adjoint = shifted(top_field, "depth", -1)
        return (adjoint, gradient_sum)

    adjoint_zero = jnp.zeros_like(surface_data)
    unused_adjoint, gradient = lax.fori_loop(
        0, layers, backward_segment, (adjoint_zero, plane_zero)
    )
    return (gradient, image_field)


ROWS = 16
HALO_TILES = 4
LANES = 128

OVERLAP = 8

sin_terms = (0.9999999995, -0.1666666515, 0.008333256964, -0.0001982776292, 2.657952479e-06)
cos_terms = (0.9999999947, -0.4999998344, 0.04166583045, -0.00138740917, 2.372928386e-05)


def window_row(tile, sub):
    group = tile - 2
    above = sub - 4 * (group + 1)
    below = sub + ROWS + 4 * group
    even = jnp.where(sub < 4, below, above - 4)
    odd = jnp.where(sub < 4, above, below - 4)
    halo = jnp.where(lax.rem(tile, 2) == 0, even, odd)
    return jnp.where(tile < 2, 8 * tile + sub, halo)


def band_kernel(plane_rows, taps, freqs, bands, back_bands, freq_tiles):
    first_row = lax.axis_index("xy") * ROWS

    def fill(ref, adjoint):
        out_tiles = ref.shape[1] // 48
        in_tiles = ref.shape[2] // 48
        shape = (16, ref.shape[2])
        col = lax.broadcasted_iota(jnp.int32, shape, 1)
        sub = lax.broadcasted_iota(jnp.int32, shape, 0)
        tile_k = sum((col >= 48 * t).astype(jnp.int32) for t in range(1, in_tiles))
        row_k = window_row(tile_k, col & 7)
        part_k = (col >> 4) - 3 * tile_k
        plane_k = (col >> 3) & 1
        plane_m = sub >> 3
        same = plane_k == plane_m
        inside_k = (row_k + first_row >= 0) & (row_k + first_row < plane_rows)
        for tile in range(out_tiles):
            row_m = window_row(jnp.full(shape, tile, jnp.int32), sub & 7)
            inside = inside_k & (row_m + first_row >= 0) & (row_m + first_row < plane_rows)
            offset = jnp.where(inside, row_k - row_m, 9)
            hits = [offset == a - 2 for a in range(5)]
            for f in range(ref.shape[0]):
                for b in range(3):
                    total = jnp.zeros(shape, jnp.float32)
                    for a in range(5):
                        tap = 3 * (4 - a) + 2 - b if adjoint else 3 * a + b
                        re = taps[f, 0, tap]
                        im = -taps[f, 1, tap] if adjoint else taps[f, 1, tap]
                        crossed = jnp.where(plane_m == 0, -im, im)
                        total = jnp.where(hits[a], jnp.where(same, re, crossed), total)
                    high = total.astype(jnp.bfloat16)
                    low = total - high.astype(jnp.float32)
                    base = 48 * tile + 16 * b
                    ref[f, base : base + 16] = jnp.where(part_k == 1, low, total).astype(jnp.bfloat16)

    fill(bands, False)
    fill(back_bands, True)
    for f in range(freq_tiles.shape[0]):
        freq_tiles[f] = jnp.full((8, LANES), freqs[f], jnp.float32)


def pack_rows(ref, values, side):
    lane = lax.broadcasted_iota(jnp.int32, (8, LANES), 1)
    overlaps = jnp.zeros((8, LANES), jnp.float32)
    blocks = (values[0].shape[1] - LANES) // LANES
    for n, value in enumerate(values):
        for block in range(blocks):
            ref[blocks * n + block] = value[:, (block + side) * LANES : (block + side + 1) * LANES]
        extra = value[:, : LANES] if side else value[:, blocks * LANES :]
        turn = (OVERLAP * (n + side)) % LANES
        extra = pltpu.roll(extra, turn, 1) if turn else extra
        overlaps = jnp.where((lane >= OVERLAP * n) & (lane < OVERLAP * (n + 1)), extra, overlaps)
    ref[blocks * len(values)] = overlaps


def unpack_rows(ref, tiles, n, side):
    blocks = (ref.shape[0] - 1) // tiles
    turn = (-OVERLAP * (n + side)) % LANES
    extra = ref[blocks * tiles]
    extra = pltpu.roll(extra, turn, 1) if turn else extra
    parts = [ref[blocks * n + block] for block in range(blocks)]
    return jnp.concatenate([extra] + parts if side else parts + [extra], axis=1)


def edge_levels(levels, slow, pert, down):
    inner, outer = (1, 0) if down else (0, 1)
    if levels == 1:
        return [slow(0, inner), pert(1, inner), pert(0, inner)]
    row = lax.broadcasted_iota(jnp.int32, slow(0, 0).shape, 0)
    turned = pltpu.roll(slow(1, outer), 4, 0)
    if down:
        extra = jnp.where(row < 2, pltpu.roll(pert(1, inner), 2, 0), turned)
        last = jnp.where(row < 4, extra, slow(0, outer))
    else:
        extra = jnp.where(row >= 6, pltpu.roll(pert(1, inner), 6, 0), turned)
        last = jnp.where(row < 4, slow(0, outer), extra)
    return [slow(0, inner), slow(1, inner), last]


def edge_surface(surf, down):
    inner, outer = (1, 0) if down else (0, 1)
    tiles = [surf(plane, inner) for plane in range(4)]
    row = lax.broadcasted_iota(jnp.int32, tiles[0].shape, 0)
    spread = surf(3, outer)
    for plane in range(3):
        turn = 6 - 2 * plane
        free = row < 2 if down else row >= 6
        tiles.append(jnp.where(free, pltpu.roll(spread, turn, 0), surf(plane, outer)))
    return tiles


def surface_edges(tiles, down):
    row = lax.broadcasted_iota(jnp.int32, tiles[0].shape, 0)
    outer = [tiles[4], tiles[5], tiles[6]]
    first = 2 if down else 0
    spread = pltpu.roll(tiles[6], 6, 0)
    spread = jnp.where((row >= first + 2) & (row < first + 4), pltpu.roll(tiles[5], 4, 0), spread)
    spread = jnp.where((row >= first) & (row < first + 2), pltpu.roll(tiles[4], 2, 0), spread)
    outer.append(spread)
    return [(tiles[plane], outer[plane]) for plane in range(4)]


def pack_kernel(width, step, surf_in, slow_in, pert_in, cross, chip, bulk, rest, cross_far, window, surf, slow, pert, sems):
    copies = [
        pltpu.make_async_copy(source, target, sems.at[n])
        for n, (source, target) in enumerate(((slow_in, slow), (pert_in, pert), (surf_in, surf)))
    ]
    for copy in copies:
        copy.start()
    for copy in copies:
        copy.wait()
    depth = lax.axis_index("depth")
    place = lax.axis_index("xy")
    for own in range(2):

        def reader(ref, side):
            lanes = slice(side * step, side * step + width)
            return lambda level, tile: ref[level, 8 * tile : 8 * tile + 8, lanes]

        def surface(plane, tile):
            return surf[plane // 2, plane % 2, 8 * tile : 8 * tile + 8, own * step : own * step + width]

        @pl.when(depth == own)
        def _():
            slow_near, pert_near = reader(slow, own), reader(pert, own)
            slow_far, pert_far = reader(slow, 1 - own), reader(pert, 1 - own)
            both = [(level, tile) for level in range(2) for tile in range(2)]
            for n, (level, tile) in enumerate(both):
                window[8 + n] = slow_near(level, tile)
                window[12 + n] = pert_near(level, tile)
            for plane in range(4):
                for tile in range(2):
                    window[2 * plane + tile] = surface(plane, tile)
            slow_tiles = [slow_far(*at) for at in both]
            pert_tiles = [pert_far(*at) for at in both]
            if own == 0:
                pack_rows(bulk, slow_tiles + pert_tiles[2:], 1)
                pack_rows(rest, pert_tiles[:2], 1)
            else:
                pack_rows(bulk, slow_tiles[:2] + pert_tiles, 0)
                pack_rows(rest, slow_tiles[2:], 0)
            for down in (False, True):

                @pl.when((lax.rem(place, 2) == 1) == down)
                def _():
                    edges = edge_surface(surface, down) + edge_levels(own, slow_near, pert_near, down)
                    pack_rows(cross, edges, own)
                    pack_rows(cross_far, edge_levels(own, slow_far, pert_far, down), 1 - own)
                    edges = edge_surface(surface, not down) + edge_levels(own, slow_near, pert_near, not down)
                    pack_rows(chip, edges, own)


def relay_kernel(bulk, chip_far, partner):
    depth = lax.axis_index("depth")
    place = lax.axis_index("xy")
    for own in range(2):

        @pl.when(depth == own)
        def _():
            other = [unpack_rows(bulk, 6, n, own) for n in range(6)]
            for n in range(6):
                partner[n] = other[n]

            def slow(level, tile):
                return other[2 * level + tile]

            def pert(level, tile):
                return other[2 + 2 * level + tile]

            for down in (False, True):

                @pl.when((lax.rem(place, 2) == 0) == down)
                def _():
                    pack_rows(chip_far, edge_levels(1 - own, slow, pert, down), own)


def phase(half):
    square = half * half
    cosine = cos_terms[-1]
    sine = sin_terms[-1]
    for term in cos_terms[-2::-1]:
        cosine = cosine * square + term
    for term in sin_terms[-2::-1]:
        sine = sine * square + term
    sine = sine * half
    twice = sine + sine
    return 1.0 - twice * sine, twice * cosine


def own_phases_kernel(freq_tiles, window, partner, rest, phases, pert):
    for own in range(2):

        @pl.when(lax.axis_index("depth") == own)
        def _():
            last = [unpack_rows(rest, 2, tile, own) for tile in range(2)]
            first = [partner[n] for n in range(6)]
            slow = first[:2] + last if own == 0 else first[:4]
            others = first[2:] if own == 0 else last + first[4:]
            for n in range(4):
                pert[n] = others[n]
            for level in range(4):
                for tile in range(2):
                    at = 2 * (level % 2) + tile
                    plane = window[8 + at] if level // 2 == own else slow[at]
                    for f in range(2):
                        cosine, sine = phase(over_columns(freq_tiles[f], plane) * 0.25 * plane)
                        phases[f, level, tile, :8] = cosine
                        phases[f, level, tile, 8:] = sine


def over_columns(tile, like):
    return jnp.concatenate([tile] * (like.shape[1] // LANES), axis=1)


def sweep_kernel(
    width, freq_tiles, bands, back_bands, own_phases, window, partner, cross, cross_far, chip, chip_far,
    gradient, image, theirs, slow_win, pert_win, operand, halo_phases, fields, image_win, grad_win,
):
    depth = lax.axis_index("depth")
    place = lax.axis_index("xy")
    half = width - LANES
    row = lax.broadcasted_iota(jnp.int32, (8, width), 0)
    upper = row < 4
    lane = lax.broadcasted_iota(jnp.int32, (16, LANES), 1)
    even = lax.rem(place, 2) == 0
    freqs = [jnp.concatenate([freq_tiles[f]] * (width // LANES), axis=1) for f in range(2)]

    def store_operand(f, tile, value):
        high = value.astype(jnp.bfloat16)
        low = (value - high.astype(jnp.float32)).astype(jnp.bfloat16)
        base = 48 * tile
        operand[f, base : base + 16] = high
        operand[f, base + 16 : base + 32] = high
        operand[f, base + 32 : base + 48] = low

    def stencil(f, matrix, out_tiles, in_tiles):
        inner_tiles = min(in_tiles, 5)
        product = jnp.dot(
            matrix[f, : 48 * out_tiles, : 48 * inner_tiles],
            operand[f, : 48 * inner_tiles],
            preferred_element_type=jnp.float32,
        )
        slabs = [product[16 * n : 16 * n + 16] for n in range(3 * out_tiles)]
        if in_tiles > inner_tiles:
            outer = jnp.dot(
                matrix[f, 48 * (out_tiles - 1) : 48 * out_tiles, 48 * inner_tiles : 48 * in_tiles],
                operand[f, 48 * inner_tiles : 48 * in_tiles],
                preferred_element_type=jnp.float32,
            )
            for n in range(3):
                slabs[3 * out_tiles - 3 + n] += outer[16 * n : 16 * n + 16]
        result = []
        for tile in range(out_tiles):
            before, same, after = slabs[3 * tile : 3 * tile + 3]
            left = pltpu.roll(before, 1, 1)
            right = pltpu.roll(after, width - 1, 1)
            left = jnp.concatenate([jnp.where(lane == 0, 0.0, left[:, :LANES]), left[:, LANES:]], axis=1)
            right = jnp.concatenate([right[:, :half], jnp.where(lane == LANES - 1, 0.0, right[:, half:])], axis=1)
            result.append(same + left + right)
        return result

    def fill(own, below_is_chip):
        chip_edges = [unpack_rows(chip, 10, n, own) for n in range(10)]
        chip_edges += [unpack_rows(chip_far, 3, n, own) for n in range(3)]
        cross_edges = [unpack_rows(cross, 10, n, own) for n in range(10)]
        cross_edges += [unpack_rows(cross_far, 3, n, own) for n in range(3)]
        above, below = (cross_edges, chip_edges) if below_is_chip else (chip_edges, cross_edges)
        for level in range(2):
            for tile in range(2):
                pert_win[2 * own + level, tile] = window[12 + 2 * level + tile]
                pert_win[2 * (1 - own) + level, tile] = partner[2 * level + tile]
        at = (7, 10) if own == 0 else (10, 7)
        up, down = above[at[0] : at[0] + 3], below[at[0] : at[0] + 3]
        for level in range(2):
            slow_win[level, 0] = jnp.where(upper, down[level], up[level])
            slow_win[level, 1] = jnp.where(upper, up[level], down[level])
        slow_win[0, 2] = jnp.where(upper, down[2], up[2])
        slow_win[1, 2] = pltpu.roll(jnp.where(upper, up[2], down[2]), 4, 0)
        pert_win[1, 2] = jnp.where(
            row < 2, pltpu.roll(down[2], 2, 0), jnp.where(row >= 6, pltpu.roll(up[2], 6, 0), 0.0)
        )
        up, down = above[at[1] : at[1] + 3], below[at[1] : at[1] + 3]
        slow_win[2, 0] = jnp.where(upper, down[0], up[0])
        slow_win[2, 1] = jnp.where(upper, up[0], down[0])
        pert_win[3, 2] = jnp.where(upper, down[1], up[1])
        pert_win[3, 3] = jnp.where(upper, up[1], down[1])
        pert_win[2, 2] = jnp.where(upper, down[2], up[2])
        up, down = surface_edges(above[:7], True), surface_edges(below[:7], False)
        planes = []
        for plane in range(4):
            up_inner, up_outer = up[plane]
            down_inner, down_outer = down[plane]
            planes.append(
                [
                    window[2 * plane],
                    window[2 * plane + 1],
                    jnp.where(upper, down_inner, up_inner),
                    jnp.where(upper, up_inner, down_inner),
                    jnp.where(upper, down_outer, up_outer),
                    jnp.where(upper, up_outer, down_outer),
                ]
            )
        for f in range(2):
            for tile in range(6):
                store_operand(f, tile, jnp.concatenate([planes[2 * f][tile], planes[2 * f + 1][tile]], axis=0))

    for own in range(2):
        for below_is_chip in (False, True):

            @pl.when((depth == own) & (even == below_is_chip))
            def _():
                fill(own, below_is_chip)

    def add_image(f, level, tile, re, im):
        part = (re * re + im * im) * 0.5
        image_win[level, tile] = part if f == 0 else image_win[level, tile] + part

    def add_gradient(f, level, tile, w_re, w_im, u_re, u_im):
        part = (0.25 * freqs[f]) * (w_im * u_re - w_re * u_im)
        grad_win[level, tile] = part if f == 0 else grad_win[level, tile] + part

    def phases_of(f, level, tile):
        if tile < 2:
            return own_phases[f, level, tile, :8], own_phases[f, level, tile, 8:]
        cosine, sine = phase(freqs[f] * 0.25 * slow_win[level, tile - 2])
        if tile == 2 and level > 0:
            halo_phases[f, level - 1, :8] = cosine
            halo_phases[f, level - 1, 8:] = sine
        return cosine, sine

    tiles = (6, 5, 5, 4)
    for level in range(3):
        for f in range(2):
            fields_now = stencil(f, bands, tiles[level + 1], tiles[level])
            for tile, value in enumerate(fields_now):
                cosine, sine = phases_of(f, level, tile)
                v_re, v_im = value[:8], value[8:]
                re = cosine * v_re - sine * v_im
                im = cosine * v_im + sine * v_re
                both = jnp.concatenate([re, im], axis=0)
                store_operand(f, tile, both)
                if tile < 3:
                    fields[f, level, tile] = both
                if tile < 2:
                    add_image(f, level, tile, re, im)
    for f in range(2):
        for tile, value in enumerate(stencil(f, bands, 4, 4)):
            twice = 2.0 * pert_win[3, tile]
            v_re, v_im = value[:8], value[8:]
            if tile < 2:
                cosine, sine = phases_of(f, 3, tile)
                re = cosine * v_re - sine * v_im
                im = cosine * v_im + sine * v_re
                add_image(f, 3, tile, re, im)
                add_gradient(f, 3, tile, twice * re, twice * im, re, im)
            store_operand(f, tile, jnp.concatenate([twice * v_re, twice * v_im], axis=0))
    tiles = (2, 3, 3, 4)
    for level in (2, 1, 0):
        for f in range(2):
            for tile, value in enumerate(stencil(f, back_bands, tiles[level], tiles[level + 1])):
                twice = 2.0 * pert_win[level, tile]
                u_re, u_im = fields[f, level, tile, :8], fields[f, level, tile, 8:]
                w_re = value[:8] + twice * u_re
                w_im = value[8:] + twice * u_im
                if tile < 2:
                    add_gradient(f, level, tile, w_re, w_im, u_re, u_im)
                if level > 0:
                    if tile < 2:
                        cosine, sine = phases_of(f, level, tile)
                    else:
                        cosine, sine = halo_phases[f, level - 1, :8], halo_phases[f, level - 1, 8:]
                    back = [cosine * w_re + sine * w_im, cosine * w_im - sine * w_re]
                    store_operand(f, tile, jnp.concatenate(back, axis=0))

    for own in range(2):

        @pl.when(depth == own)
        def _():
            inner = slice(own * LANES, own * LANES + half)
            outer = slice(own * half, own * half + half)
            for level in range(2):
                for tile in range(2):
                    rows = slice(8 * tile, 8 * tile + 8)
                    gradient[level, rows, outer] = grad_win[2 * own + level, tile, :, inner]
                    image[level, rows, outer] = image_win[2 * own + level, tile, :, inner]
                    theirs[0, level, rows] = grad_win[2 * (1 - own) + level, tile, :, inner]
                    theirs[1, level, rows] = image_win[2 * (1 - own) + level, tile, :, inner]


def split_columns(surface_data, frequencies, coefficients, slowness, perturbation):
    count = lax.axis_size("xy")
    columns = slowness.shape[2]
    half = columns // 2
    width = half + LANES
    step = half - LANES
    f32 = jnp.float32
    axes = ("depth", "xy")

    def moved(value, other_depth, neighbour):
        pairs = []
        for depth in range(2):
            for place in range(count):
                target = {"chip": place ^ 1, "cross": place + 1 if place % 2 else place - 1, "same": place}[neighbour]
                if 0 <= target < count:
                    layer = 1 - depth if other_depth else depth
                    pairs.append((depth * count + place, layer * count + target))
        return lax.ppermute(value, axes, pairs)

    vmem = pl.BlockSpec(memory_space=pltpu.VMEM)
    smem = pl.BlockSpec(memory_space=pltpu.SMEM)
    tile = lambda n: jax.ShapeDtypeStruct((n, 8, width), f32)
    packed = lambda n: jax.ShapeDtypeStruct((n * half // LANES + 1, 8, LANES), f32)
    params = lambda mib: pltpu.CompilerParams(vmem_limit_bytes=mib * 2**20)
    cross, chip, bulk, rest, cross_far, window = pl.pallas_call(
        lambda *refs: pack_kernel(width, step, *refs),
        out_shape=(packed(10), packed(10), packed(6), packed(2), packed(3), tile(16)),
        in_specs=[pl.BlockSpec(memory_space=pltpu.HBM)] * 3,
        out_specs=(vmem,) * 6,
        scratch_shapes=[
            pltpu.VMEM(surface_data.shape, f32),
            pltpu.VMEM(slowness.shape, f32),
            pltpu.VMEM(perturbation.shape, f32),
            pltpu.SemaphoreType.DMA((3,)),
        ],
        compiler_params=params(32),
        name="pack",
    )(*(pltpu.with_memory_space_constraint(x, pltpu.HBM) for x in (surface_data, slowness, perturbation)))
    cross = moved(cross, False, "cross")
    bulk = moved(bulk, True, "same")
    rest = moved(rest, True, "same")
    cross_far = moved(cross_far, True, "cross")
    bands, back_bands, freq_tiles = pl.pallas_call(
        lambda *refs: band_kernel(count * ROWS, *refs),
        out_shape=(
            jax.ShapeDtypeStruct((2, 240, 288), jnp.bfloat16),
            jax.ShapeDtypeStruct((2, 144, 192), jnp.bfloat16),
            jax.ShapeDtypeStruct((2, 8, LANES), f32),
        ),
        in_specs=[smem] * 2,
        out_specs=(vmem,) * 3,
        compiler_params=params(16),
        cost_estimate=pl.CostEstimate(flops=10**6, bytes_accessed=10**6, transcendentals=0),
        name="bands",
    )(coefficients, frequencies)
    chip_far, partner = pl.pallas_call(
        relay_kernel,
        out_shape=(packed(3), tile(6)),
        in_specs=[vmem],
        out_specs=(vmem,) * 2,
        compiler_params=params(32),
        cost_estimate=pl.CostEstimate(flops=10**6, bytes_accessed=10**6, transcendentals=0),
        name="relay",
    )(bulk)
    chip = moved(chip, False, "chip")
    chip_far = moved(chip_far, False, "chip")

    own_phases, partner = pl.pallas_call(
        own_phases_kernel,
        out_shape=(jax.ShapeDtypeStruct((2, 4, 2, 16, width), f32), tile(4)),
        in_specs=[vmem] * 4,
        out_specs=(vmem,) * 2,
        compiler_params=params(16),
        name="own_phases",
    )(freq_tiles, window, partner, rest)

    own = jax.ShapeDtypeStruct((2, ROWS, columns), f32)
    gradient, image, theirs = pl.pallas_call(
        lambda *refs: sweep_kernel(width, *refs),
        out_shape=(own, own, jax.ShapeDtypeStruct((2, 2, ROWS, half), f32)),
        in_specs=[vmem] * 10,
        out_specs=(vmem,) * 3,
        scratch_shapes=[
            pltpu.VMEM((3, 3, 8, width), f32),
            pltpu.VMEM((4, 4, 8, width), f32),
            pltpu.VMEM((2, 288, width), jnp.bfloat16),
            pltpu.VMEM((2, 2, 16, width), f32),
            pltpu.VMEM((2, 3, 3, 16, width), f32),
            pltpu.VMEM((4, 2, 8, width), f32),
            pltpu.VMEM((4, 2, 8, width), f32),
        ],
        compiler_params=params(40),
        name="sweep",
    )(
        freq_tiles, bands, back_bands, own_phases, window, partner, cross, cross_far, chip, chip_far,
    )
    theirs = moved(theirs, True, "same")
    start = (1 - lax.axis_index("depth")) * half
    gradient = lax.dynamic_update_slice(gradient, theirs[0], (0, 0, start))
    image = lax.dynamic_update_slice(image, theirs[1], (0, 0, start))
    return gradient, image


def on_slice(surface_data, frequencies, coefficients, slowness, perturbation):
    levels, rows, columns = slowness.shape
    fits = (
        lax.axis_size("depth") == 2
        and levels == 2
        and rows == ROWS
        and frequencies.shape[0] == 2
        and lax.axis_size("xy") % 2 == 0
        and columns % (2 * LANES) == 0
        and columns >= 4 * LANES
    )
    plan = split_columns if fits else on_device
    return plan(surface_data, frequencies, coefficients, slowness, perturbation)


def solution(mesh):
    in_specs = (P(None, None, "xy", None), P(), P(), P("depth", "xy", None), P("depth", "xy", None))
    out_specs = (P("depth", "xy", None), P("depth", "xy", None))
    return jax.shard_map(
        on_slice, mesh=mesh, in_specs=in_specs, out_specs=out_specs, check_vma=False
    )
```

```python
import numpy as np
import jax
import jax.numpy as jnp
from jax import lax
from jax.experimental import pallas as pl
from jax.experimental.pallas import tpu as pltpu
from jax.sharding import PartitionSpec as P

layer_thickness = 0.5


def extended_2(cells, sides, width):
    for axis, dim in sides:
        count = lax.axis_size(axis)
        ends = count - 1
        head = lax.slice_in_dim(cells, 0, width, axis=dim)
        tail = lax.slice_in_dim(cells, cells.shape[dim] - width, cells.shape[dim], axis=dim)
        cells = jnp.concatenate(
            [
                lax.ppermute(tail, axis, [(i, (i + 1) % count) for i in range(ends)]),
                cells,
                lax.ppermute(head, axis, [((i + 1) % count, i) for i in range(ends)]),
            ],
            axis=dim,
        )
    return cells


def shifted(value, axis, steps):
    count = lax.axis_size(axis)
    initial, last = (max(0, -steps), min(count, count - steps))
    return lax.ppermute(value, axis, [(source, source + steps) for source in range(initial, last)])


def apply_stencil(extended, tap_re, tap_im):
    out_rows = extended.shape[2] - 4
    col_count = extended.shape[3]
    padded = jnp.pad(extended, ((0, 0), (0, 0), (0, 0), (1, 1)))
    acc_re = jnp.zeros((extended.shape[0], out_rows, col_count), jnp.float32)
    acc_im = jnp.zeros((extended.shape[0], out_rows, col_count), jnp.float32)
    for row_off in range(5):
        for col_off in range(3):
            tap_index = row_off * 3 + col_off
            part_re = padded[:, 0, row_off : row_off + out_rows, col_off : col_off + col_count]
            part_im = padded[:, 1, row_off : row_off + out_rows, col_off : col_off + col_count]
            weight_re = tap_re[:, tap_index][:, None, None]
            weight_im = tap_im[:, tap_index][:, None, None]
            acc_re = acc_re + weight_re * part_re - weight_im * part_im
            acc_im = acc_im + weight_re * part_im + weight_im * part_re
    return (acc_re, acc_im)


def adjoint_stencil(extended, tap_re, tap_im):
    out_rows = extended.shape[2] - 4
    col_count = extended.shape[3]
    padded = jnp.pad(extended, ((0, 0), (0, 0), (0, 0), (1, 1)))
    acc_re = jnp.zeros((extended.shape[0], out_rows, col_count), jnp.float32)
    acc_im = jnp.zeros((extended.shape[0], out_rows, col_count), jnp.float32)
    for row_off in range(5):
        for col_off in range(3):
            tap_index = row_off * 3 + col_off
            row_from = 4 - row_off
            col_from = 2 - col_off
            part_re = padded[:, 0, row_from : row_from + out_rows, col_from : col_from + col_count]
            part_im = padded[:, 1, row_from : row_from + out_rows, col_from : col_from + col_count]
            weight_re = tap_re[:, tap_index][:, None, None]
            weight_im = tap_im[:, tap_index][:, None, None]
            acc_re = acc_re + weight_re * part_re + weight_im * part_im
            acc_im = acc_im + weight_re * part_im - weight_im * part_re
    return (acc_re, acc_im)


def phase_parts(freqs, slow_plane):
    angle = freqs[:, None, None] * layer_thickness * slow_plane[None]
    return (jnp.cos(angle), jnp.sin(angle))


def forward_steps(wavefield, freqs, taps, slowness, freq_total):
    tap_re = taps[:, 0]
    tap_im = taps[:, 1]
    step_count = slowness.shape[0]
    states = []
    current = wavefield
    for level in range(step_count):
        extended = extended_2(current, (("xy", 2),), 2)
        acc_re, acc_im = apply_stencil(extended, tap_re, tap_im)
        phase_re, phase_im = phase_parts(freqs, slowness[level])
        next_re = phase_re * acc_re - phase_im * acc_im
        next_im = phase_re * acc_im + phase_im * acc_re
        current = jnp.stack([next_re, next_im], axis=1)
        states.append(current)
    stacked = jnp.stack(states, axis=1)
    image_part = (
        jnp.sum(stacked[:, :, 0] * stacked[:, :, 0] + stacked[:, :, 1] * stacked[:, :, 1], axis=0)
        / freq_total
    )
    return (stacked, states[-1], image_part)


def backward_steps(adjoint, states, freqs, taps, slowness, perturbation, freq_total):
    tap_re = taps[:, 0]
    tap_im = taps[:, 1]
    step_count = slowness.shape[0]
    parts = [None] * step_count
    for level in reversed(range(step_count)):
        wave_re = states[:, level, 0]
        wave_im = states[:, level, 1]
        grad_re = adjoint[:, 0] + 2.0 * perturbation[level] * wave_re
        grad_im = adjoint[:, 1] + 2.0 * perturbation[level] * wave_im
        parts[level] = (
            layer_thickness
            / freq_total
            * jnp.sum(freqs[:, None, None] * (grad_im * wave_re - grad_re * wave_im), axis=0)
        )
        phase_re, phase_im = phase_parts(freqs, slowness[level])
        back_re = phase_re * grad_re + phase_im * grad_im
        back_im = phase_re * grad_im - phase_im * grad_re
        extended = extended_2(jnp.stack([back_re, back_im], axis=1), (("xy", 2),), 2)
        acc_re, acc_im = adjoint_stencil(extended, tap_re, tap_im)
        adjoint = jnp.stack([acc_re, acc_im], axis=1)
    return (adjoint, jnp.stack(parts, axis=0))


def on_device(surface_data, frequencies, coefficients, slowness, perturbation):
    freq_count = frequencies.shape[0]
    step_count = slowness.shape[0]
    row_count = slowness.shape[1]
    col_count = slowness.shape[2]
    layers = lax.axis_size("depth")
    depth_index = lax.axis_index("depth")
    stored_zero = jnp.zeros((freq_count, step_count, 2, row_count, col_count), jnp.float32)
    plane_zero = jnp.zeros((step_count, row_count, col_count), jnp.float32)
    start = jnp.where(depth_index == 0, surface_data, jnp.zeros_like(surface_data))

    def forward_segment(segment_no, carry):
        current, stored, image_sum = carry
        states, bottom, image_part = forward_steps(
            current, frequencies, coefficients, slowness, freq_count
        )
        chosen = depth_index == segment_no
        stored = jnp.where(chosen, states, stored)
        image_sum = jnp.where(chosen, image_part, image_sum)
        current = shifted(bottom, "depth", 1)
        return (current, stored, image_sum)

    unused_field, stored, image_field = lax.fori_loop(
        0, layers, forward_segment, (start, stored_zero, plane_zero)
    )

    def backward_segment(segment_no, carry):
        adjoint, gradient_sum = carry
        top_field, parts = backward_steps(
            adjoint, stored, frequencies, coefficients, slowness, perturbation, freq_count
        )
        gradient_sum = jnp.where(depth_index == layers - 1 - segment_no, parts, gradient_sum)
        adjoint = shifted(top_field, "depth", -1)
        return (adjoint, gradient_sum)

    adjoint_zero = jnp.zeros_like(surface_data)
    unused_adjoint, gradient = lax.fori_loop(
        0, layers, backward_segment, (adjoint_zero, plane_zero)
    )
    return (gradient, image_field)


ROWS = 16
HALO_TILES = 4
LANES = 128

OVERLAP = 8

sin_terms = (0.9999999995, -0.1666666515, 0.008333256964, -0.0001982776292, 2.657952479e-06)
cos_terms = (0.9999999947, -0.4999998344, 0.04166583045, -0.00138740917, 2.372928386e-05)


def window_row(tile, sub):
    group = tile - 2
    above = sub - 4 * (group + 1)
    below = sub + ROWS + 4 * group
    even = jnp.where(sub < 4, below, above - 4)
    odd = jnp.where(sub < 4, above, below - 4)
    halo = jnp.where(lax.rem(tile, 2) == 0, even, odd)
    return jnp.where(tile < 2, 8 * tile + sub, halo)


def band_kernel(plane_rows, taps, freqs, bands, back_bands, freq_tiles):
    first_row = lax.axis_index("xy") * ROWS

    def fill(ref, adjoint):
        out_tiles = ref.shape[1] // 48
        in_tiles = ref.shape[2] // 48
        shape = (16, ref.shape[2])
        col = lax.broadcasted_iota(jnp.int32, shape, 1)
        sub = lax.broadcasted_iota(jnp.int32, shape, 0)
        tile_k = sum((col >= 48 * t).astype(jnp.int32) for t in range(1, in_tiles))
        row_k = window_row(tile_k, col & 7)
        part_k = (col >> 4) - 3 * tile_k
        plane_k = (col >> 3) & 1
        plane_m = sub >> 3
        same = plane_k == plane_m
        inside_k = (row_k + first_row >= 0) & (row_k + first_row < plane_rows)
        for tile in range(out_tiles):
            row_m = window_row(jnp.full(shape, tile, jnp.int32), sub & 7)
            inside = inside_k & (row_m + first_row >= 0) & (row_m + first_row < plane_rows)
            offset = jnp.where(inside, row_k - row_m, 9)
            hits = [offset == a - 2 for a in range(5)]
            for f in range(ref.shape[0]):
                for b in range(3):
                    total = jnp.zeros(shape, jnp.float32)
                    for a in range(5):
                        tap = 3 * (4 - a) + 2 - b if adjoint else 3 * a + b
                        re = taps[f, 0, tap]
                        im = -taps[f, 1, tap] if adjoint else taps[f, 1, tap]
                        crossed = jnp.where(plane_m == 0, -im, im)
                        total = jnp.where(hits[a], jnp.where(same, re, crossed), total)
                    high = total.astype(jnp.bfloat16)
                    low = total - high.astype(jnp.float32)
                    base = 48 * tile + 16 * b
                    ref[f, base : base + 16] = jnp.where(part_k == 1, low, total).astype(jnp.bfloat16)

    fill(bands, False)
    fill(back_bands, True)
    for f in range(freq_tiles.shape[0]):
        freq_tiles[f] = jnp.full((8, LANES), freqs[f], jnp.float32)


def pack_rows(ref, values, side):
    lane = lax.broadcasted_iota(jnp.int32, (8, LANES), 1)
    overlaps = jnp.zeros((8, LANES), jnp.float32)
    blocks = (values[0].shape[1] - LANES) // LANES
    for n, value in enumerate(values):
        for block in range(blocks):
            ref[blocks * n + block] = value[:, (block + side) * LANES : (block + side + 1) * LANES]
        extra = value[:, : LANES] if side else value[:, blocks * LANES :]
        turn = (OVERLAP * (n + side)) % LANES
        extra = pltpu.roll(extra, turn, 1) if turn else extra
        overlaps = jnp.where((lane >= OVERLAP * n) & (lane < OVERLAP * (n + 1)), extra, overlaps)
    ref[blocks * len(values)] = overlaps


def unpack_rows(ref, tiles, n, side):
    blocks = (ref.shape[0] - 1) // tiles
    turn = (-OVERLAP * (n + side)) % LANES
    extra = ref[blocks * tiles]
    extra = pltpu.roll(extra, turn, 1) if turn else extra
    parts = [ref[blocks * n + block] for block in range(blocks)]
    return jnp.concatenate([extra] + parts if side else parts + [extra], axis=1)


def edge_levels(levels, slow, pert, down):
    inner, outer = (1, 0) if down else (0, 1)
    if levels == 1:
        return [slow(0, inner), pert(1, inner), pert(0, inner)]
    row = lax.broadcasted_iota(jnp.int32, slow(0, 0).shape, 0)
    turned = pltpu.roll(slow(1, outer), 4, 0)
    if down:
        extra = jnp.where(row < 2, pltpu.roll(pert(1, inner), 2, 0), turned)
        last = jnp.where(row < 4, extra, slow(0, outer))
    else:
        extra = jnp.where(row >= 6, pltpu.roll(pert(1, inner), 6, 0), turned)
        last = jnp.where(row < 4, slow(0, outer), extra)
    return [slow(0, inner), slow(1, inner), last]


def edge_surface(surf, down):
    inner, outer = (1, 0) if down else (0, 1)
    tiles = [surf(plane, inner) for plane in range(4)]
    row = lax.broadcasted_iota(jnp.int32, tiles[0].shape, 0)
    spread = surf(3, outer)
    for plane in range(3):
        turn = 6 - 2 * plane
        free = row < 2 if down else row >= 6
        tiles.append(jnp.where(free, pltpu.roll(spread, turn, 0), surf(plane, outer)))
    return tiles


def surface_edges(tiles, down):
    row = lax.broadcasted_iota(jnp.int32, tiles[0].shape, 0)
    outer = [tiles[4], tiles[5], tiles[6]]
    first = 2 if down else 0
    spread = pltpu.roll(tiles[6], 6, 0)
    spread = jnp.where((row >= first + 2) & (row < first + 4), pltpu.roll(tiles[5], 4, 0), spread)
    spread = jnp.where((row >= first) & (row < first + 2), pltpu.roll(tiles[4], 2, 0), spread)
    outer.append(spread)
    return [(tiles[plane], outer[plane]) for plane in range(4)]


def pack_kernel(width, step, surf_in, slow_in, pert_in, cross, chip, bulk, rest, cross_far, window, surf, slow, pert, sems):
    copies = [
        pltpu.make_async_copy(source, target, sems.at[n])
        for n, (source, target) in enumerate(((slow_in, slow), (pert_in, pert), (surf_in, surf)))
    ]
    for copy in copies:
        copy.start()
    for copy in copies:
        copy.wait()
    depth = lax.axis_index("depth")
    place = lax.axis_index("xy")
    for own in range(2):

        def reader(ref, side):
            lanes = slice(side * step, side * step + width)
            return lambda level, tile: ref[level, 8 * tile : 8 * tile + 8, lanes]

        def surface(plane, tile):
            return surf[plane // 2, plane % 2, 8 * tile : 8 * tile + 8, own * step : own * step + width]

        @pl.when(depth == own)
        def _():
            slow_near, pert_near = reader(slow, own), reader(pert, own)
            slow_far, pert_far = reader(slow, 1 - own), reader(pert, 1 - own)
            both = [(level, tile) for level in range(2) for tile in range(2)]
            for n, (level, tile) in enumerate(both):
                window[8 + n] = slow_near(level, tile)
                window[12 + n] = pert_near(level, tile)
            for plane in range(4):
                for tile in range(2):
                    window[2 * plane + tile] = surface(plane, tile)
            slow_tiles = [slow_far(*at) for at in both]
            pert_tiles = [pert_far(*at) for at in both]
            if own == 0:
                pack_rows(bulk, slow_tiles + pert_tiles[2:], 1)
                pack_rows(rest, pert_tiles[:2], 1)
            else:
                pack_rows(bulk, slow_tiles[:2] + pert_tiles, 0)
                pack_rows(rest, slow_tiles[2:], 0)
            for down in (False, True):

                @pl.when((lax.rem(place, 2) == 1) == down)
                def _():
                    edges = edge_surface(surface, down) + edge_levels(own, slow_near, pert_near, down)
                    pack_rows(cross, edges, own)
                    pack_rows(cross_far, edge_levels(own, slow_far, pert_far, down), 1 - own)
                    edges = edge_surface(surface, not down) + edge_levels(own, slow_near, pert_near, not down)
                    pack_rows(chip, edges, own)


def relay_kernel(bulk, rest, order, chip_far, partner):
    depth = lax.axis_index("depth")
    place = lax.axis_index("xy")
    for own in range(2):

        @pl.when(depth == own)
        def _():
            other = [unpack_rows(bulk, 6, n, own) for n in range(6)]
            last = [unpack_rows(rest, 2, n, own) for n in range(2)]
            other = other[:2] + last + other[2:] if own == 0 else other[:4] + last + other[4:]
            for n in range(8):
                partner[n] = other[n]
            for down in (False, True):

                @pl.when((lax.rem(place, 2) == 0) == down)
                def _():
                    edges = edge_levels(
                        1 - own,
                        lambda level, tile: other[2 * level + tile],
                        lambda level, tile: other[4 + 2 * level + tile],
                        down,
                    )
                    pack_rows(chip_far, edges, own)


def phase(half):
    square = half * half
    cosine = cos_terms[-1]
    sine = sin_terms[-1]
    for term in cos_terms[-2::-1]:
        cosine = cosine * square + term
    for term in sin_terms[-2::-1]:
        sine = sine * square + term
    sine = sine * half
    twice = sine + sine
    return 1.0 - twice * sine, twice * cosine


def own_phases_kernel(freq_tiles, window, partner, phases):
    depth = lax.axis_index("depth")
    for level in range(4):
        for tile in range(2):
            own, other = window[8 + 2 * (level % 2) + tile], partner[2 * (level % 2) + tile]
            slow = jnp.where(depth == level // 2, own, other)
            for f in range(2):
                cosine, sine = phase(over_columns(freq_tiles[f], slow) * 0.25 * slow)
                phases[f, level, tile, :8] = cosine
                phases[f, level, tile, 8:] = sine


def over_columns(tile, like):
    return jnp.concatenate([tile] * (like.shape[1] // LANES), axis=1)


def sweep_kernel(
    width, freq_tiles, bands, back_bands, own_phases, window, partner, cross, cross_far, chip, chip_far,
    gradient, image, theirs, slow_win, pert_win, operand, halo_phases, fields, image_win, grad_win,
):
    depth = lax.axis_index("depth")
    place = lax.axis_index("xy")
    half = width - LANES
    row = lax.broadcasted_iota(jnp.int32, (8, width), 0)
    upper = row < 4
    lane = lax.broadcasted_iota(jnp.int32, (16, LANES), 1)
    even = lax.rem(place, 2) == 0
    freqs = [jnp.concatenate([freq_tiles[f]] * (width // LANES), axis=1) for f in range(2)]

    def store_operand(f, tile, value):
        high = value.astype(jnp.bfloat16)
        low = (value - high.astype(jnp.float32)).astype(jnp.bfloat16)
        base = 48 * tile
        operand[f, base : base + 16] = high
        operand[f, base + 16 : base + 32] = high
        operand[f, base + 32 : base + 48] = low

    def stencil(f, matrix, out_tiles, in_tiles):
        inner_tiles = min(in_tiles, 5)
        product = jnp.dot(
            matrix[f, : 48 * out_tiles, : 48 * inner_tiles],
            operand[f, : 48 * inner_tiles],
            preferred_element_type=jnp.float32,
        )
        slabs = [product[16 * n : 16 * n + 16] for n in range(3 * out_tiles)]
        if in_tiles > inner_tiles:
            outer = jnp.dot(
                matrix[f, 48 * (out_tiles - 1) : 48 * out_tiles, 48 * inner_tiles : 48 * in_tiles],
                operand[f, 48 * inner_tiles : 48 * in_tiles],
                preferred_element_type=jnp.float32,
            )
            for n in range(3):
                slabs[3 * out_tiles - 3 + n] += outer[16 * n : 16 * n + 16]
        result = []
        for tile in range(out_tiles):
            before, same, after = slabs[3 * tile : 3 * tile + 3]
            left = pltpu.roll(before, 1, 1)
            right = pltpu.roll(after, width - 1, 1)
            left = jnp.concatenate([jnp.where(lane == 0, 0.0, left[:, :LANES]), left[:, LANES:]], axis=1)
            right = jnp.concatenate([right[:, :half], jnp.where(lane == LANES - 1, 0.0, right[:, half:])], axis=1)
            result.append(same + left + right)
        return result

    def fill(own, below_is_chip):
        chip_edges = [unpack_rows(chip, 10, n, own) for n in range(10)]
        chip_edges += [unpack_rows(chip_far, 3, n, own) for n in range(3)]
        cross_edges = [unpack_rows(cross, 10, n, own) for n in range(10)]
        cross_edges += [unpack_rows(cross_far, 3, n, own) for n in range(3)]
        above, below = (cross_edges, chip_edges) if below_is_chip else (chip_edges, cross_edges)
        for level in range(2):
            for tile in range(2):
                pert_win[2 * own + level, tile] = window[12 + 2 * level + tile]
                pert_win[2 * (1 - own) + level, tile] = partner[4 + 2 * level + tile]
        at = (7, 10) if own == 0 else (10, 7)
        up, down = above[at[0] : at[0] + 3], below[at[0] : at[0] + 3]
        for level in range(2):
            slow_win[level, 0] = jnp.where(upper, down[level], up[level])
            slow_win[level, 1] = jnp.where(upper, up[level], down[level])
        slow_win[0, 2] = jnp.where(upper, down[2], up[2])
        slow_win[1, 2] = pltpu.roll(jnp.where(upper, up[2], down[2]), 4, 0)
        pert_win[1, 2] = jnp.where(
            row < 2, pltpu.roll(down[2], 2, 0), jnp.where(row >= 6, pltpu.roll(up[2], 6, 0), 0.0)
        )
        up, down = above[at[1] : at[1] + 3], below[at[1] : at[1] + 3]
        slow_win[2, 0] = jnp.where(upper, down[0], up[0])
        slow_win[2, 1] = jnp.where(upper, up[0], down[0])
        pert_win[3, 2] = jnp.where(upper, down[1], up[1])
        pert_win[3, 3] = jnp.where(upper, up[1], down[1])
        pert_win[2, 2] = jnp.where(upper, down[2], up[2])
        up, down = surface_edges(above[:7], True), surface_edges(below[:7], False)
        planes = []
        for plane in range(4):
            up_inner, up_outer = up[plane]
            down_inner, down_outer = down[plane]
            planes.append(
                [
                    window[2 * plane],
                    window[2 * plane + 1],
                    jnp.where(upper, down_inner, up_inner),
                    jnp.where(upper, up_inner, down_inner),
                    jnp.where(upper, down_outer, up_outer),
                    jnp.where(upper, up_outer, down_outer),
                ]
            )
        for f in range(2):
            for tile in range(6):
                store_operand(f, tile, jnp.concatenate([planes[2 * f][tile], planes[2 * f + 1][tile]], axis=0))

    for own in range(2):
        for below_is_chip in (False, True):

            @pl.when((depth == own) & (even == below_is_chip))
            def _():
                fill(own, below_is_chip)

    def add_image(f, level, tile, re, im):
        part = (re * re + im * im) * 0.5
        image_win[level, tile] = part if f == 0 else image_win[level, tile] + part

    def add_gradient(f, level, tile, w_re, w_im, u_re, u_im):
        part = (0.25 * freqs[f]) * (w_im * u_re - w_re * u_im)
        grad_win[level, tile] = part if f == 0 else grad_win[level, tile] + part

    def phases_of(f, level, tile):
        if tile < 2:
            return own_phases[f, level, tile, :8], own_phases[f, level, tile, 8:]
        cosine, sine = phase(freqs[f] * 0.25 * slow_win[level, tile - 2])
        if tile == 2 and level > 0:
            halo_phases[f, level - 1, :8] = cosine
            halo_phases[f, level - 1, 8:] = sine
        return cosine, sine

    tiles = (6, 5, 5, 4)
    for level in range(3):
        for f in range(2):
            fields_now = stencil(f, bands, tiles[level + 1], tiles[level])
            for tile, value in enumerate(fields_now):
                cosine, sine = phases_of(f, level, tile)
                v_re, v_im = value[:8], value[8:]
                re = cosine * v_re - sine * v_im
                im = cosine * v_im + sine * v_re
                both = jnp.concatenate([re, im], axis=0)
                store_operand(f, tile, both)
                if tile < 3:
                    fields[f, level, tile] = both
                if tile < 2:
                    add_image(f, level, tile, re, im)
    for f in range(2):
        for tile, value in enumerate(stencil(f, bands, 4, 4)):
            twice = 2.0 * pert_win[3, tile]
            v_re, v_im = value[:8], value[8:]
            if tile < 2:
                cosine, sine = phases_of(f, 3, tile)
                re = cosine * v_re - sine * v_im
                im = cosine * v_im + sine * v_re
                add_image(f, 3, tile, re, im)
                add_gradient(f, 3, tile, twice * re, twice * im, re, im)
            store_operand(f, tile, jnp.concatenate([twice * v_re, twice * v_im], axis=0))
    tiles = (2, 3, 3, 4)
    for level in (2, 1, 0):
        for f in range(2):
            for tile, value in enumerate(stencil(f, back_bands, tiles[level], tiles[level + 1])):
                twice = 2.0 * pert_win[level, tile]
                u_re, u_im = fields[f, level, tile, :8], fields[f, level, tile, 8:]
                w_re = value[:8] + twice * u_re
                w_im = value[8:] + twice * u_im
                if tile < 2:
                    add_gradient(f, level, tile, w_re, w_im, u_re, u_im)
                if level > 0:
                    if tile < 2:
                        cosine, sine = phases_of(f, level, tile)
                    else:
                        cosine, sine = halo_phases[f, level - 1, :8], halo_phases[f, level - 1, 8:]
                    back = [cosine * w_re + sine * w_im, cosine * w_im - sine * w_re]
                    store_operand(f, tile, jnp.concatenate(back, axis=0))

    for own in range(2):

        @pl.when(depth == own)
        def _():
            inner = slice(own * LANES, own * LANES + half)
            outer = slice(own * half, own * half + half)
            for level in range(2):
                for tile in range(2):
                    rows = slice(8 * tile, 8 * tile + 8)
                    gradient[level, rows, outer] = grad_win[2 * own + level, tile, :, inner]
                    image[level, rows, outer] = image_win[2 * own + level, tile, :, inner]
                    theirs[0, level, rows] = grad_win[2 * (1 - own) + level, tile, :, inner]
                    theirs[1, level, rows] = image_win[2 * (1 - own) + level, tile, :, inner]


def split_columns(surface_data, frequencies, coefficients, slowness, perturbation):
    count = lax.axis_size("xy")
    columns = slowness.shape[2]
    half = columns // 2
    width = half + LANES
    step = half - LANES
    f32 = jnp.float32
    axes = ("depth", "xy")

    def moved(value, other_depth, neighbour):
        pairs = []
        for depth in range(2):
            for place in range(count):
                target = {"chip": place ^ 1, "cross": place + 1 if place % 2 else place - 1, "same": place}[neighbour]
                if 0 <= target < count:
                    layer = 1 - depth if other_depth else depth
                    pairs.append((depth * count + place, layer * count + target))
        return lax.ppermute(value, axes, pairs)

    vmem = pl.BlockSpec(memory_space=pltpu.VMEM)
    smem = pl.BlockSpec(memory_space=pltpu.SMEM)
    tile = lambda n: jax.ShapeDtypeStruct((n, 8, width), f32)
    packed = lambda n: jax.ShapeDtypeStruct((n * half // LANES + 1, 8, LANES), f32)
    params = lambda mib: pltpu.CompilerParams(vmem_limit_bytes=mib * 2**20)
    cross, chip, bulk, rest, cross_far, window = pl.pallas_call(
        lambda *refs: pack_kernel(width, step, *refs),
        out_shape=(packed(10), packed(10), packed(6), packed(2), packed(3), tile(16)),
        in_specs=[pl.BlockSpec(memory_space=pltpu.HBM)] * 3,
        out_specs=(vmem,) * 6,
        scratch_shapes=[
            pltpu.VMEM(surface_data.shape, f32),
            pltpu.VMEM(slowness.shape, f32),
            pltpu.VMEM(perturbation.shape, f32),
            pltpu.SemaphoreType.DMA((3,)),
        ],
        compiler_params=params(32),
        name="pack",
    )(*(pltpu.with_memory_space_constraint(x, pltpu.HBM) for x in (surface_data, slowness, perturbation)))
    cross = moved(cross, False, "cross")
    bulk = moved(bulk, True, "same")
    rest = moved(rest, True, "same")
    cross_far = moved(cross_far, True, "cross")
    bands, back_bands, freq_tiles = pl.pallas_call(
        lambda *refs: band_kernel(count * ROWS, *refs),
        out_shape=(
            jax.ShapeDtypeStruct((2, 240, 288), jnp.bfloat16),
            jax.ShapeDtypeStruct((2, 144, 192), jnp.bfloat16),
            jax.ShapeDtypeStruct((2, 8, LANES), f32),
        ),
        in_specs=[smem] * 2,
        out_specs=(vmem,) * 3,
        compiler_params=params(16),
        cost_estimate=pl.CostEstimate(flops=10**6, bytes_accessed=10**6, transcendentals=0),
        name="bands",
    )(coefficients, frequencies)
    chip_far, partner = pl.pallas_call(
        relay_kernel,
        out_shape=(packed(3), tile(8)),
        in_specs=[vmem] * 3,
        out_specs=(vmem,) * 2,
        compiler_params=params(32),
        cost_estimate=pl.CostEstimate(flops=10**6, bytes_accessed=10**6, transcendentals=0),
        name="relay",
    )(bulk, rest, freq_tiles)
    chip = moved(chip, False, "chip")
    chip_far = moved(chip_far, False, "chip")

    own_phases = pl.pallas_call(
        own_phases_kernel,
        out_shape=jax.ShapeDtypeStruct((2, 4, 2, 16, width), f32),
        in_specs=[vmem] * 3,
        out_specs=vmem,
        compiler_params=params(16),
        name="own_phases",
    )(freq_tiles, window, partner)

    own = jax.ShapeDtypeStruct((2, ROWS, columns), f32)
    gradient, image, theirs = pl.pallas_call(
        lambda *refs: sweep_kernel(width, *refs),
        out_shape=(own, own, jax.ShapeDtypeStruct((2, 2, ROWS, half), f32)),
        in_specs=[vmem] * 10,
        out_specs=(vmem,) * 3,
        scratch_shapes=[
            pltpu.VMEM((3, 3, 8, width), f32),
            pltpu.VMEM((4, 4, 8, width), f32),
            pltpu.VMEM((2, 288, width), jnp.bfloat16),
            pltpu.VMEM((2, 2, 16, width), f32),
            pltpu.VMEM((2, 3, 3, 16, width), f32),
            pltpu.VMEM((4, 2, 8, width), f32),
            pltpu.VMEM((4, 2, 8, width), f32),
        ],
        compiler_params=params(40),
        name="sweep",
    )(
        freq_tiles, bands, back_bands, own_phases, window, partner, cross, cross_far, chip, chip_far,
    )
    theirs = moved(theirs, True, "same")
    start = (1 - lax.axis_index("depth")) * half
    gradient = lax.dynamic_update_slice(gradient, theirs[0], (0, 0, start))
    image = lax.dynamic_update_slice(image, theirs[1], (0, 0, start))
    return gradient, image


def on_slice(surface_data, frequencies, coefficients, slowness, perturbation):
    levels, rows, columns = slowness.shape
    fits = (
        lax.axis_size("depth") == 2
        and levels == 2
        and rows == ROWS
        and frequencies.shape[0] == 2
        and lax.axis_size("xy") % 2 == 0
        and columns % (2 * LANES) == 0
        and columns >= 4 * LANES
    )
    plan = split_columns if fits else on_device
    return plan(surface_data, frequencies, coefficients, slowness, perturbation)


def solution(mesh):
    in_specs = (P(None, None, "xy", None), P(), P(), P("depth", "xy", None), P("depth", "xy", None))
    out_specs = (P("depth", "xy", None), P("depth", "xy", None))
    return jax.shard_map(
        on_slice, mesh=mesh, in_specs=in_specs, out_specs=out_specs, check_vma=False
    )
```

```python
import numpy as np
import jax
import jax.numpy as jnp
from jax import lax
from jax.experimental import pallas as pl
from jax.experimental.pallas import tpu as pltpu
from jax.sharding import PartitionSpec as P

layer_thickness = 0.5


def extended_2(cells, sides, width):
    for axis, dim in sides:
        count = lax.axis_size(axis)
        ends = count - 1
        head = lax.slice_in_dim(cells, 0, width, axis=dim)
        tail = lax.slice_in_dim(cells, cells.shape[dim] - width, cells.shape[dim], axis=dim)
        cells = jnp.concatenate(
            [
                lax.ppermute(tail, axis, [(i, (i + 1) % count) for i in range(ends)]),
                cells,
                lax.ppermute(head, axis, [((i + 1) % count, i) for i in range(ends)]),
            ],
            axis=dim,
        )
    return cells


def shifted(value, axis, steps):
    count = lax.axis_size(axis)
    initial, last = (max(0, -steps), min(count, count - steps))
    return lax.ppermute(value, axis, [(source, source + steps) for source in range(initial, last)])


def apply_stencil(extended, tap_re, tap_im):
    out_rows = extended.shape[2] - 4
    col_count = extended.shape[3]
    padded = jnp.pad(extended, ((0, 0), (0, 0), (0, 0), (1, 1)))
    acc_re = jnp.zeros((extended.shape[0], out_rows, col_count), jnp.float32)
    acc_im = jnp.zeros((extended.shape[0], out_rows, col_count), jnp.float32)
    for row_off in range(5):
        for col_off in range(3):
            tap_index = row_off * 3 + col_off
            part_re = padded[:, 0, row_off : row_off + out_rows, col_off : col_off + col_count]
            part_im = padded[:, 1, row_off : row_off + out_rows, col_off : col_off + col_count]
            weight_re = tap_re[:, tap_index][:, None, None]
            weight_im = tap_im[:, tap_index][:, None, None]
            acc_re = acc_re + weight_re * part_re - weight_im * part_im
            acc_im = acc_im + weight_re * part_im + weight_im * part_re
    return (acc_re, acc_im)


def adjoint_stencil(extended, tap_re, tap_im):
    out_rows = extended.shape[2] - 4
    col_count = extended.shape[3]
    padded = jnp.pad(extended, ((0, 0), (0, 0), (0, 0), (1, 1)))
    acc_re = jnp.zeros((extended.shape[0], out_rows, col_count), jnp.float32)
    acc_im = jnp.zeros((extended.shape[0], out_rows, col_count), jnp.float32)
    for row_off in range(5):
        for col_off in range(3):
            tap_index = row_off * 3 + col_off
            row_from = 4 - row_off
            col_from = 2 - col_off
            part_re = padded[:, 0, row_from : row_from + out_rows, col_from : col_from + col_count]
            part_im = padded[:, 1, row_from : row_from + out_rows, col_from : col_from + col_count]
            weight_re = tap_re[:, tap_index][:, None, None]
            weight_im = tap_im[:, tap_index][:, None, None]
            acc_re = acc_re + weight_re * part_re + weight_im * part_im
            acc_im = acc_im + weight_re * part_im - weight_im * part_re
    return (acc_re, acc_im)


def phase_parts(freqs, slow_plane):
    angle = freqs[:, None, None] * layer_thickness * slow_plane[None]
    return (jnp.cos(angle), jnp.sin(angle))


def forward_steps(wavefield, freqs, taps, slowness, freq_total):
    tap_re = taps[:, 0]
    tap_im = taps[:, 1]
    step_count = slowness.shape[0]
    states = []
    current = wavefield
    for level in range(step_count):
        extended = extended_2(current, (("xy", 2),), 2)
        acc_re, acc_im = apply_stencil(extended, tap_re, tap_im)
        phase_re, phase_im = phase_parts(freqs, slowness[level])
        next_re = phase_re * acc_re - phase_im * acc_im
        next_im = phase_re * acc_im + phase_im * acc_re
        current = jnp.stack([next_re, next_im], axis=1)
        states.append(current)
    stacked = jnp.stack(states, axis=1)
    image_part = (
        jnp.sum(stacked[:, :, 0] * stacked[:, :, 0] + stacked[:, :, 1] * stacked[:, :, 1], axis=0)
        / freq_total
    )
    return (stacked, states[-1], image_part)


def backward_steps(adjoint, states, freqs, taps, slowness, perturbation, freq_total):
    tap_re = taps[:, 0]
    tap_im = taps[:, 1]
    step_count = slowness.shape[0]
    parts = [None] * step_count
    for level in reversed(range(step_count)):
        wave_re = states[:, level, 0]
        wave_im = states[:, level, 1]
        grad_re = adjoint[:, 0] + 2.0 * perturbation[level] * wave_re
        grad_im = adjoint[:, 1] + 2.0 * perturbation[level] * wave_im
        parts[level] = (
            layer_thickness
            / freq_total
            * jnp.sum(freqs[:, None, None] * (grad_im * wave_re - grad_re * wave_im), axis=0)
        )
        phase_re, phase_im = phase_parts(freqs, slowness[level])
        back_re = phase_re * grad_re + phase_im * grad_im
        back_im = phase_re * grad_im - phase_im * grad_re
        extended = extended_2(jnp.stack([back_re, back_im], axis=1), (("xy", 2),), 2)
        acc_re, acc_im = adjoint_stencil(extended, tap_re, tap_im)
        adjoint = jnp.stack([acc_re, acc_im], axis=1)
    return (adjoint, jnp.stack(parts, axis=0))


def on_device(surface_data, frequencies, coefficients, slowness, perturbation):
    freq_count = frequencies.shape[0]
    step_count = slowness.shape[0]
    row_count = slowness.shape[1]
    col_count = slowness.shape[2]
    layers = lax.axis_size("depth")
    depth_index = lax.axis_index("depth")
    stored_zero = jnp.zeros((freq_count, step_count, 2, row_count, col_count), jnp.float32)
    plane_zero = jnp.zeros((step_count, row_count, col_count), jnp.float32)
    start = jnp.where(depth_index == 0, surface_data, jnp.zeros_like(surface_data))

    def forward_segment(segment_no, carry):
        current, stored, image_sum = carry
        states, bottom, image_part = forward_steps(
            current, frequencies, coefficients, slowness, freq_count
        )
        chosen = depth_index == segment_no
        stored = jnp.where(chosen, states, stored)
        image_sum = jnp.where(chosen, image_part, image_sum)
        current = shifted(bottom, "depth", 1)
        return (current, stored, image_sum)

    unused_field, stored, image_field = lax.fori_loop(
        0, layers, forward_segment, (start, stored_zero, plane_zero)
    )

    def backward_segment(segment_no, carry):
        adjoint, gradient_sum = carry
        top_field, parts = backward_steps(
            adjoint, stored, frequencies, coefficients, slowness, perturbation, freq_count
        )
        gradient_sum = jnp.where(depth_index == layers - 1 - segment_no, parts, gradient_sum)
        adjoint = shifted(top_field, "depth", -1)
        return (adjoint, gradient_sum)

    adjoint_zero = jnp.zeros_like(surface_data)
    unused_adjoint, gradient = lax.fori_loop(
        0, layers, backward_segment, (adjoint_zero, plane_zero)
    )
    return (gradient, image_field)


ROWS = 16
HALO_TILES = 4
LANES = 128

OVERLAP = 8

sin_terms = (0.9999999995, -0.1666666515, 0.008333256964, -0.0001982776292, 2.657952479e-06)
cos_terms = (0.9999999947, -0.4999998344, 0.04166583045, -0.00138740917, 2.372928386e-05)


def window_row(tile, sub):
    group = tile - 2
    above = sub - 4 * (group + 1)
    below = sub + ROWS + 4 * group
    even = jnp.where(sub < 4, below, above - 4)
    odd = jnp.where(sub < 4, above, below - 4)
    halo = jnp.where(lax.rem(tile, 2) == 0, even, odd)
    return jnp.where(tile < 2, 8 * tile + sub, halo)


def band_kernel(plane_rows, taps, freqs, bands, back_bands, freq_tiles):
    first_row = lax.axis_index("xy") * ROWS

    def fill(ref, adjoint):
        out_tiles = ref.shape[1] // 48
        in_tiles = ref.shape[2] // 48
        shape = (16, ref.shape[2])
        col = lax.broadcasted_iota(jnp.int32, shape, 1)
        sub = lax.broadcasted_iota(jnp.int32, shape, 0)
        tile_k = sum((col >= 48 * t).astype(jnp.int32) for t in range(1, in_tiles))
        row_k = window_row(tile_k, col & 7)
        part_k = (col >> 4) - 3 * tile_k
        plane_k = (col >> 3) & 1
        plane_m = sub >> 3
        same = plane_k == plane_m
        inside_k = (row_k + first_row >= 0) & (row_k + first_row < plane_rows)
        for tile in range(out_tiles):
            row_m = window_row(jnp.full(shape, tile, jnp.int32), sub & 7)
            inside = inside_k & (row_m + first_row >= 0) & (row_m + first_row < plane_rows)
            offset = jnp.where(inside, row_k - row_m, 9)
            hits = [offset == a - 2 for a in range(5)]
            for f in range(ref.shape[0]):
                for b in range(3):
                    total = jnp.zeros(shape, jnp.float32)
                    for a in range(5):
                        tap = 3 * (4 - a) + 2 - b if adjoint else 3 * a + b
                        re = taps[f, 0, tap]
                        im = -taps[f, 1, tap] if adjoint else taps[f, 1, tap]
                        crossed = jnp.where(plane_m == 0, -im, im)
                        total = jnp.where(hits[a], jnp.where(same, re, crossed), total)
                    high = total.astype(jnp.bfloat16)
                    low = total - high.astype(jnp.float32)
                    base = 48 * tile + 16 * b
                    ref[f, base : base + 16] = jnp.where(part_k == 1, low, total).astype(jnp.bfloat16)

    fill(bands, False)
    fill(back_bands, True)
    for f in range(freq_tiles.shape[0]):
        freq_tiles[f] = jnp.full((8, LANES), freqs[f], jnp.float32)


def pack_rows(ref, values, side):
    lane = lax.broadcasted_iota(jnp.int32, (8, LANES), 1)
    overlaps = jnp.zeros((8, LANES), jnp.float32)
    blocks = (values[0].shape[1] - LANES) // LANES
    for n, value in enumerate(values):
        for block in range(blocks):
            ref[blocks * n + block] = value[:, (block + side) * LANES : (block + side + 1) * LANES]
        extra = value[:, : LANES] if side else value[:, blocks * LANES :]
        turn = (OVERLAP * (n + side)) % LANES
        extra = pltpu.roll(extra, turn, 1) if turn else extra
        overlaps = jnp.where((lane >= OVERLAP * n) & (lane < OVERLAP * (n + 1)), extra, overlaps)
    ref[blocks * len(values)] = overlaps


def unpack_rows(ref, tiles, n, side):
    blocks = (ref.shape[0] - 1) // tiles
    turn = (-OVERLAP * (n + side)) % LANES
    extra = ref[blocks * tiles]
    extra = pltpu.roll(extra, turn, 1) if turn else extra
    parts = [ref[blocks * n + block] for block in range(blocks)]
    return jnp.concatenate([extra] + parts if side else parts + [extra], axis=1)


def edge_levels(levels, slow, pert, down):
    inner, outer = (1, 0) if down else (0, 1)
    if levels == 1:
        return [slow(0, inner), pert(1, inner), pert(0, inner)]
    row = lax.broadcasted_iota(jnp.int32, slow(0, 0).shape, 0)
    turned = pltpu.roll(slow(1, outer), 4, 0)
    if down:
        extra = jnp.where(row < 2, pltpu.roll(pert(1, inner), 2, 0), turned)
        last = jnp.where(row < 4, extra, slow(0, outer))
    else:
        extra = jnp.where(row >= 6, pltpu.roll(pert(1, inner), 6, 0), turned)
        last = jnp.where(row < 4, slow(0, outer), extra)
    return [slow(0, inner), slow(1, inner), last]


def edge_surface(surf, down):
    inner, outer = (1, 0) if down else (0, 1)
    tiles = [surf(plane, inner) for plane in range(4)]
    row = lax.broadcasted_iota(jnp.int32, tiles[0].shape, 0)
    spread = surf(3, outer)
    for plane in range(3):
        turn = 6 - 2 * plane
        free = row < 2 if down else row >= 6
        tiles.append(jnp.where(free, pltpu.roll(spread, turn, 0), surf(plane, outer)))
    return tiles


def surface_edges(tiles, down):
    row = lax.broadcasted_iota(jnp.int32, tiles[0].shape, 0)
    outer = [tiles[4], tiles[5], tiles[6]]
    first = 2 if down else 0
    spread = pltpu.roll(tiles[6], 6, 0)
    spread = jnp.where((row >= first + 2) & (row < first + 4), pltpu.roll(tiles[5], 4, 0), spread)
    spread = jnp.where((row >= first) & (row < first + 2), pltpu.roll(tiles[4], 2, 0), spread)
    outer.append(spread)
    return [(tiles[plane], outer[plane]) for plane in range(4)]


def pack_kernel(width, step, surf_in, slow_in, pert_in, cross, bulk, cross_far, window, surf, slow, pert, sems):
    copies = [
        pltpu.make_async_copy(source, target, sems.at[n])
        for n, (source, target) in enumerate(((slow_in, slow), (pert_in, pert), (surf_in, surf)))
    ]
    for copy in copies:
        copy.start()
    for copy in copies:
        copy.wait()
    depth = lax.axis_index("depth")
    place = lax.axis_index("xy")
    for own in range(2):

        def reader(ref, side):
            lanes = slice(side * step, side * step + width)
            return lambda level, tile: ref[level, 8 * tile : 8 * tile + 8, lanes]

        def surface(plane, tile):
            return surf[plane // 2, plane % 2, 8 * tile : 8 * tile + 8, own * step : own * step + width]

        @pl.when(depth == own)
        def _():
            slow_near, pert_near = reader(slow, own), reader(pert, own)
            slow_far, pert_far = reader(slow, 1 - own), reader(pert, 1 - own)
            both = [(level, tile) for level in range(2) for tile in range(2)]
            for n, (level, tile) in enumerate(both):
                window[8 + n] = slow_near(level, tile)
                window[12 + n] = pert_near(level, tile)
            for plane in range(4):
                for tile in range(2):
                    window[2 * plane + tile] = surface(plane, tile)
            pack_rows(bulk, [slow_far(*at) for at in both] + [pert_far(*at) for at in both], 1 - own)
            for down in (False, True):

                @pl.when((lax.rem(place, 2) == 1) == down)
                def _():
                    edges = edge_surface(surface, down) + edge_levels(own, slow_near, pert_near, down)
                    pack_rows(cross, edges, own)
                    pack_rows(cross_far, edge_levels(own, slow_far, pert_far, down), 1 - own)


def relay_kernel(window, bulk, chip, partner):
    depth = lax.axis_index("depth")
    place = lax.axis_index("xy")
    for own in range(2):

        @pl.when(depth == own)
        def _():
            other = [unpack_rows(bulk, 8, n, own) for n in range(8)]
            for n in range(8):
                partner[n] = other[n]
            readers = {
                own: (lambda level, tile: window[8 + 2 * level + tile], lambda level, tile: window[12 + 2 * level + tile]),
                1 - own: (lambda level, tile: other[2 * level + tile], lambda level, tile: other[4 + 2 * level + tile]),
            }
            for down in (False, True):

                @pl.when((lax.rem(place, 2) == 0) == down)
                def _():
                    edges = edge_surface(lambda plane, tile: window[2 * plane + tile], down)
                    for levels in (own, 1 - own):
                        edges = edges + edge_levels(levels, *readers[levels], down)
                    pack_rows(chip, edges, own)


def phase(half):
    square = half * half
    cosine = cos_terms[-1]
    sine = sin_terms[-1]
    for term in cos_terms[-2::-1]:
        cosine = cosine * square + term
    for term in sin_terms[-2::-1]:
        sine = sine * square + term
    sine = sine * half
    twice = sine + sine
    return 1.0 - twice * sine, twice * cosine


def own_phases_kernel(freq_tiles, window, partner, phases):
    depth = lax.axis_index("depth")
    for level in range(4):
        for tile in range(2):
            own, other = window[8 + 2 * (level % 2) + tile], partner[2 * (level % 2) + tile]
            slow = jnp.where(depth == level // 2, own, other)
            for f in range(2):
                cosine, sine = phase(over_columns(freq_tiles[f], slow) * 0.25 * slow)
                phases[f, level, tile, :8] = cosine
                phases[f, level, tile, 8:] = sine


def over_columns(tile, like):
    return jnp.concatenate([tile] * (like.shape[1] // LANES), axis=1)


def sweep_kernel(
    width, freq_tiles, bands, back_bands, own_phases, window, partner, cross, cross_far, chip,
    gradient, image, theirs, slow_win, pert_win, operand, halo_phases, fields, image_win, grad_win,
):
    depth = lax.axis_index("depth")
    place = lax.axis_index("xy")
    half = width - LANES
    row = lax.broadcasted_iota(jnp.int32, (8, width), 0)
    upper = row < 4
    lane = lax.broadcasted_iota(jnp.int32, (16, LANES), 1)
    even = lax.rem(place, 2) == 0
    freqs = [jnp.concatenate([freq_tiles[f]] * (width // LANES), axis=1) for f in range(2)]

    def store_operand(f, tile, value):
        high = value.astype(jnp.bfloat16)
        low = (value - high.astype(jnp.float32)).astype(jnp.bfloat16)
        base = 48 * tile
        operand[f, base : base + 16] = high
        operand[f, base + 16 : base + 32] = high
        operand[f, base + 32 : base + 48] = low

    def multiply(f, matrix, out_tiles, in_tiles):
        inner_tiles = min(in_tiles, 5)
        product = jnp.dot(
            matrix[f, : 48 * out_tiles, : 48 * inner_tiles],
            operand[f, : 48 * inner_tiles],
            preferred_element_type=jnp.float32,
        )
        slabs = [product[16 * n : 16 * n + 16] for n in range(3 * out_tiles)]
        if in_tiles > inner_tiles:
            outer = jnp.dot(
                matrix[f, 48 * (out_tiles - 1) : 48 * out_tiles, 48 * inner_tiles : 48 * in_tiles],
                operand[f, 48 * inner_tiles : 48 * in_tiles],
                preferred_element_type=jnp.float32,
            )
            for n in range(3):
                slabs[3 * out_tiles - 3 + n] += outer[16 * n : 16 * n + 16]
        return slabs

    def combine(slabs):
        result = []
        for tile in range(len(slabs) // 3):
            before, same, after = slabs[3 * tile : 3 * tile + 3]
            left = pltpu.roll(before, 1, 1)
            right = pltpu.roll(after, width - 1, 1)
            left = jnp.concatenate([jnp.where(lane == 0, 0.0, left[:, :LANES]), left[:, LANES:]], axis=1)
            right = jnp.concatenate([right[:, :half], jnp.where(lane == LANES - 1, 0.0, right[:, half:])], axis=1)
            result.append(same + left + right)
        return result

    def fill(own, below_is_chip):
        chip_edges = [unpack_rows(chip, 13, n, own) for n in range(13)]
        cross_edges = [unpack_rows(cross, 10, n, own) for n in range(10)]
        cross_edges += [unpack_rows(cross_far, 3, n, own) for n in range(3)]
        above, below = (cross_edges, chip_edges) if below_is_chip else (chip_edges, cross_edges)
        for level in range(2):
            for tile in range(2):
                pert_win[2 * own + level, tile] = window[12 + 2 * level + tile]
                pert_win[2 * (1 - own) + level, tile] = partner[4 + 2 * level + tile]
        at = (7, 10) if own == 0 else (10, 7)
        up, down = above[at[0] : at[0] + 3], below[at[0] : at[0] + 3]
        for level in range(2):
            slow_win[level, 0] = jnp.where(upper, down[level], up[level])
            slow_win[level, 1] = jnp.where(upper, up[level], down[level])
        slow_win[0, 2] = jnp.where(upper, down[2], up[2])
        slow_win[1, 2] = pltpu.roll(jnp.where(upper, up[2], down[2]), 4, 0)
        pert_win[1, 2] = jnp.where(
            row < 2, pltpu.roll(down[2], 2, 0), jnp.where(row >= 6, pltpu.roll(up[2], 6, 0), 0.0)
        )
        up, down = above[at[1] : at[1] + 3], below[at[1] : at[1] + 3]
        slow_win[2, 0] = jnp.where(upper, down[0], up[0])
        slow_win[2, 1] = jnp.where(upper, up[0], down[0])
        pert_win[3, 2] = jnp.where(upper, down[1], up[1])
        pert_win[3, 3] = jnp.where(upper, up[1], down[1])
        pert_win[2, 2] = jnp.where(upper, down[2], up[2])
        up, down = surface_edges(above[:7], True), surface_edges(below[:7], False)
        planes = []
        for plane in range(4):
            up_inner, up_outer = up[plane]
            down_inner, down_outer = down[plane]
            planes.append(
                [
                    window[2 * plane],
                    window[2 * plane + 1],
                    jnp.where(upper, down_inner, up_inner),
                    jnp.where(upper, up_inner, down_inner),
                    jnp.where(upper, down_outer, up_outer),
                    jnp.where(upper, up_outer, down_outer),
                ]
            )
        for f in range(2):
            for tile in range(6):
                store_operand(f, tile, jnp.concatenate([planes[2 * f][tile], planes[2 * f + 1][tile]], axis=0))

    for own in range(2):
        for below_is_chip in (False, True):

            @pl.when((depth == own) & (even == below_is_chip))
            def _():
                fill(own, below_is_chip)

    def add_image(f, level, tile, re, im):
        part = (re * re + im * im) * 0.5
        image_win[level, tile] = part if f == 0 else image_win[level, tile] + part

    def add_gradient(f, level, tile, w_re, w_im, u_re, u_im):
        part = (0.25 * freqs[f]) * (w_im * u_re - w_re * u_im)
        grad_win[level, tile] = part if f == 0 else grad_win[level, tile] + part

    def phases_of(f, level, tile):
        if tile < 2:
            return own_phases[f, level, tile, :8], own_phases[f, level, tile, 8:]
        cosine, sine = phase(freqs[f] * 0.25 * slow_win[level, tile - 2])
        if tile == 2 and level > 0:
            halo_phases[f, level - 1, :8] = cosine
            halo_phases[f, level - 1, 8:] = sine
        return cosine, sine

    def step_forward(level):
        def finish(f, values):
            for tile, value in enumerate(values):
                cosine, sine = phases_of(f, level, tile)
                v_re, v_im = value[:8], value[8:]
                re = cosine * v_re - sine * v_im
                im = cosine * v_im + sine * v_re
                both = jnp.concatenate([re, im], axis=0)
                store_operand(f, tile, both)
                if tile < 3:
                    fields[f, level, tile] = both
                if tile < 2:
                    add_image(f, level, tile, re, im)

        return finish

    def turn(f, values):
        for tile, value in enumerate(values):
            twice = 2.0 * pert_win[3, tile]
            v_re, v_im = value[:8], value[8:]
            if tile < 2:
                cosine, sine = phases_of(f, 3, tile)
                re = cosine * v_re - sine * v_im
                im = cosine * v_im + sine * v_re
                add_image(f, 3, tile, re, im)
                add_gradient(f, 3, tile, twice * re, twice * im, re, im)
            store_operand(f, tile, jnp.concatenate([twice * v_re, twice * v_im], axis=0))

    def step_back(level):
        def finish(f, values):
            for tile, value in enumerate(values):
                twice = 2.0 * pert_win[level, tile]
                u_re, u_im = fields[f, level, tile, :8], fields[f, level, tile, 8:]
                w_re = value[:8] + twice * u_re
                w_im = value[8:] + twice * u_im
                if tile < 2:
                    add_gradient(f, level, tile, w_re, w_im, u_re, u_im)
                if level > 0:
                    if tile < 2:
                        cosine, sine = phases_of(f, level, tile)
                    else:
                        cosine, sine = halo_phases[f, level - 1, :8], halo_phases[f, level - 1, 8:]
                    back = [cosine * w_re + sine * w_im, cosine * w_im - sine * w_re]
                    store_operand(f, tile, jnp.concatenate(back, axis=0))

        return finish

    steps = [
        (bands, 5, 6, step_forward(0)),
        (bands, 5, 5, step_forward(1)),
        (bands, 4, 5, step_forward(2)),
        (bands, 4, 4, turn),
        (back_bands, 3, 4, step_back(2)),
        (back_bands, 3, 3, step_back(1)),
        (back_bands, 2, 3, step_back(0)),
    ]
    work = [(f,) + step for step in steps for f in range(2)]
    slabs = multiply(*work[0][:4])
    for n, (f, matrix, out_tiles, in_tiles, finish) in enumerate(work):
        following = multiply(*work[n + 1][:4]) if n + 1 < len(work) else None
        finish(f, combine(slabs))
        slabs = following

    for own in range(2):

        @pl.when(depth == own)
        def _():
            inner = slice(own * LANES, own * LANES + half)
            outer = slice(own * half, own * half + half)
            for level in range(2):
                for tile in range(2):
                    rows = slice(8 * tile, 8 * tile + 8)
                    gradient[level, rows, outer] = grad_win[2 * own + level, tile, :, inner]
                    image[level, rows, outer] = image_win[2 * own + level, tile, :, inner]
                    theirs[0, level, rows] = grad_win[2 * (1 - own) + level, tile, :, inner]
                    theirs[1, level, rows] = image_win[2 * (1 - own) + level, tile, :, inner]


def split_columns(surface_data, frequencies, coefficients, slowness, perturbation):
    count = lax.axis_size("xy")
    columns = slowness.shape[2]
    half = columns // 2
    width = half + LANES
    step = half - LANES
    f32 = jnp.float32
    axes = ("depth", "xy")

    def moved(value, other_depth, neighbour):
        pairs = []
        for depth in range(2):
            for place in range(count):
                target = {"chip": place ^ 1, "cross": place + 1 if place % 2 else place - 1, "same": place}[neighbour]
                if 0 <= target < count:
                    layer = 1 - depth if other_depth else depth
                    pairs.append((depth * count + place, layer * count + target))
        return lax.ppermute(value, axes, pairs)

    vmem = pl.BlockSpec(memory_space=pltpu.VMEM)
    smem = pl.BlockSpec(memory_space=pltpu.SMEM)
    tile = lambda n: jax.ShapeDtypeStruct((n, 8, width), f32)
    packed = lambda n: jax.ShapeDtypeStruct((n * half // LANES + 1, 8, LANES), f32)
    params = lambda mib: pltpu.CompilerParams(vmem_limit_bytes=mib * 2**20)
    cross, bulk, cross_far, window = pl.pallas_call(
        lambda *refs: pack_kernel(width, step, *refs),
        out_shape=(packed(10), packed(8), packed(3), tile(16)),
        in_specs=[pl.BlockSpec(memory_space=pltpu.HBM)] * 3,
        out_specs=(vmem,) * 4,
        scratch_shapes=[
            pltpu.VMEM(surface_data.shape, f32),
            pltpu.VMEM(slowness.shape, f32),
            pltpu.VMEM(perturbation.shape, f32),
            pltpu.SemaphoreType.DMA((3,)),
        ],
        compiler_params=params(32),
        name="pack",
    )(*(pltpu.with_memory_space_constraint(x, pltpu.HBM) for x in (surface_data, slowness, perturbation)))
    cross = moved(cross, False, "cross")
    bulk = moved(bulk, True, "same")
    cross_far = moved(cross_far, True, "cross")
    bands, back_bands, freq_tiles = pl.pallas_call(
        lambda *refs: band_kernel(count * ROWS, *refs),
        out_shape=(
            jax.ShapeDtypeStruct((2, 240, 288), jnp.bfloat16),
            jax.ShapeDtypeStruct((2, 144, 192), jnp.bfloat16),
            jax.ShapeDtypeStruct((2, 8, LANES), f32),
        ),
        in_specs=[smem] * 2,
        out_specs=(vmem,) * 3,
        compiler_params=params(16),
        cost_estimate=pl.CostEstimate(flops=10**10, bytes_accessed=10**6, transcendentals=0),
        name="bands",
    )(coefficients, frequencies)
    chip, partner = pl.pallas_call(
        relay_kernel,
        out_shape=(packed(13), tile(8)),
        in_specs=[vmem] * 2,
        out_specs=(vmem,) * 2,
        compiler_params=params(32),
        cost_estimate=pl.CostEstimate(flops=10**10, bytes_accessed=10**6, transcendentals=0),
        name="relay",
    )(window, bulk)
    chip = moved(chip, False, "chip")

    own_phases = pl.pallas_call(
        own_phases_kernel,
        out_shape=jax.ShapeDtypeStruct((2, 4, 2, 16, width), f32),
        in_specs=[vmem] * 3,
        out_specs=vmem,
        compiler_params=params(16),
        name="own_phases",
    )(freq_tiles, window, partner)

    own = jax.ShapeDtypeStruct((2, ROWS, columns), f32)
    gradient, image, theirs = pl.pallas_call(
        lambda *refs: sweep_kernel(width, *refs),
        out_shape=(own, own, jax.ShapeDtypeStruct((2, 2, ROWS, half), f32)),
        in_specs=[vmem] * 9,
        out_specs=(vmem,) * 3,
        scratch_shapes=[
            pltpu.VMEM((3, 3, 8, width), f32),
            pltpu.VMEM((4, 4, 8, width), f32),
            pltpu.VMEM((2, 288, width), jnp.bfloat16),
            pltpu.VMEM((2, 2, 16, width), f32),
            pltpu.VMEM((2, 3, 3, 16, width), f32),
            pltpu.VMEM((4, 2, 8, width), f32),
            pltpu.VMEM((4, 2, 8, width), f32),
        ],
        compiler_params=params(40),
        name="sweep",
    )(
        freq_tiles, bands, back_bands, own_phases, window, partner, cross, cross_far, chip,
    )
    theirs = moved(theirs, True, "same")
    start = (1 - lax.axis_index("depth")) * half
    gradient = lax.dynamic_update_slice(gradient, theirs[0], (0, 0, start))
    image = lax.dynamic_update_slice(image, theirs[1], (0, 0, start))
    return gradient, image


def on_slice(surface_data, frequencies, coefficients, slowness, perturbation):
    levels, rows, columns = slowness.shape
    fits = (
        lax.axis_size("depth") == 2
        and levels == 2
        and rows == ROWS
        and frequencies.shape[0] == 2
        and lax.axis_size("xy") % 2 == 0
        and columns % (2 * LANES) == 0
        and columns >= 4 * LANES
    )
    plan = split_columns if fits else on_device
    return plan(surface_data, frequencies, coefficients, slowness, perturbation)


def solution(mesh):
    in_specs = (P(None, None, "xy", None), P(), P(), P("depth", "xy", None), P("depth", "xy", None))
    out_specs = (P("depth", "xy", None), P("depth", "xy", None))
    return jax.shard_map(
        on_slice, mesh=mesh, in_specs=in_specs, out_specs=out_specs, check_vma=False
    )
```

```python
import numpy as np
import jax
import jax.numpy as jnp
from jax import lax
from jax.experimental import pallas as pl
from jax.experimental.pallas import tpu as pltpu
from jax.sharding import PartitionSpec as P

layer_thickness = 0.5


def extended_2(cells, sides, width):
    for axis, dim in sides:
        count = lax.axis_size(axis)
        ends = count - 1
        head = lax.slice_in_dim(cells, 0, width, axis=dim)
        tail = lax.slice_in_dim(cells, cells.shape[dim] - width, cells.shape[dim], axis=dim)
        cells = jnp.concatenate(
            [
                lax.ppermute(tail, axis, [(i, (i + 1) % count) for i in range(ends)]),
                cells,
                lax.ppermute(head, axis, [((i + 1) % count, i) for i in range(ends)]),
            ],
            axis=dim,
        )
    return cells


def shifted(value, axis, steps):
    count = lax.axis_size(axis)
    initial, last = (max(0, -steps), min(count, count - steps))
    return lax.ppermute(value, axis, [(source, source + steps) for source in range(initial, last)])


def apply_stencil(extended, tap_re, tap_im):
    out_rows = extended.shape[2] - 4
    col_count = extended.shape[3]
    padded = jnp.pad(extended, ((0, 0), (0, 0), (0, 0), (1, 1)))
    acc_re = jnp.zeros((extended.shape[0], out_rows, col_count), jnp.float32)
    acc_im = jnp.zeros((extended.shape[0], out_rows, col_count), jnp.float32)
    for row_off in range(5):
        for col_off in range(3):
            tap_index = row_off * 3 + col_off
            part_re = padded[:, 0, row_off : row_off + out_rows, col_off : col_off + col_count]
            part_im = padded[:, 1, row_off : row_off + out_rows, col_off : col_off + col_count]
            weight_re = tap_re[:, tap_index][:, None, None]
            weight_im = tap_im[:, tap_index][:, None, None]
            acc_re = acc_re + weight_re * part_re - weight_im * part_im
            acc_im = acc_im + weight_re * part_im + weight_im * part_re
    return (acc_re, acc_im)


def adjoint_stencil(extended, tap_re, tap_im):
    out_rows = extended.shape[2] - 4
    col_count = extended.shape[3]
    padded = jnp.pad(extended, ((0, 0), (0, 0), (0, 0), (1, 1)))
    acc_re = jnp.zeros((extended.shape[0], out_rows, col_count), jnp.float32)
    acc_im = jnp.zeros((extended.shape[0], out_rows, col_count), jnp.float32)
    for row_off in range(5):
        for col_off in range(3):
            tap_index = row_off * 3 + col_off
            row_from = 4 - row_off
            col_from = 2 - col_off
            part_re = padded[:, 0, row_from : row_from + out_rows, col_from : col_from + col_count]
            part_im = padded[:, 1, row_from : row_from + out_rows, col_from : col_from + col_count]
            weight_re = tap_re[:, tap_index][:, None, None]
            weight_im = tap_im[:, tap_index][:, None, None]
            acc_re = acc_re + weight_re * part_re + weight_im * part_im
            acc_im = acc_im + weight_re * part_im - weight_im * part_re
    return (acc_re, acc_im)


def phase_parts(freqs, slow_plane):
    angle = freqs[:, None, None] * layer_thickness * slow_plane[None]
    return (jnp.cos(angle), jnp.sin(angle))


def forward_steps(wavefield, freqs, taps, slowness, freq_total):
    tap_re = taps[:, 0]
    tap_im = taps[:, 1]
    step_count = slowness.shape[0]
    states = []
    current = wavefield
    for level in range(step_count):
        extended = extended_2(current, (("xy", 2),), 2)
        acc_re, acc_im = apply_stencil(extended, tap_re, tap_im)
        phase_re, phase_im = phase_parts(freqs, slowness[level])
        next_re = phase_re * acc_re - phase_im * acc_im
        next_im = phase_re * acc_im + phase_im * acc_re
        current = jnp.stack([next_re, next_im], axis=1)
        states.append(current)
    stacked = jnp.stack(states, axis=1)
    image_part = (
        jnp.sum(stacked[:, :, 0] * stacked[:, :, 0] + stacked[:, :, 1] * stacked[:, :, 1], axis=0)
        / freq_total
    )
    return (stacked, states[-1], image_part)


def backward_steps(adjoint, states, freqs, taps, slowness, perturbation, freq_total):
    tap_re = taps[:, 0]
    tap_im = taps[:, 1]
    step_count = slowness.shape[0]
    parts = [None] * step_count
    for level in reversed(range(step_count)):
        wave_re = states[:, level, 0]
        wave_im = states[:, level, 1]
        grad_re = adjoint[:, 0] + 2.0 * perturbation[level] * wave_re
        grad_im = adjoint[:, 1] + 2.0 * perturbation[level] * wave_im
        parts[level] = (
            layer_thickness
            / freq_total
            * jnp.sum(freqs[:, None, None] * (grad_im * wave_re - grad_re * wave_im), axis=0)
        )
        phase_re, phase_im = phase_parts(freqs, slowness[level])
        back_re = phase_re * grad_re + phase_im * grad_im
        back_im = phase_re * grad_im - phase_im * grad_re
        extended = extended_2(jnp.stack([back_re, back_im], axis=1), (("xy", 2),), 2)
        acc_re, acc_im = adjoint_stencil(extended, tap_re, tap_im)
        adjoint = jnp.stack([acc_re, acc_im], axis=1)
    return (adjoint, jnp.stack(parts, axis=0))


def on_device(surface_data, frequencies, coefficients, slowness, perturbation):
    freq_count = frequencies.shape[0]
    step_count = slowness.shape[0]
    row_count = slowness.shape[1]
    col_count = slowness.shape[2]
    layers = lax.axis_size("depth")
    depth_index = lax.axis_index("depth")
    stored_zero = jnp.zeros((freq_count, step_count, 2, row_count, col_count), jnp.float32)
    plane_zero = jnp.zeros((step_count, row_count, col_count), jnp.float32)
    start = jnp.where(depth_index == 0, surface_data, jnp.zeros_like(surface_data))

    def forward_segment(segment_no, carry):
        current, stored, image_sum = carry
        states, bottom, image_part = forward_steps(
            current, frequencies, coefficients, slowness, freq_count
        )
        chosen = depth_index == segment_no
        stored = jnp.where(chosen, states, stored)
        image_sum = jnp.where(chosen, image_part, image_sum)
        current = shifted(bottom, "depth", 1)
        return (current, stored, image_sum)

    unused_field, stored, image_field = lax.fori_loop(
        0, layers, forward_segment, (start, stored_zero, plane_zero)
    )

    def backward_segment(segment_no, carry):
        adjoint, gradient_sum = carry
        top_field, parts = backward_steps(
            adjoint, stored, frequencies, coefficients, slowness, perturbation, freq_count
        )
        gradient_sum = jnp.where(depth_index == layers - 1 - segment_no, parts, gradient_sum)
        adjoint = shifted(top_field, "depth", -1)
        return (adjoint, gradient_sum)

    adjoint_zero = jnp.zeros_like(surface_data)
    unused_adjoint, gradient = lax.fori_loop(
        0, layers, backward_segment, (adjoint_zero, plane_zero)
    )
    return (gradient, image_field)


ROWS = 16
HALO_TILES = 4
LANES = 128

OVERLAP = 8

sin_terms = (0.9999999995, -0.1666666515, 0.008333256964, -0.0001982776292, 2.657952479e-06)
cos_terms = (0.9999999947, -0.4999998344, 0.04166583045, -0.00138740917, 2.372928386e-05)


def window_row(tile, sub):
    group = tile - 2
    above = sub - 4 * (group + 1)
    below = sub + ROWS + 4 * group
    even = jnp.where(sub < 4, below, above - 4)
    odd = jnp.where(sub < 4, above, below - 4)
    halo = jnp.where(lax.rem(tile, 2) == 0, even, odd)
    return jnp.where(tile < 2, 8 * tile + sub, halo)


def band_kernel(plane_rows, taps, freqs, bands, back_bands, freq_tiles):
    first_row = lax.axis_index("xy") * ROWS

    def fill(ref, adjoint):
        out_tiles = ref.shape[1] // 48
        in_tiles = ref.shape[2] // 48
        shape = (16, ref.shape[2])
        col = lax.broadcasted_iota(jnp.int32, shape, 1)
        sub = lax.broadcasted_iota(jnp.int32, shape, 0)
        tile_k = sum((col >= 48 * t).astype(jnp.int32) for t in range(1, in_tiles))
        row_k = window_row(tile_k, col & 7)
        part_k = (col >> 4) - 3 * tile_k
        plane_k = (col >> 3) & 1
        plane_m = sub >> 3
        same = plane_k == plane_m
        inside_k = (row_k + first_row >= 0) & (row_k + first_row < plane_rows)
        for tile in range(out_tiles):
            row_m = window_row(jnp.full(shape, tile, jnp.int32), sub & 7)
            inside = inside_k & (row_m + first_row >= 0) & (row_m + first_row < plane_rows)
            offset = jnp.where(inside, row_k - row_m, 9)
            hits = [offset == a - 2 for a in range(5)]
            for f in range(ref.shape[0]):
                for b in range(3):
                    total = jnp.zeros(shape, jnp.float32)
                    for a in range(5):
                        tap = 3 * (4 - a) + 2 - b if adjoint else 3 * a + b
                        re = taps[f, 0, tap]
                        im = -taps[f, 1, tap] if adjoint else taps[f, 1, tap]
                        crossed = jnp.where(plane_m == 0, -im, im)
                        total = jnp.where(hits[a], jnp.where(same, re, crossed), total)
                    high = total.astype(jnp.bfloat16)
                    low = total - high.astype(jnp.float32)
                    base = 48 * tile + 16 * b
                    ref[f, base : base + 16] = jnp.where(part_k == 1, low, total).astype(jnp.bfloat16)

    fill(bands, False)
    fill(back_bands, True)
    for f in range(freq_tiles.shape[0]):
        freq_tiles[f] = jnp.full((8, LANES), freqs[f], jnp.float32)


def pack_rows(ref, values, side):
    lane = lax.broadcasted_iota(jnp.int32, (8, LANES), 1)
    overlaps = jnp.zeros((8, LANES), jnp.float32)
    blocks = (values[0].shape[1] - LANES) // LANES
    for n, value in enumerate(values):
        for block in range(blocks):
            ref[blocks * n + block] = value[:, (block + side) * LANES : (block + side + 1) * LANES]
        extra = value[:, : LANES] if side else value[:, blocks * LANES :]
        turn = (OVERLAP * (n + side)) % LANES
        extra = pltpu.roll(extra, turn, 1) if turn else extra
        overlaps = jnp.where((lane >= OVERLAP * n) & (lane < OVERLAP * (n + 1)), extra, overlaps)
    ref[blocks * len(values)] = overlaps


def unpack_rows(ref, tiles, n, side):
    blocks = (ref.shape[0] - 1) // tiles
    turn = (-OVERLAP * (n + side)) % LANES
    extra = ref[blocks * tiles]
    extra = pltpu.roll(extra, turn, 1) if turn else extra
    parts = [ref[blocks * n + block] for block in range(blocks)]
    return jnp.concatenate([extra] + parts if side else parts + [extra], axis=1)


def edge_levels(levels, slow, pert, down):
    inner, outer = (1, 0) if down else (0, 1)
    if levels == 1:
        return [slow(0, inner), pert(1, inner), pert(0, inner)]
    row = lax.broadcasted_iota(jnp.int32, slow(0, 0).shape, 0)
    turned = pltpu.roll(slow(1, outer), 4, 0)
    if down:
        extra = jnp.where(row < 2, pltpu.roll(pert(1, inner), 2, 0), turned)
        last = jnp.where(row < 4, extra, slow(0, outer))
    else:
        extra = jnp.where(row >= 6, pltpu.roll(pert(1, inner), 6, 0), turned)
        last = jnp.where(row < 4, slow(0, outer), extra)
    return [slow(0, inner), slow(1, inner), last]


def edge_surface(surf, down):
    inner, outer = (1, 0) if down else (0, 1)
    tiles = [surf(plane, inner) for plane in range(4)]
    row = lax.broadcasted_iota(jnp.int32, tiles[0].shape, 0)
    spread = surf(3, outer)
    for plane in range(3):
        turn = 6 - 2 * plane
        free = row < 2 if down else row >= 6
        tiles.append(jnp.where(free, pltpu.roll(spread, turn, 0), surf(plane, outer)))
    return tiles


def surface_edges(tiles, down):
    row = lax.broadcasted_iota(jnp.int32, tiles[0].shape, 0)
    outer = [tiles[4], tiles[5], tiles[6]]
    first = 2 if down else 0
    spread = pltpu.roll(tiles[6], 6, 0)
    spread = jnp.where((row >= first + 2) & (row < first + 4), pltpu.roll(tiles[5], 4, 0), spread)
    spread = jnp.where((row >= first) & (row < first + 2), pltpu.roll(tiles[4], 2, 0), spread)
    outer.append(spread)
    return [(tiles[plane], outer[plane]) for plane in range(4)]


def pack_kernel(width, step, surf_in, slow_in, pert_in, cross, bulk, cross_far, window, surf, slow, pert, sems):
    copies = [
        pltpu.make_async_copy(source, target, sems.at[n])
        for n, (source, target) in enumerate(((slow_in, slow), (pert_in, pert), (surf_in, surf)))
    ]
    for copy in copies:
        copy.start()
    for copy in copies:
        copy.wait()
    depth = lax.axis_index("depth")
    place = lax.axis_index("xy")
    for own in range(2):

        def reader(ref, side):
            lanes = slice(side * step, side * step + width)
            return lambda level, tile: ref[level, 8 * tile : 8 * tile + 8, lanes]

        def surface_reader(side):
            lanes = slice(side * step, side * step + width)
            return lambda plane, tile: surf[plane // 2, plane % 2, 8 * tile : 8 * tile + 8, lanes]

        @pl.when(depth == own)
        def _():
            surface, surface_far = surface_reader(own), surface_reader(1 - own)
            slow_near, pert_near = reader(slow, own), reader(pert, own)
            slow_far, pert_far = reader(slow, 1 - own), reader(pert, 1 - own)
            both = [(level, tile) for level in range(2) for tile in range(2)]
            for n, (level, tile) in enumerate(both):
                window[8 + n] = slow_near(level, tile)
                window[12 + n] = pert_near(level, tile)
            for plane in range(4):
                for tile in range(2):
                    window[2 * plane + tile] = surface(plane, tile)
            pack_rows(bulk, [slow_far(*at) for at in both] + [pert_far(*at) for at in both], 1 - own)
            for down in (False, True):

                @pl.when((lax.rem(place, 2) == 1) == down)
                def _():
                    edges = edge_surface(surface, down)[:4] + edge_levels(own, slow_near, pert_near, down)
                    pack_rows(cross, edges, own)
                    edges = edge_surface(surface_far, down)[4:] + edge_levels(own, slow_far, pert_far, down)
                    pack_rows(cross_far, edges, 1 - own)


def relay_kernel(window, bulk, chip, partner):
    depth = lax.axis_index("depth")
    place = lax.axis_index("xy")
    for own in range(2):

        @pl.when(depth == own)
        def _():
            other = [unpack_rows(bulk, 8, n, own) for n in range(8)]
            for n in range(8):
                partner[n] = other[n]
            readers = {
                own: (lambda level, tile: window[8 + 2 * level + tile], lambda level, tile: window[12 + 2 * level + tile]),
                1 - own: (lambda level, tile: other[2 * level + tile], lambda level, tile: other[4 + 2 * level + tile]),
            }
            for down in (False, True):

                @pl.when((lax.rem(place, 2) == 0) == down)
                def _():
                    edges = edge_surface(lambda plane, tile: window[2 * plane + tile], down)
                    for levels in (own, 1 - own):
                        edges = edges + edge_levels(levels, *readers[levels], down)
                    pack_rows(chip, edges, own)


def phase(half):
    square = half * half
    cosine = cos_terms[-1]
    sine = sin_terms[-1]
    for term in cos_terms[-2::-1]:
        cosine = cosine * square + term
    for term in sin_terms[-2::-1]:
        sine = sine * square + term
    sine = sine * half
    twice = sine + sine
    return 1.0 - twice * sine, twice * cosine


def own_phases_kernel(freq_tiles, window, partner, phases):
    depth = lax.axis_index("depth")
    for level in range(4):
        for tile in range(2):
            own, other = window[8 + 2 * (level % 2) + tile], partner[2 * (level % 2) + tile]
            slow = jnp.where(depth == level // 2, own, other)
            for f in range(2):
                cosine, sine = phase(over_columns(freq_tiles[f], slow) * 0.25 * slow)
                phases[f, level, tile, :8] = cosine
                phases[f, level, tile, 8:] = sine


def over_columns(tile, like):
    return jnp.concatenate([tile] * (like.shape[1] // LANES), axis=1)


def sweep_kernel(
    width, freq_tiles, bands, back_bands, own_phases, window, partner, cross, cross_far, chip,
    mine, theirs, slow_win, pert_win, operand, halo_phases, fields, image_win, grad_win,
):
    depth = lax.axis_index("depth")
    place = lax.axis_index("xy")
    half = width - LANES
    row = lax.broadcasted_iota(jnp.int32, (8, width), 0)
    upper = row < 4
    lane = lax.broadcasted_iota(jnp.int32, (16, LANES), 1)
    even = lax.rem(place, 2) == 0
    freqs = [jnp.concatenate([freq_tiles[f]] * (width // LANES), axis=1) for f in range(2)]

    def store_operand(f, tile, value):
        high = value.astype(jnp.bfloat16)
        low = (value - high.astype(jnp.float32)).astype(jnp.bfloat16)
        base = 48 * tile
        operand[f, base : base + 16] = high
        operand[f, base + 16 : base + 32] = high
        operand[f, base + 32 : base + 48] = low

    def multiply(f, matrix, out_tiles, in_tiles):
        inner_tiles = min(in_tiles, 5)
        product = jnp.dot(
            matrix[f, : 48 * out_tiles, : 48 * inner_tiles],
            operand[f, : 48 * inner_tiles],
            preferred_element_type=jnp.float32,
        )
        slabs = [product[16 * n : 16 * n + 16] for n in range(3 * out_tiles)]
        if in_tiles > inner_tiles:
            outer = jnp.dot(
                matrix[f, 48 * (out_tiles - 1) : 48 * out_tiles, 48 * inner_tiles : 48 * in_tiles],
                operand[f, 48 * inner_tiles : 48 * in_tiles],
                preferred_element_type=jnp.float32,
            )
            for n in range(3):
                slabs[3 * out_tiles - 3 + n] += outer[16 * n : 16 * n + 16]
        return slabs

    def combine(slabs):
        result = []
        for tile in range(len(slabs) // 3):
            before, same, after = slabs[3 * tile : 3 * tile + 3]
            left = pltpu.roll(before, 1, 1)
            right = pltpu.roll(after, width - 1, 1)
            left = jnp.concatenate([jnp.where(lane == 0, 0.0, left[:, :LANES]), left[:, LANES:]], axis=1)
            right = jnp.concatenate([right[:, :half], jnp.where(lane == LANES - 1, 0.0, right[:, half:])], axis=1)
            result.append(same + left + right)
        return result

    def fill(own, below_is_chip):
        chip_edges = [unpack_rows(chip, 13, n, own) for n in range(13)]
        same = [unpack_rows(cross, 7, n, own) for n in range(7)]
        other = [unpack_rows(cross_far, 6, n, own) for n in range(6)]
        cross_edges = same[:4] + other[:3] + same[4:] + other[3:]
        above, below = (cross_edges, chip_edges) if below_is_chip else (chip_edges, cross_edges)
        for level in range(2):
            for tile in range(2):
                pert_win[2 * own + level, tile] = window[12 + 2 * level + tile]
                pert_win[2 * (1 - own) + level, tile] = partner[4 + 2 * level + tile]
        at = (7, 10) if own == 0 else (10, 7)
        up, down = above[at[0] : at[0] + 3], below[at[0] : at[0] + 3]
        for level in range(2):
            slow_win[level, 0] = jnp.where(upper, down[level], up[level])
            slow_win[level, 1] = jnp.where(upper, up[level], down[level])
        slow_win[0, 2] = jnp.where(upper, down[2], up[2])
        slow_win[1, 2] = pltpu.roll(jnp.where(upper, up[2], down[2]), 4, 0)
        pert_win[1, 2] = jnp.where(
            row < 2, pltpu.roll(down[2], 2, 0), jnp.where(row >= 6, pltpu.roll(up[2], 6, 0), 0.0)
        )
        up, down = above[at[1] : at[1] + 3], below[at[1] : at[1] + 3]
        slow_win[2, 0] = jnp.where(upper, down[0], up[0])
        slow_win[2, 1] = jnp.where(upper, up[0], down[0])
        pert_win[3, 2] = jnp.where(upper, down[1], up[1])
        pert_win[3, 3] = jnp.where(upper, up[1], down[1])
        pert_win[2, 2] = jnp.where(upper, down[2], up[2])
        up, down = surface_edges(above[:7], True), surface_edges(below[:7], False)
        planes = []
        for plane in range(4):
            up_inner, up_outer = up[plane]
            down_inner, down_outer = down[plane]
            planes.append(
                [
                    window[2 * plane],
                    window[2 * plane + 1],
                    jnp.where(upper, down_inner, up_inner),
                    jnp.where(upper, up_inner, down_inner),
                    jnp.where(upper, down_outer, up_outer),
                    jnp.where(upper, up_outer, down_outer),
                ]
            )
        for f in range(2):
            for tile in range(6):
                store_operand(f, tile, jnp.concatenate([planes[2 * f][tile], planes[2 * f + 1][tile]], axis=0))

    for own in range(2):
        for below_is_chip in (False, True):

            @pl.when((depth == own) & (even == below_is_chip))
            def _():
                fill(own, below_is_chip)

    def add_image(f, level, tile, re, im):
        part = (re * re + im * im) * 0.5
        image_win[level, tile] = part if f == 0 else image_win[level, tile] + part

    def add_gradient(f, level, tile, w_re, w_im, u_re, u_im):
        part = (0.25 * freqs[f]) * (w_im * u_re - w_re * u_im)
        grad_win[level, tile] = part if f == 0 else grad_win[level, tile] + part

    def phases_of(f, level, tile):
        if tile < 2:
            return own_phases[f, level, tile, :8], own_phases[f, level, tile, 8:]
        cosine, sine = phase(freqs[f] * 0.25 * slow_win[level, tile - 2])
        if tile == 2 and level > 0:
            halo_phases[f, level - 1, :8] = cosine
            halo_phases[f, level - 1, 8:] = sine
        return cosine, sine

    def step_forward(level):
        def finish(f, values):
            for tile, value in enumerate(values):
                cosine, sine = phases_of(f, level, tile)
                v_re, v_im = value[:8], value[8:]
                re = cosine * v_re - sine * v_im
                im = cosine * v_im + sine * v_re
                both = jnp.concatenate([re, im], axis=0)
                store_operand(f, tile, both)
                if tile < 3:
                    fields[f, level, tile] = both
                if tile < 2:
                    add_image(f, level, tile, re, im)

        return finish

    def turn(f, values):
        for tile, value in enumerate(values):
            twice = 2.0 * pert_win[3, tile]
            v_re, v_im = value[:8], value[8:]
            if tile < 2:
                cosine, sine = phases_of(f, 3, tile)
                re = cosine * v_re - sine * v_im
                im = cosine * v_im + sine * v_re
                add_image(f, 3, tile, re, im)
                add_gradient(f, 3, tile, twice * re, twice * im, re, im)
            store_operand(f, tile, jnp.concatenate([twice * v_re, twice * v_im], axis=0))

    def step_back(level):
        def finish(f, values):
            for tile, value in enumerate(values):
                twice = 2.0 * pert_win[level, tile]
                u_re, u_im = fields[f, level, tile, :8], fields[f, level, tile, 8:]
                w_re = value[:8] + twice * u_re
                w_im = value[8:] + twice * u_im
                if tile < 2:
                    add_gradient(f, level, tile, w_re, w_im, u_re, u_im)
                if level > 0:
                    if tile < 2:
                        cosine, sine = phases_of(f, level, tile)
                    else:
                        cosine, sine = halo_phases[f, level - 1, :8], halo_phases[f, level - 1, 8:]
                    back = [cosine * w_re + sine * w_im, cosine * w_im - sine * w_re]
                    store_operand(f, tile, jnp.concatenate(back, axis=0))

        return finish

    steps = [
        (bands, 5, 6, step_forward(0)),
        (bands, 5, 5, step_forward(1)),
        (bands, 4, 5, step_forward(2)),
        (bands, 4, 4, turn),
        (back_bands, 3, 4, step_back(2)),
        (back_bands, 3, 3, step_back(1)),
        (back_bands, 2, 3, step_back(0)),
    ]
    work = [(f,) + step for step in steps for f in range(2)]
    slabs = multiply(*work[0][:4])
    for n, (f, matrix, out_tiles, in_tiles, finish) in enumerate(work):
        following = multiply(*work[n + 1][:4]) if n + 1 < len(work) else None
        finish(f, combine(slabs))
        slabs = following

    for own in range(2):

        @pl.when(depth == own)
        def _():
            inner = slice(own * LANES, own * LANES + half)
            for level in range(2):
                for tile in range(2):
                    rows = slice(8 * tile, 8 * tile + 8)
                    mine[0, level, rows] = grad_win[2 * own + level, tile, :, inner]
                    mine[1, level, rows] = image_win[2 * own + level, tile, :, inner]
                    theirs[0, level, rows] = grad_win[2 * (1 - own) + level, tile, :, inner]
                    theirs[1, level, rows] = image_win[2 * (1 - own) + level, tile, :, inner]


def place_kernel(mine, received, gradient, image, sems):
    half = mine.shape[3]
    depth = lax.axis_index("depth")
    copies = []
    for n, whole in enumerate((gradient, image)):
        for m, (part, side) in enumerate(((mine, depth), (received, 1 - depth))):
            lanes = pl.ds(pl.multiple_of(side * half, LANES), half)
            copies.append(pltpu.make_async_copy(part.at[n], whole.at[:, :, lanes], sems.at[2 * n + m]))
    for copy in copies:
        copy.start()
    for copy in copies:
        copy.wait()


def split_columns(surface_data, frequencies, coefficients, slowness, perturbation):
    count = lax.axis_size("xy")
    columns = slowness.shape[2]
    half = columns // 2
    width = half + LANES
    step = half - LANES
    f32 = jnp.float32
    axes = ("depth", "xy")

    def moved(value, other_depth, neighbour):
        pairs = []
        for depth in range(2):
            for place in range(count):
                target = {"chip": place ^ 1, "cross": place + 1 if place % 2 else place - 1, "same": place}[neighbour]
                if 0 <= target < count:
                    layer = 1 - depth if other_depth else depth
                    pairs.append((depth * count + place, layer * count + target))
        return lax.ppermute(value, axes, pairs)

    vmem = pl.BlockSpec(memory_space=pltpu.VMEM)
    smem = pl.BlockSpec(memory_space=pltpu.SMEM)
    tile = lambda n: jax.ShapeDtypeStruct((n, 8, width), f32)
    packed = lambda n: jax.ShapeDtypeStruct((n * half // LANES + 1, 8, LANES), f32)
    params = lambda mib: pltpu.CompilerParams(vmem_limit_bytes=mib * 2**20)
    cross, bulk, cross_far, window = pl.pallas_call(
        lambda *refs: pack_kernel(width, step, *refs),
        out_shape=(packed(7), packed(8), packed(6), tile(16)),
        in_specs=[pl.BlockSpec(memory_space=pltpu.HBM)] * 3,
        out_specs=(vmem,) * 4,
        scratch_shapes=[
            pltpu.VMEM(surface_data.shape, f32),
            pltpu.VMEM(slowness.shape, f32),
            pltpu.VMEM(perturbation.shape, f32),
            pltpu.SemaphoreType.DMA((3,)),
        ],
        compiler_params=params(32),
        name="pack",
    )(*(pltpu.with_memory_space_constraint(x, pltpu.HBM) for x in (surface_data, slowness, perturbation)))
    cross = moved(cross, False, "cross")
    bulk = moved(bulk, True, "same")
    cross_far = moved(cross_far, True, "cross")
    bands, back_bands, freq_tiles = pl.pallas_call(
        lambda *refs: band_kernel(count * ROWS, *refs),
        out_shape=(
            jax.ShapeDtypeStruct((2, 240, 288), jnp.bfloat16),
            jax.ShapeDtypeStruct((2, 144, 192), jnp.bfloat16),
            jax.ShapeDtypeStruct((2, 8, LANES), f32),
        ),
        in_specs=[smem] * 2,
        out_specs=(vmem,) * 3,
        compiler_params=params(16),
        cost_estimate=pl.CostEstimate(flops=10**10, bytes_accessed=10**6, transcendentals=0),
        name="bands",
    )(coefficients, frequencies)
    chip, partner = pl.pallas_call(
        relay_kernel,
        out_shape=(packed(13), tile(8)),
        in_specs=[vmem] * 2,
        out_specs=(vmem,) * 2,
        compiler_params=params(32),
        cost_estimate=pl.CostEstimate(flops=10**10, bytes_accessed=10**6, transcendentals=0),
        name="relay",
    )(window, bulk)
    chip = moved(chip, False, "chip")

    own_phases = pl.pallas_call(
        own_phases_kernel,
        out_shape=jax.ShapeDtypeStruct((2, 4, 2, 16, width), f32),
        in_specs=[vmem] * 3,
        out_specs=vmem,
        compiler_params=params(16),
        name="own_phases",
    )(freq_tiles, window, partner)

    own = jax.ShapeDtypeStruct((2, ROWS, columns), f32)
    mine, theirs = pl.pallas_call(
        lambda *refs: sweep_kernel(width, *refs),
        out_shape=(jax.ShapeDtypeStruct((2, 2, ROWS, half), f32),) * 2,
        in_specs=[vmem] * 9,
        out_specs=(vmem,) * 2,
        scratch_shapes=[
            pltpu.VMEM((3, 3, 8, width), f32),
            pltpu.VMEM((4, 4, 8, width), f32),
            pltpu.VMEM((2, 288, width), jnp.bfloat16),
            pltpu.VMEM((2, 2, 16, width), f32),
            pltpu.VMEM((2, 3, 3, 16, width), f32),
            pltpu.VMEM((4, 2, 8, width), f32),
            pltpu.VMEM((4, 2, 8, width), f32),
        ],
        compiler_params=params(40),
        name="sweep",
    )(
        freq_tiles, bands, back_bands, own_phases, window, partner, cross, cross_far, chip,
    )
    received = moved(theirs, True, "same")
    hbm = pl.BlockSpec(memory_space=pltpu.HBM)
    return pl.pallas_call(
        place_kernel,
        out_shape=(own, own),
        in_specs=[vmem] * 2,
        out_specs=(hbm,) * 2,
        scratch_shapes=[pltpu.SemaphoreType.DMA((4,))],
        compiler_params=params(8),
        name="place",
    )(mine, received)


def on_slice(surface_data, frequencies, coefficients, slowness, perturbation):
    levels, rows, columns = slowness.shape
    fits = (
        lax.axis_size("depth") == 2
        and levels == 2
        and rows == ROWS
        and frequencies.shape[0] == 2
        and lax.axis_size("xy") % 2 == 0
        and columns % (2 * LANES) == 0
        and columns >= 4 * LANES
    )
    plan = split_columns if fits else on_device
    return plan(surface_data, frequencies, coefficients, slowness, perturbation)


def solution(mesh):
    in_specs = (P(None, None, "xy", None), P(), P(), P("depth", "xy", None), P("depth", "xy", None))
    out_specs = (P("depth", "xy", None), P("depth", "xy", None))
    return jax.shard_map(
        on_slice, mesh=mesh, in_specs=in_specs, out_specs=out_specs, check_vma=False
    )
```

```python
import numpy as np
import jax
import jax.numpy as jnp
from jax import lax
from jax.experimental import pallas as pl
from jax.experimental.pallas import tpu as pltpu
from jax.sharding import PartitionSpec as P

layer_thickness = 0.5


def extended_2(cells, sides, width):
    for axis, dim in sides:
        count = lax.axis_size(axis)
        ends = count - 1
        head = lax.slice_in_dim(cells, 0, width, axis=dim)
        tail = lax.slice_in_dim(cells, cells.shape[dim] - width, cells.shape[dim], axis=dim)
        cells = jnp.concatenate(
            [
                lax.ppermute(tail, axis, [(i, (i + 1) % count) for i in range(ends)]),
                cells,
                lax.ppermute(head, axis, [((i + 1) % count, i) for i in range(ends)]),
            ],
            axis=dim,
        )
    return cells


def shifted(value, axis, steps):
    count = lax.axis_size(axis)
    initial, last = (max(0, -steps), min(count, count - steps))
    return lax.ppermute(value, axis, [(source, source + steps) for source in range(initial, last)])


def apply_stencil(extended, tap_re, tap_im):
    out_rows = extended.shape[2] - 4
    col_count = extended.shape[3]
    padded = jnp.pad(extended, ((0, 0), (0, 0), (0, 0), (1, 1)))
    acc_re = jnp.zeros((extended.shape[0], out_rows, col_count), jnp.float32)
    acc_im = jnp.zeros((extended.shape[0], out_rows, col_count), jnp.float32)
    for row_off in range(5):
        for col_off in range(3):
            tap_index = row_off * 3 + col_off
            part_re = padded[:, 0, row_off : row_off + out_rows, col_off : col_off + col_count]
            part_im = padded[:, 1, row_off : row_off + out_rows, col_off : col_off + col_count]
            weight_re = tap_re[:, tap_index][:, None, None]
            weight_im = tap_im[:, tap_index][:, None, None]
            acc_re = acc_re + weight_re * part_re - weight_im * part_im
            acc_im = acc_im + weight_re * part_im + weight_im * part_re
    return (acc_re, acc_im)


def adjoint_stencil(extended, tap_re, tap_im):
    out_rows = extended.shape[2] - 4
    col_count = extended.shape[3]
    padded = jnp.pad(extended, ((0, 0), (0, 0), (0, 0), (1, 1)))
    acc_re = jnp.zeros((extended.shape[0], out_rows, col_count), jnp.float32)
    acc_im = jnp.zeros((extended.shape[0], out_rows, col_count), jnp.float32)
    for row_off in range(5):
        for col_off in range(3):
            tap_index = row_off * 3 + col_off
            row_from = 4 - row_off
            col_from = 2 - col_off
            part_re = padded[:, 0, row_from : row_from + out_rows, col_from : col_from + col_count]
            part_im = padded[:, 1, row_from : row_from + out_rows, col_from : col_from + col_count]
            weight_re = tap_re[:, tap_index][:, None, None]
            weight_im = tap_im[:, tap_index][:, None, None]
            acc_re = acc_re + weight_re * part_re + weight_im * part_im
            acc_im = acc_im + weight_re * part_im - weight_im * part_re
    return (acc_re, acc_im)


def phase_parts(freqs, slow_plane):
    angle = freqs[:, None, None] * layer_thickness * slow_plane[None]
    return (jnp.cos(angle), jnp.sin(angle))


def forward_steps(wavefield, freqs, taps, slowness, freq_total):
    tap_re = taps[:, 0]
    tap_im = taps[:, 1]
    step_count = slowness.shape[0]
    states = []
    current = wavefield
    for level in range(step_count):
        extended = extended_2(current, (("xy", 2),), 2)
        acc_re, acc_im = apply_stencil(extended, tap_re, tap_im)
        phase_re, phase_im = phase_parts(freqs, slowness[level])
        next_re = phase_re * acc_re - phase_im * acc_im
        next_im = phase_re * acc_im + phase_im * acc_re
        current = jnp.stack([next_re, next_im], axis=1)
        states.append(current)
    stacked = jnp.stack(states, axis=1)
    image_part = (
        jnp.sum(stacked[:, :, 0] * stacked[:, :, 0] + stacked[:, :, 1] * stacked[:, :, 1], axis=0)
        / freq_total
    )
    return (stacked, states[-1], image_part)


def backward_steps(adjoint, states, freqs, taps, slowness, perturbation, freq_total):
    tap_re = taps[:, 0]
    tap_im = taps[:, 1]
    step_count = slowness.shape[0]
    parts = [None] * step_count
    for level in reversed(range(step_count)):
        wave_re = states[:, level, 0]
        wave_im = states[:, level, 1]
        grad_re = adjoint[:, 0] + 2.0 * perturbation[level] * wave_re
        grad_im = adjoint[:, 1] + 2.0 * perturbation[level] * wave_im
        parts[level] = (
            layer_thickness
            / freq_total
            * jnp.sum(freqs[:, None, None] * (grad_im * wave_re - grad_re * wave_im), axis=0)
        )
        phase_re, phase_im = phase_parts(freqs, slowness[level])
        back_re = phase_re * grad_re + phase_im * grad_im
        back_im = phase_re * grad_im - phase_im * grad_re
        extended = extended_2(jnp.stack([back_re, back_im], axis=1), (("xy", 2),), 2)
        acc_re, acc_im = adjoint_stencil(extended, tap_re, tap_im)
        adjoint = jnp.stack([acc_re, acc_im], axis=1)
    return (adjoint, jnp.stack(parts, axis=0))


def on_device(surface_data, frequencies, coefficients, slowness, perturbation):
    freq_count = frequencies.shape[0]
    step_count = slowness.shape[0]
    row_count = slowness.shape[1]
    col_count = slowness.shape[2]
    layers = lax.axis_size("depth")
    depth_index = lax.axis_index("depth")
    stored_zero = jnp.zeros((freq_count, step_count, 2, row_count, col_count), jnp.float32)
    plane_zero = jnp.zeros((step_count, row_count, col_count), jnp.float32)
    start = jnp.where(depth_index == 0, surface_data, jnp.zeros_like(surface_data))

    def forward_segment(segment_no, carry):
        current, stored, image_sum = carry
        states, bottom, image_part = forward_steps(
            current, frequencies, coefficients, slowness, freq_count
        )
        chosen = depth_index == segment_no
        stored = jnp.where(chosen, states, stored)
        image_sum = jnp.where(chosen, image_part, image_sum)
        current = shifted(bottom, "depth", 1)
        return (current, stored, image_sum)

    unused_field, stored, image_field = lax.fori_loop(
        0, layers, forward_segment, (start, stored_zero, plane_zero)
    )

    def backward_segment(segment_no, carry):
        adjoint, gradient_sum = carry
        top_field, parts = backward_steps(
            adjoint, stored, frequencies, coefficients, slowness, perturbation, freq_count
        )
        gradient_sum = jnp.where(depth_index == layers - 1 - segment_no, parts, gradient_sum)
        adjoint = shifted(top_field, "depth", -1)
        return (adjoint, gradient_sum)

    adjoint_zero = jnp.zeros_like(surface_data)
    unused_adjoint, gradient = lax.fori_loop(
        0, layers, backward_segment, (adjoint_zero, plane_zero)
    )
    return (gradient, image_field)


ROWS = 16
HALO_TILES = 4
LANES = 128

OVERLAP = 8

sin_terms = (0.9999999995, -0.1666666515, 0.008333256964, -0.0001982776292, 2.657952479e-06)
cos_terms = (0.9999999947, -0.4999998344, 0.04166583045, -0.00138740917, 2.372928386e-05)


def window_row(tile, sub):
    group = tile - 2
    above = sub - 4 * (group + 1)
    below = sub + ROWS + 4 * group
    even = jnp.where(sub < 4, below, above - 4)
    odd = jnp.where(sub < 4, above, below - 4)
    halo = jnp.where(lax.rem(tile, 2) == 0, even, odd)
    return jnp.where(tile < 2, 8 * tile + sub, halo)


def band_kernel(plane_rows, taps, freqs, bands, back_bands, freq_tiles):
    first_row = lax.axis_index("xy") * ROWS

    def fill(ref, adjoint):
        out_tiles = ref.shape[1] // 48
        in_tiles = ref.shape[2] // 48
        shape = (16, ref.shape[2])
        col = lax.broadcasted_iota(jnp.int32, shape, 1)
        sub = lax.broadcasted_iota(jnp.int32, shape, 0)
        tile_k = sum((col >= 48 * t).astype(jnp.int32) for t in range(1, in_tiles))
        row_k = window_row(tile_k, col & 7)
        part_k = (col >> 4) - 3 * tile_k
        plane_k = (col >> 3) & 1
        plane_m = sub >> 3
        same = plane_k == plane_m
        inside_k = (row_k + first_row >= 0) & (row_k + first_row < plane_rows)
        for tile in range(out_tiles):
            row_m = window_row(jnp.full(shape, tile, jnp.int32), sub & 7)
            inside = inside_k & (row_m + first_row >= 0) & (row_m + first_row < plane_rows)
            offset = jnp.where(inside, row_k - row_m, 9)
            hits = [offset == a - 2 for a in range(5)]
            for f in range(ref.shape[0]):
                for b in range(3):
                    total = jnp.zeros(shape, jnp.float32)
                    for a in range(5):
                        tap = 3 * (4 - a) + 2 - b if adjoint else 3 * a + b
                        re = taps[f, 0, tap]
                        im = -taps[f, 1, tap] if adjoint else taps[f, 1, tap]
                        crossed = jnp.where(plane_m == 0, -im, im)
                        total = jnp.where(hits[a], jnp.where(same, re, crossed), total)
                    high = total.astype(jnp.bfloat16)
                    low = total - high.astype(jnp.float32)
                    base = 48 * tile + 16 * b
                    ref[f, base : base + 16] = jnp.where(part_k == 1, low, total).astype(jnp.bfloat16)

    fill(bands, False)
    fill(back_bands, True)
    for f in range(freq_tiles.shape[0]):
        freq_tiles[f] = jnp.full((8, LANES), freqs[f], jnp.float32)


def pack_rows(ref, values, side):
    lane = lax.broadcasted_iota(jnp.int32, (8, LANES), 1)
    overlaps = jnp.zeros((8, LANES), jnp.float32)
    blocks = (values[0].shape[1] - LANES) // LANES
    for n, value in enumerate(values):
        for block in range(blocks):
            ref[blocks * n + block] = value[:, (block + side) * LANES : (block + side + 1) * LANES]
        extra = value[:, : LANES] if side else value[:, blocks * LANES :]
        turn = (OVERLAP * (n + side)) % LANES
        extra = pltpu.roll(extra, turn, 1) if turn else extra
        overlaps = jnp.where((lane >= OVERLAP * n) & (lane < OVERLAP * (n + 1)), extra, overlaps)
    ref[blocks * len(values)] = overlaps


def unpack_rows(ref, tiles, n, side):
    blocks = (ref.shape[0] - 1) // tiles
    turn = (-OVERLAP * (n + side)) % LANES
    extra = ref[blocks * tiles]
    extra = pltpu.roll(extra, turn, 1) if turn else extra
    parts = [ref[blocks * n + block] for block in range(blocks)]
    return jnp.concatenate([extra] + parts if side else parts + [extra], axis=1)


def edge_levels(levels, slow, pert, down):
    inner, outer = (1, 0) if down else (0, 1)
    if levels == 1:
        return [slow(0, inner), pert(1, inner), pert(0, inner)]
    row = lax.broadcasted_iota(jnp.int32, slow(0, 0).shape, 0)
    turned = pltpu.roll(slow(1, outer), 4, 0)
    if down:
        extra = jnp.where(row < 2, pltpu.roll(pert(1, inner), 2, 0), turned)
        last = jnp.where(row < 4, extra, slow(0, outer))
    else:
        extra = jnp.where(row >= 6, pltpu.roll(pert(1, inner), 6, 0), turned)
        last = jnp.where(row < 4, slow(0, outer), extra)
    return [slow(0, inner), slow(1, inner), last]


def edge_surface(surf, down):
    inner, outer = (1, 0) if down else (0, 1)
    tiles = [surf(plane, inner) for plane in range(4)]
    row = lax.broadcasted_iota(jnp.int32, tiles[0].shape, 0)
    spread = surf(3, outer)
    for plane in range(3):
        turn = 6 - 2 * plane
        free = row < 2 if down else row >= 6
        tiles.append(jnp.where(free, pltpu.roll(spread, turn, 0), surf(plane, outer)))
    return tiles


def surface_edges(tiles, down):
    row = lax.broadcasted_iota(jnp.int32, tiles[0].shape, 0)
    outer = [tiles[4], tiles[5], tiles[6]]
    first = 2 if down else 0
    spread = pltpu.roll(tiles[6], 6, 0)
    spread = jnp.where((row >= first + 2) & (row < first + 4), pltpu.roll(tiles[5], 4, 0), spread)
    spread = jnp.where((row >= first) & (row < first + 2), pltpu.roll(tiles[4], 2, 0), spread)
    outer.append(spread)
    return [(tiles[plane], outer[plane]) for plane in range(4)]


def pack_kernel(width, step, surf_in, slow_in, pert_in, cross, bulk, cross_far, window, surf, slow, pert, sems):
    copies = [
        pltpu.make_async_copy(source, target, sems.at[n])
        for n, (source, target) in enumerate(((slow_in, slow), (pert_in, pert), (surf_in, surf)))
    ]
    for copy in copies:
        copy.start()
    for copy in copies:
        copy.wait()
    depth = lax.axis_index("depth")
    place = lax.axis_index("xy")
    for own in range(2):

        def reader(ref, side):
            lanes = slice(side * step, side * step + width)
            return lambda level, tile: ref[level, 8 * tile : 8 * tile + 8, lanes]

        def surface(plane, tile):
            return surf[plane // 2, plane % 2, 8 * tile : 8 * tile + 8, own * step : own * step + width]

        @pl.when(depth == own)
        def _():
            slow_near, pert_near = reader(slow, own), reader(pert, own)
            slow_far, pert_far = reader(slow, 1 - own), reader(pert, 1 - own)
            both = [(level, tile) for level in range(2) for tile in range(2)]
            for n, (level, tile) in enumerate(both):
                window[8 + n] = slow_near(level, tile)
                window[12 + n] = pert_near(level, tile)
            for plane in range(4):
                for tile in range(2):
                    window[2 * plane + tile] = surface(plane, tile)
            pack_rows(bulk, [slow_far(*at) for at in both] + [pert_far(*at) for at in both], 1 - own)
            for down in (False, True):

                @pl.when((lax.rem(place, 2) == 1) == down)
                def _():
                    edges = edge_surface(surface, down) + edge_levels(own, slow_near, pert_near, down)
                    pack_rows(cross, edges, own)
                    pack_rows(cross_far, edge_levels(own, slow_far, pert_far, down), 1 - own)


def relay_kernel(window, bulk, chip, partner):
    depth = lax.axis_index("depth")
    place = lax.axis_index("xy")
    for own in range(2):

        @pl.when(depth == own)
        def _():
            other = [unpack_rows(bulk, 8, n, own) for n in range(8)]
            for n in range(8):
                partner[n] = other[n]
            readers = {
                own: (lambda level, tile: window[8 + 2 * level + tile], lambda level, tile: window[12 + 2 * level + tile]),
                1 - own: (lambda level, tile: other[2 * level + tile], lambda level, tile: other[4 + 2 * level + tile]),
            }
            for down in (False, True):

                @pl.when((lax.rem(place, 2) == 0) == down)
                def _():
                    edges = edge_surface(lambda plane, tile: window[2 * plane + tile], down)
                    for levels in (own, 1 - own):
                        edges = edges + edge_levels(levels, *readers[levels], down)
                    pack_rows(chip, edges, own)


def phase(half):
    square = half * half
    cosine = cos_terms[-1]
    sine = sin_terms[-1]
    for term in cos_terms[-2::-1]:
        cosine = cosine * square + term
    for term in sin_terms[-2::-1]:
        sine = sine * square + term
    sine = sine * half
    twice = sine + sine
    return 1.0 - twice * sine, twice * cosine


def own_phases_kernel(freq_tiles, window, partner, phases):
    depth = lax.axis_index("depth")
    for level in range(4):
        for tile in range(2):
            own, other = window[8 + 2 * (level % 2) + tile], partner[2 * (level % 2) + tile]
            slow = jnp.where(depth == level // 2, own, other)
            for f in range(2):
                cosine, sine = phase(over_columns(freq_tiles[f], slow) * 0.25 * slow)
                phases[f, level, tile, :8] = cosine
                phases[f, level, tile, 8:] = sine


def over_columns(tile, like):
    return jnp.concatenate([tile] * (like.shape[1] // LANES), axis=1)


def sweep_kernel(
    width, freq_tiles, bands, back_bands, own_phases, window, partner, cross, cross_far, chip,
    mine, theirs, slow_win, pert_win, operand, halo_phases, fields, image_win, grad_win,
):
    depth = lax.axis_index("depth")
    place = lax.axis_index("xy")
    half = width - LANES
    row = lax.broadcasted_iota(jnp.int32, (8, width), 0)
    upper = row < 4
    lane = lax.broadcasted_iota(jnp.int32, (16, LANES), 1)
    even = lax.rem(place, 2) == 0
    freqs = [jnp.concatenate([freq_tiles[f]] * (width // LANES), axis=1) for f in range(2)]

    def store_operand(f, tile, value):
        high = value.astype(jnp.bfloat16)
        low = (value - high.astype(jnp.float32)).astype(jnp.bfloat16)
        base = 48 * tile
        operand[f, base : base + 16] = high
        operand[f, base + 16 : base + 32] = high
        operand[f, base + 32 : base + 48] = low

    def multiply(f, matrix, out_tiles, in_tiles):
        inner_tiles = min(in_tiles, 5)
        product = jnp.dot(
            matrix[f, : 48 * out_tiles, : 48 * inner_tiles],
            operand[f, : 48 * inner_tiles],
            preferred_element_type=jnp.float32,
        )
        slabs = [product[16 * n : 16 * n + 16] for n in range(3 * out_tiles)]
        if in_tiles > inner_tiles:
            outer = jnp.dot(
                matrix[f, 48 * (out_tiles - 1) : 48 * out_tiles, 48 * inner_tiles : 48 * in_tiles],
                operand[f, 48 * inner_tiles : 48 * in_tiles],
                preferred_element_type=jnp.float32,
            )
            for n in range(3):
                slabs[3 * out_tiles - 3 + n] += outer[16 * n : 16 * n + 16]
        return slabs

    def combine(slabs):
        result = []
        for tile in range(len(slabs) // 3):
            before, same, after = slabs[3 * tile : 3 * tile + 3]
            left = pltpu.roll(before, 1, 1)
            right = pltpu.roll(after, width - 1, 1)
            left = jnp.concatenate([jnp.where(lane == 0, 0.0, left[:, :LANES]), left[:, LANES:]], axis=1)
            right = jnp.concatenate([right[:, :half], jnp.where(lane == LANES - 1, 0.0, right[:, half:])], axis=1)
            result.append(same + left + right)
        return result

    def fill(own, below_is_chip):
        chip_edges = [unpack_rows(chip, 13, n, own) for n in range(13)]
        cross_edges = [unpack_rows(cross, 10, n, own) for n in range(10)]
        cross_edges += [unpack_rows(cross_far, 3, n, own) for n in range(3)]
        above, below = (cross_edges, chip_edges) if below_is_chip else (chip_edges, cross_edges)
        for level in range(2):
            for tile in range(2):
                pert_win[2 * own + level, tile] = window[12 + 2 * level + tile]
                pert_win[2 * (1 - own) + level, tile] = partner[4 + 2 * level + tile]
        at = (7, 10) if own == 0 else (10, 7)
        up, down = above[at[0] : at[0] + 3], below[at[0] : at[0] + 3]
        for level in range(2):
            slow_win[level, 0] = jnp.where(upper, down[level], up[level])
            slow_win[level, 1] = jnp.where(upper, up[level], down[level])
        slow_win[0, 2] = jnp.where(upper, down[2], up[2])
        slow_win[1, 2] = pltpu.roll(jnp.where(upper, up[2], down[2]), 4, 0)
        pert_win[1, 2] = jnp.where(
            row < 2, pltpu.roll(down[2], 2, 0), jnp.where(row >= 6, pltpu.roll(up[2], 6, 0), 0.0)
        )
        up, down = above[at[1] : at[1] + 3], below[at[1] : at[1] + 3]
        slow_win[2, 0] = jnp.where(upper, down[0], up[0])
        slow_win[2, 1] = jnp.where(upper, up[0], down[0])
        pert_win[3, 2] = jnp.where(upper, down[1], up[1])
        pert_win[3, 3] = jnp.where(upper, up[1], down[1])
        pert_win[2, 2] = jnp.where(upper, down[2], up[2])
        up, down = surface_edges(above[:7], True), surface_edges(below[:7], False)
        planes = []
        for plane in range(4):
            up_inner, up_outer = up[plane]
            down_inner, down_outer = down[plane]
            planes.append(
                [
                    window[2 * plane],
                    window[2 * plane + 1],
                    jnp.where(upper, down_inner, up_inner),
                    jnp.where(upper, up_inner, down_inner),
                    jnp.where(upper, down_outer, up_outer),
                    jnp.where(upper, up_outer, down_outer),
                ]
            )
        for f in range(2):
            for tile in range(6):
                store_operand(f, tile, jnp.concatenate([planes[2 * f][tile], planes[2 * f + 1][tile]], axis=0))

    for own in range(2):
        for below_is_chip in (False, True):

            @pl.when((depth == own) & (even == below_is_chip))
            def _():
                fill(own, below_is_chip)

    def add_image(f, level, tile, re, im):
        part = (re * re + im * im) * 0.5
        image_win[level, tile] = part if f == 0 else image_win[level, tile] + part

    def add_gradient(f, level, tile, w_re, w_im, u_re, u_im):
        part = (0.25 * freqs[f]) * (w_im * u_re - w_re * u_im)
        grad_win[level, tile] = part if f == 0 else grad_win[level, tile] + part

    def phases_of(f, level, tile):
        if tile < 2:
            return own_phases[f, level, tile, :8], own_phases[f, level, tile, 8:]
        cosine, sine = phase(freqs[f] * 0.25 * slow_win[level, tile - 2])
        if tile == 2 and level > 0:
            halo_phases[f, level - 1, :8] = cosine
            halo_phases[f, level - 1, 8:] = sine
        return cosine, sine

    def step_forward(level):
        def finish(f, values):
            for tile, value in enumerate(values):
                cosine, sine = phases_of(f, level, tile)
                v_re, v_im = value[:8], value[8:]
                re = cosine * v_re - sine * v_im
                im = cosine * v_im + sine * v_re
                both = jnp.concatenate([re, im], axis=0)
                store_operand(f, tile, both)
                if tile < 3:
                    fields[f, level, tile] = both
                if tile < 2:
                    add_image(f, level, tile, re, im)

        return finish

    def turn(f, values):
        for tile, value in enumerate(values):
            twice = 2.0 * pert_win[3, tile]
            v_re, v_im = value[:8], value[8:]
            if tile < 2:
                cosine, sine = phases_of(f, 3, tile)
                re = cosine * v_re - sine * v_im
                im = cosine * v_im + sine * v_re
                add_image(f, 3, tile, re, im)
                add_gradient(f, 3, tile, twice * re, twice * im, re, im)
            store_operand(f, tile, jnp.concatenate([twice * v_re, twice * v_im], axis=0))

    def step_back(level):
        def finish(f, values):
            for tile, value in enumerate(values):
                twice = 2.0 * pert_win[level, tile]
                u_re, u_im = fields[f, level, tile, :8], fields[f, level, tile, 8:]
                w_re = value[:8] + twice * u_re
                w_im = value[8:] + twice * u_im
                if tile < 2:
                    add_gradient(f, level, tile, w_re, w_im, u_re, u_im)
                if level > 0:
                    if tile < 2:
                        cosine, sine = phases_of(f, level, tile)
                    else:
                        cosine, sine = halo_phases[f, level - 1, :8], halo_phases[f, level - 1, 8:]
                    back = [cosine * w_re + sine * w_im, cosine * w_im - sine * w_re]
                    store_operand(f, tile, jnp.concatenate(back, axis=0))

        return finish

    steps = [
        (bands, 5, 6, step_forward(0)),
        (bands, 5, 5, step_forward(1)),
        (bands, 4, 5, step_forward(2)),
        (bands, 4, 4, turn),
        (back_bands, 3, 4, step_back(2)),
        (back_bands, 3, 3, step_back(1)),
        (back_bands, 2, 3, step_back(0)),
    ]
    work = [(f,) + step for step in steps for f in range(2)]
    slabs = multiply(*work[0][:4])
    for n, (f, matrix, out_tiles, in_tiles, finish) in enumerate(work):
        following = multiply(*work[n + 1][:4]) if n + 1 < len(work) else None
        finish(f, combine(slabs))
        slabs = following

    for own in range(2):

        @pl.when(depth == own)
        def _():
            inner = slice(own * LANES, own * LANES + half)
            for level in range(2):
                for tile in range(2):
                    rows = slice(8 * tile, 8 * tile + 8)
                    mine[0, level, rows] = grad_win[2 * own + level, tile, :, inner]
                    mine[1, level, rows] = image_win[2 * own + level, tile, :, inner]
                    theirs[0, level, rows] = grad_win[2 * (1 - own) + level, tile, :, inner]
                    theirs[1, level, rows] = image_win[2 * (1 - own) + level, tile, :, inner]


def place_kernel(mine, received, gradient, image, sems):
    half = mine.shape[3]
    depth = lax.axis_index("depth")
    copies = []
    for n, whole in enumerate((gradient, image)):
        for m, (part, side) in enumerate(((mine, depth), (received, 1 - depth))):
            lanes = pl.ds(pl.multiple_of(side * half, LANES), half)
            copies.append(pltpu.make_async_copy(part.at[n], whole.at[:, :, lanes], sems.at[2 * n + m]))
    for copy in copies:
        copy.start()
    for copy in copies:
        copy.wait()


def split_columns(surface_data, frequencies, coefficients, slowness, perturbation):
    count = lax.axis_size("xy")
    columns = slowness.shape[2]
    half = columns // 2
    width = half + LANES
    step = half - LANES
    f32 = jnp.float32
    axes = ("depth", "xy")

    def moved(value, other_depth, neighbour):
        pairs = []
        for depth in range(2):
            for place in range(count):
                target = {"chip": place ^ 1, "cross": place + 1 if place % 2 else place - 1, "same": place}[neighbour]
                if 0 <= target < count:
                    layer = 1 - depth if other_depth else depth
                    pairs.append((depth * count + place, layer * count + target))
        return lax.ppermute(value, axes, pairs)

    vmem = pl.BlockSpec(memory_space=pltpu.VMEM)
    smem = pl.BlockSpec(memory_space=pltpu.SMEM)
    tile = lambda n: jax.ShapeDtypeStruct((n, 8, width), f32)
    packed = lambda n: jax.ShapeDtypeStruct((n * half // LANES + 1, 8, LANES), f32)
    params = lambda mib: pltpu.CompilerParams(vmem_limit_bytes=mib * 2**20)
    cross, bulk, cross_far, window = pl.pallas_call(
        lambda *refs: pack_kernel(width, step, *refs),
        out_shape=(packed(10), packed(8), packed(3), tile(16)),
        in_specs=[pl.BlockSpec(memory_space=pltpu.HBM)] * 3,
        out_specs=(vmem,) * 4,
        scratch_shapes=[
            pltpu.VMEM(surface_data.shape, f32),
            pltpu.VMEM(slowness.shape, f32),
            pltpu.VMEM(perturbation.shape, f32),
            pltpu.SemaphoreType.DMA((3,)),
        ],
        compiler_params=params(32),
        name="pack",
    )(*(pltpu.with_memory_space_constraint(x, pltpu.HBM) for x in (surface_data, slowness, perturbation)))
    cross = moved(cross, False, "cross")
    bulk = moved(bulk, True, "same")
    cross_far = moved(cross_far, True, "cross")
    bands, back_bands, freq_tiles = pl.pallas_call(
        lambda *refs: band_kernel(count * ROWS, *refs),
        out_shape=(
            jax.ShapeDtypeStruct((2, 240, 288), jnp.bfloat16),
            jax.ShapeDtypeStruct((2, 144, 192), jnp.bfloat16),
            jax.ShapeDtypeStruct((2, 8, LANES), f32),
        ),
        in_specs=[smem] * 2,
        out_specs=(vmem,) * 3,
        compiler_params=params(16),
        cost_estimate=pl.CostEstimate(flops=10**10, bytes_accessed=10**6, transcendentals=0),
        name="bands",
    )(coefficients, frequencies)
    chip, partner = pl.pallas_call(
        relay_kernel,
        out_shape=(packed(13), tile(8)),
        in_specs=[vmem] * 2,
        out_specs=(vmem,) * 2,
        compiler_params=params(32),
        cost_estimate=pl.CostEstimate(flops=10**10, bytes_accessed=10**6, transcendentals=0),
        name="relay",
    )(window, bulk)
    chip = moved(chip, False, "chip")

    own_phases = pl.pallas_call(
        own_phases_kernel,
        out_shape=jax.ShapeDtypeStruct((2, 4, 2, 16, width), f32),
        in_specs=[vmem] * 3,
        out_specs=vmem,
        compiler_params=params(16),
        name="own_phases",
    )(freq_tiles, window, partner)

    own = jax.ShapeDtypeStruct((2, ROWS, columns), f32)
    mine, theirs = pl.pallas_call(
        lambda *refs: sweep_kernel(width, *refs),
        out_shape=(jax.ShapeDtypeStruct((2, 2, ROWS, half), f32),) * 2,
        in_specs=[vmem] * 9,
        out_specs=(vmem,) * 2,
        scratch_shapes=[
            pltpu.VMEM((3, 3, 8, width), f32),
            pltpu.VMEM((4, 4, 8, width), f32),
            pltpu.VMEM((2, 288, width), jnp.bfloat16),
            pltpu.VMEM((2, 2, 16, width), f32),
            pltpu.VMEM((2, 3, 3, 16, width), f32),
            pltpu.VMEM((4, 2, 8, width), f32),
            pltpu.VMEM((4, 2, 8, width), f32),
        ],
        compiler_params=params(40),
        name="sweep",
    )(
        freq_tiles, bands, back_bands, own_phases, window, partner, cross, cross_far, chip,
    )
    received = moved(theirs, True, "same")
    start = lax.axis_index("depth") * half
    whole = jnp.zeros((2, ROWS, columns), f32)
    at = [lax.dynamic_update_slice(whole, mine[n], (0, 0, start)) for n in range(2)]
    return tuple(lax.dynamic_update_slice(at[n], received[n], (0, 0, half - start)) for n in range(2))


def on_slice(surface_data, frequencies, coefficients, slowness, perturbation):
    levels, rows, columns = slowness.shape
    fits = (
        lax.axis_size("depth") == 2
        and levels == 2
        and rows == ROWS
        and frequencies.shape[0] == 2
        and lax.axis_size("xy") % 2 == 0
        and columns % (2 * LANES) == 0
        and columns >= 4 * LANES
    )
    plan = split_columns if fits else on_device
    return plan(surface_data, frequencies, coefficients, slowness, perturbation)


def solution(mesh):
    in_specs = (P(None, None, "xy", None), P(), P(), P("depth", "xy", None), P("depth", "xy", None))
    out_specs = (P("depth", "xy", None), P("depth", "xy", None))
    return jax.shard_map(
        on_slice, mesh=mesh, in_specs=in_specs, out_specs=out_specs, check_vma=False
    )
```
